32 devices in a mesh: paths: 2 (over x), qa: 8 (over z, y), qb: 2 (over core).
Axes of the slice: x: 2, y: 2, z: 4, core: 2. Of those that a mesh axis runs over, the one named last changes fastest.
Arguments:
- state: float32 [2, 4194304], P(None, ('paths', 'qa', 'qb')), parts along dimension 1, may hold values from -6 to 6
- gate_terms: float32 [18, 2, 2, 128, 128], replicated, may hold values from -0.375 to 0.375
- path_bits: int32 [36], P('paths'), parts along dimension 0, may hold values from 0 to 1
Outputs:
- final_state: float32 [2, 4194304], P(None, ('paths', 'qa', 'qb')), parts along dimension 1
The draws below stay inside these ranges and needn't reach their ends.
There are 2 independent parts, one for each index of `paths`. The reference program is written for one: setup_inputs(seed, part) draws one part's arguments, and reference() takes and returns one part's arrays. A program takes and returns all parts, laid end to end along the dimension named above; an argument that names none is the same for every part. Nothing has to cross between parts.
All inputs are finite; a program needn't handle non-finite values.
Results may differ from the reference program's by a relative error of at most 0.00013.
Values sent between devices are 32-bit elements; how exact they have to be, the bound alone decides.
No kernel may reach another device: no remote copies, remote signals or barrier semaphores. Data moves between devices by JAX's collectives and lax.ppermute only.
A program may use at most 64 MiB of HBM per device.

```python
import jax
import jax.numpy as jnp
from jax import lax

LOCAL = 17
GQ = 7
GDIM = 128
TERMS = 2
NGATES = 18
AMPS = 2097152
N_QA = 8


def plant(entries, stream_key, least, largest):
    longest = entries.shape.index(max(entries.shape))
    spots = []
    for shift in (0, 1):
        where = [jax.random.randint(jax.random.fold_in(stream_key, axis), (), 0, length) for axis, length in enumerate(entries.shape)]
        where[longest] = (where[longest] + shift) % entries.shape[longest]
        spots.append(tuple(where))
    return entries.at[spots[0]].set(least).at[spots[1]].set(largest)


def level_of(rng, dims, cuts, least, largest):
    level = 1.0
    for axis_at, blocks in cuts:
        steps = jax.random.uniform(jax.random.fold_in(jax.random.fold_in(rng, 6), axis_at), (blocks,), jnp.float32, least / len(cuts), largest / len(cuts))
        level = level * jnp.repeat(jnp.exp(steps), dims[axis_at] // blocks).reshape((-1,) + (1,) * (len(dims) - 1 - axis_at))
    return level


def normal_values(key, extent, spread, limit, split=(), kind=jnp.bfloat16):
    array = spread * jax.random.normal(key, extent, jnp.float32)
    if split:
        array = array * level_of(key, extent, split, -0.22, 0.18)
    return jnp.clip(array, -limit, limit).astype(kind)


def setup_inputs(seed: int = 0, part: int = 0) -> dict:
    key_list = jax.random.split(jax.random.key(seed), 4)
    part_keys = jax.random.split(jax.random.fold_in(key_list[3], part), 4)
    return {
        "state": normal_values(part_keys[0], (2, AMPS), 1.0, 6.0, ((1, 16),), jnp.float32),
        "gate_terms": normal_values(key_list[1], (NGATES, TERMS, 2, GDIM, GDIM), (2 * GDIM) ** -0.5, 0.375, (), jnp.float32),
        "path_bits": plant(jax.random.randint(part_keys[2], (NGATES,), 0, TERMS), jax.random.fold_in(part_keys[2], 1), 0, TERMS - 1).astype(jnp.int32),
    }


def window_offsets(span, gate_bits):
    return [0, span, gate_bits, span - 1, gate_bits + 1, span - 2]


def swap_bits(amplitudes, lower, upper, how_many):
    total_bits = amplitudes.shape[1].bit_length() - 1
    shaped = amplitudes.reshape(2, 2 ** (total_bits - upper - how_many), 2 ** how_many, 2 ** (upper - lower - how_many), 2 ** how_many, 2 ** lower)
    return jnp.swapaxes(shaped, 2, 4).reshape(2, -1)


def apply_gate(amplitudes, matrix, offset):
    gate_dim = matrix.shape[-1]
    blocked = jnp.stack([jnp.stack([matrix[0], -matrix[1]]), jnp.stack([matrix[1], matrix[0]])])
    shaped = amplitudes.reshape(2, -1, gate_dim, 2 ** offset)
    result = jnp.einsum("pqrc,qhcl->phrl", blocked, shaped, precision=lax.Precision.HIGHEST)
    return result.reshape(2, -1)


def reference(state, gate_terms, path_bits):
    local_bits = LOCAL
    qa_bits = N_QA.bit_length() - 1
    outer_span = local_bits - GQ
    inner_span = local_bits - GQ - 1
    gates = gate_terms[jnp.arange(NGATES, dtype=jnp.int32), path_bits.astype(jnp.int32)]
    amplitudes = swap_bits(state, local_bits - qa_bits, local_bits + 1, qa_bits)
    for index, offset in enumerate(window_offsets(outer_span, GQ)):
        amplitudes = apply_gate(amplitudes, gates[index], offset)
    amplitudes = swap_bits(amplitudes, local_bits - 2 * qa_bits, local_bits + 1, qa_bits)
    for index, offset in enumerate(window_offsets(inner_span, GQ)):
        amplitudes = apply_gate(amplitudes, gates[6 + index], offset)
    amplitudes = swap_bits(amplitudes, local_bits - 1, local_bits, 1)
    for index, offset in enumerate(window_offsets(outer_span, GQ)):
        amplitudes = apply_gate(amplitudes, gates[12 + index], offset)
    return amplitudes
```

```python
import functools

import jax
import jax.numpy as jnp
from jax import lax
from jax.experimental import pallas as pl
from jax.experimental.pallas import tpu as pltpu
from jax.sharding import PartitionSpec as P

F32 = jnp.float32
BF16 = jnp.bfloat16
VMEM_LIMIT = 48 * 1024 * 1024


def window_offsets(span, gate_bits):
    return [0, span, gate_bits, span - 1, gate_bits + 1, span - 2]


def plan_gates(local_bits, gate_bits):
    outer = window_offsets(local_bits - gate_bits, gate_bits)
    inner = window_offsets(local_bits - gate_bits - 1, gate_bits)
    low, sections = [], []
    for number, offsets in enumerate((outer, inner, outer)):
        section = []
        for index, offset in enumerate(offsets):
            gate = 6 * number + index
            if offset == 0:
                low.append(gate)
            elif section and section[-1][0] == offset:
                section[-1][1].append(gate)
            else:
                section.append((offset, [gate]))
        sections.append(section)
    return low, sections


def exact_dot(a, b):
    return lax.dot_general(
        a, b, (((1,), (0,)), ((), ())), precision=lax.Precision.HIGHEST, preferred_element_type=F32
    )


def split(x):
    high = x.astype(BF16)
    return high, (x - high.astype(F32)).astype(BF16)


def bf_dot(a, b):
    return jnp.dot(a, b, preferred_element_type=F32)


def prepare_kernel(low, products, bits_ref, gates_ref, low_ref, rows_ref, held, sems):
    count = held.shape[0]
    copies = []
    for gate in range(count):
        copy = pltpu.make_async_copy(gates_ref.at[gate, bits_ref[gate]], held.at[gate], sems.at[gate])
        copy.start()
        copies.append(copy)
    for copy in copies:
        copy.wait()

    def block(real, imag):
        return jnp.concatenate(
            [jnp.concatenate([real, -imag], axis=1), jnp.concatenate([imag, real], axis=1)], axis=0
        )

    def product(gates):
        real, imag = held[gates[0], 0], held[gates[0], 1]
        for gate in gates[1:]:
            column = exact_dot(block(held[gate, 0], held[gate, 1]), jnp.concatenate([real, imag], axis=0))
            half = column.shape[0] // 2
            real, imag = column[:half], column[half:]
        return real, imag

    real, imag = product(low)
    real, imag = real.T, imag.T
    high, rest = split(block(real, -imag))
    low_ref[0], low_ref[1] = high, rest
    for slot, gates in enumerate(products):
        high, rest = split(block(*product(gates)))
        rows_ref[slot, 0], rows_ref[slot, 1] = high, rest


def three_dots(high_w, rest_w, x):
    high, rest = split(x)
    return bf_dot(high_w, rest) + bf_dot(rest_w, high) + bf_dot(high_w, high)


def apply_rows(weights_ref, slot, offset, lane_bits, rows, load, store):
    dim = weights_ref.shape[-1] // 2
    stride = 2 ** (offset - lane_bits)
    starts = [h * dim * stride + l for h in range(rows // (dim * stride)) for l in range(stride)]
    high_w, rest_w = weights_ref[slot, 0], weights_ref[slot, 1]
    for pair in range(0, len(starts), 2):
        group = starts[pair : pair + 2]
        x = jnp.concatenate(
            [jnp.concatenate([load(part, start, stride) for start in group], axis=1) for part in range(2)],
            axis=0,
        )
        y = three_dots(high_w, rest_w, x)
        lanes = y.shape[1] // len(group)
        for part in range(2):
            for place, start in enumerate(group):
                store(part, start, stride, y[part * dim : (part + 1) * dim, place * lanes : (place + 1) * lanes])


def run_gates(section, first_slot, weights_ref, lane_bits, buffers, last_store):
    dim = weights_ref.shape[-1] // 2
    rows = buffers[0].shape[1]

    def loader(ref):
        return lambda part, start, stride: ref[part, pl.ds(start, dim, stride=stride), :]

    def storer(ref):
        def store(part, start, stride, value):
            ref[part, pl.ds(start, dim, stride=stride), :] = value

        return store

    now = 0
    for index, (offset, _) in enumerate(section):
        last = index == len(section) - 1
        store = last_store if last and last_store is not None else storer(buffers[1 - now])
        apply_rows(weights_ref, first_slot + index, offset, lane_bits, rows, loader(buffers[now]), store)
        now = 1 - now
    return now


def first_kernel(section, lane_bits, x_ref, low_ref, rows_ref, out_ref, one, two):
    rows = one.shape[1]
    lanes = one.shape[2]
    step = 256
    for start in range(0, rows, step):
        real = x_ref[pl.ds(2 * start, step, stride=2), :]
        imag = x_ref[pl.ds(2 * start + 1, step, stride=2), :]
        high, rest = split(jnp.concatenate([real, imag], axis=1))
        y = bf_dot(rest, low_ref[0]) + bf_dot(high, low_ref[1]) + bf_dot(high, low_ref[0])
        one[0, pl.ds(start, step), :] = y[:, :lanes]
        one[1, pl.ds(start, step), :] = y[:, lanes:]
    buffers = (one, two)
    now = run_gates(section, 0, rows_ref, lane_bits, buffers, None)
    done = buffers[now]
    dests, tops, mids, _, inner, _ = out_ref.shape
    for top in range(tops):
        for mid in range(mids):
            for dest in range(dests):
                start = ((top * mids + mid) * dests + dest) * inner
                for part in range(2):
                    out_ref[dest, top, mid, part] = done[part, pl.ds(start, inner), :]


def second_kernel(section, lane_bits, x_ref, rows_ref, out_ref, one, two):
    dim = rows_ref.shape[-1] // 2
    dests, tops, mids, _, inner, _ = x_ref.shape
    for top in range(tops):
        for mid in range(mids):
            for dest in range(dests):
                start = ((top * mids + mid) * dests + dest) * inner
                for part in range(2):
                    one[part, pl.ds(start, inner), :] = x_ref[dest, top, mid, part]

    def last_store(part, start, stride, value):
        out_ref[pl.ds(2 * start + part, dim, stride=2 * stride), :] = value

    run_gates(section, 0, rows_ref, lane_bits, (one, two), last_store)


def in_vmem(count):
    return [pl.BlockSpec(memory_space=pltpu.VMEM)] * count


def matmul_cost(matmuls, order, columns, moved):
    return pl.CostEstimate(flops=matmuls * 3 * 2 * order * order * columns, bytes_accessed=moved, transcendentals=0)


def per_device(state, gate_terms, path_bits):
    amps_local = state.shape[1]
    local_bits = amps_local.bit_length() - 1
    dim = gate_terms.shape[-1]
    gate_bits = dim.bit_length() - 1
    lanes = dim
    lane_bits = gate_bits
    rows = amps_local // lanes
    qa = lax.axis_size("qa")
    qb = lax.axis_size("qb")
    low, sections = plan_gates(local_bits, gate_bits)
    head = sections[0]
    tail = sections[1] + sections[2]
    products = [gates for _, gates in head + tail]
    order = 2 * dim

    params = pltpu.CompilerParams(vmem_limit_bytes=VMEM_LIMIT)
    low_w, rows_w = pl.pallas_call(
        functools.partial(prepare_kernel, low, products),
        out_shape=(
            jax.ShapeDtypeStruct((2, order, order), BF16),
            jax.ShapeDtypeStruct((len(products), 2, order, order), BF16),
        ),
        in_specs=[pl.BlockSpec(memory_space=pltpu.SMEM), pl.BlockSpec(memory_space=pl.ANY)],
        out_specs=tuple(in_vmem(2)),
        scratch_shapes=[
            pltpu.VMEM((gate_terms.shape[0], 2, dim, dim), F32),
            pltpu.SemaphoreType.DMA((gate_terms.shape[0],)),
        ],
        compiler_params=params,
        cost_estimate=matmul_cost(10, order, order, 6 * 2**20),
        name="prepare_gates",
    )(path_bits, gate_terms)

    amplitudes = state.reshape(2, rows, lanes).swapaxes(0, 1).reshape(qa, 2 * rows // qa, lanes)
    amplitudes = lax.all_to_all(amplitudes, "qa", split_axis=0, concat_axis=0, tiled=True)

    inner = rows // (qa * qa)
    view = (qa, qb, qa // qb, 2, inner, lanes)
    buffers = [pltpu.VMEM((2, rows, lanes), F32)] * 2
    amplitudes = pl.pallas_call(
        functools.partial(first_kernel, head, lane_bits),
        out_shape=jax.ShapeDtypeStruct(view, F32),
        in_specs=in_vmem(3),
        out_specs=in_vmem(1)[0],
        scratch_shapes=buffers,
        compiler_params=params,
        cost_estimate=matmul_cost(len(head) + 1, order, rows, 4 * 2**20),
        name="first_section",
    )(amplitudes.reshape(2 * rows, lanes), low_w, rows_w[: len(head)])

    amplitudes = amplitudes.reshape(qa * qb, 2 * rows // (qa * qb), lanes)
    amplitudes = lax.all_to_all(amplitudes, ("qa", "qb"), split_axis=0, concat_axis=0, tiled=True)

    amplitudes = pl.pallas_call(
        functools.partial(second_kernel, tail, lane_bits),
        out_shape=jax.ShapeDtypeStruct((2 * rows, lanes), F32),
        in_specs=in_vmem(2),
        out_specs=in_vmem(1)[0],
        scratch_shapes=buffers,
        compiler_params=params,
        cost_estimate=matmul_cost(len(tail), order, rows, 4 * 2**20),
        name="later_sections",
    )(amplitudes.reshape(view), rows_w[len(head) :])
    return amplitudes.reshape(rows, 2, lanes).swapaxes(0, 1).reshape(2, amps_local)


def solution(mesh):
    return jax.shard_map(
        per_device,
        mesh=mesh,
        in_specs=(P(None, ("paths", "qa", "qb")), P(), P("paths")),
        out_specs=P(None, ("paths", "qa", "qb")),
        check_vma=False,
    )
```

```python
import functools

import jax
import jax.numpy as jnp
from jax import lax
from jax.experimental import pallas as pl
from jax.experimental.layout import Layout, with_layout_constraint
from jax.experimental.pallas import tpu as pltpu
from jax.sharding import PartitionSpec as P

F32 = jnp.float32
BF16 = jnp.bfloat16
VMEM_LIMIT = 48 * 1024 * 1024
CHUNKS = 2


def window_offsets(span, gate_bits):
    return [0, span, gate_bits, span - 1, gate_bits + 1, span - 2]


def plan_gates(local_bits, gate_bits):
    outer = window_offsets(local_bits - gate_bits, gate_bits)
    inner = window_offsets(local_bits - gate_bits - 1, gate_bits)
    low, sections = [], []
    for number, offsets in enumerate((outer, inner, outer)):
        section = []
        for index, offset in enumerate(offsets):
            gate = 6 * number + index
            if offset == 0:
                low.append(gate)
            elif section and section[-1][0] == offset:
                section[-1][1].append(gate)
            else:
                section.append((offset, [gate]))
        sections.append(section)
    return low, sections


def exact_dot(a, b):
    return lax.dot_general(
        a, b, (((1,), (0,)), ((), ())), precision=lax.Precision.HIGHEST, preferred_element_type=F32
    )


def split(x):
    high = x.astype(BF16)
    return high, (x - high.astype(F32)).astype(BF16)


def bf_dot(a, b):
    return jnp.dot(a, b, preferred_element_type=F32)


def prepare_kernel(low, heads, tails, bits_ref, gates_ref, low_ref, heads_ref, tails_ref, held, sems):
    copies = []
    for gate in range(held.shape[0]):
        copy = pltpu.make_async_copy(gates_ref.at[gate, bits_ref[gate]], held.at[gate], sems.at[gate])
        copy.start()
        copies.append(copy)
    for copy in copies:
        copy.wait()

    def block(real, imag):
        return jnp.concatenate(
            [jnp.concatenate([real, -imag], axis=1), jnp.concatenate([imag, real], axis=1)], axis=0
        )

    def product(gates):
        real, imag = held[gates[0], 0], held[gates[0], 1]
        for gate in gates[1:]:
            column = exact_dot(block(held[gate, 0], held[gate, 1]), jnp.concatenate([real, imag], axis=0))
            half = column.shape[0] // 2
            real, imag = column[:half], column[half:]
        return real, imag

    for target, products in ((heads_ref, heads), (tails_ref, tails)):
        for slot, gates in enumerate(products):
            high, rest = split(jnp.concatenate(product(gates), axis=1))
            target[slot] = jnp.concatenate([high, rest], axis=0)
    real, imag = product(low)
    dim = real.shape[0]
    part = dim // CHUNKS
    whole = block(real.T, -imag.T)
    pieces = []
    for chunk in range(CHUNKS):
        pieces += [whole[chunk * part : (chunk + 1) * part], whole[dim + chunk * part : dim + (chunk + 1) * part]]
    low_ref[0], low_ref[1] = split(jnp.concatenate(pieces, axis=0))


def pack_kernel(chunk, x_ref, out_ref):
    rows, lanes = out_ref.shape
    half = lanes // 2
    step = min(rows, 256)
    for start in range(0, rows, step):
        real = x_ref[pl.ds(2 * start, step, stride=2), :]
        imag = x_ref[pl.ds(2 * start + 1, step, stride=2), :]
        left = lax.broadcasted_iota(jnp.int32, real.shape, 1) < half
        if chunk == 0:
            value = jnp.where(left, real, pltpu.roll(imag, half, 1))
        else:
            value = jnp.where(left, pltpu.roll(real, half, 1), imag)
        out_ref[pl.ds(start, step), :] = value


def apply_rows(weights, offset, lane_bits, source, target):
    dim = weights.shape[0] // 2
    rows, lanes = source.shape
    stride = 2 ** (offset - lane_bits)
    starts = [h * dim * stride + l for h in range(rows // (dim * stride)) for l in range(stride)]
    high_w = weights[:dim]
    for pair in range(0, len(starts), 2):
        group = starts[pair : pair + 2]
        plain, turned = [], []
        for start in group:
            x = source[pl.ds(start, dim, stride=stride), :]
            left = lax.broadcasted_iota(jnp.int32, x.shape, 1) < lanes // 2
            moved = pltpu.roll(x, lanes // 2, 1)
            plain.append(x)
            turned.append(jnp.where(left, -moved, moved))
        x = jnp.concatenate([jnp.concatenate(plain, axis=1), jnp.concatenate(turned, axis=1)], axis=0)
        high, rest = split(x)
        both = bf_dot(weights, high)
        y = bf_dot(high_w, rest) + both[dim:] + both[:dim]
        for place, start in enumerate(group):
            target[pl.ds(start, dim, stride=stride), :] = y[:, place * lanes : (place + 1) * lanes]


def run_gates(section, weights_ref, lane_bits, source, buffers, target):
    for index, (offset, _) in enumerate(section):
        into = target if index == len(section) - 1 else buffers[index % 2]
        apply_rows(weights_ref[index], offset, lane_bits, source, into)
        source = into


def blocks_of(view):
    dests, tops, mids, inner, _ = view
    for top in range(tops):
        for mid in range(mids):
            for dest in range(dests):
                yield dest, top, mid, ((top * mids + mid) * dests + dest) * inner


def head_kernel(section, lane_bits, x_ref, weights_ref, out_ref, one, two):
    run_gates(section, weights_ref, lane_bits, x_ref, (one, two), two)
    inner = out_ref.shape[3]
    for dest, top, mid, start in blocks_of(out_ref.shape):
        out_ref[dest, top, mid] = two[pl.ds(start, inner), :]


def tail_rows(section, lane_bits, x_ref, weights_ref, one, two, target):
    inner = x_ref.shape[3]
    for dest, top, mid, start in blocks_of(x_ref.shape):
        two[pl.ds(start, inner), :] = x_ref[dest, top, mid]
    run_gates(section, weights_ref, lane_bits, two, (one, two), target)


def tail_kernel(section, lane_bits, x_ref, weights_ref, out_ref, one, two):
    tail_rows(section, lane_bits, x_ref, weights_ref, one, two, out_ref)


def last_kernel(section, lane_bits, x_ref, weights_ref, low_ref, other_ref, out_ref, one, two, three):
    tail_rows(section, lane_bits, x_ref, weights_ref, one, two, three)
    rows, lanes = three.shape
    step = min(rows, 256)
    for start in range(0, rows, step):
        high, rest = split(jnp.concatenate([other_ref[pl.ds(start, step), :], three[pl.ds(start, step), :]], axis=1))
        y = bf_dot(rest, low_ref[0]) + bf_dot(high, low_ref[1]) + bf_dot(high, low_ref[0])
        out_ref[pl.ds(2 * start, step, stride=2), :] = y[:, :lanes]
        out_ref[pl.ds(2 * start + 1, step, stride=2), :] = y[:, lanes:]


def in_vmem(count):
    return [pl.BlockSpec(memory_space=pltpu.VMEM)] * count


def call(kernel, name, out_shapes, in_specs, scratch, matmuls, *operands):
    many = isinstance(out_shapes, tuple)
    return pl.pallas_call(
        kernel,
        out_shape=out_shapes,
        in_specs=in_specs,
        out_specs=tuple(in_vmem(len(out_shapes))) if many else in_vmem(1)[0],
        scratch_shapes=scratch,
        compiler_params=pltpu.CompilerParams(vmem_limit_bytes=VMEM_LIMIT),
        cost_estimate=pl.CostEstimate(
            flops=matmuls * 3 * 2 * 128 * 256 * 1024, bytes_accessed=4 * 2**20, transcendentals=0
        ),
        name=name,
    )(*operands)


def per_device(state, gate_terms, path_bits):
    amps_local = state.shape[1]
    local_bits = amps_local.bit_length() - 1
    dim = gate_terms.shape[-1]
    gate_bits = dim.bit_length() - 1
    lanes = dim
    lane_bits = gate_bits
    rows = amps_local // lanes
    qa = lax.axis_size("qa")
    qb = lax.axis_size("qb")
    low, sections = plan_gates(local_bits, gate_bits)
    head = sections[0]
    tail = sections[1] + sections[2]

    low_w, head_w, tail_w = call(
        functools.partial(prepare_kernel, low, [g for _, g in head], [g for _, g in tail]),
        "prepare_gates",
        (
            jax.ShapeDtypeStruct((2, 2 * dim, 2 * dim), BF16),
            jax.ShapeDtypeStruct((len(head), 2 * dim, 2 * dim), BF16),
            jax.ShapeDtypeStruct((len(tail), 2 * dim, 2 * dim), BF16),
        ),
        [pl.BlockSpec(memory_space=pltpu.SMEM), pl.BlockSpec(memory_space=pl.ANY)],
        [
            pltpu.VMEM((gate_terms.shape[0], 2, dim, dim), F32),
            pltpu.SemaphoreType.DMA((gate_terms.shape[0],)),
        ],
        4,
        path_bits,
        gate_terms,
    )

    state = with_layout_constraint(state.reshape(2, rows, lanes), Layout(major_to_minor=(1, 0, 2)))
    state = state.swapaxes(0, 1).reshape(2 * rows, lanes)
    inner = rows // (qa * qa)
    view = (qa, qb, qa // qb, inner, lanes)
    buffer = pltpu.VMEM((rows, lanes), F32)

    packed = []
    for chunk in range(CHUNKS):
        piece = call(
            functools.partial(pack_kernel, chunk),
            f"pack_{chunk}",
            jax.ShapeDtypeStruct((rows, lanes), F32),
            in_vmem(1),
            [],
            0,
            state,
        )
        packed.append(piece.reshape(qa, rows // qa, lanes))
    arrived = [lax.all_to_all(piece, "qa", split_axis=0, concat_axis=0, tiled=True) for piece in packed]
    halfway = []
    for chunk in range(CHUNKS):
        piece = call(
            functools.partial(head_kernel, head, lane_bits),
            f"first_section_{chunk}",
            jax.ShapeDtypeStruct(view, F32),
            in_vmem(2),
            [buffer] * 2,
            len(head),
            arrived[chunk].reshape(rows, lanes),
            head_w,
        )
        piece = lax.all_to_all(
            piece.reshape(qa * qb, rows // (qa * qb), lanes), ("qa", "qb"), split_axis=0, concat_axis=0, tiled=True
        )
        halfway.append(piece.reshape(view))
    done = call(
        functools.partial(tail_kernel, tail, lane_bits),
        "later_sections_0",
        jax.ShapeDtypeStruct((rows, lanes), F32),
        in_vmem(2),
        [buffer] * 2,
        len(tail),
        halfway[0],
        tail_w,
    )
    final = call(
        functools.partial(last_kernel, tail, lane_bits),
        "later_sections_1",
        jax.ShapeDtypeStruct((2 * rows, lanes), F32),
        in_vmem(4),
        [buffer] * 3,
        len(tail) + 2,
        halfway[1],
        tail_w,
        low_w,
        done,
    )
    return final.reshape(rows, 2, lanes).swapaxes(0, 1).reshape(2, amps_local)


def solution(mesh):
    return jax.shard_map(
        per_device,
        mesh=mesh,
        in_specs=(P(None, ("paths", "qa", "qb")), P(), P("paths")),
        out_specs=P(None, ("paths", "qa", "qb")),
        check_vma=False,
    )
```

```python
import functools

import jax
import jax.numpy as jnp
from jax import lax
from jax.experimental import pallas as pl
from jax.experimental.layout import Layout, with_layout_constraint
from jax.experimental.pallas import tpu as pltpu
from jax.sharding import PartitionSpec as P

F32 = jnp.float32
BF16 = jnp.bfloat16
VMEM_LIMIT = 48 * 1024 * 1024
CHUNKS = 2


def window_offsets(span, gate_bits):
    return [0, span, gate_bits, span - 1, gate_bits + 1, span - 2]


def plan_gates(local_bits, gate_bits):
    outer = window_offsets(local_bits - gate_bits, gate_bits)
    inner = window_offsets(local_bits - gate_bits - 1, gate_bits)
    low, sections = [], []
    for number, offsets in enumerate((outer, inner, outer)):
        section = []
        for index, offset in enumerate(offsets):
            gate = 6 * number + index
            if offset == 0:
                low.append(gate)
            elif section and section[-1][0] == offset:
                section[-1][1].append(gate)
            else:
                section.append((offset, [gate]))
        sections.append(section)
    return low, sections


def exact_dot(a, b):
    return lax.dot_general(
        a, b, (((1,), (0,)), ((), ())), precision=lax.Precision.HIGHEST, preferred_element_type=F32
    )


def split(x):
    high = x.astype(BF16)
    return high, (x - high.astype(F32)).astype(BF16)


def bf_dot(a, b):
    return jnp.dot(a, b, preferred_element_type=F32)


def prepare_kernel(low, heads, tails, bits_ref, gates_ref, low_ref, heads_ref, tails_ref, held, sems):
    copies = []
    for gate in range(held.shape[0]):
        copy = pltpu.make_async_copy(gates_ref.at[gate, bits_ref[gate]], held.at[gate], sems.at[gate])
        copy.start()
        copies.append(copy)
    for copy in copies:
        copy.wait()

    def block(real, imag):
        return jnp.concatenate(
            [jnp.concatenate([real, -imag], axis=1), jnp.concatenate([imag, real], axis=1)], axis=0
        )

    def product(gates):
        real, imag = held[gates[0], 0], held[gates[0], 1]
        for gate in gates[1:]:
            column = exact_dot(block(held[gate, 0], held[gate, 1]), jnp.concatenate([real, imag], axis=0))
            half = column.shape[0] // 2
            real, imag = column[:half], column[half:]
        return real, imag

    for target, products in ((heads_ref, heads), (tails_ref, tails)):
        for slot, gates in enumerate(products):
            high, rest = split(jnp.concatenate(product(gates), axis=1))
            target[slot] = jnp.concatenate([high, rest], axis=0)
    real, imag = product(low)
    dim = real.shape[0]
    part = dim // CHUNKS
    whole = block(real.T, -imag.T)
    pieces = []
    for chunk in range(CHUNKS):
        pieces += [whole[chunk * part : (chunk + 1) * part], whole[dim + chunk * part : dim + (chunk + 1) * part]]
    low_ref[0], low_ref[1] = split(jnp.concatenate(pieces, axis=0))


def pack_kernel(chunk, x_ref, *outs):
    me = lax.axis_index("qa")
    for distance, out_ref in enumerate(outs):
        block = jnp.bitwise_xor(me, distance)
        rows, lanes = out_ref.shape
        half = lanes // 2
        real = x_ref[block, pl.ds(0, rows, stride=2), :]
        imag = x_ref[block, pl.ds(1, rows, stride=2), :]
        left = lax.broadcasted_iota(jnp.int32, real.shape, 1) < half
        if chunk == 0:
            out_ref[...] = jnp.where(left, real, pltpu.roll(imag, half, 1))
        else:
            out_ref[...] = jnp.where(left, pltpu.roll(real, half, 1), imag)


def apply_rows(weights, offset, lane_bits, source, target):
    dim = weights.shape[0] // 2
    rows, lanes = source.shape
    stride = 2 ** (offset - lane_bits)
    starts = [h * dim * stride + l for h in range(rows // (dim * stride)) for l in range(stride)]
    high_w = weights[:dim]
    for pair in range(0, len(starts), 2):
        group = starts[pair : pair + 2]
        plain, turned = [], []
        for start in group:
            x = source[pl.ds(start, dim, stride=stride), :]
            left = lax.broadcasted_iota(jnp.int32, x.shape, 1) < lanes // 2
            moved = pltpu.roll(x, lanes // 2, 1)
            plain.append(x)
            turned.append(jnp.where(left, -moved, moved))
        x = jnp.concatenate([jnp.concatenate(plain, axis=1), jnp.concatenate(turned, axis=1)], axis=0)
        high, rest = split(x)
        both = bf_dot(weights, high)
        y = bf_dot(high_w, rest) + both[dim:] + both[:dim]
        for place, start in enumerate(group):
            target[pl.ds(start, dim, stride=stride), :] = y[:, place * lanes : (place + 1) * lanes]


def run_gates(section, weights_ref, lane_bits, source, buffers, target):
    for index, (offset, _) in enumerate(section):
        into = target if index == len(section) - 1 else buffers[index % 2]
        apply_rows(weights_ref[index], offset, lane_bits, source, into)
        source = into


def head_kernel(section, lane_bits, *refs):
    *blocks, weights_ref, keep_ref, send_ref, one, two = refs
    me = lax.axis_index("qa")
    size = blocks[0].shape[0]
    for distance, block_ref in enumerate(blocks):
        start = pl.multiple_of(jnp.bitwise_xor(me, distance) * size, size)
        one[pl.ds(start, size), :] = block_ref[...]
    run_gates(section, weights_ref, lane_bits, one, (two, one), two)
    half = two.shape[0] // 2
    core = lax.axis_index("qb")
    mine = pl.multiple_of(core * half, half)
    other = pl.multiple_of((1 - core) * half, half)
    keep_ref[...] = two[pl.ds(mine, half), :]
    send_ref[...] = two[pl.ds(other, half), :]


def middle_kernel(section, first, lane_bits, keep_ref, came_ref, weights_ref, *refs):
    *outs, one, two = refs
    half = keep_ref.shape[0]
    core = lax.axis_index("qb")
    one[pl.ds(pl.multiple_of(core * half, half), half), :] = keep_ref[...]
    one[pl.ds(pl.multiple_of((1 - core) * half, half), half), :] = came_ref[...]
    run_gates(section, weights_ref.at[pl.ds(first, len(section))], lane_bits, one, (two, one), two)
    me = lax.axis_index("qa")
    count = len(outs)
    for distance, out_ref in enumerate(outs):
        dest = jnp.bitwise_xor(me, distance)
        inner = out_ref.shape[1]
        for outer in range(out_ref.shape[0]):
            start = pl.multiple_of((outer * count + dest) * inner, inner)
            out_ref[outer] = two[pl.ds(start, inner), :]


def tail_rows(section, lane_bits, blocks, weights_ref, one, two, target):
    me = lax.axis_index("qa")
    count = len(blocks)
    for distance, block_ref in enumerate(blocks):
        source = jnp.bitwise_xor(me, distance)
        inner = block_ref.shape[1]
        for outer in range(block_ref.shape[0]):
            start = pl.multiple_of((outer * count + source) * inner, inner)
            two[pl.ds(start, inner), :] = block_ref[outer]
    run_gates(section, weights_ref, lane_bits, two, (one, two), target)


def tail_kernel(section, lane_bits, *refs):
    *blocks, weights_ref, out_ref, one, two = refs
    tail_rows(section, lane_bits, blocks, weights_ref, one, two, out_ref)


def last_kernel(section, lane_bits, *refs):
    *blocks, weights_ref, low_ref, other_ref, out_ref, one, two, three = refs
    tail_rows(section, lane_bits, blocks, weights_ref, one, two, three)
    rows, lanes = three.shape
    step = min(rows, 256)
    for start in range(0, rows, step):
        high, rest = split(jnp.concatenate([other_ref[pl.ds(start, step), :], three[pl.ds(start, step), :]], axis=1))
        y = bf_dot(rest, low_ref[0]) + bf_dot(high, low_ref[1]) + bf_dot(high, low_ref[0])
        out_ref[pl.ds(2 * start, step, stride=2), :] = y[:, :lanes]
        out_ref[pl.ds(2 * start + 1, step, stride=2), :] = y[:, lanes:]


def in_vmem(count):
    return [pl.BlockSpec(memory_space=pltpu.VMEM)] * count


def call(kernel, name, out_shapes, in_specs, scratch, matmuls, *operands):
    many = isinstance(out_shapes, tuple)
    return pl.pallas_call(
        kernel,
        out_shape=out_shapes,
        in_specs=in_specs,
        out_specs=tuple(in_vmem(len(out_shapes))) if many else in_vmem(1)[0],
        scratch_shapes=scratch,
        compiler_params=pltpu.CompilerParams(vmem_limit_bytes=VMEM_LIMIT),
        cost_estimate=pl.CostEstimate(
            flops=matmuls * 3 * 2 * 128 * 256 * 1024, bytes_accessed=4 * 2**20, transcendentals=0
        ),
        name=name,
    )(*operands)


def per_device(state, gate_terms, path_bits):
    amps_local = state.shape[1]
    local_bits = amps_local.bit_length() - 1
    dim = gate_terms.shape[-1]
    gate_bits = dim.bit_length() - 1
    lanes = dim
    lane_bits = gate_bits
    rows = amps_local // lanes
    qa = lax.axis_size("qa")
    qb = lax.axis_size("qb")
    low, sections = plan_gates(local_bits, gate_bits)
    head = sections[0]
    tail = sections[1] + sections[2]

    low_w, head_w, tail_w = call(
        functools.partial(prepare_kernel, low, [g for _, g in head], [g for _, g in tail]),
        "prepare_gates",
        (
            jax.ShapeDtypeStruct((2, 2 * dim, 2 * dim), BF16),
            jax.ShapeDtypeStruct((len(head), 2 * dim, 2 * dim), BF16),
            jax.ShapeDtypeStruct((len(tail), 2 * dim, 2 * dim), BF16),
        ),
        [pl.BlockSpec(memory_space=pltpu.SMEM), pl.BlockSpec(memory_space=pl.ANY)],
        [
            pltpu.VMEM((gate_terms.shape[0], 2, dim, dim), F32),
            pltpu.SemaphoreType.DMA((gate_terms.shape[0],)),
        ],
        4,
        path_bits,
        gate_terms,
    )

    state = with_layout_constraint(state.reshape(2, rows, lanes), Layout(major_to_minor=(1, 0, 2)))
    state = state.swapaxes(0, 1).reshape(qa, 2 * rows // qa, lanes)
    inner = rows // (qa * qa)
    buffer = pltpu.VMEM((rows, lanes), F32)
    reach = max(i for i, (offset, _) in enumerate(head) if offset + gate_bits == local_bits) + 1

    def exchange(blocks):
        came = list(blocks)
        for distance in reversed(range(1, qa)):
            came[distance] = lax.ppermute(blocks[distance], "qa", [(i, i ^ distance) for i in range(qa)])
        return came

    arrived = []
    for chunk in range(CHUNKS):
        blocks = call(
            functools.partial(pack_kernel, chunk),
            f"pack_{chunk}",
            (jax.ShapeDtypeStruct((rows // qa, lanes), F32),) * qa,
            in_vmem(1),
            [],
            0,
            state,
        )
        arrived.append(exchange(blocks))
    halfway = []
    for chunk in range(CHUNKS):
        keep, send = call(
            functools.partial(head_kernel, head[:reach], lane_bits),
            f"first_section_top_{chunk}",
            (jax.ShapeDtypeStruct((rows // 2, lanes), F32),) * 2,
            in_vmem(qa + 1),
            [buffer] * 2,
            reach,
            *arrived[chunk],
            head_w,
        )
        came = lax.ppermute(send, "qb", [(i, 1 - i) for i in range(qb)])
        blocks = call(
            functools.partial(middle_kernel, head[reach:], reach, lane_bits),
            f"first_section_rest_{chunk}",
            (jax.ShapeDtypeStruct((qa, inner, lanes), F32),) * qa,
            in_vmem(3),
            [buffer] * 2,
            len(head) - reach,
            keep,
            came,
            head_w,
        )
        halfway.append(exchange(blocks))
    done = call(
        functools.partial(tail_kernel, tail, lane_bits),
        "later_sections_0",
        jax.ShapeDtypeStruct((rows, lanes), F32),
        in_vmem(qa + 1),
        [buffer] * 2,
        len(tail),
        *halfway[0],
        tail_w,
    )
    final = call(
        functools.partial(last_kernel, tail, lane_bits),
        "later_sections_1",
        jax.ShapeDtypeStruct((2 * rows, lanes), F32),
        in_vmem(qa + 3),
        [buffer] * 3,
        len(tail) + 2,
        *halfway[1],
        tail_w,
        low_w,
        done,
    )
    return final.reshape(rows, 2, lanes).swapaxes(0, 1).reshape(2, amps_local)


def solution(mesh):
    return jax.shard_map(
        per_device,
        mesh=mesh,
        in_specs=(P(None, ("paths", "qa", "qb")), P(), P("paths")),
        out_specs=P(None, ("paths", "qa", "qb")),
        check_vma=False,
    )
```

```python
import functools

import jax
import jax.numpy as jnp
from jax import lax
from jax.experimental import pallas as pl
from jax.experimental.layout import Layout, with_layout_constraint
from jax.experimental.pallas import tpu as pltpu
from jax.sharding import PartitionSpec as P

F32 = jnp.float32
BF16 = jnp.bfloat16
VMEM_LIMIT = 48 * 1024 * 1024


def window_offsets(span, gate_bits):
    return [0, span, gate_bits, span - 1, gate_bits + 1, span - 2]


def plan_gates(local_bits, gate_bits):
    outer = window_offsets(local_bits - gate_bits, gate_bits)
    inner = window_offsets(local_bits - gate_bits - 1, gate_bits)
    low, sections = [], []
    for number, offsets in enumerate((outer, inner, outer)):
        section = []
        for index, offset in enumerate(offsets):
            gate = 6 * number + index
            if offset == 0:
                low.append(gate)
            elif section and section[-1][0] == offset:
                section[-1][1].append(gate)
            else:
                section.append((offset, [gate]))
        sections.append(section)
    return low, sections


def exact_dot(a, b):
    return lax.dot_general(
        a, b, (((1,), (0,)), ((), ())), precision=lax.Precision.HIGHEST, preferred_element_type=F32
    )


def split(x):
    high = x.astype(BF16)
    return high, (x - high.astype(F32)).astype(BF16)


def bf_dot(a, b):
    return jnp.dot(a, b, preferred_element_type=F32)


def prepare_kernel(low, heads, tails, bits_ref, gates_ref, low_ref, heads_ref, tails_ref, held, sems):
    count = held.shape[0]
    copies = []
    for gate in range(count):
        copy = pltpu.make_async_copy(gates_ref.at[gate, bits_ref[gate]], held.at[gate], sems.at[gate])
        copy.start()
        copies.append(copy)
    for copy in copies:
        copy.wait()

    def block(real, imag):
        return jnp.concatenate(
            [jnp.concatenate([real, -imag], axis=1), jnp.concatenate([imag, real], axis=1)], axis=0
        )

    def product(gates):
        real, imag = held[gates[0], 0], held[gates[0], 1]
        for gate in gates[1:]:
            column = exact_dot(block(held[gate, 0], held[gate, 1]), jnp.concatenate([real, imag], axis=0))
            half = column.shape[0] // 2
            real, imag = column[:half], column[half:]
        return real, imag

    real, imag = product(low)
    real, imag = real.T, imag.T
    high, rest = split(block(real, -imag))
    low_ref[0], low_ref[1] = high, rest
    for target, products in ((heads_ref, heads), (tails_ref, tails)):
        for slot, gates in enumerate(products):
            high, rest = split(block(*product(gates)))
            target[slot, 0], target[slot, 1] = high, rest


def three_dots(high_w, rest_w, x):
    high, rest = split(x)
    return bf_dot(high_w, rest) + bf_dot(rest_w, high) + bf_dot(high_w, high)


def apply_rows(weights_ref, slot, offset, lane_bits, rows, load, store):
    dim = weights_ref.shape[-1] // 2
    stride = 2 ** (offset - lane_bits)
    starts = [h * dim * stride + l for h in range(rows // (dim * stride)) for l in range(stride)]
    high_w, rest_w = weights_ref[slot, 0], weights_ref[slot, 1]
    for pair in range(0, len(starts), 2):
        group = starts[pair : pair + 2]
        x = jnp.concatenate(
            [jnp.concatenate([load(part, start, stride) for start in group], axis=1) for part in range(2)],
            axis=0,
        )
        y = three_dots(high_w, rest_w, x)
        lanes = y.shape[1] // len(group)
        for part in range(2):
            for place, start in enumerate(group):
                store(part, start, stride, y[part * dim : (part + 1) * dim, place * lanes : (place + 1) * lanes])


def run_gates(section, first_slot, weights_ref, lane_bits, buffers, last_store):
    dim = weights_ref.shape[-1] // 2
    rows = buffers[0].shape[1]

    def loader(ref):
        return lambda part, start, stride: ref[part, pl.ds(start, dim, stride=stride), :]

    def storer(ref):
        def store(part, start, stride, value):
            ref[part, pl.ds(start, dim, stride=stride), :] = value

        return store

    now = 0
    for index, (offset, _) in enumerate(section):
        last = index == len(section) - 1
        store = last_store if last and last_store is not None else storer(buffers[1 - now])
        apply_rows(weights_ref, first_slot + index, offset, lane_bits, rows, loader(buffers[now]), store)
        now = 1 - now
    return now


def first_kernel(section, lane_bits, x_ref, low_ref, rows_ref, out_hbm, one, two, out_ref, sem):
    rows = one.shape[1]
    lanes = one.shape[2]
    step = 256
    for start in range(0, rows, step):
        real = x_ref[pl.ds(2 * start, step, stride=2), :]
        imag = x_ref[pl.ds(2 * start + 1, step, stride=2), :]
        high, rest = split(jnp.concatenate([real, imag], axis=1))
        y = bf_dot(rest, low_ref[0]) + bf_dot(high, low_ref[1]) + bf_dot(high, low_ref[0])
        one[0, pl.ds(start, step), :] = y[:, :lanes]
        one[1, pl.ds(start, step), :] = y[:, lanes:]
    buffers = (one, two)
    now = run_gates(section, 0, rows_ref, lane_bits, buffers, None)
    done = buffers[now]
    dests, tops, mids, _, inner, _ = out_ref.shape
    for top in range(tops):
        for mid in range(mids):
            for dest in range(dests):
                start = ((top * mids + mid) * dests + dest) * inner
                for part in range(2):
                    out_ref[dest, top, mid, part] = done[part, pl.ds(start, inner), :]
    copy = pltpu.make_async_copy(out_ref, out_hbm, sem)
    copy.start()
    copy.wait()


def second_kernel(section, lane_bits, x_ref, rows_ref, out_ref, one, two):
    dim = rows_ref.shape[-1] // 2
    dests, tops, mids, _, inner, _ = x_ref.shape
    for top in range(tops):
        for mid in range(mids):
            for dest in range(dests):
                start = ((top * mids + mid) * dests + dest) * inner
                for part in range(2):
                    one[part, pl.ds(start, inner), :] = x_ref[dest, top, mid, part]

    def last_store(part, start, stride, value):
        out_ref[pl.ds(2 * start + part, dim, stride=2 * stride), :] = value

    run_gates(section, 0, rows_ref, lane_bits, (one, two), last_store)


def in_vmem(count):
    return [pl.BlockSpec(memory_space=pltpu.VMEM)] * count


def matmul_cost(matmuls, order, columns, moved):
    return pl.CostEstimate(flops=matmuls * 3 * 2 * order * order * columns, bytes_accessed=moved, transcendentals=0)


def per_device(state, gate_terms, path_bits):
    amps_local = state.shape[1]
    local_bits = amps_local.bit_length() - 1
    dim = gate_terms.shape[-1]
    gate_bits = dim.bit_length() - 1
    lanes = dim
    lane_bits = gate_bits
    rows = amps_local // lanes
    qa = lax.axis_size("qa")
    qb = lax.axis_size("qb")
    low, sections = plan_gates(local_bits, gate_bits)
    head = sections[0]
    tail = sections[1] + sections[2]
    order = 2 * dim

    params = pltpu.CompilerParams(vmem_limit_bytes=VMEM_LIMIT)
    low_w, head_w, tail_w = pl.pallas_call(
        functools.partial(prepare_kernel, low, [gates for _, gates in head], [gates for _, gates in tail]),
        out_shape=(
            jax.ShapeDtypeStruct((2, order, order), BF16),
            jax.ShapeDtypeStruct((len(head), 2, order, order), BF16),
            jax.ShapeDtypeStruct((len(tail), 2, order, order), BF16),
        ),
        in_specs=[pl.BlockSpec(memory_space=pltpu.SMEM), pl.BlockSpec(memory_space=pl.ANY)],
        out_specs=tuple(in_vmem(3)),
        scratch_shapes=[
            pltpu.VMEM((gate_terms.shape[0], 2, dim, dim), F32),
            pltpu.SemaphoreType.DMA((gate_terms.shape[0],)),
        ],
        compiler_params=params,
        cost_estimate=matmul_cost(10, order, order, 6 * 2**20),
        name="prepare_gates",
    )(path_bits, gate_terms)

    amplitudes = with_layout_constraint(state.reshape(2, rows, lanes), Layout(major_to_minor=(1, 0, 2)))
    amplitudes = amplitudes.swapaxes(0, 1).reshape(qa, 2 * rows // qa, lanes)
    amplitudes = lax.all_to_all(amplitudes, "qa", split_axis=0, concat_axis=0, tiled=True)

    inner = rows // (qa * qa)
    view = (qa, qb, qa // qb, 2, inner, lanes)
    buffers = [pltpu.VMEM((2, rows, lanes), F32)] * 2
    amplitudes = pl.pallas_call(
        functools.partial(first_kernel, head, lane_bits),
        out_shape=pltpu.HBM(view, F32),
        in_specs=in_vmem(3),
        out_specs=pl.BlockSpec(memory_space=pltpu.HBM),
        scratch_shapes=buffers + [pltpu.VMEM(view, F32), pltpu.SemaphoreType.DMA],
        compiler_params=params,
        cost_estimate=matmul_cost(len(head) + 1, order, rows, 4 * 2**20),
        name="first_section",
    )(amplitudes.reshape(2 * rows, lanes), low_w, head_w)

    amplitudes = amplitudes.reshape(qa * qb, 2 * rows // (qa * qb), lanes)
    amplitudes = lax.all_to_all(amplitudes, ("qa", "qb"), split_axis=0, concat_axis=0, tiled=True)

    amplitudes = pl.pallas_call(
        functools.partial(second_kernel, tail, lane_bits),
        out_shape=jax.ShapeDtypeStruct((2 * rows, lanes), F32),
        in_specs=in_vmem(2),
        out_specs=in_vmem(1)[0],
        scratch_shapes=buffers,
        compiler_params=params,
        cost_estimate=matmul_cost(len(tail), order, rows, 4 * 2**20),
        name="later_sections",
    )(amplitudes.reshape(view), tail_w)
    return amplitudes.reshape(rows, 2, lanes).swapaxes(0, 1).reshape(2, amps_local)


def solution(mesh):
    return jax.shard_map(
        per_device,
        mesh=mesh,
        in_specs=(P(None, ("paths", "qa", "qb")), P(), P("paths")),
        out_specs=P(None, ("paths", "qa", "qb")),
        check_vma=False,
    )
```

```python
import functools

import jax
import jax.numpy as jnp
from jax import lax
from jax.experimental import pallas as pl
from jax.experimental.layout import Layout, with_layout_constraint
from jax.experimental.pallas import tpu as pltpu
from jax.sharding import PartitionSpec as P

F32 = jnp.float32
BF16 = jnp.bfloat16
VMEM_LIMIT = 14 * 1024 * 1024
WHOLE_VMEM = 60 * 1024 * 1024


def window_offsets(span, gate_bits):
    return [0, span, gate_bits, span - 1, gate_bits + 1, span - 2]


def plan_gates(local_bits, gate_bits):
    outer = window_offsets(local_bits - gate_bits, gate_bits)
    inner = window_offsets(local_bits - gate_bits - 1, gate_bits)
    low, sections = [], []
    for number, offsets in enumerate((outer, inner, outer)):
        section = []
        for index, offset in enumerate(offsets):
            gate = 6 * number + index
            if offset == 0:
                low.append(gate)
            elif section and section[-1][0] == offset:
                section[-1][1].append(gate)
            else:
                section.append((offset, [gate]))
        sections.append(section)
    return low, sections


def exact_dot(a, b):
    return lax.dot_general(
        a, b, (((1,), (0,)), ((), ())), precision=lax.Precision.HIGHEST, preferred_element_type=F32
    )


def split(x):
    high = x.astype(BF16)
    return high, (x - high.astype(F32)).astype(BF16)


def bf_dot(a, b):
    return jnp.dot(a, b, preferred_element_type=F32)


def block(real, imag):
    return jnp.concatenate(
        [jnp.concatenate([real, -imag], axis=1), jnp.concatenate([imag, real], axis=1)], axis=0
    )


def prepare_kernel(low, sections, bits_ref, gates_ref, low_ref, *refs):
    *targets, held, sems = refs
    copies = []
    for gate in range(held.shape[0]):
        copy = pltpu.make_async_copy(gates_ref.at[gate, bits_ref[gate]], held.at[gate], sems.at[gate])
        copy.start()
        copies.append(copy)
    for copy in copies:
        copy.wait()

    def product(gates):
        real, imag = held[gates[0], 0], held[gates[0], 1]
        for gate in gates[1:]:
            column = exact_dot(block(held[gate, 0], held[gate, 1]), jnp.concatenate([real, imag], axis=0))
            half = column.shape[0] // 2
            real, imag = column[:half], column[half:]
        return real, imag

    real, imag = product(low)
    low_ref[0], low_ref[1] = split(block(real.T, -imag.T))
    for target, section in zip(targets, sections):
        for slot, (_, gates) in enumerate(section):
            target[slot, 0], target[slot, 1] = split(block(*product(gates)))


def distances_of(count):
    half = count // 2
    return [0, half - 1, *range(count - 1, half - 1, -1), *range(half - 2, 0, -1)]


def partner(distance):
    return jnp.bitwise_xor(lax.axis_index("qa"), distance)


def split_kernel(x_ref, *refs):
    *outs, sems = refs
    copies = []
    for place, distance in enumerate(distances_of(len(outs))):
        copy = pltpu.make_async_copy(x_ref.at[partner(distance)], outs[place], sems.at[place])
        copy.start()
        copies.append(copy)
    for copy in copies:
        copy.wait()


def apply_rows(weights_ref, slot, offset, lane_bits, rows, load, store):
    dim = weights_ref.shape[-1] // 2
    stride = 2 ** (offset - lane_bits)
    starts = [h * dim * stride + l for h in range(rows // (dim * stride)) for l in range(stride)]
    high_w, rest_w = weights_ref[slot, 0], weights_ref[slot, 1]
    for pair in range(0, len(starts), 2):
        group = starts[pair : pair + 2]
        x = jnp.concatenate(
            [jnp.concatenate([load(part, start, stride) for start in group], axis=1) for part in range(2)],
            axis=0,
        )
        high, rest = split(x)
        y = bf_dot(high_w, rest) + bf_dot(rest_w, high) + bf_dot(high_w, high)
        lanes = y.shape[1] // len(group)
        for part in range(2):
            for place, start in enumerate(group):
                store(part, start, stride, y[part * dim : (part + 1) * dim, place * lanes : (place + 1) * lanes])


def run_gates(section, weights_ref, lane_bits, buffers, last_store=None):
    dim = weights_ref.shape[-1] // 2
    rows = buffers[0].shape[1]

    def loader(ref):
        return lambda part, start, stride: ref[part, pl.ds(start, dim, stride=stride), :]

    def storer(ref):
        def store(part, start, stride, value):
            ref[part, pl.ds(start, dim, stride=stride), :] = value

        return store

    now = 0
    for index, (offset, _) in enumerate(section):
        last = index == len(section) - 1
        store = last_store if last and last_store is not None else storer(buffers[1 - now])
        apply_rows(weights_ref, index, offset, lane_bits, rows, loader(buffers[now]), store)
        now = 1 - now
    return now


def first_kernel(section, lane_bits, count, *refs):
    blocks, (low_ref, rows_ref), outs, (one, two) = (
        refs[:count],
        refs[count : count + 2],
        refs[count + 2 : -2],
        refs[-2:],
    )
    lanes = one.shape[2]
    for distance, block_ref in zip(distances_of(count), blocks):
        size = block_ref.shape[0] // 2
        start = pl.multiple_of(partner(distance) * size, size)
        real = block_ref[pl.ds(0, size, stride=2), :]
        imag = block_ref[pl.ds(1, size, stride=2), :]
        high, rest = split(jnp.concatenate([real, imag], axis=1))
        y = bf_dot(rest, low_ref[0]) + bf_dot(high, low_ref[1]) + bf_dot(high, low_ref[0])
        one[0, pl.ds(start, size), :] = y[:, :lanes]
        one[1, pl.ds(start, size), :] = y[:, lanes:]
    buffers = (one, two)
    done = buffers[run_gates(section, rows_ref, lane_bits, buffers)]
    for distance, out_ref in zip(distances_of(count), outs):
        dest = partner(distance)
        tops, mids, _, inner, _ = out_ref.shape
        for top in range(tops):
            for mid in range(mids):
                start = pl.multiple_of(((top * mids + mid) * count + dest) * inner, inner)
                for part in range(2):
                    out_ref[top, mid, part] = done[part, pl.ds(start, inner), :]


def second_kernel(section, lane_bits, count, stays, *refs):
    blocks, (rows_ref, out_ref, one, two) = refs[:count], refs[count:]
    core = lax.axis_index("qb")
    top = core if stays else 1 - core
    for distance, block_ref in zip(distances_of(count), blocks):
        source = partner(distance)
        _, mids, _, inner, _ = block_ref.shape
        for mid in range(mids):
            start = pl.multiple_of((mid * count + source) * inner, inner)
            for part in range(2):
                one[part, pl.ds(start, inner), :] = block_ref[top, mid, part]
    dim = rows_ref.shape[-1] // 2

    def last_store(part, start, stride, value):
        out_ref[part, pl.ds(start, dim, stride=stride), :] = value

    run_gates(section, rows_ref, lane_bits, (one, two), last_store)


def third_kernel(section, lane_bits, kept_ref, came_ref, rows_ref, out_ref, one, two):
    dim = rows_ref.shape[-1] // 2
    half = kept_ref.shape[1]
    core = lax.axis_index("qb")
    one[:, pl.ds(pl.multiple_of(core * half, half), half), :] = kept_ref[...]
    one[:, pl.ds(pl.multiple_of((1 - core) * half, half), half), :] = came_ref[...]

    def last_store(part, start, stride, value):
        out_ref[pl.ds(2 * start + part, dim, stride=2 * stride), :] = value

    run_gates(section, rows_ref, lane_bits, (one, two), last_store)


def call(kernel, name, out_shapes, in_specs, scratch, matmuls, *operands, limit=VMEM_LIMIT):
    many = isinstance(out_shapes, tuple)
    vmem = pl.BlockSpec(memory_space=pltpu.VMEM)
    return pl.pallas_call(
        kernel,
        out_shape=out_shapes,
        in_specs=in_specs,
        out_specs=(vmem,) * len(out_shapes) if many else vmem,
        scratch_shapes=scratch,
        compiler_params=pltpu.CompilerParams(vmem_limit_bytes=limit),
        cost_estimate=pl.CostEstimate(
            flops=int(matmuls * 3 * 2 * 256 * 256 * 1024), bytes_accessed=4 * 2**20, transcendentals=0
        ),
        name=name,
    )(*operands)


def per_device(state, gate_terms, path_bits):
    amps_local = state.shape[1]
    local_bits = amps_local.bit_length() - 1
    dim = gate_terms.shape[-1]
    gate_bits = dim.bit_length() - 1
    lanes, lane_bits = dim, gate_bits
    rows = amps_local // lanes
    qa = lax.axis_size("qa")
    qb = lax.axis_size("qb")
    low, sections = plan_gates(local_bits, gate_bits)
    order = 2 * dim
    vmem = pl.BlockSpec(memory_space=pltpu.VMEM)
    hbm = pl.BlockSpec(memory_space=pltpu.HBM)
    shape = jax.ShapeDtypeStruct

    state = with_layout_constraint(state.reshape(2, rows, lanes), Layout(major_to_minor=(1, 0, 2)))
    state = state.swapaxes(0, 1).reshape(qa, 2 * rows // qa, lanes)
    blocks = call(
        split_kernel,
        "split_state",
        (shape((2 * rows // qa, lanes), F32),) * qa,
        [hbm],
        [pltpu.SemaphoreType.DMA((qa,))],
        0,
        state,
        limit=WHOLE_VMEM,
    )

    def exchange(blocks):
        came = [blocks[0]]
        for distance, piece in zip(distances_of(qa)[1:], blocks[1:]):
            came.append(lax.ppermute(piece, "qa", [(i, i ^ distance) for i in range(qa)]))
        return came

    blocks = exchange(blocks)
    low_w, *weights = call(
        functools.partial(prepare_kernel, low, sections),
        "prepare_gates",
        (shape((2, order, order), BF16),) + tuple(shape((len(s), 2, order, order), BF16) for s in sections),
        [pl.BlockSpec(memory_space=pltpu.SMEM), hbm],
        [pltpu.VMEM((gate_terms.shape[0], 2, dim, dim), F32), pltpu.SemaphoreType.DMA((gate_terms.shape[0],))],
        4,
        path_bits,
        gate_terms,
    )
    inner = rows // (qa * qa)
    blocks = call(
        functools.partial(first_kernel, sections[0], lane_bits, qa),
        "first_section",
        (shape((qb, qa // qb, 2, inner, lanes), F32),) * qa,
        [vmem] * (qa + 2),
        [pltpu.VMEM((2, rows, lanes), F32)] * 2,
        len(sections[0]) + 1,
        *blocks,
        low_w,
        weights[0],
    )
    blocks = exchange(blocks)
    halves = []
    for stays in (False, True):
        halves.append(
            call(
                functools.partial(second_kernel, sections[1], lane_bits, qa, stays),
                "second_section_kept" if stays else "second_section_sent",
                shape((2, rows // qb, lanes), F32),
                [vmem] * (qa + 1),
                [pltpu.VMEM((2, rows // qb, lanes), F32)] * 2,
                len(sections[1]) / 2,
                *blocks,
                weights[1],
            )
        )
        if not stays:
            came = lax.ppermute(halves[0], "qb", [(i, 1 - i) for i in range(qb)])
    final = call(
        functools.partial(third_kernel, sections[2], lane_bits),
        "third_section",
        shape((2 * rows, lanes), F32),
        [vmem] * 3,
        [pltpu.VMEM((2, rows, lanes), F32)] * 2,
        len(sections[2]),
        halves[1],
        came,
        weights[2],
    )
    return final.reshape(rows, 2, lanes).swapaxes(0, 1).reshape(2, amps_local)


def solution(mesh):
    return jax.shard_map(
        per_device,
        mesh=mesh,
        in_specs=(P(None, ("paths", "qa", "qb")), P(), P("paths")),
        out_specs=P(None, ("paths", "qa", "qb")),
        check_vma=False,
    )
```

```python
import functools

import jax
import jax.numpy as jnp
from jax import lax
from jax.experimental import pallas as pl
from jax.experimental.layout import Layout, with_layout_constraint
from jax.experimental.pallas import tpu as pltpu
from jax.sharding import PartitionSpec as P

F32 = jnp.float32
BF16 = jnp.bfloat16
VMEM_LIMIT = 14 * 1024 * 1024
LARGE_VMEM = 48 * 1024 * 1024


def window_offsets(span, gate_bits):
    return [0, span, gate_bits, span - 1, gate_bits + 1, span - 2]


def plan_gates(local_bits, gate_bits):
    outer = window_offsets(local_bits - gate_bits, gate_bits)
    inner = window_offsets(local_bits - gate_bits - 1, gate_bits)
    low, sections = [], []
    for number, offsets in enumerate((outer, inner, outer)):
        section = []
        for index, offset in enumerate(offsets):
            gate = 6 * number + index
            if offset == 0:
                low.append(gate)
            elif section and section[-1][0] == offset:
                section[-1][1].append(gate)
            else:
                section.append((offset, [gate]))
        sections.append(section)
    return low, sections


def exact_dot(a, b):
    return lax.dot_general(
        a, b, (((1,), (0,)), ((), ())), precision=lax.Precision.HIGHEST, preferred_element_type=F32
    )


def split(x):
    high = x.astype(BF16)
    return high, (x - high.astype(F32)).astype(BF16)


def bf_dot(a, b):
    return jnp.dot(a, b, preferred_element_type=F32)


def block(real, imag):
    return jnp.concatenate(
        [jnp.concatenate([real, -imag], axis=1), jnp.concatenate([imag, real], axis=1)], axis=0
    )


def prepare_kernel(low, sections, bits_ref, gates_ref, low_ref, *refs):
    *targets, held, sems = refs
    copies = []
    for gate in range(held.shape[0]):
        copy = pltpu.make_async_copy(gates_ref.at[gate, bits_ref[gate]], held.at[gate], sems.at[gate])
        copy.start()
        copies.append(copy)
    for copy in copies:
        copy.wait()

    def product(gates):
        real, imag = held[gates[0], 0], held[gates[0], 1]
        for gate in gates[1:]:
            column = exact_dot(block(held[gate, 0], held[gate, 1]), jnp.concatenate([real, imag], axis=0))
            half = column.shape[0] // 2
            real, imag = column[:half], column[half:]
        return real, imag

    real, imag = product(low)
    low_ref[0], low_ref[1] = split(block(real.T, -imag.T))
    for target, section in zip(targets, sections):
        for slot, (_, gates) in enumerate(section):
            target[slot, 0], target[slot, 1] = split(block(*product(gates)))


def distances_of(count):
    return [0, *range(count - 1, 0, -1)]


def partner(distance):
    return jnp.bitwise_xor(lax.axis_index("qa"), distance)


def split_kernel(x_ref, *outs):
    for distance, out_ref in zip(distances_of(len(outs)), outs):
        out_ref[...] = x_ref[partner(distance)]


def apply_rows(weights_ref, slot, offset, lane_bits, rows, load, store):
    dim = weights_ref.shape[-1] // 2
    stride = 2 ** (offset - lane_bits)
    starts = [h * dim * stride + l for h in range(rows // (dim * stride)) for l in range(stride)]
    high_w, rest_w = weights_ref[slot, 0], weights_ref[slot, 1]
    for pair in range(0, len(starts), 2):
        group = starts[pair : pair + 2]
        x = jnp.concatenate(
            [jnp.concatenate([load(part, start, stride) for start in group], axis=1) for part in range(2)],
            axis=0,
        )
        high, rest = split(x)
        y = bf_dot(high_w, rest) + bf_dot(rest_w, high) + bf_dot(high_w, high)
        lanes = y.shape[1] // len(group)
        for part in range(2):
            for place, start in enumerate(group):
                store(part, start, stride, y[part * dim : (part + 1) * dim, place * lanes : (place + 1) * lanes])


def run_gates(section, weights_ref, lane_bits, buffers, last_store=None):
    dim = weights_ref.shape[-1] // 2
    rows = buffers[0].shape[1]

    def loader(ref):
        return lambda part, start, stride: ref[part, pl.ds(start, dim, stride=stride), :]

    def storer(ref):
        def store(part, start, stride, value):
            ref[part, pl.ds(start, dim, stride=stride), :] = value

        return store

    now = 0
    for index, (offset, _) in enumerate(section):
        last = index == len(section) - 1
        store = last_store if last and last_store is not None else storer(buffers[1 - now])
        apply_rows(weights_ref, index, offset, lane_bits, rows, loader(buffers[now]), store)
        now = 1 - now
    return now


def first_kernel(section, lane_bits, count, *refs):
    blocks, (low_ref, rows_ref), outs, (one, two) = (
        refs[:count],
        refs[count : count + 2],
        refs[count + 2 : -2],
        refs[-2:],
    )
    lanes = one.shape[2]
    for distance, block_ref in zip(distances_of(count), blocks):
        size = block_ref.shape[0] // 2
        start = pl.multiple_of(partner(distance) * size, size)
        real = block_ref[pl.ds(0, size, stride=2), :]
        imag = block_ref[pl.ds(1, size, stride=2), :]
        high, rest = split(jnp.concatenate([real, imag], axis=1))
        y = bf_dot(rest, low_ref[0]) + bf_dot(high, low_ref[1]) + bf_dot(high, low_ref[0])
        one[0, pl.ds(start, size), :] = y[:, :lanes]
        one[1, pl.ds(start, size), :] = y[:, lanes:]
    buffers = (one, two)
    done = buffers[run_gates(section, rows_ref, lane_bits, buffers)]
    for distance, out_ref in zip(distances_of(count), outs):
        dest = partner(distance)
        tops, mids, _, inner, _ = out_ref.shape
        for top in range(tops):
            for mid in range(mids):
                start = pl.multiple_of(((top * mids + mid) * count + dest) * inner, inner)
                for part in range(2):
                    out_ref[top, mid, part] = done[part, pl.ds(start, inner), :]


def second_kernel(section, lane_bits, count, stays, *refs):
    blocks, (rows_ref, out_ref, one, two) = refs[:count], refs[count:]
    core = lax.axis_index("qb")
    top = core if stays else 1 - core
    for distance, block_ref in zip(distances_of(count), blocks):
        source = partner(distance)
        _, mids, _, inner, _ = block_ref.shape
        for mid in range(mids):
            start = pl.multiple_of((mid * count + source) * inner, inner)
            for part in range(2):
                one[part, pl.ds(start, inner), :] = block_ref[top, mid, part]
    dim = rows_ref.shape[-1] // 2

    def last_store(part, start, stride, value):
        out_ref[part, pl.ds(start, dim, stride=stride), :] = value

    run_gates(section, rows_ref, lane_bits, (one, two), last_store)


def third_kernel(section, lane_bits, kept_ref, came_ref, rows_ref, out_ref, one, two):
    dim = rows_ref.shape[-1] // 2
    half = kept_ref.shape[1]
    core = lax.axis_index("qb")
    one[:, pl.ds(pl.multiple_of(core * half, half), half), :] = kept_ref[...]
    one[:, pl.ds(pl.multiple_of((1 - core) * half, half), half), :] = came_ref[...]

    def last_store(part, start, stride, value):
        out_ref[pl.ds(2 * start + part, dim, stride=2 * stride), :] = value

    run_gates(section, rows_ref, lane_bits, (one, two), last_store)


def call(kernel, name, out_shapes, in_specs, scratch, matmuls, *operands, limit=VMEM_LIMIT):
    many = isinstance(out_shapes, tuple)
    vmem = pl.BlockSpec(memory_space=pltpu.VMEM)
    return pl.pallas_call(
        kernel,
        out_shape=out_shapes,
        in_specs=in_specs,
        out_specs=(vmem,) * len(out_shapes) if many else vmem,
        scratch_shapes=scratch,
        compiler_params=pltpu.CompilerParams(vmem_limit_bytes=limit),
        cost_estimate=pl.CostEstimate(
            flops=int(matmuls * 3 * 2 * 256 * 256 * 1024), bytes_accessed=4 * 2**20, transcendentals=0
        ),
        name=name,
    )(*operands)


def per_device(state, gate_terms, path_bits):
    amps_local = state.shape[1]
    local_bits = amps_local.bit_length() - 1
    dim = gate_terms.shape[-1]
    gate_bits = dim.bit_length() - 1
    lanes, lane_bits = dim, gate_bits
    rows = amps_local // lanes
    qa = lax.axis_size("qa")
    qb = lax.axis_size("qb")
    low, sections = plan_gates(local_bits, gate_bits)
    order = 2 * dim
    vmem = pl.BlockSpec(memory_space=pltpu.VMEM)
    hbm = pl.BlockSpec(memory_space=pltpu.HBM)
    shape = jax.ShapeDtypeStruct

    state = with_layout_constraint(state.reshape(2, rows, lanes), Layout(major_to_minor=(1, 0, 2)))
    state = state.swapaxes(0, 1).reshape(qa, 2 * rows // qa, lanes)
    blocks = call(
        split_kernel,
        "split_state",
        (shape((2 * rows // qa, lanes), F32),) * qa,
        [vmem],
        [],
        0,
        state,
    )

    def exchange(blocks):
        came = [blocks[0]]
        for distance, piece in zip(distances_of(qa)[1:], blocks[1:]):
            came.append(lax.ppermute(piece, "qa", [(i, i ^ distance) for i in range(qa)]))
        return came

    blocks = exchange(blocks)
    low_w, *weights = call(
        functools.partial(prepare_kernel, low, sections),
        "prepare_gates",
        (shape((2, order, order), BF16),) + tuple(shape((len(s), 2, order, order), BF16) for s in sections),
        [pl.BlockSpec(memory_space=pltpu.SMEM), hbm],
        [pltpu.VMEM((gate_terms.shape[0], 2, dim, dim), F32), pltpu.SemaphoreType.DMA((gate_terms.shape[0],))],
        4,
        path_bits,
        gate_terms,
        limit=LARGE_VMEM,
    )
    inner = rows // (qa * qa)
    blocks = call(
        functools.partial(first_kernel, sections[0], lane_bits, qa),
        "first_section",
        (shape((qb, qa // qb, 2, inner, lanes), F32),) * qa,
        [vmem] * (qa + 2),
        [pltpu.VMEM((2, rows, lanes), F32)] * 2,
        len(sections[0]) + 1,
        *blocks,
        low_w,
        weights[0],
    )
    blocks = exchange(blocks)
    halves = []
    for stays in (False, True):
        halves.append(
            call(
                functools.partial(second_kernel, sections[1], lane_bits, qa, stays),
                "second_section_kept" if stays else "second_section_sent",
                shape((2, rows // qb, lanes), F32),
                [vmem] * (qa + 1),
                [pltpu.VMEM((2, rows // qb, lanes), F32)] * 2,
                len(sections[1]) / 2,
                *blocks,
                weights[1],
            )
        )
        if not stays:
            came = lax.ppermute(halves[0], "qb", [(i, 1 - i) for i in range(qb)])
    final = call(
        functools.partial(third_kernel, sections[2], lane_bits),
        "third_section",
        shape((2 * rows, lanes), F32),
        [vmem] * 3,
        [pltpu.VMEM((2, rows, lanes), F32)] * 2,
        len(sections[2]),
        halves[1],
        came,
        weights[2],
    )
    return final.reshape(rows, 2, lanes).swapaxes(0, 1).reshape(2, amps_local)


def solution(mesh):
    return jax.shard_map(
        per_device,
        mesh=mesh,
        in_specs=(P(None, ("paths", "qa", "qb")), P(), P("paths")),
        out_specs=P(None, ("paths", "qa", "qb")),
        check_vma=False,
    )
```

```python
import functools

import jax
import jax.numpy as jnp
from jax import lax
from jax.experimental import pallas as pl
from jax.experimental.layout import Layout, with_layout_constraint
from jax.experimental.pallas import tpu as pltpu
from jax.sharding import PartitionSpec as P

F32 = jnp.float32
BF16 = jnp.bfloat16
VMEM_LIMIT = 14 * 1024 * 1024
LARGE_VMEM = 48 * 1024 * 1024


def window_offsets(span, gate_bits):
    return [0, span, gate_bits, span - 1, gate_bits + 1, span - 2]


def plan_gates(local_bits, gate_bits):
    outer = window_offsets(local_bits - gate_bits, gate_bits)
    inner = window_offsets(local_bits - gate_bits - 1, gate_bits)
    low, sections = [], []
    for number, offsets in enumerate((outer, inner, outer)):
        section = []
        for index, offset in enumerate(offsets):
            gate = 6 * number + index
            if offset == 0:
                low.append(gate)
            elif section and section[-1][0] == offset:
                section[-1][1].append(gate)
            else:
                section.append((offset, [gate]))
        sections.append(section)
    return low, sections


def exact_dot(a, b):
    return lax.dot_general(
        a, b, (((1,), (0,)), ((), ())), precision=lax.Precision.HIGHEST, preferred_element_type=F32
    )


def split(x):
    high = x.astype(BF16)
    return high, (x - high.astype(F32)).astype(BF16)


def bf_dot(a, b):
    return jnp.dot(a, b, preferred_element_type=F32)


def block(real, imag):
    return jnp.concatenate(
        [jnp.concatenate([real, -imag], axis=1), jnp.concatenate([imag, real], axis=1)], axis=0
    )


def prepare_kernel(low, sections, bits_ref, gates_ref, low_ref, *refs):
    *targets, held, sems = refs
    copies = []
    for gate in range(held.shape[0]):
        copy = pltpu.make_async_copy(gates_ref.at[gate, bits_ref[gate]], held.at[gate], sems.at[gate])
        copy.start()
        copies.append(copy)
    for copy in copies:
        copy.wait()

    def product(gates):
        real, imag = held[gates[0], 0], held[gates[0], 1]
        for gate in gates[1:]:
            column = exact_dot(block(held[gate, 0], held[gate, 1]), jnp.concatenate([real, imag], axis=0))
            half = column.shape[0] // 2
            real, imag = column[:half], column[half:]
        return real, imag

    real, imag = product(low)
    low_ref[0], low_ref[1] = split(block(real.T, -imag.T))
    for target, section in zip(targets, sections):
        for slot, (_, gates) in enumerate(section):
            target[slot, 0], target[slot, 1] = split(block(*product(gates)))


def distances_of(count):
    half = count // 2
    far, near = list(range(count - 1, half - 1, -1)), list(range(half - 1, 0, -1))
    order = [0]
    while far or near:
        order += far[:2] + near[:2]
        far, near = far[2:], near[2:]
    return order


def partner(distance):
    return jnp.bitwise_xor(lax.axis_index("qa"), distance)


def split_kernel(x_ref, *outs):
    for distance, out_ref in zip(distances_of(len(outs)), outs):
        out_ref[...] = x_ref[partner(distance)]


def apply_rows(weights_ref, slot, offset, lane_bits, rows, load, store):
    dim = weights_ref.shape[-1] // 2
    stride = 2 ** (offset - lane_bits)
    starts = [h * dim * stride + l for h in range(rows // (dim * stride)) for l in range(stride)]
    high_w, rest_w = weights_ref[slot, 0], weights_ref[slot, 1]
    for pair in range(0, len(starts), 2):
        group = starts[pair : pair + 2]
        x = jnp.concatenate(
            [jnp.concatenate([load(part, start, stride) for start in group], axis=1) for part in range(2)],
            axis=0,
        )
        high, rest = split(x)
        y = bf_dot(high_w, rest) + bf_dot(rest_w, high) + bf_dot(high_w, high)
        lanes = y.shape[1] // len(group)
        for part in range(2):
            for place, start in enumerate(group):
                store(part, start, stride, y[part * dim : (part + 1) * dim, place * lanes : (place + 1) * lanes])


def run_gates(section, weights_ref, lane_bits, buffers, last_store=None):
    dim = weights_ref.shape[-1] // 2
    rows = buffers[0].shape[1]

    def loader(ref):
        return lambda part, start, stride: ref[part, pl.ds(start, dim, stride=stride), :]

    def storer(ref):
        def store(part, start, stride, value):
            ref[part, pl.ds(start, dim, stride=stride), :] = value

        return store

    now = 0
    for index, (offset, _) in enumerate(section):
        last = index == len(section) - 1
        store = last_store if last and last_store is not None else storer(buffers[1 - now])
        apply_rows(weights_ref, index, offset, lane_bits, rows, loader(buffers[now]), store)
        now = 1 - now
    return now


def first_kernel(section, lane_bits, count, *refs):
    blocks, (low_ref, rows_ref), outs, (one, two) = (
        refs[:count],
        refs[count : count + 2],
        refs[count + 2 : -2],
        refs[-2:],
    )
    lanes = one.shape[2]
    for distance, block_ref in zip(distances_of(count), blocks):
        size = block_ref.shape[0] // 2
        start = pl.multiple_of(partner(distance) * size, size)
        real = block_ref[pl.ds(0, size, stride=2), :]
        imag = block_ref[pl.ds(1, size, stride=2), :]
        high, rest = split(jnp.concatenate([real, imag], axis=1))
        y = bf_dot(rest, low_ref[0]) + bf_dot(high, low_ref[1]) + bf_dot(high, low_ref[0])
        one[0, pl.ds(start, size), :] = y[:, :lanes]
        one[1, pl.ds(start, size), :] = y[:, lanes:]
    buffers = (one, two)
    done = buffers[run_gates(section, rows_ref, lane_bits, buffers)]
    for distance, out_ref in zip(distances_of(count), outs):
        dest = partner(distance)
        tops, mids, _, inner, _ = out_ref.shape
        for top in range(tops):
            for mid in range(mids):
                start = pl.multiple_of(((top * mids + mid) * count + dest) * inner, inner)
                for part in range(2):
                    out_ref[top, mid, part] = done[part, pl.ds(start, inner), :]


def second_kernel(section, lane_bits, count, stays, *refs):
    blocks, (rows_ref, out_ref, one, two) = refs[:count], refs[count:]
    core = lax.axis_index("qb")
    top = core if stays else 1 - core
    for distance, block_ref in zip(distances_of(count), blocks):
        source = partner(distance)
        _, mids, _, inner, _ = block_ref.shape
        for mid in range(mids):
            start = pl.multiple_of((mid * count + source) * inner, inner)
            for part in range(2):
                one[part, pl.ds(start, inner), :] = block_ref[top, mid, part]
    dim = rows_ref.shape[-1] // 2

    def last_store(part, start, stride, value):
        out_ref[part, pl.ds(start, dim, stride=stride), :] = value

    run_gates(section, rows_ref, lane_bits, (one, two), last_store)


def third_kernel(section, lane_bits, kept_ref, came_ref, rows_ref, out_ref, one, two):
    dim = rows_ref.shape[-1] // 2
    half = kept_ref.shape[1]
    core = lax.axis_index("qb")
    one[:, pl.ds(pl.multiple_of(core * half, half), half), :] = kept_ref[...]
    one[:, pl.ds(pl.multiple_of((1 - core) * half, half), half), :] = came_ref[...]

    def last_store(part, start, stride, value):
        out_ref[pl.ds(2 * start + part, dim, stride=2 * stride), :] = value

    run_gates(section, rows_ref, lane_bits, (one, two), last_store)


def call(kernel, name, out_shapes, in_specs, scratch, matmuls, *operands, limit=VMEM_LIMIT):
    many = isinstance(out_shapes, tuple)
    vmem = pl.BlockSpec(memory_space=pltpu.VMEM)
    return pl.pallas_call(
        kernel,
        out_shape=out_shapes,
        in_specs=in_specs,
        out_specs=(vmem,) * len(out_shapes) if many else vmem,
        scratch_shapes=scratch,
        compiler_params=pltpu.CompilerParams(vmem_limit_bytes=limit),
        cost_estimate=pl.CostEstimate(
            flops=int(matmuls * 3 * 2 * 256 * 256 * 1024), bytes_accessed=4 * 2**20, transcendentals=0
        ),
        name=name,
    )(*operands)


def per_device(state, gate_terms, path_bits):
    amps_local = state.shape[1]
    local_bits = amps_local.bit_length() - 1
    dim = gate_terms.shape[-1]
    gate_bits = dim.bit_length() - 1
    lanes, lane_bits = dim, gate_bits
    rows = amps_local // lanes
    qa = lax.axis_size("qa")
    qb = lax.axis_size("qb")
    low, sections = plan_gates(local_bits, gate_bits)
    order = 2 * dim
    vmem = pl.BlockSpec(memory_space=pltpu.VMEM)
    hbm = pl.BlockSpec(memory_space=pltpu.HBM)
    shape = jax.ShapeDtypeStruct

    state = with_layout_constraint(state.reshape(2, rows, lanes), Layout(major_to_minor=(1, 0, 2)))
    state = state.swapaxes(0, 1).reshape(qa, 2 * rows // qa, lanes)
    blocks = call(
        split_kernel,
        "split_state",
        (shape((2 * rows // qa, lanes), F32),) * qa,
        [vmem],
        [],
        0,
        state,
    )

    def exchange(blocks):
        came = [blocks[0]]
        for distance, piece in zip(distances_of(qa)[1:], blocks[1:]):
            came.append(lax.ppermute(piece, "qa", [(i, i ^ distance) for i in range(qa)]))
        return came

    blocks = exchange(blocks)
    low_w, *weights = call(
        functools.partial(prepare_kernel, low, sections),
        "prepare_gates",
        (shape((2, order, order), BF16),) + tuple(shape((len(s), 2, order, order), BF16) for s in sections),
        [pl.BlockSpec(memory_space=pltpu.SMEM), hbm],
        [pltpu.VMEM((gate_terms.shape[0], 2, dim, dim), F32), pltpu.SemaphoreType.DMA((gate_terms.shape[0],))],
        4,
        path_bits,
        gate_terms,
        limit=LARGE_VMEM,
    )
    inner = rows // (qa * qa)
    blocks = call(
        functools.partial(first_kernel, sections[0], lane_bits, qa),
        "first_section",
        (shape((qb, qa // qb, 2, inner, lanes), F32),) * qa,
        [vmem] * (qa + 2),
        [pltpu.VMEM((2, rows, lanes), F32)] * 2,
        len(sections[0]) + 1,
        *blocks,
        low_w,
        weights[0],
    )
    blocks = exchange(blocks)
    halves = []
    for stays in (False, True):
        halves.append(
            call(
                functools.partial(second_kernel, sections[1], lane_bits, qa, stays),
                "second_section_kept" if stays else "second_section_sent",
                shape((2, rows // qb, lanes), F32),
                [vmem] * (qa + 1),
                [pltpu.VMEM((2, rows // qb, lanes), F32)] * 2,
                len(sections[1]) / 2,
                *blocks,
                weights[1],
            )
        )
        if not stays:
            came = lax.ppermute(halves[0], "qb", [(i, 1 - i) for i in range(qb)])
    final = call(
        functools.partial(third_kernel, sections[2], lane_bits),
        "third_section",
        shape((2 * rows, lanes), F32),
        [vmem] * 3,
        [pltpu.VMEM((2, rows, lanes), F32)] * 2,
        len(sections[2]),
        halves[1],
        came,
        weights[2],
    )
    return final.reshape(rows, 2, lanes).swapaxes(0, 1).reshape(2, amps_local)


def solution(mesh):
    return jax.shard_map(
        per_device,
        mesh=mesh,
        in_specs=(P(None, ("paths", "qa", "qb")), P(), P("paths")),
        out_specs=P(None, ("paths", "qa", "qb")),
        check_vma=False,
    )
```

```python
import functools

import jax
import jax.numpy as jnp
from jax import lax
from jax.experimental import pallas as pl
from jax.experimental.layout import Layout, with_layout_constraint
from jax.experimental.pallas import tpu as pltpu
from jax.sharding import PartitionSpec as P

F32 = jnp.float32
BF16 = jnp.bfloat16
VMEM_LIMIT = 14 * 1024 * 1024
LARGE_VMEM = 48 * 1024 * 1024


def window_offsets(span, gate_bits):
    return [0, span, gate_bits, span - 1, gate_bits + 1, span - 2]


def plan_gates(local_bits, gate_bits):
    outer = window_offsets(local_bits - gate_bits, gate_bits)
    inner = window_offsets(local_bits - gate_bits - 1, gate_bits)
    low, sections = [], []
    for number, offsets in enumerate((outer, inner, outer)):
        section = []
        for index, offset in enumerate(offsets):
            gate = 6 * number + index
            if offset == 0:
                low.append(gate)
            elif section and section[-1][0] == offset:
                section[-1][1].append(gate)
            else:
                section.append((offset, [gate]))
        sections.append(section)
    return low, sections


def join_windows(section, gate_bits):
    stages = []
    for offset, gates in section:
        if stages:
            offsets = [o for o, _ in stages[-1]] + [offset]
            if max(offsets) - min(offsets) <= 1:
                stages[-1].append((offset, gates))
                continue
        stages.append([(offset, gates)])
    return [
        (min(o for o, _ in parts), gate_bits + (len(parts) > 1), parts)
        for parts in stages
    ]


def interleaved(stage):
    base, _, parts = stage
    return parts[0][0] != base


def exact_dot(a, b):
    return lax.dot_general(
        a, b, (((1,), (0,)), ((), ())), precision=lax.Precision.HIGHEST, preferred_element_type=F32
    )


def split(x):
    high = x.astype(BF16)
    return high, (x - high.astype(F32)).astype(BF16)


def bf_dot(a, b):
    return jnp.dot(a, b, preferred_element_type=F32)


def block(real, imag):
    return jnp.concatenate(
        [jnp.concatenate([real, -imag], axis=1), jnp.concatenate([imag, real], axis=1)], axis=0
    )


def prepare_kernel(low, sections, bits_ref, gates_ref, low_ref, *refs):
    *targets, held, wide, sems = refs
    copies = []
    for gate in range(held.shape[0]):
        copy = pltpu.make_async_copy(gates_ref.at[gate, bits_ref[gate]], held.at[gate], sems.at[gate])
        copy.start()
        copies.append(copy)
    for copy in copies:
        copy.wait()
    dim = held.shape[-1]

    def product(gates):
        real, imag = held[gates[0], 0], held[gates[0], 1]
        for gate in gates[1:]:
            column = exact_dot(block(held[gate, 0], held[gate, 1]), jnp.concatenate([real, imag], axis=0))
            real, imag = column[:dim], column[dim:]
        return real, imag

    def joined(base, parts):
        wide[...] = jnp.zeros_like(wide)
        for index, (offset, gates) in enumerate(parts):
            real, imag = product(gates)
            for t in range(2):
                at = pl.ds(t * dim, dim) if offset == base else pl.ds(t, dim, stride=2)
                if index == 0:
                    wide[0, t, at, :] = real
                    wide[1, t, at, :] = imag
                else:
                    x = jnp.concatenate(
                        [jnp.concatenate([wide[p, c, at, :] for c in range(2)], axis=1) for p in range(2)], axis=0
                    )
                    y = exact_dot(block(real, imag), x)
                    for p in range(2):
                        for c in range(2):
                            wide[p, c, at, :] = y[p * dim : (p + 1) * dim, c * dim : (c + 1) * dim]
        return [jnp.concatenate([wide[p, 0], wide[p, 1]], axis=1) for p in range(2)]

    targets = iter(targets)
    for section in sections:
        for base, _, parts in section:
            target = next(targets)
            target[0], target[1] = split(block(*(joined(base, parts) if len(parts) > 1 else product(parts[0][1]))))
    real, imag = product(low)
    low_ref[0], low_ref[1] = split(block(real.T, -imag.T))


def distances_of(count):
    half = count // 2
    far, near = list(range(count - 1, half - 1, -1)), list(range(half - 1, 0, -1))
    order = [0]
    while far or near:
        order += far[:2] + near[:2]
        far, near = far[2:], near[2:]
    return order


def partner(distance):
    return jnp.bitwise_xor(lax.axis_index("qa"), distance)


def split_kernel(x_ref, *outs):
    for distance, out_ref in zip(distances_of(len(outs)), outs):
        out_ref[...] = x_ref[partner(distance)]


def apply_stage(weights_ref, starts, load, store):
    dim = weights_ref.shape[-1] // 2
    high_w, rest_w = weights_ref[0], weights_ref[1]
    for pair in range(0, len(starts), 2):
        group = starts[pair : pair + 2]
        x = jnp.concatenate(
            [jnp.concatenate([load(part, start) for start in group], axis=1) for part in range(2)], axis=0
        )
        high, rest = split(x)
        y = bf_dot(high_w, rest) + bf_dot(rest_w, high) + bf_dot(high_w, high)
        lanes = y.shape[1] // len(group)
        for part in range(2):
            for place, start in enumerate(group):
                store(part, start, y[part * dim : (part + 1) * dim, place * lanes : (place + 1) * lanes])


def stage_starts(stage, lane_bits, rows):
    base, bits, _ = stage
    dim, stride = 2**bits, 2 ** (base - lane_bits)
    return dim, stride, [h * dim * stride + l for h in range(rows // (dim * stride)) for l in range(stride)]


def run_stage(stage, weights_ref, lane_bits, source, target=None, store=None):
    dim, stride, starts = stage_starts(stage, lane_bits, source.shape[1])

    def load(part, start):
        if not interleaved(stage):
            return source[part, pl.ds(start, dim, stride=stride), :]
        half = dim // 2
        return jnp.concatenate(
            [source[part, pl.ds(start + t * stride, half, stride=2 * stride), :] for t in range(2)], axis=0
        )

    def plain(part, start, value):
        target[part, pl.ds(start, dim, stride=stride), :] = value

    apply_stage(weights_ref, starts, load, store or plain)


def run_top_stage(stage, weights_ref, lane_bits, source, halves):
    dim, stride, starts = stage_starts(stage, lane_bits, source.shape[1])

    def store(part, start, value):
        for t in range(2):
            halves[t][part, pl.ds(start, dim // 2, stride=stride), :] = value[t * dim // 2 : (t + 1) * dim // 2]

    apply_stage(weights_ref, starts, lambda part, start: source[part, pl.ds(start, dim, stride=stride), :], store)


def run_halves(stages, weights, lane_bits, halves, spares, last_store=None):
    for index, (stage, weights_ref) in enumerate(zip(stages, weights)):
        for t in range(2):
            store = None
            if last_store is not None and index == len(stages) - 1:
                store = functools.partial(last_store, t)
            run_stage(stage, weights_ref, lane_bits, halves[t], spares[t], store)
        halves, spares = spares, halves
    return halves


def first_kernel(stages, lane_bits, count, *refs):
    blocks, refs = refs[:count], refs[count:]
    low_ref, weights, refs = refs[0], refs[1 : 1 + len(stages)], refs[1 + len(stages) :]
    outs, (whole, *halves) = refs[:count], refs[count:]
    lanes = whole.shape[2]
    for distance, block_ref in zip(distances_of(count), blocks):
        size = block_ref.shape[0] // 2
        start = pl.multiple_of(partner(distance) * size, size)
        real = block_ref[pl.ds(0, size, stride=2), :]
        imag = block_ref[pl.ds(1, size, stride=2), :]
        high, rest = split(jnp.concatenate([real, imag], axis=1))
        y = bf_dot(rest, low_ref[0]) + bf_dot(high, low_ref[1]) + bf_dot(high, low_ref[0])
        whole[0, pl.ds(start, size), :] = y[:, :lanes]
        whole[1, pl.ds(start, size), :] = y[:, lanes:]
    run_top_stage(stages[0], weights[0], lane_bits, whole, halves[:2])
    done = run_halves(stages[1:], weights[1:], lane_bits, halves[:2], halves[2:])
    tops, mids, _, inner, _ = outs[0].shape
    for top in range(tops):
        for distance, out_ref in zip(distances_of(count), outs):
            dest = partner(distance)
            for mid in range(mids):
                start = pl.multiple_of((mid * count + dest) * inner, inner)
                for part in range(2):
                    out_ref[top, mid, part] = done[top][part, pl.ds(start, inner), :]


def second_kernel(stages, lane_bits, count, stays, *refs):
    blocks, weights, refs = refs[:count], refs[count : count + len(stages)], refs[count + len(stages) :]
    out_ref, one, two = refs
    core = lax.axis_index("qb")
    top = core if stays else 1 - core
    for distance, block_ref in zip(distances_of(count), blocks):
        source = partner(distance)
        _, mids, _, inner, _ = block_ref.shape
        for mid in range(mids):
            start = pl.multiple_of((mid * count + source) * inner, inner)
            for part in range(2):
                one[part, pl.ds(start, inner), :] = block_ref[top, mid, part]
    for index, (stage, weights_ref) in enumerate(zip(stages, weights)):
        run_stage(stage, weights_ref, lane_bits, one, out_ref if index == len(stages) - 1 else two)
        one, two = two, one


def third_kernel(stages, lane_bits, kept_ref, came_ref, *refs):
    weights, (out_ref, whole, *halves, sems) = refs[: len(stages)], refs[len(stages) :]
    results = halves[4:]
    half = kept_ref.shape[1]
    core = lax.axis_index("qb")
    whole[:, pl.ds(pl.multiple_of(core * half, half), half), :] = kept_ref[...]
    whole[:, pl.ds(pl.multiple_of((1 - core) * half, half), half), :] = came_ref[...]
    run_top_stage(stages[0], weights[0], lane_bits, whole, halves[:2])
    done = run_halves(stages[1:-1], weights[1:-1], lane_bits, halves[:2], halves[2:4])
    copies = []
    for t in range(2):
        dim, stride, _ = stage_starts(stages[-1], lane_bits, half)

        def store(part, start, value, t=t):
            results[t][pl.ds(2 * start + part, dim, stride=2 * stride), :] = value

        run_stage(stages[-1], weights[-1], lane_bits, done[t], store=store)
        copies.append(pltpu.make_async_copy(results[t], out_ref.at[pl.ds(t * 2 * half, 2 * half)], sems.at[t]))
        copies[-1].start()
    for copy in copies:
        copy.wait()


def call(kernel, name, out_shapes, in_specs, scratch, matmuls, *operands, limit=VMEM_LIMIT, out_spec=None):
    many = isinstance(out_shapes, tuple)
    vmem = out_spec or pl.BlockSpec(memory_space=pltpu.VMEM)
    return pl.pallas_call(
        kernel,
        out_shape=out_shapes,
        in_specs=in_specs,
        out_specs=(vmem,) * len(out_shapes) if many else vmem,
        scratch_shapes=scratch,
        compiler_params=pltpu.CompilerParams(vmem_limit_bytes=limit),
        cost_estimate=pl.CostEstimate(
            flops=int(matmuls * 3 * 2 * 256 * 256 * 1024), bytes_accessed=4 * 2**20, transcendentals=0
        ),
        name=name,
    )(*operands)


def per_device(state, gate_terms, path_bits):
    amps_local = state.shape[1]
    local_bits = amps_local.bit_length() - 1
    dim = gate_terms.shape[-1]
    gate_bits = dim.bit_length() - 1
    lanes, lane_bits = dim, gate_bits
    rows = amps_local // lanes
    qa = lax.axis_size("qa")
    qb = lax.axis_size("qb")
    low, sections = plan_gates(local_bits, gate_bits)
    sections = [join_windows(section, gate_bits) for section in sections]
    order = 2 * dim
    vmem = pl.BlockSpec(memory_space=pltpu.VMEM)
    hbm = pl.BlockSpec(memory_space=pltpu.HBM)
    shape = jax.ShapeDtypeStruct

    state = with_layout_constraint(state.reshape(2, rows, lanes), Layout(major_to_minor=(1, 0, 2)))
    state = state.swapaxes(0, 1).reshape(qa, 2 * rows // qa, lanes)
    blocks = call(
        split_kernel,
        "split_state",
        (shape((2 * rows // qa, lanes), F32),) * qa,
        [vmem],
        [],
        0,
        state,
    )

    def exchange(blocks):
        came = [blocks[0]]
        for distance, piece in zip(distances_of(qa)[1:], blocks[1:]):
            came.append(lax.ppermute(piece, "qa", [(i, i ^ distance) for i in range(qa)]))
        return came

    blocks = exchange(blocks)
    low_w, *weights = call(
        functools.partial(prepare_kernel, low, sections),
        "prepare_gates",
        (shape((2, order, order), BF16),)
        + tuple(shape((2, 2 * 2**bits, 2 * 2**bits), BF16) for section in sections for _, bits, _ in section),
        [pl.BlockSpec(memory_space=pltpu.SMEM), hbm],
        [
            pltpu.VMEM((gate_terms.shape[0], 2, dim, dim), F32),
            pltpu.VMEM((2, 2, 2 * dim, dim), F32),
            pltpu.SemaphoreType.DMA((gate_terms.shape[0],)),
        ],
        8,
        path_bits,
        gate_terms,
        limit=LARGE_VMEM,
    )
    counts = [len(section) for section in sections]
    weights = [weights[: counts[0]], weights[counts[0] : counts[0] + counts[1]], weights[counts[0] + counts[1] :]]
    inner = rows // (qa * qa)
    whole = pltpu.VMEM((2, rows, lanes), F32)
    half = pltpu.VMEM((2, rows // 2, lanes), F32)
    blocks = call(
        functools.partial(first_kernel, sections[0], lane_bits, qa),
        "first_section",
        (shape((qb, qa // qb, 2, inner, lanes), F32),) * qa,
        [vmem] * (qa + 1 + counts[0]),
        [whole] + [half] * 4,
        5,
        *blocks,
        low_w,
        *weights[0],
    )
    blocks = exchange(blocks)
    halves = []
    for stays in (False, True):
        halves.append(
            call(
                functools.partial(second_kernel, sections[1], lane_bits, qa, stays),
                "second_section_kept" if stays else "second_section_sent",
                shape((2, rows // qb, lanes), F32),
                [vmem] * (qa + counts[1]),
                [half] * 2,
                1.5,
                *blocks,
                *weights[1],
            )
        )
        if not stays:
            came = lax.ppermute(halves[0], "qb", [(i, 1 - i) for i in range(qb)])
    final = call(
        functools.partial(third_kernel, sections[2], lane_bits),
        "third_section",
        shape((2 * rows, lanes), F32),
        [vmem] * (2 + counts[2]),
        [whole] + [half] * 4 + [pltpu.VMEM((rows, lanes), F32)] * 2 + [pltpu.SemaphoreType.DMA((2,))],
        4,
        halves[1],
        came,
        *weights[2],
        out_spec=hbm,
    )
    return final.reshape(rows, 2, lanes).swapaxes(0, 1).reshape(2, amps_local)


def solution(mesh):
    return jax.shard_map(
        per_device,
        mesh=mesh,
        in_specs=(P(None, ("paths", "qa", "qb")), P(), P("paths")),
        out_specs=P(None, ("paths", "qa", "qb")),
        check_vma=False,
    )
```

```python
import functools

import jax
import jax.numpy as jnp
from jax import lax
from jax.experimental import pallas as pl
from jax.experimental.layout import Layout, with_layout_constraint
from jax.experimental.pallas import tpu as pltpu
from jax.sharding import PartitionSpec as P

F32 = jnp.float32
BF16 = jnp.bfloat16
VMEM_LIMIT = 14 * 1024 * 1024
LARGE_VMEM = 48 * 1024 * 1024
SPLIT_VMEM = 62 * 1024 * 1024
PIECES = 4
FIRST = 2


def window_offsets(span, gate_bits):
    return [0, span, gate_bits, span - 1, gate_bits + 1, span - 2]


def plan_gates(local_bits, gate_bits):
    outer = window_offsets(local_bits - gate_bits, gate_bits)
    inner = window_offsets(local_bits - gate_bits - 1, gate_bits)
    low, sections = [], []
    for number, offsets in enumerate((outer, inner, outer)):
        section = []
        for index, offset in enumerate(offsets):
            gate = 6 * number + index
            if offset == 0:
                low.append(gate)
            elif section and section[-1][0] == offset:
                section[-1][1].append(gate)
            else:
                section.append((offset, [gate]))
        sections.append(section)
    return low, sections


def join_windows(section, gate_bits):
    stages = []
    for offset, gates in section:
        if stages:
            offsets = [o for o, _ in stages[-1]] + [offset]
            if max(offsets) - min(offsets) <= 1:
                stages[-1].append((offset, gates))
                continue
        stages.append([(offset, gates)])
    return [
        (min(o for o, _ in parts), gate_bits + (len(parts) > 1), parts)
        for parts in stages
    ]


def interleaved(stage):
    base, _, parts = stage
    return parts[0][0] != base


def exact_dot(a, b):
    return lax.dot_general(
        a, b, (((1,), (0,)), ((), ())), precision=lax.Precision.HIGHEST, preferred_element_type=F32
    )


def split(x):
    high = x.astype(BF16)
    return high, (x - high.astype(F32)).astype(BF16)


def bf_dot(a, b):
    return jnp.dot(a, b, preferred_element_type=F32)


def block(real, imag):
    return jnp.concatenate(
        [jnp.concatenate([real, -imag], axis=1), jnp.concatenate([imag, real], axis=1)], axis=0
    )


def prepare_kernel(low, sections, bits_ref, gates_ref, low_ref, *refs):
    *targets, held, wide, sems = refs
    copies = []
    for gate in range(held.shape[0]):
        copy = pltpu.make_async_copy(gates_ref.at[gate, bits_ref[gate]], held.at[gate], sems.at[gate])
        copy.start()
        copies.append(copy)
    for copy in copies:
        copy.wait()
    dim = held.shape[-1]

    def product(gates):
        real, imag = held[gates[0], 0], held[gates[0], 1]
        for gate in gates[1:]:
            column = exact_dot(block(held[gate, 0], held[gate, 1]), jnp.concatenate([real, imag], axis=0))
            real, imag = column[:dim], column[dim:]
        return real, imag

    def joined(base, parts):
        wide[...] = jnp.zeros_like(wide)
        for index, (offset, gates) in enumerate(parts):
            real, imag = product(gates)
            for t in range(2):
                at = pl.ds(t * dim, dim) if offset == base else pl.ds(t, dim, stride=2)
                if index == 0:
                    wide[0, t, at, :] = real
                    wide[1, t, at, :] = imag
                else:
                    x = jnp.concatenate(
                        [jnp.concatenate([wide[p, c, at, :] for c in range(2)], axis=1) for p in range(2)], axis=0
                    )
                    y = exact_dot(block(real, imag), x)
                    for p in range(2):
                        for c in range(2):
                            wide[p, c, at, :] = y[p * dim : (p + 1) * dim, c * dim : (c + 1) * dim]
        return [jnp.concatenate([wide[p, 0], wide[p, 1]], axis=1) for p in range(2)]

    targets = iter(targets)
    for section in sections:
        for base, _, parts in section:
            target = next(targets)
            target[0], target[1] = split(block(*(joined(base, parts) if len(parts) > 1 else product(parts[0][1]))))
    real, imag = product(low)
    low_ref[0], low_ref[1] = split(block(real.T, -imag.T))


def distances_of(count):
    half = count // 2
    far, near = list(range(count - 1, half - 1, -1)), list(range(half - 1, 0, -1))
    order = [0]
    while far or near:
        order += far[:2] + near[:2]
        far, near = far[2:], near[2:]
    return order


def partner(distance):
    return jnp.bitwise_xor(lax.axis_index("qa"), distance)


def far_kernel(distances, x_ref, *refs):
    *outs, sems = refs
    copies = []
    for place, distance in enumerate(distances):
        copy = pltpu.make_async_copy(x_ref.at[partner(distance)], outs[place], sems.at[place])
        copy.start()
        copies.append(copy)
    for copy in copies:
        copy.wait()


def rest_kernel(distances, x_ref, *outs):
    for distance, out_ref in zip(distances, outs):
        out_ref[...] = x_ref[partner(distance)]


def apply_stage(weights_ref, starts, load, store):
    dim = weights_ref.shape[-1] // 2
    both_w = weights_ref[...].reshape(4 * dim, 2 * dim)
    high_w = weights_ref[0]
    for pair in range(0, len(starts), 2):
        group = starts[pair : pair + 2]
        x = jnp.concatenate(
            [jnp.concatenate([load(part, start) for start in group], axis=1) for part in range(2)], axis=0
        )
        high, rest = split(x)
        both = bf_dot(both_w, high)
        y = bf_dot(high_w, rest) + both[2 * dim :] + both[: 2 * dim]
        lanes = y.shape[1] // len(group)
        for part in range(2):
            for place, start in enumerate(group):
                store(part, start, y[part * dim : (part + 1) * dim, place * lanes : (place + 1) * lanes])


def stage_starts(stage, lane_bits, rows):
    base, bits, _ = stage
    dim, stride = 2**bits, 2 ** (base - lane_bits)
    return dim, stride, [h * dim * stride + l for h in range(rows // (dim * stride)) for l in range(stride)]


def run_stage(stage, weights_ref, lane_bits, source, target=None, store=None):
    dim, stride, starts = stage_starts(stage, lane_bits, source.shape[1])

    def load(part, start):
        if not interleaved(stage):
            return source[part, pl.ds(start, dim, stride=stride), :]
        half = dim // 2
        return jnp.concatenate(
            [source[part, pl.ds(start + t * stride, half, stride=2 * stride), :] for t in range(2)], axis=0
        )

    def plain(part, start, value):
        target[part, pl.ds(start, dim, stride=stride), :] = value

    apply_stage(weights_ref, starts, load, store or plain)


def run_top_stage(stage, weights_ref, lane_bits, source, halves):
    dim, stride, starts = stage_starts(stage, lane_bits, source.shape[1])

    def store(part, start, value):
        for t in range(2):
            halves[t][part, pl.ds(start, dim // 2, stride=stride), :] = value[t * dim // 2 : (t + 1) * dim // 2]

    apply_stage(weights_ref, starts, lambda part, start: source[part, pl.ds(start, dim, stride=stride), :], store)


def run_halves(stages, weights, lane_bits, halves, spares, last_store=None):
    for index, (stage, weights_ref) in enumerate(zip(stages, weights)):
        for t in range(2):
            store = None
            if last_store is not None and index == len(stages) - 1:
                store = functools.partial(last_store, t)
            run_stage(stage, weights_ref, lane_bits, halves[t], spares[t], store)
        halves, spares = spares, halves
    return halves


def first_kernel(stages, lane_bits, count, *refs):
    blocks, refs = refs[:count], refs[count:]
    low_ref, weights, refs = refs[0], refs[1 : 1 + len(stages)], refs[1 + len(stages) :]
    outs, (whole, *halves) = refs[:count], refs[count:]
    lanes = whole.shape[2]
    for distance, block_ref in zip(distances_of(count), blocks):
        size = block_ref.shape[0] // 2
        start = pl.multiple_of(partner(distance) * size, size)
        real = block_ref[pl.ds(0, size, stride=2), :]
        imag = block_ref[pl.ds(1, size, stride=2), :]
        high, rest = split(jnp.concatenate([real, imag], axis=1))
        y = bf_dot(rest, low_ref[0]) + bf_dot(high, low_ref[1]) + bf_dot(high, low_ref[0])
        whole[0, pl.ds(start, size), :] = y[:, :lanes]
        whole[1, pl.ds(start, size), :] = y[:, lanes:]
    run_top_stage(stages[0], weights[0], lane_bits, whole, halves[:2])
    done = run_halves(stages[1:], weights[1:], lane_bits, halves[:2], halves[2:])
    tops, mids, _, inner, _ = outs[0].shape
    for top in range(tops):
        for distance, out_ref in zip(distances_of(count), outs):
            dest = partner(distance)
            for mid in range(mids):
                start = pl.multiple_of((mid * count + dest) * inner, inner)
                for part in range(2):
                    out_ref[top, mid, part] = done[top][part, pl.ds(start, inner), :]


def second_kernel(stages, lane_bits, count, stays, *refs):
    blocks, weights, refs = refs[:count], refs[count : count + len(stages)], refs[count + len(stages) :]
    out_ref, one, two = refs
    core = lax.axis_index("qb")
    top = core if stays else 1 - core
    for distance, block_ref in zip(distances_of(count), blocks):
        source = partner(distance)
        _, mids, _, inner, _ = block_ref.shape
        for mid in range(mids):
            start = pl.multiple_of((mid * count + source) * inner, inner)
            for part in range(2):
                one[part, pl.ds(start, inner), :] = block_ref[top, mid, part]
    for index, (stage, weights_ref) in enumerate(zip(stages, weights)):
        run_stage(stage, weights_ref, lane_bits, one, out_ref if index == len(stages) - 1 else two)
        one, two = two, one


def third_kernel(stages, lane_bits, kept_ref, came_ref, *refs):
    weights, (out_ref, whole, *halves, sems) = refs[: len(stages)], refs[len(stages) :]
    results = halves[4:]
    half = kept_ref.shape[1]
    core = lax.axis_index("qb")
    whole[:, pl.ds(pl.multiple_of(core * half, half), half), :] = kept_ref[...]
    whole[:, pl.ds(pl.multiple_of((1 - core) * half, half), half), :] = came_ref[...]
    run_top_stage(stages[0], weights[0], lane_bits, whole, halves[:2])
    done = run_halves(stages[1:-1], weights[1:-1], lane_bits, halves[:2], halves[2:4])
    copies = []
    for t in range(2):
        dim, stride, _ = stage_starts(stages[-1], lane_bits, half)

        def store(part, start, value, t=t):
            results[t][pl.ds(2 * start + part, dim, stride=2 * stride), :] = value

        run_stage(stages[-1], weights[-1], lane_bits, done[t], store=store)
        size = 2 * half // PIECES
        for piece in range(PIECES):
            to = out_ref.at[pl.ds(t * 2 * half + piece * size, size)]
            copies.append(
                pltpu.make_async_copy(results[t].at[pl.ds(piece * size, size)], to, sems.at[t * PIECES + piece])
            )
            copies[-1].start()
    for copy in copies:
        copy.wait()


def call(kernel, name, out_shapes, in_specs, scratch, matmuls, *operands, limit=VMEM_LIMIT, out_spec=None):
    many = isinstance(out_shapes, tuple)
    vmem = out_spec or pl.BlockSpec(memory_space=pltpu.VMEM)
    return pl.pallas_call(
        kernel,
        out_shape=out_shapes,
        in_specs=in_specs,
        out_specs=(vmem,) * len(out_shapes) if many else vmem,
        scratch_shapes=scratch,
        compiler_params=pltpu.CompilerParams(vmem_limit_bytes=limit),
        cost_estimate=pl.CostEstimate(
            flops=int(matmuls * 3 * 2 * 256 * 256 * 1024), bytes_accessed=4 * 2**20, transcendentals=0
        ),
        name=name,
    )(*operands)


def per_device(state, gate_terms, path_bits):
    amps_local = state.shape[1]
    local_bits = amps_local.bit_length() - 1
    dim = gate_terms.shape[-1]
    gate_bits = dim.bit_length() - 1
    lanes, lane_bits = dim, gate_bits
    rows = amps_local // lanes
    qa = lax.axis_size("qa")
    qb = lax.axis_size("qb")
    low, sections = plan_gates(local_bits, gate_bits)
    sections = [join_windows(section, gate_bits) for section in sections]
    order = 2 * dim
    vmem = pl.BlockSpec(memory_space=pltpu.VMEM)
    hbm = pl.BlockSpec(memory_space=pltpu.HBM)
    shape = jax.ShapeDtypeStruct

    state = with_layout_constraint(state.reshape(2, rows, lanes), Layout(major_to_minor=(1, 0, 2)))
    state = state.swapaxes(0, 1).reshape(qa, 2 * rows // qa, lanes)
    order_of = distances_of(qa)
    first, rest = order_of[1 : 1 + FIRST], [0, *order_of[1 + FIRST :]]
    one_block = shape((2 * rows // qa, lanes), F32)
    early = call(
        functools.partial(far_kernel, first),
        "split_first",
        (one_block,) * len(first),
        [hbm],
        [pltpu.SemaphoreType.DMA((len(first),))],
        0,
        state,
        limit=SPLIT_VMEM,
    )
    late = call(
        functools.partial(rest_kernel, rest), "split_rest", (one_block,) * len(rest), [vmem], [], 0, state
    )
    blocks = [late[0], *early, *late[1:]]

    def exchange(blocks):
        came = [blocks[0]]
        for distance, piece in zip(distances_of(qa)[1:], blocks[1:]):
            came.append(lax.ppermute(piece, "qa", [(i, i ^ distance) for i in range(qa)]))
        return came

    blocks = exchange(blocks)
    low_w, *weights = call(
        functools.partial(prepare_kernel, low, sections),
        "prepare_gates",
        (shape((2, order, order), BF16),)
        + tuple(shape((2, 2 * 2**bits, 2 * 2**bits), BF16) for section in sections for _, bits, _ in section),
        [pl.BlockSpec(memory_space=pltpu.SMEM), hbm],
        [
            pltpu.VMEM((gate_terms.shape[0], 2, dim, dim), F32),
            pltpu.VMEM((2, 2, 2 * dim, dim), F32),
            pltpu.SemaphoreType.DMA((gate_terms.shape[0],)),
        ],
        8,
        path_bits,
        gate_terms,
        limit=LARGE_VMEM,
    )
    counts = [len(section) for section in sections]
    weights = [weights[: counts[0]], weights[counts[0] : counts[0] + counts[1]], weights[counts[0] + counts[1] :]]
    inner = rows // (qa * qa)
    whole = pltpu.VMEM((2, rows, lanes), F32)
    half = pltpu.VMEM((2, rows // 2, lanes), F32)
    blocks = call(
        functools.partial(first_kernel, sections[0], lane_bits, qa),
        "first_section",
        (shape((qb, qa // qb, 2, inner, lanes), F32),) * qa,
        [vmem] * (qa + 1 + counts[0]),
        [whole] + [half] * 4,
        5,
        *blocks,
        low_w,
        *weights[0],
    )
    blocks = exchange(blocks)
    halves = []
    for stays in (False, True):
        halves.append(
            call(
                functools.partial(second_kernel, sections[1], lane_bits, qa, stays),
                "second_section_kept" if stays else "second_section_sent",
                shape((2, rows // qb, lanes), F32),
                [vmem] * (qa + counts[1]),
                [half] * 2,
                1.5,
                *blocks,
                *weights[1],
            )
        )
        if not stays:
            came = lax.ppermute(halves[0], "qb", [(i, 1 - i) for i in range(qb)])
    final = call(
        functools.partial(third_kernel, sections[2], lane_bits),
        "third_section",
        shape((2 * rows, lanes), F32),
        [vmem] * (2 + counts[2]),
        [whole] + [half] * 4 + [pltpu.VMEM((rows, lanes), F32)] * 2 + [pltpu.SemaphoreType.DMA((2 * PIECES,))],
        4,
        halves[1],
        came,
        *weights[2],
        out_spec=hbm,
    )
    return final.reshape(rows, 2, lanes).swapaxes(0, 1).reshape(2, amps_local)


def solution(mesh):
    return jax.shard_map(
        per_device,
        mesh=mesh,
        in_specs=(P(None, ("paths", "qa", "qb")), P(), P("paths")),
        out_specs=P(None, ("paths", "qa", "qb")),
        check_vma=False,
    )
```

```python
import functools

import jax
import jax.numpy as jnp
from jax import lax
from jax.experimental import pallas as pl
from jax.experimental.layout import Layout, with_layout_constraint
from jax.experimental.pallas import tpu as pltpu
from jax.sharding import PartitionSpec as P

F32 = jnp.float32
BF16 = jnp.bfloat16
VMEM_LIMIT = 14 * 1024 * 1024
LARGE_VMEM = 48 * 1024 * 1024
PIECES = 4


def window_offsets(span, gate_bits):
    return [0, span, gate_bits, span - 1, gate_bits + 1, span - 2]


def plan_gates(local_bits, gate_bits):
    outer = window_offsets(local_bits - gate_bits, gate_bits)
    inner = window_offsets(local_bits - gate_bits - 1, gate_bits)
    low, sections = [], []
    for number, offsets in enumerate((outer, inner, outer)):
        section = []
        for index, offset in enumerate(offsets):
            gate = 6 * number + index
            if offset == 0:
                low.append(gate)
            elif section and section[-1][0] == offset:
                section[-1][1].append(gate)
            else:
                section.append((offset, [gate]))
        sections.append(section)
    return low, sections


def join_windows(section, gate_bits):
    stages = []
    for offset, gates in section:
        if stages:
            offsets = [o for o, _ in stages[-1]] + [offset]
            if max(offsets) - min(offsets) <= 1:
                stages[-1].append((offset, gates))
                continue
        stages.append([(offset, gates)])
    return [
        (min(o for o, _ in parts), gate_bits + (len(parts) > 1), parts)
        for parts in stages
    ]


def interleaved(stage):
    base, _, parts = stage
    return parts[0][0] != base


def exact_dot(a, b):
    return lax.dot_general(
        a, b, (((1,), (0,)), ((), ())), precision=lax.Precision.HIGHEST, preferred_element_type=F32
    )


def split(x):
    high = x.astype(BF16)
    return high, (x - high.astype(F32)).astype(BF16)


def bf_dot(a, b):
    return jnp.dot(a, b, preferred_element_type=F32)


def block(real, imag):
    return jnp.concatenate(
        [jnp.concatenate([real, -imag], axis=1), jnp.concatenate([imag, real], axis=1)], axis=0
    )


def prepare_kernel(low, sections, bits_ref, gates_ref, low_ref, *refs):
    *targets, held, wide, sems = refs
    copies = []
    for gate in range(held.shape[0]):
        copy = pltpu.make_async_copy(gates_ref.at[gate, bits_ref[gate]], held.at[gate], sems.at[gate])
        copy.start()
        copies.append(copy)
    for copy in copies:
        copy.wait()
    dim = held.shape[-1]

    def product(gates):
        real, imag = held[gates[0], 0], held[gates[0], 1]
        for gate in gates[1:]:
            column = exact_dot(block(held[gate, 0], held[gate, 1]), jnp.concatenate([real, imag], axis=0))
            real, imag = column[:dim], column[dim:]
        return real, imag

    def joined(base, parts):
        wide[...] = jnp.zeros_like(wide)
        for index, (offset, gates) in enumerate(parts):
            real, imag = product(gates)
            for t in range(2):
                at = pl.ds(t * dim, dim) if offset == base else pl.ds(t, dim, stride=2)
                if index == 0:
                    wide[0, t, at, :] = real
                    wide[1, t, at, :] = imag
                else:
                    x = jnp.concatenate(
                        [jnp.concatenate([wide[p, c, at, :] for c in range(2)], axis=1) for p in range(2)], axis=0
                    )
                    y = exact_dot(block(real, imag), x)
                    for p in range(2):
                        for c in range(2):
                            wide[p, c, at, :] = y[p * dim : (p + 1) * dim, c * dim : (c + 1) * dim]
        return [jnp.concatenate([wide[p, 0], wide[p, 1]], axis=1) for p in range(2)]

    targets = iter(targets)
    for section in sections:
        for base, _, parts in section:
            target = next(targets)
            high, rest = split(block(*(joined(base, parts) if len(parts) > 1 else product(parts[0][1]))))
            target[...] = jnp.concatenate([high, rest, high], axis=1)
    real, imag = product(low)
    high, rest = split(block(real.T, -imag.T))
    low_ref[...] = jnp.concatenate([high, rest, high], axis=0)


def distances_of(count):
    half = count // 2
    far, near = list(range(count - 1, half - 1, -1)), list(range(half - 1, 0, -1))
    order = [0]
    while far or near:
        order += far[:2] + near[:2]
        far, near = far[2:], near[2:]
    return order


def partner(distance):
    return jnp.bitwise_xor(lax.axis_index("qa"), distance)


def split_kernel(x_ref, *outs):
    for distance, out_ref in zip(distances_of(len(outs)), outs):
        out_ref[...] = x_ref[partner(distance)]


def apply_stage(weights_ref, starts, load, store):
    dim = weights_ref.shape[0] // 2
    for pair in range(0, len(starts), 2):
        group = starts[pair : pair + 2]
        x = jnp.concatenate(
            [jnp.concatenate([load(part, start) for start in group], axis=1) for part in range(2)], axis=0
        )
        high, rest = split(x)
        y = bf_dot(weights_ref[...], jnp.concatenate([rest, high, high], axis=0))
        lanes = y.shape[1] // len(group)
        for part in range(2):
            for place, start in enumerate(group):
                store(part, start, y[part * dim : (part + 1) * dim, place * lanes : (place + 1) * lanes])


def stage_starts(stage, lane_bits, rows):
    base, bits, _ = stage
    dim, stride = 2**bits, 2 ** (base - lane_bits)
    return dim, stride, [h * dim * stride + l for h in range(rows // (dim * stride)) for l in range(stride)]


def run_stage(stage, weights_ref, lane_bits, source, target=None, store=None):
    dim, stride, starts = stage_starts(stage, lane_bits, source.shape[1])

    def load(part, start):
        if not interleaved(stage):
            return source[part, pl.ds(start, dim, stride=stride), :]
        half = dim // 2
        return jnp.concatenate(
            [source[part, pl.ds(start + t * stride, half, stride=2 * stride), :] for t in range(2)], axis=0
        )

    def plain(part, start, value):
        target[part, pl.ds(start, dim, stride=stride), :] = value

    apply_stage(weights_ref, starts, load, store or plain)


def run_top_stage(stage, weights_ref, lane_bits, source, halves):
    dim, stride, starts = stage_starts(stage, lane_bits, source.shape[1])

    def store(part, start, value):
        for t in range(2):
            halves[t][part, pl.ds(start, dim // 2, stride=stride), :] = value[t * dim // 2 : (t + 1) * dim // 2]

    apply_stage(weights_ref, starts, lambda part, start: source[part, pl.ds(start, dim, stride=stride), :], store)


def run_halves(stages, weights, lane_bits, halves, spares, last_store=None):
    for index, (stage, weights_ref) in enumerate(zip(stages, weights)):
        for t in range(2):
            store = None
            if last_store is not None and index == len(stages) - 1:
                store = functools.partial(last_store, t)
            run_stage(stage, weights_ref, lane_bits, halves[t], spares[t], store)
        halves, spares = spares, halves
    return halves


def first_kernel(stages, lane_bits, count, *refs):
    blocks, refs = refs[:count], refs[count:]
    low_ref, weights, refs = refs[0], refs[1 : 1 + len(stages)], refs[1 + len(stages) :]
    outs, (whole, *halves) = refs[:count], refs[count:]
    lanes = whole.shape[2]
    for distance, block_ref in zip(distances_of(count), blocks):
        size = block_ref.shape[0] // 2
        start = pl.multiple_of(partner(distance) * size, size)
        real = block_ref[pl.ds(0, size, stride=2), :]
        imag = block_ref[pl.ds(1, size, stride=2), :]
        high, rest = split(jnp.concatenate([real, imag], axis=1))
        y = bf_dot(jnp.concatenate([rest, high, high], axis=1), low_ref[...])
        whole[0, pl.ds(start, size), :] = y[:, :lanes]
        whole[1, pl.ds(start, size), :] = y[:, lanes:]
    run_top_stage(stages[0], weights[0], lane_bits, whole, halves[:2])
    done = run_halves(stages[1:], weights[1:], lane_bits, halves[:2], halves[2:])
    tops, mids, _, inner, _ = outs[0].shape
    for top in range(tops):
        for distance, out_ref in zip(distances_of(count), outs):
            dest = partner(distance)
            for mid in range(mids):
                start = pl.multiple_of((mid * count + dest) * inner, inner)
                for part in range(2):
                    out_ref[top, mid, part] = done[top][part, pl.ds(start, inner), :]


def second_kernel(stages, lane_bits, count, stays, *refs):
    blocks, weights, refs = refs[:count], refs[count : count + len(stages)], refs[count + len(stages) :]
    out_ref, one, two = refs
    core = lax.axis_index("qb")
    top = core if stays else 1 - core
    for distance, block_ref in zip(distances_of(count), blocks):
        source = partner(distance)
        _, mids, _, inner, _ = block_ref.shape
        for mid in range(mids):
            start = pl.multiple_of((mid * count + source) * inner, inner)
            for part in range(2):
                one[part, pl.ds(start, inner), :] = block_ref[top, mid, part]
    for index, (stage, weights_ref) in enumerate(zip(stages, weights)):
        run_stage(stage, weights_ref, lane_bits, one, out_ref if index == len(stages) - 1 else two)
        one, two = two, one


def third_kernel(stages, lane_bits, kept_ref, came_ref, *refs):
    weights, (out_ref, whole, *halves, sems) = refs[: len(stages)], refs[len(stages) :]
    results = halves[4:]
    half = kept_ref.shape[1]
    core = lax.axis_index("qb")
    whole[:, pl.ds(pl.multiple_of(core * half, half), half), :] = kept_ref[...]
    whole[:, pl.ds(pl.multiple_of((1 - core) * half, half), half), :] = came_ref[...]
    run_top_stage(stages[0], weights[0], lane_bits, whole, halves[:2])
    done = run_halves(stages[1:-1], weights[1:-1], lane_bits, halves[:2], halves[2:4])
    copies = []
    for t in range(2):
        dim, stride, _ = stage_starts(stages[-1], lane_bits, half)

        def store(part, start, value, t=t):
            results[t][pl.ds(2 * start + part, dim, stride=2 * stride), :] = value

        run_stage(stages[-1], weights[-1], lane_bits, done[t], store=store)
        size = 2 * half // PIECES
        for piece in range(PIECES):
            to = out_ref.at[pl.ds(t * 2 * half + piece * size, size)]
            copies.append(
                pltpu.make_async_copy(results[t].at[pl.ds(piece * size, size)], to, sems.at[t * PIECES + piece])
            )
            copies[-1].start()
    for copy in copies:
        copy.wait()


def call(kernel, name, out_shapes, in_specs, scratch, matmuls, *operands, limit=VMEM_LIMIT, out_spec=None):
    many = isinstance(out_shapes, tuple)
    vmem = out_spec or pl.BlockSpec(memory_space=pltpu.VMEM)
    return pl.pallas_call(
        kernel,
        out_shape=out_shapes,
        in_specs=in_specs,
        out_specs=(vmem,) * len(out_shapes) if many else vmem,
        scratch_shapes=scratch,
        compiler_params=pltpu.CompilerParams(vmem_limit_bytes=limit),
        cost_estimate=pl.CostEstimate(
            flops=int(matmuls * 3 * 2 * 256 * 256 * 1024), bytes_accessed=4 * 2**20, transcendentals=0
        ),
        name=name,
    )(*operands)


def per_device(state, gate_terms, path_bits):
    amps_local = state.shape[1]
    local_bits = amps_local.bit_length() - 1
    dim = gate_terms.shape[-1]
    gate_bits = dim.bit_length() - 1
    lanes, lane_bits = dim, gate_bits
    rows = amps_local // lanes
    qa = lax.axis_size("qa")
    qb = lax.axis_size("qb")
    low, sections = plan_gates(local_bits, gate_bits)
    sections = [join_windows(section, gate_bits) for section in sections]
    order = 2 * dim
    vmem = pl.BlockSpec(memory_space=pltpu.VMEM)
    hbm = pl.BlockSpec(memory_space=pltpu.HBM)
    shape = jax.ShapeDtypeStruct

    state = with_layout_constraint(state.reshape(2, rows, lanes), Layout(major_to_minor=(1, 0, 2)))
    state = state.swapaxes(0, 1).reshape(qa, 2 * rows // qa, lanes)
    blocks = call(
        split_kernel,
        "split_state",
        (shape((2 * rows // qa, lanes), F32),) * qa,
        [vmem],
        [],
        0,
        state,
    )

    def exchange(blocks):
        came = [blocks[0]]
        for distance, piece in zip(distances_of(qa)[1:], blocks[1:]):
            came.append(lax.ppermute(piece, "qa", [(i, i ^ distance) for i in range(qa)]))
        return came

    blocks = exchange(blocks)
    low_w, *weights = call(
        functools.partial(prepare_kernel, low, sections),
        "prepare_gates",
        (shape((3 * order, order), BF16),)
        + tuple(shape((2 * 2**bits, 6 * 2**bits), BF16) for section in sections for _, bits, _ in section),
        [pl.BlockSpec(memory_space=pltpu.SMEM), hbm],
        [
            pltpu.VMEM((gate_terms.shape[0], 2, dim, dim), F32),
            pltpu.VMEM((2, 2, 2 * dim, dim), F32),
            pltpu.SemaphoreType.DMA((gate_terms.shape[0],)),
        ],
        8,
        path_bits,
        gate_terms,
        limit=LARGE_VMEM,
    )
    counts = [len(section) for section in sections]
    weights = [weights[: counts[0]], weights[counts[0] : counts[0] + counts[1]], weights[counts[0] + counts[1] :]]
    inner = rows // (qa * qa)
    whole = pltpu.VMEM((2, rows, lanes), F32)
    half = pltpu.VMEM((2, rows // 2, lanes), F32)
    blocks = call(
        functools.partial(first_kernel, sections[0], lane_bits, qa),
        "first_section",
        (shape((qb, qa // qb, 2, inner, lanes), F32),) * qa,
        [vmem] * (qa + 1 + counts[0]),
        [whole] + [half] * 4,
        5,
        *blocks,
        low_w,
        *weights[0],
    )
    blocks = exchange(blocks)
    halves = []
    for stays in (False, True):
        halves.append(
            call(
                functools.partial(second_kernel, sections[1], lane_bits, qa, stays),
                "second_section_kept" if stays else "second_section_sent",
                shape((2, rows // qb, lanes), F32),
                [vmem] * (qa + counts[1]),
                [half] * 2,
                1.5,
                *blocks,
                *weights[1],
            )
        )
        if not stays:
            came = lax.ppermute(halves[0], "qb", [(i, 1 - i) for i in range(qb)])
    final = call(
        functools.partial(third_kernel, sections[2], lane_bits),
        "third_section",
        shape((2 * rows, lanes), F32),
        [vmem] * (2 + counts[2]),
        [whole] + [half] * 4 + [pltpu.VMEM((rows, lanes), F32)] * 2 + [pltpu.SemaphoreType.DMA((2 * PIECES,))],
        4,
        halves[1],
        came,
        *weights[2],
        out_spec=hbm,
    )
    return final.reshape(rows, 2, lanes).swapaxes(0, 1).reshape(2, amps_local)


def solution(mesh):
    return jax.shard_map(
        per_device,
        mesh=mesh,
        in_specs=(P(None, ("paths", "qa", "qb")), P(), P("paths")),
        out_specs=P(None, ("paths", "qa", "qb")),
        check_vma=False,
    )
```

```python
import functools

import jax
import jax.numpy as jnp
from jax import lax
from jax.experimental import pallas as pl
from jax.experimental.layout import Layout, with_layout_constraint
from jax.experimental.pallas import tpu as pltpu
from jax.sharding import PartitionSpec as P

F32 = jnp.float32
BF16 = jnp.bfloat16
VMEM_LIMIT = 14 * 1024 * 1024
LARGE_VMEM = 51 * 1024 * 1024
PIECES = 4
CHUNKS = 2


def window_offsets(span, gate_bits):
    return [0, span, gate_bits, span - 1, gate_bits + 1, span - 2]


def plan_gates(local_bits, gate_bits):
    outer = window_offsets(local_bits - gate_bits, gate_bits)
    inner = window_offsets(local_bits - gate_bits - 1, gate_bits)
    low, sections = [], []
    for number, offsets in enumerate((outer, inner, outer)):
        section = []
        for index, offset in enumerate(offsets):
            gate = 6 * number + index
            if offset == 0:
                low.append(gate)
            elif section and section[-1][0] == offset:
                section[-1][1].append(gate)
            else:
                section.append((offset, [gate]))
        sections.append(section)
    return low, sections


def join_windows(section, gate_bits):
    stages = []
    for offset, gates in section:
        if stages:
            offsets = [o for o, _ in stages[-1]] + [offset]
            if max(offsets) - min(offsets) <= 1:
                stages[-1].append((offset, gates))
                continue
        stages.append([(offset, gates)])
    return [
        (min(o for o, _ in parts), gate_bits + (len(parts) > 1), parts)
        for parts in stages
    ]


def interleaved(stage):
    base, _, parts = stage
    return parts[0][0] != base


def exact_dot(a, b):
    return lax.dot_general(
        a, b, (((1,), (0,)), ((), ())), precision=lax.Precision.HIGHEST, preferred_element_type=F32
    )


def split(x):
    high = x.astype(BF16)
    return high, (x - high.astype(F32)).astype(BF16)


def bf_dot(a, b):
    return jnp.dot(a, b, preferred_element_type=F32)


def block(real, imag):
    return jnp.concatenate(
        [jnp.concatenate([real, -imag], axis=1), jnp.concatenate([imag, real], axis=1)], axis=0
    )


def prepare_kernel(low, stages, bits_ref, gates_ref, *refs):
    mark_ref, *targets, held, wides, sems = refs
    mark_ref[...] = jnp.zeros(mark_ref.shape, F32)
    copies = []
    for gate in sorted(low + [gate for _, _, parts in stages for _, gates in parts for gate in gates]):
        copy = pltpu.make_async_copy(gates_ref.at[gate, bits_ref[gate]], held.at[gate], sems.at[gate])
        copy.start()
        copies.append(copy)
    for copy in copies:
        copy.wait()
    dim = held.shape[-1]

    def product(gates):
        real, imag = held[gates[0], 0], held[gates[0], 1]
        for gate in gates[1:]:
            column = exact_dot(block(held[gate, 0], held[gate, 1]), jnp.concatenate([real, imag], axis=0))
            real, imag = column[:dim], column[dim:]
        return real, imag

    def joined(wide, base, parts):
        wide[...] = jnp.zeros(wide.shape, F32)
        for index, (offset, gates) in enumerate(parts):
            real, imag = product(gates)
            for t in range(2):
                at = pl.ds(t * dim, dim) if offset == base else pl.ds(t, dim, stride=2)
                if index == 0:
                    wide[0, t, at, :] = real
                    wide[1, t, at, :] = imag
                else:
                    x = jnp.concatenate(
                        [jnp.concatenate([wide[p, c, at, :] for c in range(2)], axis=1) for p in range(2)], axis=0
                    )
                    y = exact_dot(block(real, imag), x)
                    for p in range(2):
                        for c in range(2):
                            wide[p, c, at, :] = y[p * dim : (p + 1) * dim, c * dim : (c + 1) * dim]
        return [jnp.concatenate([wide[p, 0], wide[p, 1]], axis=1) for p in range(2)]

    for slot, (target, (base, _, parts)) in enumerate(zip(targets, stages)):
        both = joined(wides.at[slot], base, parts) if len(parts) > 1 else product(parts[0][1])
        high, rest = split(jnp.concatenate(both, axis=0))
        target[...] = jnp.concatenate([high, rest, high], axis=1)
    if low:
        real, imag = product(low)
        whole = block(real.T, -imag.T)
        part = dim // CHUNKS
        pieces = []
        for chunk in range(CHUNKS):
            pieces += [whole[chunk * part : (chunk + 1) * part], whole[dim + chunk * part : dim + (chunk + 1) * part]]
        high, rest = split(jnp.concatenate(pieces, axis=0))
        targets[-1][...] = jnp.concatenate([high, rest, high], axis=0)


def place(count):
    me = lax.axis_index("qa")
    return me // count, lax.rem(me, count)


def packed(chunk, rows_ref, index):
    size = rows_ref.shape[1] // 2
    real = rows_ref[index, pl.ds(0, size, stride=2), :]
    imag = rows_ref[index, pl.ds(1, size, stride=2), :]
    half = real.shape[1] // 2
    left = lax.broadcasted_iota(jnp.int32, real.shape, 1) < half
    if chunk == 0:
        return jnp.where(left, real, pltpu.roll(imag, half, 1))
    return jnp.where(left, pltpu.roll(real, half, 1), imag)


def pack_far_kernel(count, x_ref, keep_ref, send_ref):
    far, _ = place(count)
    for j in range(count):
        keep_ref[j] = packed(0, x_ref, far * count + j)
        send_ref[j] = packed(0, x_ref, (1 - far) * count + j)


def pack_near_kernel(count, x_ref, *outs):
    _, near = place(count)
    for distance, out_ref in enumerate(outs):
        for t in range(2):
            out_ref[t] = packed(1, x_ref, t * count + jnp.bitwise_xor(near, distance))


def to_near_kernel(count, keep_ref, came_ref, *outs):
    far, near = place(count)
    for distance, out_ref in enumerate(outs):
        index = jnp.bitwise_xor(near, distance)
        out_ref[far] = keep_ref[index]
        out_ref[1 - far] = came_ref[index]


def to_far_kernel(count, *refs):
    blocks, (keep_ref, send_ref) = refs[:count], refs[count:]
    far, _ = place(count)
    for distance, block_ref in enumerate(blocks):
        keep_ref[distance] = block_ref[far]
        send_ref[distance] = block_ref[1 - far]


def pieces_of_pairs(count, blocks):
    _, near = place(count)
    for distance, block_ref in enumerate(blocks):
        for t in range(2):
            yield t, jnp.bitwise_xor(near, distance), block_ref.at[t]


def pieces_of_sides(count, keep_ref, came_ref):
    far, near = place(count)
    for distance in range(count):
        yield far, jnp.bitwise_xor(near, distance), keep_ref.at[distance]
        yield 1 - far, jnp.bitwise_xor(near, distance), came_ref.at[distance]


def put_sources(count, pieces, target):
    for t, index, piece in pieces:
        size = piece.shape[0]
        target[pl.ds(pl.multiple_of((t * count + index) * size, size), size), :] = piece[...]


def put_middles(count, pieces, target):
    for t, index, piece in pieces:
        outer, inner, _ = piece.shape
        for a in range(outer):
            start = (a * 2 * count + t * count + index) * inner
            target[pl.ds(pl.multiple_of(start, inner), inner), :] = piece[a]


def take_middle(count, source, t, index, piece):
    outer, inner, _ = piece.shape
    for a in range(outer):
        start = (a * 2 * count + t * count + index) * inner
        piece[a] = source[pl.ds(pl.multiple_of(start, inner), inner), :]


def apply_stage(stage, weights_ref, lane_bits, source, target):
    base, bits, _ = stage
    dim, stride = 2**bits, 2 ** (base - lane_bits)
    rows, lanes = source.shape
    starts = [h * dim * stride + l for h in range(rows // (dim * stride)) for l in range(stride)]

    def load(start):
        if not interleaved(stage):
            return source[pl.ds(start, dim, stride=stride), :]
        return jnp.concatenate(
            [source[pl.ds(start + t * stride, dim // 2, stride=2 * stride), :] for t in range(2)], axis=0
        )

    for pair in range(0, len(starts), 2):
        group = starts[pair : pair + 2]
        high, rest = split(jnp.concatenate([load(start) for start in group], axis=1))
        both = bf_dot(weights_ref[...], jnp.concatenate([rest, high, high], axis=0))
        for spot, start in enumerate(group):
            straight = both[:dim, spot * lanes : (spot + 1) * lanes]
            turned = pltpu.roll(both[dim:, spot * lanes : (spot + 1) * lanes], lanes // 2, 1)
            left = lax.broadcasted_iota(jnp.int32, turned.shape, 1) < lanes // 2
            target[pl.ds(start, dim, stride=stride), :] = straight + jnp.where(left, -turned, turned)


def run_stages(stages, weights, lane_bits, one, two):
    for stage, weights_ref in zip(stages, weights):
        apply_stage(stage, weights_ref, lane_bits, one, two)
        one, two = two, one
    return one


def give_halves(done, keep_ref, send_ref):
    half = done.shape[0] // 2
    core = lax.axis_index("qb")
    keep_ref[...] = done[pl.ds(pl.multiple_of(core * half, half), half), :]
    send_ref[...] = done[pl.ds(pl.multiple_of((1 - core) * half, half), half), :]


def put_halves(keep_ref, came_ref, target):
    half = keep_ref.shape[0]
    core = lax.axis_index("qb")
    target[pl.ds(pl.multiple_of(core * half, half), half), :] = keep_ref[...]
    target[pl.ds(pl.multiple_of((1 - core) * half, half), half), :] = came_ref[...]


def early_top_kernel(stages, lane_bits, count, *refs):
    blocks, weights, refs = refs[:count], refs[count : count + len(stages)], refs[count + len(stages) :]
    keep_ref, send_ref, one, two = refs
    put_sources(count, pieces_of_pairs(count, blocks), one)
    give_halves(run_stages(stages, weights, lane_bits, one, two), keep_ref, send_ref)


def early_rest_kernel(stages, lane_bits, count, half_ref, came_ref, *refs):
    weights, (keep_ref, send_ref, one, two) = refs[: len(stages)], refs[len(stages) :]
    put_halves(half_ref, came_ref, one)
    done = run_stages(stages, weights, lane_bits, one, two)
    far, _ = place(count)
    for j in range(count):
        take_middle(count, done, far, j, keep_ref.at[j])
        take_middle(count, done, 1 - far, j, send_ref.at[j])


def early_later_kernel(stages, lane_bits, count, *refs):
    blocks, weights, refs = refs[:count], refs[count : count + len(stages)], refs[count + len(stages) :]
    out_ref, one, two = refs
    put_middles(count, pieces_of_pairs(count, blocks), one)
    done = run_stages(stages[:-1], weights[:-1], lane_bits, one, two)
    apply_stage(stages[-1], weights[-1], lane_bits, done, out_ref)


def late_top_kernel(stages, lane_bits, count, *refs):
    keep_ref, came_ref, weights, refs = refs[0], refs[1], refs[2 : 2 + len(stages)], refs[2 + len(stages) :]
    half_ref, send_ref, one, two = refs
    put_sources(count, pieces_of_sides(count, keep_ref, came_ref), one)
    give_halves(run_stages(stages, weights, lane_bits, one, two), half_ref, send_ref)


def late_rest_kernel(stages, lane_bits, count, keep_ref, came_ref, *refs):
    weights, refs = refs[: len(stages)], refs[len(stages) :]
    outs, (one, two) = refs[:count], refs[count:]
    put_halves(keep_ref, came_ref, one)
    done = run_stages(stages, weights, lane_bits, one, two)
    _, near = place(count)
    for distance, out_ref in enumerate(outs):
        for t in range(2):
            take_middle(count, done, t, jnp.bitwise_xor(near, distance), out_ref.at[t])


def last_kernel(stages, lane_bits, count, keep_ref, came_ref, *refs):
    weights, refs = refs[: len(stages)], refs[len(stages) :]
    low_ref, other_ref, out_ref, one, two, result, sems = refs
    put_middles(count, pieces_of_sides(count, keep_ref, came_ref), one)
    done = run_stages(stages, weights, lane_bits, one, two)
    rows, lanes = done.shape
    step = rows // PIECES
    copies = []
    for piece in range(PIECES):
        start = piece * step
        x = jnp.concatenate([other_ref[pl.ds(start, step), :], done[pl.ds(start, step), :]], axis=1)
        high, rest = split(x)
        y = bf_dot(jnp.concatenate([rest, high, high], axis=1), low_ref[...])
        result[pl.ds(2 * start, step, stride=2), :] = y[:, :lanes]
        result[pl.ds(2 * start + 1, step, stride=2), :] = y[:, lanes:]
        at = pl.ds(2 * start, 2 * step)
        copies.append(pltpu.make_async_copy(result.at[at], out_ref.at[at], sems.at[piece]))
        copies[-1].start()
    for copy in copies:
        copy.wait()


def call(kernel, name, out_shapes, in_specs, scratch, matmuls, *operands, limit=VMEM_LIMIT, out_spec=None, after=()):
    many = isinstance(out_shapes, tuple)
    vmem = out_spec or pl.BlockSpec(memory_space=pltpu.VMEM)
    count = len(operands)

    def body(*refs):
        kernel(*refs[:count], *refs[count + len(after) :])

    return pl.pallas_call(
        body,
        out_shape=out_shapes,
        in_specs=list(in_specs) + [pl.BlockSpec(memory_space=pl.ANY)] * len(after),
        out_specs=(vmem,) * len(out_shapes) if many else vmem,
        scratch_shapes=scratch,
        compiler_params=pltpu.CompilerParams(vmem_limit_bytes=limit),
        cost_estimate=pl.CostEstimate(flops=1, bytes_accessed=1, transcendentals=0),
        name=name,
    )(*operands, *after)


def per_device(state, gate_terms, path_bits):
    amps_local = state.shape[1]
    local_bits = amps_local.bit_length() - 1
    dim = gate_terms.shape[-1]
    gate_bits = dim.bit_length() - 1
    lanes, lane_bits = dim, gate_bits
    rows = amps_local // lanes
    qa = lax.axis_size("qa")
    qb = lax.axis_size("qb")
    near = qa // 2
    low, sections = plan_gates(local_bits, gate_bits)
    first, second, third = [join_windows(section, gate_bits) for section in sections]
    vmem = pl.BlockSpec(memory_space=pltpu.VMEM)
    hbm = pl.BlockSpec(memory_space=pltpu.HBM)
    shape = jax.ShapeDtypeStruct
    buffer = pltpu.VMEM((rows, lanes), F32)
    half = shape((rows // qb, lanes), F32)

    def prepare(name, stages, low):
        outs = tuple(shape((2 * 2**bits, 3 * 2**bits), BF16) for _, bits, _ in stages)
        return call(
            functools.partial(prepare_kernel, low, stages),
            name,
            (shape((8, lanes), F32),) + outs + ((shape((6 * dim, 2 * dim), BF16),) if low else ()),
            [pl.BlockSpec(memory_space=pltpu.SMEM), hbm],
            [
                pltpu.VMEM((gate_terms.shape[0], 2, dim, dim), F32),
                pltpu.VMEM((len(stages), 2, 2, 2 * dim, dim), F32),
                pltpu.SemaphoreType.DMA((gate_terms.shape[0],)),
            ],
            4,
            path_bits,
            gate_terms,
            limit=LARGE_VMEM,
        )

    def far_step(piece):
        return lax.ppermute(piece, "qa", [(i, i ^ near) for i in range(qa)])

    def near_step(blocks):
        moved = [
            lax.ppermute(piece, "qa", [(i, i ^ distance) for i in range(qa)])
            for distance, piece in enumerate(blocks)
            if distance
        ]
        return [blocks[0], *moved]

    def core_step(piece):
        return lax.ppermute(piece, "qb", [(i, 1 - i) for i in range(qb)])

    def to_near(name, keep, came, after):
        outs = (shape((2,) + keep.shape[1:], F32),) * near
        return call(functools.partial(to_near_kernel, near), name, outs, [vmem] * 2, [], 0, keep, came, after=after)

    def to_far(name, blocks, after=()):
        outs = (shape((near,) + blocks[0].shape[1:], F32),) * 2
        return call(functools.partial(to_far_kernel, near), name, outs, [vmem] * near, [], 0, *blocks, after=after)

    state = with_layout_constraint(state.reshape(2, rows, lanes), Layout(major_to_minor=(1, 0, 2)))
    state = state.swapaxes(0, 1).reshape(qa, 2 * rows // qa, lanes)
    source = (rows // qa, lanes)
    middle = (qa, rows // (qa * qa), lanes)

    early_keep, send = call(
        functools.partial(pack_far_kernel, near), "pack_far", (shape((near,) + source, F32),) * 2, [vmem], [], 0, state
    )
    early_came = far_step(send)
    late = call(
        functools.partial(pack_near_kernel, near),
        "pack_near",
        (shape((2,) + source, F32),) * near,
        [vmem],
        [],
        0,
        state,
    )
    late = near_step(late)
    mark_first, *first_w = prepare("prepare_first", first, [])
    late_keep, send = to_far("late_to_far", late, [mark_first])
    late_came = far_step(send)
    mark_second, *second_w = prepare("prepare_second", second, [])
    early = near_step(to_near("early_to_near", early_keep, early_came, [mark_second]))
    mark_third, *third_w, low_w = prepare("prepare_third", third, low)

    keep, send = call(
        functools.partial(early_top_kernel, first[:1], lane_bits, near),
        "early_first_top",
        (half,) * 2,
        [vmem] * (near + 1),
        [buffer] * 2,
        0.5,
        *early,
        first_w[0],
        after=[mark_third],
    )
    came = core_step(send)
    early_keep, send = call(
        functools.partial(early_rest_kernel, first[1:], lane_bits, near),
        "early_first_rest",
        (shape((near,) + middle, F32),) * 2,
        [vmem] * (2 + len(first) - 1),
        [buffer] * 2,
        1.5,
        keep,
        came,
        *first_w[1:],
    )
    early_came = far_step(send)

    keep, send = call(
        functools.partial(late_top_kernel, first[:1], lane_bits, near),
        "late_first_top",
        (half,) * 2,
        [vmem] * 3,
        [buffer] * 2,
        0.5,
        late_keep,
        late_came,
        first_w[0],
    )
    came = core_step(send)
    late = call(
        functools.partial(late_rest_kernel, first[1:], lane_bits, near),
        "late_first_rest",
        (shape((2,) + middle, F32),) * near,
        [vmem] * (2 + len(first) - 1),
        [buffer] * 2,
        1.5,
        keep,
        came,
        *first_w[1:],
    )
    late = near_step(late)
    late_keep, send = to_far("late_to_far_again", late)
    late_came = far_step(send)

    early = near_step(to_near("early_to_near_again", early_keep, early_came, ()))
    done = call(
        functools.partial(early_later_kernel, second + third, lane_bits, near),
        "early_later",
        shape((rows, lanes), F32),
        [vmem] * (near + len(second) + len(third)),
        [buffer] * 2,
        3.5,
        *early,
        *second_w,
        *third_w,
    )
    final = call(
        functools.partial(last_kernel, second + third, lane_bits, near),
        "late_last",
        shape((2 * rows, lanes), F32),
        [vmem] * (4 + len(second) + len(third)),
        [buffer] * 2 + [pltpu.VMEM((2 * rows, lanes), F32), pltpu.SemaphoreType.DMA((PIECES,))],
        4.5,
        late_keep,
        late_came,
        *second_w,
        *third_w,
        low_w,
        done,
        out_spec=hbm,
    )
    return final.reshape(rows, 2, lanes).swapaxes(0, 1).reshape(2, amps_local)


def solution(mesh):
    return jax.shard_map(
        per_device,
        mesh=mesh,
        in_specs=(P(None, ("paths", "qa", "qb")), P(), P("paths")),
        out_specs=P(None, ("paths", "qa", "qb")),
        check_vma=False,
    )
```

```python
import functools

import jax
import jax.numpy as jnp
from jax import lax
from jax.experimental import pallas as pl
from jax.experimental.layout import Layout, with_layout_constraint
from jax.experimental.pallas import tpu as pltpu
from jax.sharding import PartitionSpec as P

F32 = jnp.float32
BF16 = jnp.bfloat16
VMEM_LIMIT = 14 * 1024 * 1024
LARGE_VMEM = 48 * 1024 * 1024
PIECES = 4


def window_offsets(span, gate_bits):
    return [0, span, gate_bits, span - 1, gate_bits + 1, span - 2]


def plan_gates(local_bits, gate_bits):
    outer = window_offsets(local_bits - gate_bits, gate_bits)
    inner = window_offsets(local_bits - gate_bits - 1, gate_bits)
    low, sections = [], []
    for number, offsets in enumerate((outer, inner, outer)):
        section = []
        for index, offset in enumerate(offsets):
            gate = 6 * number + index
            if offset == 0:
                low.append(gate)
            elif section and section[-1][0] == offset:
                section[-1][1].append(gate)
            else:
                section.append((offset, [gate]))
        sections.append(section)
    return low, sections


def join_windows(section, gate_bits):
    stages = []
    for offset, gates in section:
        if stages:
            offsets = [o for o, _ in stages[-1]] + [offset]
            if max(offsets) - min(offsets) <= 1:
                stages[-1].append((offset, gates))
                continue
        stages.append([(offset, gates)])
    return [
        (min(o for o, _ in parts), gate_bits + (len(parts) > 1), parts)
        for parts in stages
    ]


def interleaved(stage):
    base, _, parts = stage
    return parts[0][0] != base


def exact_dot(a, b):
    return lax.dot_general(
        a, b, (((1,), (0,)), ((), ())), precision=lax.Precision.HIGHEST, preferred_element_type=F32
    )


def split(x):
    high = x.astype(BF16)
    return high, (x - high.astype(F32)).astype(BF16)


def bf_dot(a, b):
    return jnp.dot(a, b, preferred_element_type=F32)


def block(real, imag):
    return jnp.concatenate(
        [jnp.concatenate([real, -imag], axis=1), jnp.concatenate([imag, real], axis=1)], axis=0
    )


def relative(matrix, number, count):
    dim = matrix.shape[1]
    column = lax.broadcasted_iota(jnp.int32, matrix.shape, 1)
    row = lax.broadcasted_iota(jnp.int32, matrix.shape, 0)
    if number == 0:
        size = dim // count
        spot, source = column // size, jnp.zeros_like(column)
        for index, distance in enumerate(distances_of(count)):
            source = jnp.where(spot == index, partner(distance), source)
        natural = source * size + lax.rem(column, size)
    else:
        natural = jnp.bitwise_xor(column, lax.axis_index("qb") * (dim // 2))
    return exact_dot(matrix, jnp.where(row == natural, 1.0, 0.0).astype(F32))


def prepare_kernel(low, sections, count, bits_ref, gates_ref, low_ref, *refs):
    *targets, held, wide, sems = refs
    copies = []
    for gate in range(held.shape[0]):
        copy = pltpu.make_async_copy(gates_ref.at[gate, bits_ref[gate]], held.at[gate], sems.at[gate])
        copy.start()
        copies.append(copy)
    for copy in copies:
        copy.wait()
    dim = held.shape[-1]

    def product(gates):
        real, imag = held[gates[0], 0], held[gates[0], 1]
        for gate in gates[1:]:
            column = exact_dot(block(held[gate, 0], held[gate, 1]), jnp.concatenate([real, imag], axis=0))
            real, imag = column[:dim], column[dim:]
        return real, imag

    def joined(base, parts):
        wide[...] = jnp.zeros_like(wide)
        for index, (offset, gates) in enumerate(parts):
            real, imag = product(gates)
            for t in range(2):
                at = pl.ds(t * dim, dim) if offset == base else pl.ds(t, dim, stride=2)
                if index == 0:
                    wide[0, t, at, :] = real
                    wide[1, t, at, :] = imag
                else:
                    x = jnp.concatenate(
                        [jnp.concatenate([wide[p, c, at, :] for c in range(2)], axis=1) for p in range(2)], axis=0
                    )
                    y = exact_dot(block(real, imag), x)
                    for p in range(2):
                        for c in range(2):
                            wide[p, c, at, :] = y[p * dim : (p + 1) * dim, c * dim : (c + 1) * dim]
        return [jnp.concatenate([wide[p, 0], wide[p, 1]], axis=1) for p in range(2)]

    for number, section in enumerate(sections):
        weights, targets = targets[: len(section)], targets[len(section) :]
        for target, (base, _, parts) in zip(weights, section):
            if len(parts) > 1:
                high, rest = split(block(*joined(base, parts)))
                target[...] = jnp.concatenate([high, rest, high], axis=1)
                continue
            pair = product(parts[0][1])
            if number != 1 and target is weights[0]:
                pair = [relative(x, number, count) for x in pair]
            high, rest = split(block(*pair))
            target[...] = jnp.concatenate([high, rest], axis=0)
    real, imag = product(low)
    high, rest = split(block(real.T, -imag.T))
    low_ref[...] = jnp.concatenate([high, rest, high], axis=0)


def distances_of(count):
    half = count // 2
    far, near = list(range(count - 1, half - 1, -1)), list(range(half - 1, 0, -1))
    order = [0]
    while far or near:
        order += far[:2] + near[:2]
        far, near = far[2:], near[2:]
    return order


def partner(distance):
    return jnp.bitwise_xor(lax.axis_index("qa"), distance)


def split_kernel(x_ref, *outs):
    for distance, out_ref in zip(distances_of(len(outs)), outs):
        out_ref[...] = x_ref[partner(distance)]


def apply_stage(weights_ref, starts, load, store):
    stacked = weights_ref.shape[0] > weights_ref.shape[1]
    dim = weights_ref.shape[1] // 2 if stacked else weights_ref.shape[0] // 2
    for pair in range(0, len(starts), 2):
        group = starts[pair : pair + 2]
        x = jnp.concatenate(
            [jnp.concatenate([load(part, start) for start in group], axis=1) for part in range(2)], axis=0
        )
        high, rest = split(x)
        if stacked:
            both = bf_dot(weights_ref[...], high)
            y = bf_dot(weights_ref[: 2 * dim], rest) + both[2 * dim :] + both[: 2 * dim]
        else:
            y = bf_dot(weights_ref[...], jnp.concatenate([rest, high, high], axis=0))
        lanes = y.shape[1] // len(group)
        for part in range(2):
            for place, start in enumerate(group):
                store(part, start, y[part * dim : (part + 1) * dim, place * lanes : (place + 1) * lanes])


def stage_starts(stage, lane_bits, rows):
    base, bits, _ = stage
    dim, stride = 2**bits, 2 ** (base - lane_bits)
    return dim, stride, [h * dim * stride + l for h in range(rows // (dim * stride)) for l in range(stride)]


def run_stage(stage, weights_ref, lane_bits, source, target=None, store=None):
    dim, stride, starts = stage_starts(stage, lane_bits, source.shape[1])

    def load(part, start):
        if not interleaved(stage):
            return source[part, pl.ds(start, dim, stride=stride), :]
        half = dim // 2
        return jnp.concatenate(
            [source[part, pl.ds(start + t * stride, half, stride=2 * stride), :] for t in range(2)], axis=0
        )

    def plain(part, start, value):
        target[part, pl.ds(start, dim, stride=stride), :] = value

    apply_stage(weights_ref, starts, load, store or plain)


def run_top_stage(stage, weights_ref, lane_bits, source, halves):
    rows = 2 * halves[0].shape[1]
    dim, stride, starts = stage_starts(stage, lane_bits, rows)

    def store(part, start, value):
        for t in range(2):
            halves[t][part, pl.ds(start, dim // 2, stride=stride), :] = value[t * dim // 2 : (t + 1) * dim // 2]

    def load(part, start):
        if not isinstance(source, tuple):
            return source[part, pl.ds(start, dim, stride=stride), :]
        return jnp.concatenate([half[part, pl.ds(start, dim // 2, stride=stride), :] for half in source], axis=0)

    apply_stage(weights_ref, starts, load, store)


def run_halves(stages, weights, lane_bits, halves, spares, last_store=None):
    for index, (stage, weights_ref) in enumerate(zip(stages, weights)):
        for t in range(2):
            store = None
            if last_store is not None and index == len(stages) - 1:
                store = functools.partial(last_store, t)
            run_stage(stage, weights_ref, lane_bits, halves[t], spares[t], store)
        halves, spares = spares, halves
    return halves


def low_gate(blocks, low_ref, whole):
    lanes = whole.shape[2]
    for spot, block_ref in blocks:
        size = block_ref.shape[0] // 2
        real = block_ref[pl.ds(0, size, stride=2), :]
        imag = block_ref[pl.ds(1, size, stride=2), :]
        high, rest = split(jnp.concatenate([real, imag], axis=1))
        y = bf_dot(jnp.concatenate([rest, high, high], axis=1), low_ref[...])
        whole[0, pl.ds(spot * size, size), :] = y[:, :lanes]
        whole[1, pl.ds(spot * size, size), :] = y[:, lanes:]


def low_kernel(spots, *refs):
    *blocks, low_ref, whole = refs
    low_gate(zip(spots, blocks), low_ref, whole)


def first_kernel(stages, lane_bits, count, spots, *refs):
    _, *blocks = refs[: 1 + len(spots)]
    refs = refs[1 + len(spots) :]
    low_ref, weights, refs = refs[0], refs[1 : 1 + len(stages)], refs[1 + len(stages) :]
    outs, (whole, *halves) = refs[:count], refs[count:]
    low_gate(zip(spots, blocks), low_ref, whole)
    run_top_stage(stages[0], weights[0], lane_bits, whole, halves[:2])
    done = run_halves(stages[1:], weights[1:], lane_bits, halves[:2], halves[2:])
    tops, mids, _, inner, _ = outs[0].shape
    for top in range(tops):
        for distance, out_ref in zip(distances_of(count), outs):
            dest = partner(distance)
            for mid in range(mids):
                start = pl.multiple_of((mid * count + dest) * inner, inner)
                for part in range(2):
                    out_ref[top, mid, part] = done[top][part, pl.ds(start, inner), :]


def second_kernel(stages, lane_bits, count, stays, *refs):
    blocks, weights, refs = refs[:count], refs[count : count + len(stages)], refs[count + len(stages) :]
    out_ref, one, two = refs
    core = lax.axis_index("qb")
    top = core if stays else 1 - core
    for distance, block_ref in zip(distances_of(count), blocks):
        source = partner(distance)
        _, mids, _, inner, _ = block_ref.shape
        for mid in range(mids):
            start = pl.multiple_of((mid * count + source) * inner, inner)
            for part in range(2):
                one[part, pl.ds(start, inner), :] = block_ref[top, mid, part]
    for index, (stage, weights_ref) in enumerate(zip(stages, weights)):
        run_stage(stage, weights_ref, lane_bits, one, out_ref if index == len(stages) - 1 else two)
        one, two = two, one


def third_kernel(stages, lane_bits, kept_ref, came_ref, *refs):
    weights, (out_ref, *halves, sems) = refs[: len(stages)], refs[len(stages) :]
    results = halves[4:]
    half = kept_ref.shape[1]
    run_top_stage(stages[0], weights[0], lane_bits, (kept_ref, came_ref), halves[:2])
    done = run_halves(stages[1:-1], weights[1:-1], lane_bits, halves[:2], halves[2:4])
    copies = []
    for t in range(2):
        dim, stride, _ = stage_starts(stages[-1], lane_bits, half)

        def store(part, start, value, t=t):
            results[t][pl.ds(2 * start + part, dim, stride=2 * stride), :] = value

        run_stage(stages[-1], weights[-1], lane_bits, done[t], store=store)
        size = 2 * half // PIECES
        for piece in range(PIECES):
            to = out_ref.at[pl.ds(t * 2 * half + piece * size, size)]
            copies.append(
                pltpu.make_async_copy(results[t].at[pl.ds(piece * size, size)], to, sems.at[t * PIECES + piece])
            )
            copies[-1].start()
    for copy in copies:
        copy.wait()


def call(kernel, name, out_shapes, in_specs, scratch, matmuls, *operands, limit=VMEM_LIMIT, out_spec=None, aliases=None):
    many = isinstance(out_shapes, tuple)
    vmem = out_spec or pl.BlockSpec(memory_space=pltpu.VMEM)
    return pl.pallas_call(
        kernel,
        out_shape=out_shapes,
        in_specs=in_specs,
        out_specs=(vmem,) * len(out_shapes) if many else vmem,
        scratch_shapes=scratch,
        input_output_aliases=aliases or {},
        compiler_params=pltpu.CompilerParams(vmem_limit_bytes=limit),
        cost_estimate=pl.CostEstimate(
            flops=int(matmuls * 3 * 2 * 256 * 256 * 1024), bytes_accessed=4 * 2**20, transcendentals=0
        ),
        name=name,
    )(*operands)


def per_device(state, gate_terms, path_bits):
    amps_local = state.shape[1]
    local_bits = amps_local.bit_length() - 1
    dim = gate_terms.shape[-1]
    gate_bits = dim.bit_length() - 1
    lanes, lane_bits = dim, gate_bits
    rows = amps_local // lanes
    qa = lax.axis_size("qa")
    qb = lax.axis_size("qb")
    low, sections = plan_gates(local_bits, gate_bits)
    sections = [join_windows(section, gate_bits) for section in sections]
    order = 2 * dim
    vmem = pl.BlockSpec(memory_space=pltpu.VMEM)
    hbm = pl.BlockSpec(memory_space=pltpu.HBM)
    shape = jax.ShapeDtypeStruct

    state = with_layout_constraint(state.reshape(2, rows, lanes), Layout(major_to_minor=(1, 0, 2)))
    state = state.swapaxes(0, 1).reshape(qa, 2 * rows // qa, lanes)
    blocks = call(
        split_kernel,
        "split_state",
        (shape((2 * rows // qa, lanes), F32),) * qa,
        [vmem],
        [],
        0,
        state,
    )

    index = jnp.bitwise_xor(lax.axis_index("qa"), distances_of(qa)[1])
    blocks = list(blocks)
    blocks[1] = lax.dynamic_index_in_dim(state, index, 0, keepdims=False)

    def exchange(blocks):
        came = [blocks[0]]
        for distance, piece in zip(distances_of(qa)[1:], blocks[1:]):
            came.append(lax.ppermute(piece, "qa", [(i, i ^ distance) for i in range(qa)]))
        return came

    blocks = exchange(blocks)
    low_w, *weights = call(
        functools.partial(prepare_kernel, low, sections, qa),
        "prepare_gates",
        (shape((3 * order, order), BF16),)
        + tuple(
            shape((2 * 2**bits, 6 * 2**bits) if len(parts) > 1 else (4 * 2**bits, 2 * 2**bits), BF16)
            for section in sections
            for _, bits, parts in section
        ),
        [pl.BlockSpec(memory_space=pltpu.SMEM), hbm],
        [
            pltpu.VMEM((gate_terms.shape[0], 2, dim, dim), F32),
            pltpu.VMEM((2, 2, 2 * dim, dim), F32),
            pltpu.SemaphoreType.DMA((gate_terms.shape[0],)),
        ],
        8,
        path_bits,
        gate_terms,
        limit=LARGE_VMEM,
    )
    counts = [len(section) for section in sections]
    weights = [weights[: counts[0]], weights[counts[0] : counts[0] + counts[1]], weights[counts[0] + counts[1] :]]
    inner = rows // (qa * qa)
    half = pltpu.VMEM((2, rows // 2, lanes), F32)
    late = [spot for spot, distance in enumerate(distances_of(qa)) if distance in (qa // 2, qa // 2 + 1, 1)]
    early = [spot for spot in range(qa) if spot not in late]
    planes = shape((2, rows, lanes), F32)
    begun = call(
        functools.partial(low_kernel, early),
        "low_gate_early",
        planes,
        [vmem] * (len(early) + 1),
        [],
        1,
        *[blocks[spot] for spot in early],
        low_w,
    )
    *blocks, _ = call(
        functools.partial(first_kernel, sections[0], lane_bits, qa, late),
        "first_section",
        (shape((qb, qa // qb, 2, inner, lanes), F32),) * qa + (planes,),
        [vmem] * (2 + len(late) + counts[0]),
        [half] * 4,
        5,
        begun,
        *[blocks[spot] for spot in late],
        low_w,
        *weights[0],
        aliases={0: qa},
    )
    blocks = exchange(blocks)
    halves = []
    for stays in (False, True):
        halves.append(
            call(
                functools.partial(second_kernel, sections[1], lane_bits, qa, stays),
                "second_section_kept" if stays else "second_section_sent",
                shape((2, rows // qb, lanes), F32),
                [vmem] * (qa + counts[1]),
                [half] * 2,
                1.5,
                *blocks,
                *weights[1],
            )
        )
        if not stays:
            came = lax.ppermute(halves[0], "qb", [(i, 1 - i) for i in range(qb)])
    final = call(
        functools.partial(third_kernel, sections[2], lane_bits),
        "third_section",
        shape((2 * rows, lanes), F32),
        [vmem] * (2 + counts[2]),
        [half] * 4 + [pltpu.VMEM((rows, lanes), F32)] * 2 + [pltpu.SemaphoreType.DMA((2 * PIECES,))],
        4,
        halves[1],
        came,
        *weights[2],
        out_spec=hbm,
    )
    return final.reshape(rows, 2, lanes).swapaxes(0, 1).reshape(2, amps_local)


def solution(mesh):
    return jax.shard_map(
        per_device,
        mesh=mesh,
        in_specs=(P(None, ("paths", "qa", "qb")), P(), P("paths")),
        out_specs=P(None, ("paths", "qa", "qb")),
        check_vma=False,
    )
```

```python
import functools

import jax
import jax.numpy as jnp
from jax import lax
from jax.experimental import pallas as pl
from jax.experimental.layout import Layout, with_layout_constraint
from jax.experimental.pallas import tpu as pltpu
from jax.sharding import PartitionSpec as P

F32 = jnp.float32
BF16 = jnp.bfloat16
VMEM_LIMIT = 14 * 1024 * 1024
LARGE_VMEM = 48 * 1024 * 1024
PIECES = 4
ORDER = [(1, 0), (2, 0), (1, 1), (2, 1), (3, 0), (3, 1), (0, 1)]


def window_offsets(span, gate_bits):
    return [0, span, gate_bits, span - 1, gate_bits + 1, span - 2]


def plan_gates(local_bits, gate_bits):
    outer = window_offsets(local_bits - gate_bits, gate_bits)
    inner = window_offsets(local_bits - gate_bits - 1, gate_bits)
    low, sections = [], []
    for number, offsets in enumerate((outer, inner, outer)):
        section = []
        for index, offset in enumerate(offsets):
            gate = 6 * number + index
            if offset == 0:
                low.append(gate)
            elif section and section[-1][0] == offset:
                section[-1][1].append(gate)
            else:
                section.append((offset, [gate]))
        sections.append(section)
    return low, sections


def join_windows(section, gate_bits):
    stages = []
    for offset, gates in section:
        if stages:
            offsets = [o for o, _ in stages[-1]] + [offset]
            if max(offsets) - min(offsets) <= 1:
                stages[-1].append((offset, gates))
                continue
        stages.append([(offset, gates)])
    return [
        (min(o for o, _ in parts), gate_bits + (len(parts) > 1), parts)
        for parts in stages
    ]


def interleaved(stage):
    base, _, parts = stage
    return parts[0][0] != base


def exact_dot(a, b):
    return lax.dot_general(
        a, b, (((1,), (0,)), ((), ())), precision=lax.Precision.HIGHEST, preferred_element_type=F32
    )


def split(x):
    high = x.astype(BF16)
    return high, (x - high.astype(F32)).astype(BF16)


def bf_dot(a, b):
    return jnp.dot(a, b, preferred_element_type=F32)


def block(real, imag):
    return jnp.concatenate(
        [jnp.concatenate([real, -imag], axis=1), jnp.concatenate([imag, real], axis=1)], axis=0
    )


def relative(matrix, number, count):
    dim = matrix.shape[1]
    column = lax.broadcasted_iota(jnp.int32, matrix.shape, 1)
    row = lax.broadcasted_iota(jnp.int32, matrix.shape, 0)
    if number == 0:
        size = dim // count
        spot, source = column // size, jnp.zeros_like(column)
        for index, partner in enumerate(sources_of(count)):
            source = jnp.where(spot == index, partner, source)
        natural = source * size + lax.rem(column, size)
    else:
        natural = jnp.bitwise_xor(column, lax.axis_index("qb") * (dim // 2))
    return exact_dot(matrix, jnp.where(row == natural, 1.0, 0.0).astype(F32))


def prepare_kernel(low, sections, count, bits_ref, gates_ref, low_ref, *refs):
    *targets, held, wide, sems = refs
    copies = []
    for gate in range(held.shape[0]):
        copy = pltpu.make_async_copy(gates_ref.at[gate, bits_ref[gate]], held.at[gate], sems.at[gate])
        copy.start()
        copies.append(copy)
    for copy in copies:
        copy.wait()
    dim = held.shape[-1]

    def product(gates):
        real, imag = held[gates[0], 0], held[gates[0], 1]
        for gate in gates[1:]:
            column = exact_dot(block(held[gate, 0], held[gate, 1]), jnp.concatenate([real, imag], axis=0))
            real, imag = column[:dim], column[dim:]
        return real, imag

    def joined(base, parts):
        wide[...] = jnp.zeros_like(wide)
        for index, (offset, gates) in enumerate(parts):
            real, imag = product(gates)
            for t in range(2):
                at = pl.ds(t * dim, dim) if offset == base else pl.ds(t, dim, stride=2)
                if index == 0:
                    wide[0, t, at, :] = real
                    wide[1, t, at, :] = imag
                else:
                    x = jnp.concatenate(
                        [jnp.concatenate([wide[p, c, at, :] for c in range(2)], axis=1) for p in range(2)], axis=0
                    )
                    y = exact_dot(block(real, imag), x)
                    for p in range(2):
                        for c in range(2):
                            wide[p, c, at, :] = y[p * dim : (p + 1) * dim, c * dim : (c + 1) * dim]
        return [jnp.concatenate([wide[p, 0], wide[p, 1]], axis=1) for p in range(2)]

    for number, section in enumerate(sections):
        weights, targets = targets[: len(section)], targets[len(section) :]
        for target, (base, _, parts) in zip(weights, section):
            pair = joined(base, parts) if len(parts) > 1 else product(parts[0][1])
            if number != 1 and target is weights[0]:
                pair = [relative(x, number, count) for x in pair]
            high, rest = split(block(*pair))
            target[...] = jnp.concatenate([high, rest, high], axis=1)
    real, imag = product(low)
    high, rest = split(block(real.T, -imag.T))
    low_ref[...] = jnp.concatenate([high, rest, high], axis=0)


def partners_of(count):
    if count == 8:
        cycle = [0, 1, 3, 2]
        tables = [list(range(count))]
        for shift, crossed in ORDER:
            line = [cycle[(cycle.index(z) + shift) % 4] for z in range(4)]
            tables.append([2 * line[i // 2] + (i % 2 ^ crossed) for i in range(count)])
        return tables
    half = count // 2
    far, near = list(range(count - 1, half - 1, -1)), list(range(half - 1, 0, -1))
    order = [0]
    while far or near:
        order += far[:2] + near[:2]
        far, near = far[2:], near[2:]
    return [[i ^ distance for i in range(count)] for distance in order]


def look_up(table):
    me = lax.axis_index("qa")
    if table == [i ^ table[0] for i in range(len(table))]:
        return jnp.bitwise_xor(me, table[0])
    found = jnp.int32(table[0])
    for index in range(1, len(table)):
        found = jnp.where(me == index, jnp.int32(table[index]), found)
    return found


def dests_of(count):
    return [look_up(table) for table in partners_of(count)]


def sources_of(count):
    return [look_up([table.index(i) for i in range(count)]) for table in partners_of(count)]


def split_kernel(x_ref, *outs):
    for dest, out_ref in zip(dests_of(len(outs)), outs):
        out_ref[...] = x_ref[dest]


def apply_stage(weights_ref, starts, load, store):
    dim = weights_ref.shape[0] // 2
    for pair in range(0, len(starts), 2):
        group = starts[pair : pair + 2]
        x = jnp.concatenate(
            [jnp.concatenate([load(part, start) for start in group], axis=1) for part in range(2)], axis=0
        )
        high, rest = split(x)
        y = bf_dot(weights_ref[...], jnp.concatenate([rest, high, high], axis=0))
        lanes = y.shape[1] // len(group)
        for part in range(2):
            for place, start in enumerate(group):
                store(part, start, y[part * dim : (part + 1) * dim, place * lanes : (place + 1) * lanes])


def stage_starts(stage, lane_bits, rows):
    base, bits, _ = stage
    dim, stride = 2**bits, 2 ** (base - lane_bits)
    return dim, stride, [h * dim * stride + l for h in range(rows // (dim * stride)) for l in range(stride)]


def run_stage(stage, weights_ref, lane_bits, source, target=None, store=None):
    dim, stride, starts = stage_starts(stage, lane_bits, source.shape[1])

    def load(part, start):
        if not interleaved(stage):
            return source[part, pl.ds(start, dim, stride=stride), :]
        half = dim // 2
        return jnp.concatenate(
            [source[part, pl.ds(start + t * stride, half, stride=2 * stride), :] for t in range(2)], axis=0
        )

    def plain(part, start, value):
        target[part, pl.ds(start, dim, stride=stride), :] = value

    apply_stage(weights_ref, starts, load, store or plain)


def run_top_stage(stage, weights_ref, lane_bits, source, halves):
    rows = 2 * halves[0].shape[1]
    dim, stride, starts = stage_starts(stage, lane_bits, rows)

    def store(part, start, value):
        for t in range(2):
            halves[t][part, pl.ds(start, dim // 2, stride=stride), :] = value[t * dim // 2 : (t + 1) * dim // 2]

    def load(part, start):
        if not isinstance(source, tuple):
            return source[part, pl.ds(start, dim, stride=stride), :]
        return jnp.concatenate([half[part, pl.ds(start, dim // 2, stride=stride), :] for half in source], axis=0)

    apply_stage(weights_ref, starts, load, store)


def run_halves(stages, weights, lane_bits, halves, spares, last_store=None):
    for index, (stage, weights_ref) in enumerate(zip(stages, weights)):
        for t in range(2):
            store = None
            if last_store is not None and index == len(stages) - 1:
                store = functools.partial(last_store, t)
            run_stage(stage, weights_ref, lane_bits, halves[t], spares[t], store)
        halves, spares = spares, halves
    return halves


def low_gate(blocks, low_ref, whole):
    lanes = whole.shape[2]
    for spot, block_ref in blocks:
        size = block_ref.shape[0] // 2
        real = block_ref[pl.ds(0, size, stride=2), :]
        imag = block_ref[pl.ds(1, size, stride=2), :]
        high, rest = split(jnp.concatenate([real, imag], axis=1))
        y = bf_dot(jnp.concatenate([rest, high, high], axis=1), low_ref[...])
        whole[0, pl.ds(spot * size, size), :] = y[:, :lanes]
        whole[1, pl.ds(spot * size, size), :] = y[:, lanes:]


def low_kernel(spots, *refs):
    *blocks, low_ref, whole = refs
    low_gate(zip(spots, blocks), low_ref, whole)


def first_kernel(stages, lane_bits, count, spots, *refs):
    _, *blocks = refs[: 1 + len(spots)]
    refs = refs[1 + len(spots) :]
    low_ref, weights, refs = refs[0], refs[1 : 1 + len(stages)], refs[1 + len(stages) :]
    outs, (whole, *halves) = refs[:count], refs[count:]
    low_gate(zip(spots, blocks), low_ref, whole)
    run_top_stage(stages[0], weights[0], lane_bits, whole, halves[:2])
    done = run_halves(stages[1:], weights[1:], lane_bits, halves[:2], halves[2:])
    tops, mids, _, inner, _ = outs[0].shape
    dests = dests_of(count)
    for top in range(tops):
        for dest, out_ref in zip(dests, outs):
            for mid in range(mids):
                start = pl.multiple_of((mid * count + dest) * inner, inner)
                for part in range(2):
                    out_ref[top, mid, part] = done[top][part, pl.ds(start, inner), :]


def second_kernel(stages, lane_bits, count, stays, *refs):
    blocks, weights, refs = refs[:count], refs[count : count + len(stages)], refs[count + len(stages) :]
    out_ref, one, two = refs
    core = lax.axis_index("qb")
    top = core if stays else 1 - core
    for source, block_ref in zip(sources_of(count), blocks):
        _, mids, _, inner, _ = block_ref.shape
        for mid in range(mids):
            start = pl.multiple_of((mid * count + source) * inner, inner)
            for part in range(2):
                one[part, pl.ds(start, inner), :] = block_ref[top, mid, part]
    for index, (stage, weights_ref) in enumerate(zip(stages, weights)):
        run_stage(stage, weights_ref, lane_bits, one, out_ref if index == len(stages) - 1 else two)
        one, two = two, one


def third_kernel(stages, lane_bits, kept_ref, came_ref, *refs):
    weights, (out_ref, *halves, sems) = refs[: len(stages)], refs[len(stages) :]
    results = halves[4:]
    half = kept_ref.shape[1]
    run_top_stage(stages[0], weights[0], lane_bits, (kept_ref, came_ref), halves[:2])
    done = run_halves(stages[1:-1], weights[1:-1], lane_bits, halves[:2], halves[2:4])
    copies = []
    for t in range(2):
        dim, stride, _ = stage_starts(stages[-1], lane_bits, half)

        def store(part, start, value, t=t):
            results[t][pl.ds(2 * start + part, dim, stride=2 * stride), :] = value

        run_stage(stages[-1], weights[-1], lane_bits, done[t], store=store)
        size = 2 * half // PIECES
        for piece in range(PIECES):
            to = out_ref.at[pl.ds(t * 2 * half + piece * size, size)]
            copies.append(
                pltpu.make_async_copy(results[t].at[pl.ds(piece * size, size)], to, sems.at[t * PIECES + piece])
            )
            copies[-1].start()
    for copy in copies:
        copy.wait()


def call(kernel, name, out_shapes, in_specs, scratch, matmuls, *operands, limit=VMEM_LIMIT, out_spec=None, aliases=None):
    many = isinstance(out_shapes, tuple)
    vmem = out_spec or pl.BlockSpec(memory_space=pltpu.VMEM)
    return pl.pallas_call(
        kernel,
        out_shape=out_shapes,
        in_specs=in_specs,
        out_specs=(vmem,) * len(out_shapes) if many else vmem,
        scratch_shapes=scratch,
        input_output_aliases=aliases or {},
        compiler_params=pltpu.CompilerParams(vmem_limit_bytes=limit),
        cost_estimate=pl.CostEstimate(
            flops=int(matmuls * 3 * 2 * 256 * 256 * 1024), bytes_accessed=4 * 2**20, transcendentals=0
        ),
        name=name,
    )(*operands)


def per_device(state, gate_terms, path_bits):
    amps_local = state.shape[1]
    local_bits = amps_local.bit_length() - 1
    dim = gate_terms.shape[-1]
    gate_bits = dim.bit_length() - 1
    lanes, lane_bits = dim, gate_bits
    rows = amps_local // lanes
    qa = lax.axis_size("qa")
    qb = lax.axis_size("qb")
    low, sections = plan_gates(local_bits, gate_bits)
    sections = [join_windows(section, gate_bits) for section in sections]
    order = 2 * dim
    vmem = pl.BlockSpec(memory_space=pltpu.VMEM)
    hbm = pl.BlockSpec(memory_space=pltpu.HBM)
    shape = jax.ShapeDtypeStruct

    state = with_layout_constraint(state.reshape(2, rows, lanes), Layout(major_to_minor=(1, 0, 2)))
    state = state.swapaxes(0, 1).reshape(qa, 2 * rows // qa, lanes)
    blocks = call(
        split_kernel,
        "split_state",
        (shape((2 * rows // qa, lanes), F32),) * qa,
        [vmem],
        [],
        0,
        state,
    )

    blocks = list(blocks)
    blocks[1] = lax.dynamic_index_in_dim(state, look_up(partners_of(qa)[1]), 0, keepdims=False)

    def exchange(blocks):
        came = [blocks[0]]
        for table, piece in zip(partners_of(qa)[1:], blocks[1:]):
            came.append(lax.ppermute(piece, "qa", list(enumerate(table))))
        return came

    blocks = exchange(blocks)
    low_w, *weights = call(
        functools.partial(prepare_kernel, low, sections, qa),
        "prepare_gates",
        (shape((3 * order, order), BF16),)
        + tuple(shape((2 * 2**bits, 6 * 2**bits), BF16) for section in sections for _, bits, _ in section),
        [pl.BlockSpec(memory_space=pltpu.SMEM), hbm],
        [
            pltpu.VMEM((gate_terms.shape[0], 2, dim, dim), F32),
            pltpu.VMEM((2, 2, 2 * dim, dim), F32),
            pltpu.SemaphoreType.DMA((gate_terms.shape[0],)),
        ],
        8,
        path_bits,
        gate_terms,
        limit=LARGE_VMEM,
    )
    counts = [len(section) for section in sections]
    weights = [weights[: counts[0]], weights[counts[0] : counts[0] + counts[1]], weights[counts[0] + counts[1] :]]
    inner = rows // (qa * qa)
    half = pltpu.VMEM((2, rows // 2, lanes), F32)
    early, late = list(range(qa - 3)), list(range(qa - 3, qa))
    planes = shape((2, rows, lanes), F32)
    begun = call(
        functools.partial(low_kernel, early),
        "low_gate_early",
        planes,
        [vmem] * (len(early) + 1),
        [],
        1,
        *[blocks[spot] for spot in early],
        low_w,
    )
    *blocks, _ = call(
        functools.partial(first_kernel, sections[0], lane_bits, qa, late),
        "first_section",
        (shape((qb, qa // qb, 2, inner, lanes), F32),) * qa + (planes,),
        [vmem] * (2 + len(late) + counts[0]),
        [half] * 4,
        5,
        begun,
        *[blocks[spot] for spot in late],
        low_w,
        *weights[0],
        aliases={0: qa},
    )
    blocks = exchange(blocks)
    halves = []
    for stays in (False, True):
        halves.append(
            call(
                functools.partial(second_kernel, sections[1], lane_bits, qa, stays),
                "second_section_kept" if stays else "second_section_sent",
                shape((2, rows // qb, lanes), F32),
                [vmem] * (qa + counts[1]),
                [half] * 2,
                1.5,
                *blocks,
                *weights[1],
            )
        )
        if not stays:
            came = lax.ppermute(halves[0], "qb", [(i, 1 - i) for i in range(qb)])
    final = call(
        functools.partial(third_kernel, sections[2], lane_bits),
        "third_section",
        shape((2 * rows, lanes), F32),
        [vmem] * (2 + counts[2]),
        [half] * 4 + [pltpu.VMEM((rows, lanes), F32)] * 2 + [pltpu.SemaphoreType.DMA((2 * PIECES,))],
        4,
        halves[1],
        came,
        *weights[2],
        out_spec=hbm,
    )
    return final.reshape(rows, 2, lanes).swapaxes(0, 1).reshape(2, amps_local)


def solution(mesh):
    return jax.shard_map(
        per_device,
        mesh=mesh,
        in_specs=(P(None, ("paths", "qa", "qb")), P(), P("paths")),
        out_specs=P(None, ("paths", "qa", "qb")),
        check_vma=False,
    )
```

```python
import functools

import jax
import jax.numpy as jnp
from jax import lax
from jax.experimental import pallas as pl
from jax.experimental.layout import Layout, with_layout_constraint
from jax.experimental.pallas import tpu as pltpu
from jax.sharding import PartitionSpec as P

F32 = jnp.float32
BF16 = jnp.bfloat16
VMEM_LIMIT = 14 * 1024 * 1024
LARGE_VMEM = 48 * 1024 * 1024
PIECES = 4
ORDERS = {
    (0, 1): [7, 6, 3, 2, 5, 4, 1],
    (0, 0): [7, 1, 3, 2, 5, 4, 6],
    (1, 1): [3, 7, 6, 2, 5, 4, 1],
    (1, 0): [3, 7, 1, 2, 5, 4, 6],
}


def window_offsets(span, gate_bits):
    return [0, span, gate_bits, span - 1, gate_bits + 1, span - 2]


def plan_gates(local_bits, gate_bits):
    outer = window_offsets(local_bits - gate_bits, gate_bits)
    inner = window_offsets(local_bits - gate_bits - 1, gate_bits)
    low, sections = [], []
    for number, offsets in enumerate((outer, inner, outer)):
        section = []
        for index, offset in enumerate(offsets):
            gate = 6 * number + index
            if offset == 0:
                low.append(gate)
            elif section and section[-1][0] == offset:
                section[-1][1].append(gate)
            else:
                section.append((offset, [gate]))
        sections.append(section)
    return low, sections


def join_windows(section, gate_bits):
    stages = []
    for offset, gates in section:
        if stages:
            offsets = [o for o, _ in stages[-1]] + [offset]
            if max(offsets) - min(offsets) <= 1:
                stages[-1].append((offset, gates))
                continue
        stages.append([(offset, gates)])
    return [
        (min(o for o, _ in parts), gate_bits + (len(parts) > 1), parts)
        for parts in stages
    ]


def interleaved(stage):
    base, _, parts = stage
    return parts[0][0] != base


def exact_dot(a, b):
    return lax.dot_general(
        a, b, (((1,), (0,)), ((), ())), precision=lax.Precision.HIGHEST, preferred_element_type=F32
    )


def split(x):
    high = x.astype(BF16)
    return high, (x - high.astype(F32)).astype(BF16)


def bf_dot(a, b):
    return jnp.dot(a, b, preferred_element_type=F32)


def block(real, imag):
    return jnp.concatenate(
        [jnp.concatenate([real, -imag], axis=1), jnp.concatenate([imag, real], axis=1)], axis=0
    )


def relative(matrix, number, count):
    dim = matrix.shape[1]
    column = lax.broadcasted_iota(jnp.int32, matrix.shape, 1)
    row = lax.broadcasted_iota(jnp.int32, matrix.shape, 0)
    if number == 0:
        size = dim // count
        spot, source = column // size, jnp.zeros_like(column)
        for index, partner in enumerate(partners_of(count)):
            source = jnp.where(spot == index, partner, source)
        natural = source * size + lax.rem(column, size)
    else:
        natural = jnp.bitwise_xor(column, lax.axis_index("qb") * (dim // 2))
    return exact_dot(matrix, jnp.where(row == natural, 1.0, 0.0).astype(F32))


def prepare_kernel(low, sections, count, bits_ref, gates_ref, low_ref, *refs):
    *targets, held, wide, sems = refs
    copies = []
    for gate in range(held.shape[0]):
        copy = pltpu.make_async_copy(gates_ref.at[gate, bits_ref[gate]], held.at[gate], sems.at[gate])
        copy.start()
        copies.append(copy)
    for copy in copies:
        copy.wait()
    dim = held.shape[-1]

    def product(gates):
        real, imag = held[gates[0], 0], held[gates[0], 1]
        for gate in gates[1:]:
            column = exact_dot(block(held[gate, 0], held[gate, 1]), jnp.concatenate([real, imag], axis=0))
            real, imag = column[:dim], column[dim:]
        return real, imag

    def joined(base, parts):
        wide[...] = jnp.zeros_like(wide)
        for index, (offset, gates) in enumerate(parts):
            real, imag = product(gates)
            for t in range(2):
                at = pl.ds(t * dim, dim) if offset == base else pl.ds(t, dim, stride=2)
                if index == 0:
                    wide[0, t, at, :] = real
                    wide[1, t, at, :] = imag
                else:
                    x = jnp.concatenate(
                        [jnp.concatenate([wide[p, c, at, :] for c in range(2)], axis=1) for p in range(2)], axis=0
                    )
                    y = exact_dot(block(real, imag), x)
                    for p in range(2):
                        for c in range(2):
                            wide[p, c, at, :] = y[p * dim : (p + 1) * dim, c * dim : (c + 1) * dim]
        return [jnp.concatenate([wide[p, 0], wide[p, 1]], axis=1) for p in range(2)]

    for number, section in enumerate(sections):
        weights, targets = targets[: len(section)], targets[len(section) :]
        for target, (base, _, parts) in zip(weights, section):
            pair = joined(base, parts) if len(parts) > 1 else product(parts[0][1])
            if number != 1 and target is weights[0]:
                pair = [relative(x, number, count) for x in pair]
            high, rest = split(block(*pair))
            target[...] = jnp.concatenate([high, rest, high], axis=1)
    real, imag = product(low)
    high, rest = split(block(real.T, -imag.T))
    low_ref[...] = jnp.concatenate([high, rest, high], axis=0)


def orders_of(count):
    if count == 8:
        return ORDERS
    half = count // 2
    far, near = list(range(count - 1, half - 1, -1)), list(range(half - 1, 0, -1))
    order = []
    while far or near:
        order += far[:2] + near[:2]
        far, near = far[2:], near[2:]
    return {(core, 0): order for core in range(2)}


def place_of(index, count):
    return int(index // 2 in (0, 3)) if count == 8 else 0


def tables_of(count, cores):
    orders = orders_of(count)
    return [
        [
            (index ^ orders[core, place_of(index, count)][spot]) * cores + core
            for index in range(count)
            for core in range(cores)
        ]
        for spot in range(count - 1)
    ]


def partners_of(count):
    me, core = lax.axis_index("qa"), lax.axis_index("qb")
    orders = orders_of(count)
    places = sorted({place for _, place in orders})
    found = [me]
    for spot in range(count - 1):
        per_core = []
        for c in range(2):
            distance = jnp.int32(orders[c, places[0]][spot])
            if len(places) > 1:
                at_end = jnp.logical_or(me < 2, me >= 6)
                distance = jnp.where(at_end, jnp.int32(orders[c, 1][spot]), distance)
            per_core.append(distance)
        found.append(jnp.bitwise_xor(me, jnp.where(core == 0, per_core[0], per_core[1])))
    return found


def split_kernel(x_ref, *outs):
    for dest, out_ref in zip(partners_of(len(outs)), outs):
        out_ref[...] = x_ref[dest]


def apply_stage(weights_ref, starts, load, store):
    dim = weights_ref.shape[0] // 2
    for pair in range(0, len(starts), 2):
        group = starts[pair : pair + 2]
        x = jnp.concatenate(
            [jnp.concatenate([load(part, start) for start in group], axis=1) for part in range(2)], axis=0
        )
        high, rest = split(x)
        y = bf_dot(weights_ref[...], jnp.concatenate([rest, high, high], axis=0))
        lanes = y.shape[1] // len(group)
        for part in range(2):
            for place, start in enumerate(group):
                store(part, start, y[part * dim : (part + 1) * dim, place * lanes : (place + 1) * lanes])


def stage_starts(stage, lane_bits, rows):
    base, bits, _ = stage
    dim, stride = 2**bits, 2 ** (base - lane_bits)
    return dim, stride, [h * dim * stride + l for h in range(rows // (dim * stride)) for l in range(stride)]


def run_stage(stage, weights_ref, lane_bits, source, target=None, store=None):
    dim, stride, starts = stage_starts(stage, lane_bits, source.shape[1])

    def load(part, start):
        if not interleaved(stage):
            return source[part, pl.ds(start, dim, stride=stride), :]
        half = dim // 2
        return jnp.concatenate(
            [source[part, pl.ds(start + t * stride, half, stride=2 * stride), :] for t in range(2)], axis=0
        )

    def plain(part, start, value):
        target[part, pl.ds(start, dim, stride=stride), :] = value

    apply_stage(weights_ref, starts, load, store or plain)


def run_top_stage(stage, weights_ref, lane_bits, source, halves):
    rows = 2 * halves[0].shape[1]
    dim, stride, starts = stage_starts(stage, lane_bits, rows)

    def store(part, start, value):
        for t in range(2):
            halves[t][part, pl.ds(start, dim // 2, stride=stride), :] = value[t * dim // 2 : (t + 1) * dim // 2]

    def load(part, start):
        if not isinstance(source, tuple):
            return source[part, pl.ds(start, dim, stride=stride), :]
        return jnp.concatenate([half[part, pl.ds(start, dim // 2, stride=stride), :] for half in source], axis=0)

    apply_stage(weights_ref, starts, load, store)


def run_halves(stages, weights, lane_bits, halves, spares, last_store=None):
    for index, (stage, weights_ref) in enumerate(zip(stages, weights)):
        for t in range(2):
            store = None
            if last_store is not None and index == len(stages) - 1:
                store = functools.partial(last_store, t)
            run_stage(stage, weights_ref, lane_bits, halves[t], spares[t], store)
        halves, spares = spares, halves
    return halves


def low_gate(blocks, low_ref, whole):
    lanes = whole.shape[2]
    for spot, block_ref in blocks:
        size = block_ref.shape[0] // 2
        real = block_ref[pl.ds(0, size, stride=2), :]
        imag = block_ref[pl.ds(1, size, stride=2), :]
        high, rest = split(jnp.concatenate([real, imag], axis=1))
        y = bf_dot(jnp.concatenate([rest, high, high], axis=1), low_ref[...])
        whole[0, pl.ds(spot * size, size), :] = y[:, :lanes]
        whole[1, pl.ds(spot * size, size), :] = y[:, lanes:]


def low_kernel(spots, *refs):
    *blocks, low_ref, whole = refs
    low_gate(zip(spots, blocks), low_ref, whole)


def first_kernel(stages, lane_bits, count, spots, *refs):
    _, *blocks = refs[: 1 + len(spots)]
    refs = refs[1 + len(spots) :]
    low_ref, weights, refs = refs[0], refs[1 : 1 + len(stages)], refs[1 + len(stages) :]
    outs, (whole, *halves) = refs[:count], refs[count:]
    low_gate(zip(spots, blocks), low_ref, whole)
    run_top_stage(stages[0], weights[0], lane_bits, whole, halves[:2])
    done = run_halves(stages[1:], weights[1:], lane_bits, halves[:2], halves[2:])
    tops, mids, _, inner, _ = outs[0].shape
    dests = partners_of(count)
    for top in range(tops):
        for dest, out_ref in zip(dests, outs):
            for mid in range(mids):
                start = pl.multiple_of((mid * count + dest) * inner, inner)
                for part in range(2):
                    out_ref[top, mid, part] = done[top][part, pl.ds(start, inner), :]


def second_kernel(stages, lane_bits, count, stays, *refs):
    blocks, weights, refs = refs[:count], refs[count : count + len(stages)], refs[count + len(stages) :]
    out_ref, one, two = refs
    core = lax.axis_index("qb")
    top = core if stays else 1 - core
    for source, block_ref in zip(partners_of(count), blocks):
        _, mids, _, inner, _ = block_ref.shape
        for mid in range(mids):
            start = pl.multiple_of((mid * count + source) * inner, inner)
            for part in range(2):
                one[part, pl.ds(start, inner), :] = block_ref[top, mid, part]
    for index, (stage, weights_ref) in enumerate(zip(stages, weights)):
        run_stage(stage, weights_ref, lane_bits, one, out_ref if index == len(stages) - 1 else two)
        one, two = two, one


def third_kernel(stages, lane_bits, kept_ref, came_ref, *refs):
    weights, (out_ref, *halves, sems) = refs[: len(stages)], refs[len(stages) :]
    results = halves[4:]
    half = kept_ref.shape[1]
    run_top_stage(stages[0], weights[0], lane_bits, (kept_ref, came_ref), halves[:2])
    done = run_halves(stages[1:-1], weights[1:-1], lane_bits, halves[:2], halves[2:4])
    copies = []
    for t in range(2):
        dim, stride, _ = stage_starts(stages[-1], lane_bits, half)

        def store(part, start, value, t=t):
            results[t][pl.ds(2 * start + part, dim, stride=2 * stride), :] = value

        run_stage(stages[-1], weights[-1], lane_bits, done[t], store=store)
        size = 2 * half // PIECES
        for piece in range(PIECES):
            to = out_ref.at[pl.ds(t * 2 * half + piece * size, size)]
            copies.append(
                pltpu.make_async_copy(results[t].at[pl.ds(piece * size, size)], to, sems.at[t * PIECES + piece])
            )
            copies[-1].start()
    for copy in copies:
        copy.wait()


def call(kernel, name, out_shapes, in_specs, scratch, matmuls, *operands, limit=VMEM_LIMIT, out_spec=None, aliases=None):
    many = isinstance(out_shapes, tuple)
    vmem = out_spec or pl.BlockSpec(memory_space=pltpu.VMEM)
    return pl.pallas_call(
        kernel,
        out_shape=out_shapes,
        in_specs=in_specs,
        out_specs=(vmem,) * len(out_shapes) if many else vmem,
        scratch_shapes=scratch,
        input_output_aliases=aliases or {},
        compiler_params=pltpu.CompilerParams(vmem_limit_bytes=limit),
        cost_estimate=pl.CostEstimate(
            flops=int(matmuls * 3 * 2 * 256 * 256 * 1024), bytes_accessed=4 * 2**20, transcendentals=0
        ),
        name=name,
    )(*operands)


def per_device(state, gate_terms, path_bits):
    amps_local = state.shape[1]
    local_bits = amps_local.bit_length() - 1
    dim = gate_terms.shape[-1]
    gate_bits = dim.bit_length() - 1
    lanes, lane_bits = dim, gate_bits
    rows = amps_local // lanes
    qa = lax.axis_size("qa")
    qb = lax.axis_size("qb")
    low, sections = plan_gates(local_bits, gate_bits)
    sections = [join_windows(section, gate_bits) for section in sections]
    order = 2 * dim
    vmem = pl.BlockSpec(memory_space=pltpu.VMEM)
    hbm = pl.BlockSpec(memory_space=pltpu.HBM)
    shape = jax.ShapeDtypeStruct

    state = with_layout_constraint(state.reshape(2, rows, lanes), Layout(major_to_minor=(1, 0, 2)))
    state = state.swapaxes(0, 1).reshape(qa, 2 * rows // qa, lanes)
    blocks = call(
        split_kernel,
        "split_state",
        (shape((2 * rows // qa, lanes), F32),) * qa,
        [vmem],
        [],
        0,
        state,
    )

    blocks = list(blocks)
    blocks[1] = lax.dynamic_index_in_dim(state, partners_of(qa)[1], 0, keepdims=False)

    def exchange(blocks):
        came = [blocks[0]]
        for table, piece in zip(tables_of(qa, qb), blocks[1:]):
            came.append(lax.ppermute(piece, ("qa", "qb"), list(enumerate(table))))
        return came

    blocks = exchange(blocks)
    low_w, *weights = call(
        functools.partial(prepare_kernel, low, sections, qa),
        "prepare_gates",
        (shape((3 * order, order), BF16),)
        + tuple(shape((2 * 2**bits, 6 * 2**bits), BF16) for section in sections for _, bits, _ in section),
        [pl.BlockSpec(memory_space=pltpu.SMEM), hbm],
        [
            pltpu.VMEM((gate_terms.shape[0], 2, dim, dim), F32),
            pltpu.VMEM((2, 2, 2 * dim, dim), F32),
            pltpu.SemaphoreType.DMA((gate_terms.shape[0],)),
        ],
        8,
        path_bits,
        gate_terms,
        limit=LARGE_VMEM,
    )
    counts = [len(section) for section in sections]
    weights = [weights[: counts[0]], weights[counts[0] : counts[0] + counts[1]], weights[counts[0] + counts[1] :]]
    inner = rows // (qa * qa)
    half = pltpu.VMEM((2, rows // 2, lanes), F32)
    early, late = list(range(qa - 3)), list(range(qa - 3, qa))
    planes = shape((2, rows, lanes), F32)
    begun = call(
        functools.partial(low_kernel, early),
        "low_gate_early",
        planes,
        [vmem] * (len(early) + 1),
        [],
        1,
        *[blocks[spot] for spot in early],
        low_w,
    )
    *blocks, _ = call(
        functools.partial(first_kernel, sections[0], lane_bits, qa, late),
        "first_section",
        (shape((qb, qa // qb, 2, inner, lanes), F32),) * qa + (planes,),
        [vmem] * (2 + len(late) + counts[0]),
        [half] * 4,
        5,
        begun,
        *[blocks[spot] for spot in late],
        low_w,
        *weights[0],
        aliases={0: qa},
    )
    blocks = exchange(blocks)
    halves = []
    for stays in (False, True):
        halves.append(
            call(
                functools.partial(second_kernel, sections[1], lane_bits, qa, stays),
                "second_section_kept" if stays else "second_section_sent",
                shape((2, rows // qb, lanes), F32),
                [vmem] * (qa + counts[1]),
                [half] * 2,
                1.5,
                *blocks,
                *weights[1],
            )
        )
        if not stays:
            came = lax.ppermute(halves[0], "qb", [(i, 1 - i) for i in range(qb)])
    final = call(
        functools.partial(third_kernel, sections[2], lane_bits),
        "third_section",
        shape((2 * rows, lanes), F32),
        [vmem] * (2 + counts[2]),
        [half] * 4 + [pltpu.VMEM((rows, lanes), F32)] * 2 + [pltpu.SemaphoreType.DMA((2 * PIECES,))],
        4,
        halves[1],
        came,
        *weights[2],
        out_spec=hbm,
    )
    return final.reshape(rows, 2, lanes).swapaxes(0, 1).reshape(2, amps_local)


def solution(mesh):
    return jax.shard_map(
        per_device,
        mesh=mesh,
        in_specs=(P(None, ("paths", "qa", "qb")), P(), P("paths")),
        out_specs=P(None, ("paths", "qa", "qb")),
        check_vma=False,
    )
```

```python
import functools

import jax
import jax.numpy as jnp
from jax import lax
from jax.experimental import pallas as pl
from jax.experimental.layout import Layout, with_layout_constraint
from jax.experimental.pallas import tpu as pltpu
from jax.sharding import PartitionSpec as P

F32 = jnp.float32
BF16 = jnp.bfloat16
VMEM_LIMIT = 14 * 1024 * 1024
LARGE_VMEM = 48 * 1024 * 1024
PIECES = 4


def window_offsets(span, gate_bits):
    return [0, span, gate_bits, span - 1, gate_bits + 1, span - 2]


def plan_gates(local_bits, gate_bits):
    outer = window_offsets(local_bits - gate_bits, gate_bits)
    inner = window_offsets(local_bits - gate_bits - 1, gate_bits)
    low, sections = [], []
    for number, offsets in enumerate((outer, inner, outer)):
        section = []
        for index, offset in enumerate(offsets):
            gate = 6 * number + index
            if offset == 0:
                low.append(gate)
            elif section and section[-1][0] == offset:
                section[-1][1].append(gate)
            else:
                section.append((offset, [gate]))
        sections.append(section)
    return low, sections


def join_windows(section, gate_bits):
    stages = []
    for offset, gates in section:
        if stages:
            offsets = [o for o, _ in stages[-1]] + [offset]
            if max(offsets) - min(offsets) <= 1:
                stages[-1].append((offset, gates))
                continue
        stages.append([(offset, gates)])
    return [
        (min(o for o, _ in parts), gate_bits + (len(parts) > 1), parts)
        for parts in stages
    ]


def interleaved(stage):
    base, _, parts = stage
    return parts[0][0] != base


def exact_dot(a, b):
    return lax.dot_general(
        a, b, (((1,), (0,)), ((), ())), precision=lax.Precision.HIGHEST, preferred_element_type=F32
    )


def split(x):
    high = x.astype(BF16)
    return high, (x - high.astype(F32)).astype(BF16)


def bf_dot(a, b):
    return jnp.dot(a, b, preferred_element_type=F32)


def block(real, imag):
    return jnp.concatenate(
        [jnp.concatenate([real, -imag], axis=1), jnp.concatenate([imag, real], axis=1)], axis=0
    )


def relative(matrix, number, count):
    dim = matrix.shape[1]
    column = lax.broadcasted_iota(jnp.int32, matrix.shape, 1)
    row = lax.broadcasted_iota(jnp.int32, matrix.shape, 0)
    if number == 0:
        size = dim // count
        spot, source = column // size, jnp.zeros_like(column)
        for index, partner in enumerate(partners_of(count)):
            source = jnp.where(spot == index, partner, source)
        natural = source * size + lax.rem(column, size)
    else:
        natural = jnp.bitwise_xor(column, lax.axis_index("qb") * (dim // 2))
    return exact_dot(matrix, jnp.where(row == natural, 1.0, 0.0).astype(F32))


def prepare_kernel(low, sections, count, bits_ref, gates_ref, low_ref, *refs):
    *targets, held, wide, sems = refs
    copies = []
    for gate in range(held.shape[0]):
        copy = pltpu.make_async_copy(gates_ref.at[gate, bits_ref[gate]], held.at[gate], sems.at[gate])
        copy.start()
        copies.append(copy)
    for copy in copies:
        copy.wait()
    dim = held.shape[-1]

    def product(gates):
        real, imag = held[gates[0], 0], held[gates[0], 1]
        for gate in gates[1:]:
            column = exact_dot(block(held[gate, 0], held[gate, 1]), jnp.concatenate([real, imag], axis=0))
            real, imag = column[:dim], column[dim:]
        return real, imag

    def joined(base, parts):
        wide[...] = jnp.zeros_like(wide)
        for index, (offset, gates) in enumerate(parts):
            real, imag = product(gates)
            for t in range(2):
                at = pl.ds(t * dim, dim) if offset == base else pl.ds(t, dim, stride=2)
                if index == 0:
                    wide[0, t, at, :] = real
                    wide[1, t, at, :] = imag
                else:
                    x = jnp.concatenate(
                        [jnp.concatenate([wide[p, c, at, :] for c in range(2)], axis=1) for p in range(2)], axis=0
                    )
                    y = exact_dot(block(real, imag), x)
                    for p in range(2):
                        for c in range(2):
                            wide[p, c, at, :] = y[p * dim : (p + 1) * dim, c * dim : (c + 1) * dim]
        return [jnp.concatenate([wide[p, 0], wide[p, 1]], axis=1) for p in range(2)]

    for number, section in enumerate(sections):
        weights, targets = targets[: len(section)], targets[len(section) :]
        for target, (base, _, parts) in zip(weights, section):
            pair = joined(base, parts) if len(parts) > 1 else product(parts[0][1])
            if number != 1 and target is weights[0]:
                pair = [relative(x, number, count) for x in pair]
            high, rest = split(block(*pair))
            target[...] = jnp.concatenate([high, rest, high], axis=1)
    real, imag = product(low)
    high, rest = split(block(real.T, -imag.T))
    low_ref[...] = jnp.concatenate([high, rest, high], axis=0)


def distances_of(count):
    half = count // 2
    far, near = list(range(count - 1, half - 1, -1)), list(range(half - 1, 0, -1))
    order = [0]
    while far or near:
        order += far[:2] + near[:2]
        far, near = far[2:], near[2:]
    return order


def partners_of(count):
    me = lax.axis_index("qa")
    return [jnp.bitwise_xor(me, distance) for distance in distances_of(count)]


def split_kernel(x_ref, *outs):
    for dest, out_ref in zip(partners_of(len(outs)), outs):
        out_ref[...] = x_ref[dest]


def apply_stage(weights_ref, starts, load, store):
    dim = weights_ref.shape[0] // 2
    for pair in range(0, len(starts), 2):
        group = starts[pair : pair + 2]
        x = jnp.concatenate(
            [jnp.concatenate([load(part, start) for start in group], axis=1) for part in range(2)], axis=0
        )
        high, rest = split(x)
        y = bf_dot(weights_ref[...], jnp.concatenate([rest, high, high], axis=0))
        lanes = y.shape[1] // len(group)
        for part in range(2):
            for place, start in enumerate(group):
                store(part, start, y[part * dim : (part + 1) * dim, place * lanes : (place + 1) * lanes])


def stage_starts(stage, lane_bits, rows):
    base, bits, _ = stage
    dim, stride = 2**bits, 2 ** (base - lane_bits)
    return dim, stride, [h * dim * stride + l for h in range(rows // (dim * stride)) for l in range(stride)]


def run_stage(stage, weights_ref, lane_bits, source, target=None, store=None):
    dim, stride, starts = stage_starts(stage, lane_bits, source.shape[1])

    def load(part, start):
        if not interleaved(stage):
            return source[part, pl.ds(start, dim, stride=stride), :]
        half = dim // 2
        return jnp.concatenate(
            [source[part, pl.ds(start + t * stride, half, stride=2 * stride), :] for t in range(2)], axis=0
        )

    def plain(part, start, value):
        target[part, pl.ds(start, dim, stride=stride), :] = value

    apply_stage(weights_ref, starts, load, store or plain)


def run_top_stage(stage, weights_ref, lane_bits, source, halves):
    rows = 2 * halves[0].shape[1]
    dim, stride, starts = stage_starts(stage, lane_bits, rows)

    def store(part, start, value):
        for t in range(2):
            halves[t][part, pl.ds(start, dim // 2, stride=stride), :] = value[t * dim // 2 : (t + 1) * dim // 2]

    def load(part, start):
        if not isinstance(source, tuple):
            return source[part, pl.ds(start, dim, stride=stride), :]
        return jnp.concatenate([half[part][pl.ds(start, dim // 2, stride=stride), :] for half in source], axis=0)

    apply_stage(weights_ref, starts, load, store)


def run_halves(stages, weights, lane_bits, halves, spares, last_store=None):
    for index, (stage, weights_ref) in enumerate(zip(stages, weights)):
        for t in range(2):
            store = None
            if last_store is not None and index == len(stages) - 1:
                store = functools.partial(last_store, t)
            run_stage(stage, weights_ref, lane_bits, halves[t], spares[t], store)
        halves, spares = spares, halves
    return halves


def low_gate(blocks, low_ref, whole):
    lanes = whole.shape[2]
    for spot, block_ref in blocks:
        size = block_ref.shape[0] // 2
        real = block_ref[pl.ds(0, size, stride=2), :]
        imag = block_ref[pl.ds(1, size, stride=2), :]
        high, rest = split(jnp.concatenate([real, imag], axis=1))
        y = bf_dot(jnp.concatenate([rest, high, high], axis=1), low_ref[...])
        whole[0, pl.ds(spot * size, size), :] = y[:, :lanes]
        whole[1, pl.ds(spot * size, size), :] = y[:, lanes:]


def low_kernel(spots, *refs):
    *blocks, low_ref, whole = refs
    low_gate(zip(spots, blocks), low_ref, whole)


def first_kernel(stages, lane_bits, count, spots, *refs):
    _, *blocks = refs[: 1 + len(spots)]
    refs = refs[1 + len(spots) :]
    low_ref, weights, refs = refs[0], refs[1 : 1 + len(stages)], refs[1 + len(stages) :]
    outs, (whole, *halves) = refs[:count], refs[count:]
    low_gate(zip(spots, blocks), low_ref, whole)
    run_top_stage(stages[0], weights[0], lane_bits, whole, halves[:2])
    done = run_halves(stages[1:], weights[1:], lane_bits, halves[:2], halves[2:])
    tops, mids, _, inner, _ = outs[0].shape
    dests = partners_of(count)
    for top in range(tops):
        for dest, out_ref in zip(dests, outs):
            for mid in range(mids):
                start = pl.multiple_of((mid * count + dest) * inner, inner)
                for part in range(2):
                    out_ref[top, mid, part] = done[top][part, pl.ds(start, inner), :]


def second_kernel(stages, lane_bits, count, stays, *refs):
    blocks, weights, refs = refs[:count], refs[count : count + len(stages)], refs[count + len(stages) :]
    *outs, one, two = refs
    core = lax.axis_index("qb")
    top = core if stays else 1 - core
    for source, block_ref in zip(partners_of(count), blocks):
        _, mids, _, inner, _ = block_ref.shape
        for mid in range(mids):
            start = pl.multiple_of((mid * count + source) * inner, inner)
            for part in range(2):
                one[part, pl.ds(start, inner), :] = block_ref[top, mid, part]
    for stage, weights_ref in zip(stages[:-1], weights):
        run_stage(stage, weights_ref, lane_bits, one, two)
        one, two = two, one
    dim, stride, _ = stage_starts(stages[-1], lane_bits, one.shape[1])

    def store(part, start, value):
        outs[part][pl.ds(start, dim, stride=stride), :] = value

    run_stage(stages[-1], weights[-1], lane_bits, one, store=store)


def third_kernel(stages, lane_bits, *refs):
    kept, came, refs = refs[:2], refs[2:4], refs[4:]
    weights, (out_ref, *halves, sems) = refs[: len(stages)], refs[len(stages) :]
    results = halves[4:]
    half = kept[0].shape[0]
    run_top_stage(stages[0], weights[0], lane_bits, (kept, came), halves[:2])
    done = run_halves(stages[1:-1], weights[1:-1], lane_bits, halves[:2], halves[2:4])
    copies = []
    for t in range(2):
        dim, stride, _ = stage_starts(stages[-1], lane_bits, half)

        def store(part, start, value, t=t):
            results[t][pl.ds(2 * start + part, dim, stride=2 * stride), :] = value

        run_stage(stages[-1], weights[-1], lane_bits, done[t], store=store)
        size = 2 * half // PIECES
        for piece in range(PIECES):
            to = out_ref.at[pl.ds(t * 2 * half + piece * size, size)]
            copies.append(
                pltpu.make_async_copy(results[t].at[pl.ds(piece * size, size)], to, sems.at[t * PIECES + piece])
            )
            copies[-1].start()
    for copy in copies:
        copy.wait()


def call(kernel, name, out_shapes, in_specs, scratch, matmuls, *operands, limit=VMEM_LIMIT, out_spec=None, aliases=None):
    many = isinstance(out_shapes, tuple)
    vmem = out_spec or pl.BlockSpec(memory_space=pltpu.VMEM)
    return pl.pallas_call(
        kernel,
        out_shape=out_shapes,
        in_specs=in_specs,
        out_specs=(vmem,) * len(out_shapes) if many else vmem,
        scratch_shapes=scratch,
        input_output_aliases=aliases or {},
        compiler_params=pltpu.CompilerParams(vmem_limit_bytes=limit),
        cost_estimate=pl.CostEstimate(
            flops=int(matmuls * 3 * 2 * 256 * 256 * 1024), bytes_accessed=4 * 2**20, transcendentals=0
        ),
        name=name,
    )(*operands)


def per_device(state, gate_terms, path_bits):
    amps_local = state.shape[1]
    local_bits = amps_local.bit_length() - 1
    dim = gate_terms.shape[-1]
    gate_bits = dim.bit_length() - 1
    lanes, lane_bits = dim, gate_bits
    rows = amps_local // lanes
    qa = lax.axis_size("qa")
    qb = lax.axis_size("qb")
    low, sections = plan_gates(local_bits, gate_bits)
    sections = [join_windows(section, gate_bits) for section in sections]
    order = 2 * dim
    vmem = pl.BlockSpec(memory_space=pltpu.VMEM)
    hbm = pl.BlockSpec(memory_space=pltpu.HBM)
    shape = jax.ShapeDtypeStruct

    state = with_layout_constraint(state.reshape(2, rows, lanes), Layout(major_to_minor=(1, 0, 2)))
    state = state.swapaxes(0, 1).reshape(qa, 2 * rows // qa, lanes)
    blocks = call(
        split_kernel,
        "split_state",
        (shape((2 * rows // qa, lanes), F32),) * qa,
        [vmem],
        [],
        0,
        state,
    )

    blocks = list(blocks)
    blocks[1] = lax.dynamic_index_in_dim(state, partners_of(qa)[1], 0, keepdims=False)

    def exchange(blocks):
        came = [blocks[0]]
        for distance, piece in zip(distances_of(qa)[1:], blocks[1:]):
            came.append(lax.ppermute(piece, "qa", [(i, i ^ distance) for i in range(qa)]))
        return came

    blocks = exchange(blocks)
    low_w, *weights = call(
        functools.partial(prepare_kernel, low, sections, qa),
        "prepare_gates",
        (shape((3 * order, order), BF16),)
        + tuple(shape((2 * 2**bits, 6 * 2**bits), BF16) for section in sections for _, bits, _ in section),
        [pl.BlockSpec(memory_space=pltpu.SMEM), hbm],
        [
            pltpu.VMEM((gate_terms.shape[0], 2, dim, dim), F32),
            pltpu.VMEM((2, 2, 2 * dim, dim), F32),
            pltpu.SemaphoreType.DMA((gate_terms.shape[0],)),
        ],
        8,
        path_bits,
        gate_terms,
        limit=LARGE_VMEM,
    )
    counts = [len(section) for section in sections]
    weights = [weights[: counts[0]], weights[counts[0] : counts[0] + counts[1]], weights[counts[0] + counts[1] :]]
    inner = rows // (qa * qa)
    half = pltpu.VMEM((2, rows // 2, lanes), F32)
    early, late = list(range(qa - 3)), list(range(qa - 3, qa))
    planes = shape((2, rows, lanes), F32)
    begun = call(
        functools.partial(low_kernel, early),
        "low_gate_early",
        planes,
        [vmem] * (len(early) + 1),
        [],
        1,
        *[blocks[spot] for spot in early],
        low_w,
    )
    *blocks, _ = call(
        functools.partial(first_kernel, sections[0], lane_bits, qa, late),
        "first_section",
        (shape((qb, qa // qb, 2, inner, lanes), F32),) * qa + (planes,),
        [vmem] * (2 + len(late) + counts[0]),
        [half] * 4,
        5,
        begun,
        *[blocks[spot] for spot in late],
        low_w,
        *weights[0],
        aliases={0: qa},
    )
    blocks = exchange(blocks)
    halves = []
    for stays in (False, True):
        halves.append(
            call(
                functools.partial(second_kernel, sections[1], lane_bits, qa, stays),
                "second_section_kept" if stays else "second_section_sent",
                (shape((rows // qb, lanes), F32),) * 2,
                [vmem] * (qa + counts[1]),
                [half] * 2,
                1.5,
                *blocks,
                *weights[1],
            )
        )
        if not stays:
            came = [lax.ppermute(part, "qb", [(i, 1 - i) for i in range(qb)]) for part in halves[0]]
    final = call(
        functools.partial(third_kernel, sections[2], lane_bits),
        "third_section",
        shape((2 * rows, lanes), F32),
        [vmem] * (4 + counts[2]),
        [half] * 4 + [pltpu.VMEM((rows, lanes), F32)] * 2 + [pltpu.SemaphoreType.DMA((2 * PIECES,))],
        4,
        *halves[1],
        *came,
        *weights[2],
        out_spec=hbm,
    )
    return final.reshape(rows, 2, lanes).swapaxes(0, 1).reshape(2, amps_local)


def solution(mesh):
    return jax.shard_map(
        per_device,
        mesh=mesh,
        in_specs=(P(None, ("paths", "qa", "qb")), P(), P("paths")),
        out_specs=P(None, ("paths", "qa", "qb")),
        check_vma=False,
    )
```

```python
import functools

import jax
import jax.numpy as jnp
from jax import lax
from jax.experimental import pallas as pl
from jax.experimental.layout import Layout, with_layout_constraint
from jax.experimental.pallas import tpu as pltpu
from jax.sharding import PartitionSpec as P

F32 = jnp.float32
BF16 = jnp.bfloat16
VMEM_LIMIT = 14 * 1024 * 1024
LARGE_VMEM = 48 * 1024 * 1024
PIECES = 4
ORDERS = {
    (0, 1): [7, 6, 3, 2, 1, 5, 4],
    (0, 0): [7, 1, 3, 2, 6, 5, 4],
    (1, 1): [7, 1, 3, 2, 6, 5, 4],
    (1, 0): [7, 1, 3, 2, 6, 5, 4],
}


def window_offsets(span, gate_bits):
    return [0, span, gate_bits, span - 1, gate_bits + 1, span - 2]


def plan_gates(local_bits, gate_bits):
    outer = window_offsets(local_bits - gate_bits, gate_bits)
    inner = window_offsets(local_bits - gate_bits - 1, gate_bits)
    low, sections = [], []
    for number, offsets in enumerate((outer, inner, outer)):
        section = []
        for index, offset in enumerate(offsets):
            gate = 6 * number + index
            if offset == 0:
                low.append(gate)
            elif section and section[-1][0] == offset:
                section[-1][1].append(gate)
            else:
                section.append((offset, [gate]))
        sections.append(section)
    return low, sections


def join_windows(section, gate_bits):
    stages = []
    for offset, gates in section:
        if stages:
            offsets = [o for o, _ in stages[-1]] + [offset]
            if max(offsets) - min(offsets) <= 1:
                stages[-1].append((offset, gates))
                continue
        stages.append([(offset, gates)])
    return [
        (min(o for o, _ in parts), gate_bits + (len(parts) > 1), parts)
        for parts in stages
    ]


def interleaved(stage):
    base, _, parts = stage
    return parts[0][0] != base


def exact_dot(a, b):
    return lax.dot_general(
        a, b, (((1,), (0,)), ((), ())), precision=lax.Precision.HIGHEST, preferred_element_type=F32
    )


def split(x):
    high = x.astype(BF16)
    return high, (x - high.astype(F32)).astype(BF16)


def bf_dot(a, b):
    return jnp.dot(a, b, preferred_element_type=F32)


def block(real, imag):
    return jnp.concatenate(
        [jnp.concatenate([real, -imag], axis=1), jnp.concatenate([imag, real], axis=1)], axis=0
    )


def relative(matrix, number, count):
    dim = matrix.shape[1]
    column = lax.broadcasted_iota(jnp.int32, matrix.shape, 1)
    row = lax.broadcasted_iota(jnp.int32, matrix.shape, 0)
    if number == 0:
        size = dim // count
        spot, source = column // size, jnp.zeros_like(column)
        for index, partner in enumerate(partners_of(count)):
            source = jnp.where(spot == index, partner, source)
        natural = source * size + lax.rem(column, size)
    else:
        natural = jnp.bitwise_xor(column, lax.axis_index("qb") * (dim // 2))
    return exact_dot(matrix, jnp.where(row == natural, 1.0, 0.0).astype(F32))


def prepare_kernel(low, sections, count, bits_ref, gates_ref, low_ref, *refs):
    *targets, held, wide, sems = refs
    copies = []
    for gate in range(held.shape[0]):
        copy = pltpu.make_async_copy(gates_ref.at[gate, bits_ref[gate]], held.at[gate], sems.at[gate])
        copy.start()
        copies.append(copy)
    for copy in copies:
        copy.wait()
    dim = held.shape[-1]

    def product(gates):
        real, imag = held[gates[0], 0], held[gates[0], 1]
        for gate in gates[1:]:
            column = exact_dot(block(held[gate, 0], held[gate, 1]), jnp.concatenate([real, imag], axis=0))
            real, imag = column[:dim], column[dim:]
        return real, imag

    def joined(base, parts):
        wide[...] = jnp.zeros_like(wide)
        for index, (offset, gates) in enumerate(parts):
            real, imag = product(gates)
            for t in range(2):
                at = pl.ds(t * dim, dim) if offset == base else pl.ds(t, dim, stride=2)
                if index == 0:
                    wide[0, t, at, :] = real
                    wide[1, t, at, :] = imag
                else:
                    x = jnp.concatenate(
                        [jnp.concatenate([wide[p, c, at, :] for c in range(2)], axis=1) for p in range(2)], axis=0
                    )
                    y = exact_dot(block(real, imag), x)
                    for p in range(2):
                        for c in range(2):
                            wide[p, c, at, :] = y[p * dim : (p + 1) * dim, c * dim : (c + 1) * dim]
        return [jnp.concatenate([wide[p, 0], wide[p, 1]], axis=1) for p in range(2)]

    for number, section in enumerate(sections):
        weights, targets = targets[: len(section)], targets[len(section) :]
        for target, (base, _, parts) in zip(weights, section):
            pair = joined(base, parts) if len(parts) > 1 else product(parts[0][1])
            if number != 1 and target is weights[0]:
                pair = [relative(x, number, count) for x in pair]
            high, rest = split(block(*pair))
            target[...] = jnp.concatenate([high, rest, high], axis=1)
    real, imag = product(low)
    high, rest = split(block(real.T, -imag.T))
    low_ref[...] = jnp.concatenate([high, rest, high], axis=0)


def orders_of(count):
    if count == 8:
        return ORDERS
    half = count // 2
    far, near = list(range(count - 1, half - 1, -1)), list(range(half - 1, 0, -1))
    order = []
    while far or near:
        order += far[:2] + near[:2]
        far, near = far[2:], near[2:]
    return {(core, 0): order for core in range(2)}


def place_of(index, count):
    return int(index // 2 in (0, 3)) if count == 8 else 0


def tables_of(count, cores):
    orders = orders_of(count)
    return [
        [
            (index ^ orders[core, place_of(index, count)][spot]) * cores + core
            for index in range(count)
            for core in range(cores)
        ]
        for spot in range(count - 1)
    ]


def partners_of(count):
    me, core = lax.axis_index("qa"), lax.axis_index("qb")
    orders = orders_of(count)
    places = sorted({place for _, place in orders})
    found = [me]
    for spot in range(count - 1):
        per_core = []
        for c in range(2):
            distance = jnp.int32(orders[c, places[0]][spot])
            if len(places) > 1:
                at_end = jnp.logical_or(me < 2, me >= 6)
                distance = jnp.where(at_end, jnp.int32(orders[c, 1][spot]), distance)
            per_core.append(distance)
        found.append(jnp.bitwise_xor(me, jnp.where(core == 0, per_core[0], per_core[1])))
    return found


def split_kernel(x_ref, *outs):
    for dest, out_ref in zip(partners_of(len(outs)), outs):
        out_ref[...] = x_ref[dest]


def apply_stage(weights_ref, starts, load, store):
    dim = weights_ref.shape[0] // 2
    for pair in range(0, len(starts), 2):
        group = starts[pair : pair + 2]
        x = jnp.concatenate(
            [jnp.concatenate([load(part, start) for start in group], axis=1) for part in range(2)], axis=0
        )
        high, rest = split(x)
        y = bf_dot(weights_ref[...], jnp.concatenate([rest, high, high], axis=0))
        lanes = y.shape[1] // len(group)
        for part in range(2):
            for place, start in enumerate(group):
                store(part, start, y[part * dim : (part + 1) * dim, place * lanes : (place + 1) * lanes])


def stage_starts(stage, lane_bits, rows):
    base, bits, _ = stage
    dim, stride = 2**bits, 2 ** (base - lane_bits)
    return dim, stride, [h * dim * stride + l for h in range(rows // (dim * stride)) for l in range(stride)]


def run_stage(stage, weights_ref, lane_bits, source, target=None, store=None):
    dim, stride, starts = stage_starts(stage, lane_bits, source.shape[1])

    def load(part, start):
        if not interleaved(stage):
            return source[part, pl.ds(start, dim, stride=stride), :]
        half = dim // 2
        return jnp.concatenate(
            [source[part, pl.ds(start + t * stride, half, stride=2 * stride), :] for t in range(2)], axis=0
        )

    def plain(part, start, value):
        target[part, pl.ds(start, dim, stride=stride), :] = value

    apply_stage(weights_ref, starts, load, store or plain)


def run_top_stage(stage, weights_ref, lane_bits, source, halves):
    rows = 2 * halves[0].shape[1]
    dim, stride, starts = stage_starts(stage, lane_bits, rows)

    def store(part, start, value):
        for t in range(2):
            halves[t][part, pl.ds(start, dim // 2, stride=stride), :] = value[t * dim // 2 : (t + 1) * dim // 2]

    def load(part, start):
        if not isinstance(source, tuple):
            return source[part, pl.ds(start, dim, stride=stride), :]
        return jnp.concatenate([half[part, pl.ds(start, dim // 2, stride=stride), :] for half in source], axis=0)

    apply_stage(weights_ref, starts, load, store)


def run_halves(stages, weights, lane_bits, halves, spares, last_store=None):
    for index, (stage, weights_ref) in enumerate(zip(stages, weights)):
        for t in range(2):
            store = None
            if last_store is not None and index == len(stages) - 1:
                store = functools.partial(last_store, t)
            run_stage(stage, weights_ref, lane_bits, halves[t], spares[t], store)
        halves, spares = spares, halves
    return halves


def low_gate(blocks, low_ref, whole):
    lanes = whole.shape[2]
    for spot, block_ref in blocks:
        size = block_ref.shape[0] // 2
        real = block_ref[pl.ds(0, size, stride=2), :]
        imag = block_ref[pl.ds(1, size, stride=2), :]
        high, rest = split(jnp.concatenate([real, imag], axis=1))
        y = bf_dot(jnp.concatenate([rest, high, high], axis=1), low_ref[...])
        whole[0, pl.ds(spot * size, size), :] = y[:, :lanes]
        whole[1, pl.ds(spot * size, size), :] = y[:, lanes:]


def low_kernel(spots, *refs):
    *blocks, low_ref, whole = refs
    low_gate(zip(spots, blocks), low_ref, whole)


def first_kernel(stages, lane_bits, count, spots, *refs):
    _, *blocks = refs[: 1 + len(spots)]
    refs = refs[1 + len(spots) :]
    low_ref, weights, refs = refs[0], refs[1 : 1 + len(stages)], refs[1 + len(stages) :]
    outs, (whole, *halves) = refs[:count], refs[count:]
    low_gate(zip(spots, blocks), low_ref, whole)
    run_top_stage(stages[0], weights[0], lane_bits, whole, halves[:2])
    done = run_halves(stages[1:], weights[1:], lane_bits, halves[:2], halves[2:])
    tops, mids, _, inner, _ = outs[0].shape
    dests = partners_of(count)
    for top in range(tops):
        for dest, out_ref in zip(dests, outs):
            for mid in range(mids):
                start = pl.multiple_of((mid * count + dest) * inner, inner)
                for part in range(2):
                    out_ref[top, mid, part] = done[top][part, pl.ds(start, inner), :]


def second_kernel(stages, lane_bits, count, stays, *refs):
    blocks, weights, refs = refs[:count], refs[count : count + len(stages)], refs[count + len(stages) :]
    out_ref, one, two = refs
    core = lax.axis_index("qb")
    top = core if stays else 1 - core
    for source, block_ref in zip(partners_of(count), blocks):
        _, mids, _, inner, _ = block_ref.shape
        for mid in range(mids):
            start = pl.multiple_of((mid * count + source) * inner, inner)
            for part in range(2):
                one[part, pl.ds(start, inner), :] = block_ref[top, mid, part]
    for index, (stage, weights_ref) in enumerate(zip(stages, weights)):
        run_stage(stage, weights_ref, lane_bits, one, out_ref if index == len(stages) - 1 else two)
        one, two = two, one


def third_kernel(stages, lane_bits, kept_ref, came_ref, *refs):
    weights, (out_ref, *halves, sems) = refs[: len(stages)], refs[len(stages) :]
    results = halves[4:]
    half = kept_ref.shape[1]
    run_top_stage(stages[0], weights[0], lane_bits, (kept_ref, came_ref), halves[:2])
    done = run_halves(stages[1:-1], weights[1:-1], lane_bits, halves[:2], halves[2:4])
    copies = []
    for t in range(2):
        dim, stride, _ = stage_starts(stages[-1], lane_bits, half)

        def store(part, start, value, t=t):
            results[t][pl.ds(2 * start + part, dim, stride=2 * stride), :] = value

        run_stage(stages[-1], weights[-1], lane_bits, done[t], store=store)
        size = 2 * half // PIECES
        for piece in range(PIECES):
            to = out_ref.at[pl.ds(t * 2 * half + piece * size, size)]
            copies.append(
                pltpu.make_async_copy(results[t].at[pl.ds(piece * size, size)], to, sems.at[t * PIECES + piece])
            )
            copies[-1].start()
    for copy in copies:
        copy.wait()


def call(kernel, name, out_shapes, in_specs, scratch, matmuls, *operands, limit=VMEM_LIMIT, out_spec=None, aliases=None):
    many = isinstance(out_shapes, tuple)
    vmem = out_spec or pl.BlockSpec(memory_space=pltpu.VMEM)
    return pl.pallas_call(
        kernel,
        out_shape=out_shapes,
        in_specs=in_specs,
        out_specs=(vmem,) * len(out_shapes) if many else vmem,
        scratch_shapes=scratch,
        input_output_aliases=aliases or {},
        compiler_params=pltpu.CompilerParams(vmem_limit_bytes=limit),
        cost_estimate=pl.CostEstimate(
            flops=int(matmuls * 3 * 2 * 256 * 256 * 1024), bytes_accessed=4 * 2**20, transcendentals=0
        ),
        name=name,
    )(*operands)


def per_device(state, gate_terms, path_bits):
    amps_local = state.shape[1]
    local_bits = amps_local.bit_length() - 1
    dim = gate_terms.shape[-1]
    gate_bits = dim.bit_length() - 1
    lanes, lane_bits = dim, gate_bits
    rows = amps_local // lanes
    qa = lax.axis_size("qa")
    qb = lax.axis_size("qb")
    low, sections = plan_gates(local_bits, gate_bits)
    sections = [join_windows(section, gate_bits) for section in sections]
    order = 2 * dim
    vmem = pl.BlockSpec(memory_space=pltpu.VMEM)
    hbm = pl.BlockSpec(memory_space=pltpu.HBM)
    shape = jax.ShapeDtypeStruct

    state = with_layout_constraint(state.reshape(2, rows, lanes), Layout(major_to_minor=(1, 0, 2)))
    state = state.swapaxes(0, 1).reshape(qa, 2 * rows // qa, lanes)
    blocks = call(
        split_kernel,
        "split_state",
        (shape((2 * rows // qa, lanes), F32),) * qa,
        [vmem],
        [],
        0,
        state,
    )

    blocks = list(blocks)
    blocks[1] = lax.dynamic_index_in_dim(state, partners_of(qa)[1], 0, keepdims=False)

    def exchange(blocks):
        came = [blocks[0]]
        for table, piece in zip(tables_of(qa, qb), blocks[1:]):
            came.append(lax.ppermute(piece, ("qa", "qb"), list(enumerate(table))))
        return came

    blocks = exchange(blocks)
    low_w, *weights = call(
        functools.partial(prepare_kernel, low, sections, qa),
        "prepare_gates",
        (shape((3 * order, order), BF16),)
        + tuple(shape((2 * 2**bits, 6 * 2**bits), BF16) for section in sections for _, bits, _ in section),
        [pl.BlockSpec(memory_space=pltpu.SMEM), hbm],
        [
            pltpu.VMEM((gate_terms.shape[0], 2, dim, dim), F32),
            pltpu.VMEM((2, 2, 2 * dim, dim), F32),
            pltpu.SemaphoreType.DMA((gate_terms.shape[0],)),
        ],
        8,
        path_bits,
        gate_terms,
        limit=LARGE_VMEM,
    )
    counts = [len(section) for section in sections]
    weights = [weights[: counts[0]], weights[counts[0] : counts[0] + counts[1]], weights[counts[0] + counts[1] :]]
    inner = rows // (qa * qa)
    half = pltpu.VMEM((2, rows // 2, lanes), F32)
    early, late = list(range(qa - 3)), list(range(qa - 3, qa))
    planes = shape((2, rows, lanes), F32)
    begun = call(
        functools.partial(low_kernel, early),
        "low_gate_early",
        planes,
        [vmem] * (len(early) + 1),
        [],
        1,
        *[blocks[spot] for spot in early],
        low_w,
    )
    *blocks, _ = call(
        functools.partial(first_kernel, sections[0], lane_bits, qa, late),
        "first_section",
        (shape((qb, qa // qb, 2, inner, lanes), F32),) * qa + (planes,),
        [vmem] * (2 + len(late) + counts[0]),
        [half] * 4,
        5,
        begun,
        *[blocks[spot] for spot in late],
        low_w,
        *weights[0],
        aliases={0: qa},
    )
    blocks = exchange(blocks)
    halves = []
    for stays in (False, True):
        halves.append(
            call(
                functools.partial(second_kernel, sections[1], lane_bits, qa, stays),
                "second_section_kept" if stays else "second_section_sent",
                shape((2, rows // qb, lanes), F32),
                [vmem] * (qa + counts[1]),
                [half] * 2,
                1.5,
                *blocks,
                *weights[1],
            )
        )
        if not stays:
            came = lax.ppermute(halves[0], "qb", [(i, 1 - i) for i in range(qb)])
    final = call(
        functools.partial(third_kernel, sections[2], lane_bits),
        "third_section",
        shape((2 * rows, lanes), F32),
        [vmem] * (2 + counts[2]),
        [half] * 4 + [pltpu.VMEM((rows, lanes), F32)] * 2 + [pltpu.SemaphoreType.DMA((2 * PIECES,))],
        4,
        halves[1],
        came,
        *weights[2],
        out_spec=hbm,
    )
    return final.reshape(rows, 2, lanes).swapaxes(0, 1).reshape(2, amps_local)


def solution(mesh):
    return jax.shard_map(
        per_device,
        mesh=mesh,
        in_specs=(P(None, ("paths", "qa", "qb")), P(), P("paths")),
        out_specs=P(None, ("paths", "qa", "qb")),
        check_vma=False,
    )
```

```python
import functools

import jax
import jax.numpy as jnp
from jax import lax
from jax.experimental import pallas as pl
from jax.experimental.layout import Layout, with_layout_constraint
from jax.experimental.pallas import tpu as pltpu
from jax.sharding import PartitionSpec as P

F32 = jnp.float32
BF16 = jnp.bfloat16
VMEM_LIMIT = 14 * 1024 * 1024
LARGE_VMEM = 48 * 1024 * 1024
PIECES = 4


def window_offsets(span, gate_bits):
    return [0, span, gate_bits, span - 1, gate_bits + 1, span - 2]


def plan_gates(local_bits, gate_bits):
    outer = window_offsets(local_bits - gate_bits, gate_bits)
    inner = window_offsets(local_bits - gate_bits - 1, gate_bits)
    low, sections = [], []
    for number, offsets in enumerate((outer, inner, outer)):
        section = []
        for index, offset in enumerate(offsets):
            gate = 6 * number + index
            if offset == 0:
                low.append(gate)
            elif section and section[-1][0] == offset:
                section[-1][1].append(gate)
            else:
                section.append((offset, [gate]))
        sections.append(section)
    return low, sections


def join_windows(section, gate_bits):
    stages = []
    for offset, gates in section:
        if stages:
            offsets = [o for o, _ in stages[-1]] + [offset]
            if max(offsets) - min(offsets) <= 1:
                stages[-1].append((offset, gates))
                continue
        stages.append([(offset, gates)])
    return [
        (min(o for o, _ in parts), gate_bits + (len(parts) > 1), parts)
        for parts in stages
    ]


def interleaved(stage):
    base, _, parts = stage
    return parts[0][0] != base


def exact_dot(a, b):
    return lax.dot_general(
        a, b, (((1,), (0,)), ((), ())), precision=lax.Precision.HIGHEST, preferred_element_type=F32
    )


def split(x):
    high = x.astype(BF16)
    return high, (x - high.astype(F32)).astype(BF16)


def bf_dot(a, b):
    return jnp.dot(a, b, preferred_element_type=F32)


def block(real, imag):
    return jnp.concatenate(
        [jnp.concatenate([real, -imag], axis=1), jnp.concatenate([imag, real], axis=1)], axis=0
    )


def relative(matrix, number, count):
    dim = matrix.shape[1]
    column = lax.broadcasted_iota(jnp.int32, matrix.shape, 1)
    row = lax.broadcasted_iota(jnp.int32, matrix.shape, 0)
    if number == 0:
        size = dim // count
        spot, source = column // size, jnp.zeros_like(column)
        for index, partner in enumerate(partners_of(count)):
            source = jnp.where(spot == index, partner, source)
        natural = source * size + lax.rem(column, size)
    else:
        natural = jnp.bitwise_xor(column, lax.axis_index("qb") * (dim // 2))
    matrix = exact_dot(matrix, jnp.where(row == natural, 1.0, 0.0).astype(F32))
    if number == 0:
        swapped = jnp.bitwise_xor(row, (1 - lax.axis_index("qb")) * (dim // 2))
        matrix = exact_dot(jnp.where(column == swapped, 1.0, 0.0).astype(F32), matrix)
    return matrix


def prepare_kernel(low, sections, count, bits_ref, gates_ref, low_ref, *refs):
    *targets, held, wide, sems = refs
    copies = []
    for gate in range(held.shape[0]):
        copy = pltpu.make_async_copy(gates_ref.at[gate, bits_ref[gate]], held.at[gate], sems.at[gate])
        copy.start()
        copies.append(copy)
    for copy in copies:
        copy.wait()
    dim = held.shape[-1]

    def product(gates):
        real, imag = held[gates[0], 0], held[gates[0], 1]
        for gate in gates[1:]:
            column = exact_dot(block(held[gate, 0], held[gate, 1]), jnp.concatenate([real, imag], axis=0))
            real, imag = column[:dim], column[dim:]
        return real, imag

    def joined(base, parts):
        wide[...] = jnp.zeros_like(wide)
        for index, (offset, gates) in enumerate(parts):
            real, imag = product(gates)
            for t in range(2):
                at = pl.ds(t * dim, dim) if offset == base else pl.ds(t, dim, stride=2)
                if index == 0:
                    wide[0, t, at, :] = real
                    wide[1, t, at, :] = imag
                else:
                    x = jnp.concatenate(
                        [jnp.concatenate([wide[p, c, at, :] for c in range(2)], axis=1) for p in range(2)], axis=0
                    )
                    y = exact_dot(block(real, imag), x)
                    for p in range(2):
                        for c in range(2):
                            wide[p, c, at, :] = y[p * dim : (p + 1) * dim, c * dim : (c + 1) * dim]
        return [jnp.concatenate([wide[p, 0], wide[p, 1]], axis=1) for p in range(2)]

    for number, section in enumerate(sections):
        weights, targets = targets[: len(section)], targets[len(section) :]
        for target, (base, _, parts) in zip(weights, section):
            pair = joined(base, parts) if len(parts) > 1 else product(parts[0][1])
            if number != 1 and target is weights[0]:
                pair = [relative(x, number, count) for x in pair]
            high, rest = split(block(*pair))
            target[...] = jnp.concatenate([high, rest, high], axis=1)
    real, imag = product(low)
    high, rest = split(block(real.T, -imag.T))
    low_ref[...] = jnp.concatenate([high, rest, high], axis=0)


def distances_of(count):
    half = count // 2
    far, near = list(range(count - 1, half - 1, -1)), list(range(half - 1, 0, -1))
    order = [0]
    while far or near:
        order += far[:2] + near[:2]
        far, near = far[2:], near[2:]
    return order


def partners_of(count):
    me = lax.axis_index("qa")
    return [jnp.bitwise_xor(me, distance) for distance in distances_of(count)]


def split_kernel(x_ref, *outs):
    for dest, out_ref in zip(partners_of(len(outs)), outs):
        out_ref[...] = x_ref[dest]


def apply_stage(weights_ref, starts, load, store):
    dim = weights_ref.shape[0] // 2
    for pair in range(0, len(starts), 2):
        group = starts[pair : pair + 2]
        x = jnp.concatenate(
            [jnp.concatenate([load(part, start) for start in group], axis=1) for part in range(2)], axis=0
        )
        high, rest = split(x)
        y = bf_dot(weights_ref[...], jnp.concatenate([rest, high, high], axis=0))
        lanes = y.shape[1] // len(group)
        for part in range(2):
            for place, start in enumerate(group):
                store(part, start, y[part * dim : (part + 1) * dim, place * lanes : (place + 1) * lanes])


def stage_starts(stage, lane_bits, rows):
    base, bits, _ = stage
    dim, stride = 2**bits, 2 ** (base - lane_bits)
    return dim, stride, [h * dim * stride + l for h in range(rows // (dim * stride)) for l in range(stride)]


def run_stage(stage, weights_ref, lane_bits, source, target=None, store=None):
    dim, stride, starts = stage_starts(stage, lane_bits, source.shape[1])

    def load(part, start):
        if not interleaved(stage):
            return source[part, pl.ds(start, dim, stride=stride), :]
        half = dim // 2
        return jnp.concatenate(
            [source[part, pl.ds(start + t * stride, half, stride=2 * stride), :] for t in range(2)], axis=0
        )

    def plain(part, start, value):
        target[part, pl.ds(start, dim, stride=stride), :] = value

    apply_stage(weights_ref, starts, load, store or plain)


def run_top_stage(stage, weights_ref, lane_bits, source, halves):
    rows = 2 * halves[0].shape[1]
    dim, stride, starts = stage_starts(stage, lane_bits, rows)

    def store(part, start, value):
        for t in range(2):
            halves[t][part, pl.ds(start, dim // 2, stride=stride), :] = value[t * dim // 2 : (t + 1) * dim // 2]

    def load(part, start):
        if not isinstance(source, tuple):
            return source[part, pl.ds(start, dim, stride=stride), :]
        return jnp.concatenate([half[part, pl.ds(start, dim // 2, stride=stride), :] for half in source], axis=0)

    apply_stage(weights_ref, starts, load, store)


def run_halves(stages, weights, lane_bits, halves, spares, last_store=None):
    for index, (stage, weights_ref) in enumerate(zip(stages, weights)):
        for t in range(2):
            store = None
            if last_store is not None and index == len(stages) - 1:
                store = functools.partial(last_store, t)
            run_stage(stage, weights_ref, lane_bits, halves[t], spares[t], store)
        halves, spares = spares, halves
    return halves


def low_gate(blocks, low_ref, whole):
    lanes = whole.shape[2]
    for spot, block_ref in blocks:
        size = block_ref.shape[0] // 2
        real = block_ref[pl.ds(0, size, stride=2), :]
        imag = block_ref[pl.ds(1, size, stride=2), :]
        high, rest = split(jnp.concatenate([real, imag], axis=1))
        y = bf_dot(jnp.concatenate([rest, high, high], axis=1), low_ref[...])
        whole[0, pl.ds(spot * size, size), :] = y[:, :lanes]
        whole[1, pl.ds(spot * size, size), :] = y[:, lanes:]


def low_kernel(spots, *refs):
    *blocks, low_ref, whole = refs
    low_gate(zip(spots, blocks), low_ref, whole)


def first_top_kernel(stage, lane_bits, spots, *refs):
    blocks, (low_ref, weights_ref, away_ref, stay_ref, whole) = refs[1 : 1 + len(spots)], refs[1 + len(spots) :]
    low_gate(zip(spots, blocks), low_ref, whole)
    run_top_stage(stage, weights_ref, lane_bits, whole, (away_ref, stay_ref))


def pieces_for(done, dest, count, piece):
    mids, _, inner, _ = piece.shape
    for mid in range(mids):
        start = pl.multiple_of((mid * count + dest) * inner, inner)
        for part in range(2):
            piece[mid, part] = done[part, pl.ds(start, inner), :]


def far_spots(count):
    return [spot for spot, distance in enumerate(distances_of(count)) if distance >= count // 2]


def near_spots(count):
    return [spot for spot, distance in enumerate(distances_of(count)) if distance < count // 2]


def first_rest_kernel(stages, lane_bits, count, *refs):
    half_ref, weights, refs = refs[0], refs[1 : 1 + len(stages)], refs[1 + len(stages) :]
    *outs, done, spare = refs
    buffers = [half_ref, spare] if len(stages) == 2 else None
    for index, (stage, weights_ref) in enumerate(zip(stages, weights)):
        run_stage(stage, weights_ref, lane_bits, buffers[index], done if index == len(stages) - 1 else spare)
    dests = partners_of(count)
    for spot, out_ref in zip(far_spots(count), outs):
        pieces_for(done, dests[spot], count, out_ref)


def first_last_kernel(stages, lane_bits, count, half_ref, before_ref, *refs):
    weights, refs = refs[: len(stages)], refs[len(stages) :]
    *outs, done, spare = refs
    first_rest_kernel(stages, lane_bits, count, half_ref, *weights, *outs[: count // 2], done, spare)
    dests = partners_of(count)
    for spot, out_ref in zip(near_spots(count), outs[count // 2 :]):
        pieces_for(before_ref, dests[spot], count, out_ref.at[0])
        pieces_for(done, dests[spot], count, out_ref.at[1])


def second_kernel(stages, lane_bits, count, which, *refs):
    blocks, weights, refs = refs[:count], refs[count : count + len(stages)], refs[count + len(stages) :]
    out_ref, one, two = refs
    sources = partners_of(count)
    half = count // 2
    pieces = [block_ref.at[which] for block_ref in blocks[:half]] + list(blocks[half:])
    for spot, piece in zip(near_spots(count) + far_spots(count), pieces):
        mids, _, inner, _ = piece.shape
        for mid in range(mids):
            start = pl.multiple_of((mid * count + sources[spot]) * inner, inner)
            for part in range(2):
                one[part, pl.ds(start, inner), :] = piece[mid, part]
    for index, (stage, weights_ref) in enumerate(zip(stages, weights)):
        run_stage(stage, weights_ref, lane_bits, one, out_ref if index == len(stages) - 1 else two)
        one, two = two, one


def third_kernel(stages, lane_bits, kept_ref, came_ref, *refs):
    weights, (out_ref, *halves, sems) = refs[: len(stages)], refs[len(stages) :]
    results = halves[4:]
    half = kept_ref.shape[1]
    run_top_stage(stages[0], weights[0], lane_bits, (kept_ref, came_ref), halves[:2])
    done = run_halves(stages[1:-1], weights[1:-1], lane_bits, halves[:2], halves[2:4])
    copies = []
    for t in range(2):
        dim, stride, _ = stage_starts(stages[-1], lane_bits, half)

        def store(part, start, value, t=t):
            results[t][pl.ds(2 * start + part, dim, stride=2 * stride), :] = value

        run_stage(stages[-1], weights[-1], lane_bits, done[t], store=store)
        size = 2 * half // PIECES
        for piece in range(PIECES):
            to = out_ref.at[pl.ds(t * 2 * half + piece * size, size)]
            copies.append(
                pltpu.make_async_copy(results[t].at[pl.ds(piece * size, size)], to, sems.at[t * PIECES + piece])
            )
            copies[-1].start()
    for copy in copies:
        copy.wait()


def call(kernel, name, out_shapes, in_specs, scratch, matmuls, *operands, limit=VMEM_LIMIT, out_spec=None, aliases=None):
    many = isinstance(out_shapes, tuple)
    vmem = out_spec or pl.BlockSpec(memory_space=pltpu.VMEM)
    return pl.pallas_call(
        kernel,
        out_shape=out_shapes,
        in_specs=in_specs,
        out_specs=(vmem,) * len(out_shapes) if many else vmem,
        scratch_shapes=scratch,
        input_output_aliases=aliases or {},
        compiler_params=pltpu.CompilerParams(vmem_limit_bytes=limit),
        cost_estimate=pl.CostEstimate(
            flops=int(matmuls * 3 * 2 * 256 * 256 * 1024), bytes_accessed=4 * 2**20, transcendentals=0
        ),
        name=name,
    )(*operands)


def per_device(state, gate_terms, path_bits):
    amps_local = state.shape[1]
    local_bits = amps_local.bit_length() - 1
    dim = gate_terms.shape[-1]
    gate_bits = dim.bit_length() - 1
    lanes, lane_bits = dim, gate_bits
    rows = amps_local // lanes
    qa = lax.axis_size("qa")
    qb = lax.axis_size("qb")
    low, sections = plan_gates(local_bits, gate_bits)
    sections = [join_windows(section, gate_bits) for section in sections]
    order = 2 * dim
    vmem = pl.BlockSpec(memory_space=pltpu.VMEM)
    hbm = pl.BlockSpec(memory_space=pltpu.HBM)
    shape = jax.ShapeDtypeStruct

    state = with_layout_constraint(state.reshape(2, rows, lanes), Layout(major_to_minor=(1, 0, 2)))
    state = state.swapaxes(0, 1).reshape(qa, 2 * rows // qa, lanes)
    blocks = call(
        split_kernel,
        "split_state",
        (shape((2 * rows // qa, lanes), F32),) * qa,
        [vmem],
        [],
        0,
        state,
    )

    blocks = list(blocks)
    blocks[1] = lax.dynamic_index_in_dim(state, partners_of(qa)[1], 0, keepdims=False)

    def exchange(blocks):
        came = [blocks[0]]
        for distance, piece in zip(distances_of(qa)[1:], blocks[1:]):
            came.append(lax.ppermute(piece, "qa", [(i, i ^ distance) for i in range(qa)]))
        return came

    blocks = exchange(blocks)
    low_w, *weights = call(
        functools.partial(prepare_kernel, low, sections, qa),
        "prepare_gates",
        (shape((3 * order, order), BF16),)
        + tuple(shape((2 * 2**bits, 6 * 2**bits), BF16) for section in sections for _, bits, _ in section),
        [pl.BlockSpec(memory_space=pltpu.SMEM), hbm],
        [
            pltpu.VMEM((gate_terms.shape[0], 2, dim, dim), F32),
            pltpu.VMEM((2, 2, 2 * dim, dim), F32),
            pltpu.SemaphoreType.DMA((gate_terms.shape[0],)),
        ],
        8,
        path_bits,
        gate_terms,
        limit=LARGE_VMEM,
    )
    counts = [len(section) for section in sections]
    weights = [weights[: counts[0]], weights[counts[0] : counts[0] + counts[1]], weights[counts[0] + counts[1] :]]
    inner = rows // (qa * qa)
    half = pltpu.VMEM((2, rows // 2, lanes), F32)
    early, late = list(range(qa - 3)), list(range(qa - 3, qa))
    planes = shape((2, rows, lanes), F32)
    begun = call(
        functools.partial(low_kernel, early),
        "low_gate_early",
        planes,
        [vmem] * (len(early) + 1),
        [],
        1,
        *[blocks[spot] for spot in early],
        low_w,
    )
    part = shape((2, rows // qb, lanes), F32)
    away, stay, _ = call(
        functools.partial(first_top_kernel, sections[0][0], lane_bits, late),
        "first_section_top",
        (part, part, planes),
        [vmem] * (3 + len(late)),
        [],
        1.5,
        begun,
        *[blocks[spot] for spot in late],
        low_w,
        weights[0][0],
        aliases={0: 2},
    )
    far_block = shape((qa // qb, 2, inner, lanes), F32)
    near_block = shape((qb, qa // qb, 2, inner, lanes), F32)
    *far_away, done = call(
        functools.partial(first_rest_kernel, sections[0][1:], lane_bits, qa),
        "first_section_away",
        (far_block,) * (qa // 2) + (part,),
        [vmem] * counts[0],
        [half],
        1.5,
        away,
        *weights[0][1:],
    )
    outs = call(
        functools.partial(first_last_kernel, sections[0][1:], lane_bits, qa),
        "first_section_stay",
        (far_block,) * (qa // 2) + (near_block,) * (qa // 2),
        [vmem] * (1 + counts[0]),
        [half] * 2,
        1.5,
        stay,
        done,
        *weights[0][1:],
    )
    far_stay, near_both = outs[: qa // 2], outs[qa // 2 :]

    def send(pieces, spots):
        return [
            lax.ppermute(piece, "qa", [(i, i ^ distances_of(qa)[spot]) for i in range(qa)]) if spot else piece
            for spot, piece in zip(spots, pieces)
        ]

    far_away = send(far_away, far_spots(qa))
    near_both = send(near_both, near_spots(qa))
    far_stay = send(far_stay, far_spots(qa))
    halves = []
    for which, far in enumerate((far_away, far_stay)):
        halves.append(
            call(
                functools.partial(second_kernel, sections[1], lane_bits, qa, which),
                ("second_section_away", "second_section_stay")[which],
                part,
                [vmem] * (qa + counts[1]),
                [half] * 2,
                (0.001, 100)[which],
                *near_both,
                *far,
                *weights[1],
            )
        )
        if which == 0:
            came = lax.ppermute(halves[0], "qb", [(i, 1 - i) for i in range(qb)])
    final = call(
        functools.partial(third_kernel, sections[2], lane_bits),
        "third_section",
        shape((2 * rows, lanes), F32),
        [vmem] * (2 + counts[2]),
        [half] * 4 + [pltpu.VMEM((rows, lanes), F32)] * 2 + [pltpu.SemaphoreType.DMA((2 * PIECES,))],
        4,
        halves[1],
        came,
        *weights[2],
        out_spec=hbm,
    )
    return final.reshape(rows, 2, lanes).swapaxes(0, 1).reshape(2, amps_local)


def solution(mesh):
    return jax.shard_map(
        per_device,
        mesh=mesh,
        in_specs=(P(None, ("paths", "qa", "qb")), P(), P("paths")),
        out_specs=P(None, ("paths", "qa", "qb")),
        check_vma=False,
    )
```

```python
import functools

import jax
import jax.numpy as jnp
from jax import lax
from jax.experimental import pallas as pl
from jax.experimental.layout import Layout, with_layout_constraint
from jax.experimental.pallas import tpu as pltpu
from jax.sharding import PartitionSpec as P

F32 = jnp.float32
BF16 = jnp.bfloat16
VMEM_LIMIT = 14 * 1024 * 1024
LARGE_VMEM = 48 * 1024 * 1024
PIECES = 4


def window_offsets(span, gate_bits):
    return [0, span, gate_bits, span - 1, gate_bits + 1, span - 2]


def plan_gates(local_bits, gate_bits):
    outer = window_offsets(local_bits - gate_bits, gate_bits)
    inner = window_offsets(local_bits - gate_bits - 1, gate_bits)
    low, sections = [], []
    for number, offsets in enumerate((outer, inner, outer)):
        section = []
        for index, offset in enumerate(offsets):
            gate = 6 * number + index
            if offset == 0:
                low.append(gate)
            elif section and section[-1][0] == offset:
                section[-1][1].append(gate)
            else:
                section.append((offset, [gate]))
        sections.append(section)
    return low, sections


def join_windows(section, gate_bits):
    stages = []
    for offset, gates in section:
        if stages:
            offsets = [o for o, _ in stages[-1]] + [offset]
            if max(offsets) - min(offsets) <= 1:
                stages[-1].append((offset, gates))
                continue
        stages.append([(offset, gates)])
    return [
        (min(o for o, _ in parts), gate_bits + (len(parts) > 1), parts)
        for parts in stages
    ]


def interleaved(stage):
    base, _, parts = stage
    return parts[0][0] != base


def split(x):
    high = x.astype(BF16)
    return high, (x - high.astype(F32)).astype(BF16)


def bf_dot(a, b):
    return jnp.dot(a, b, preferred_element_type=F32)


def pair_dot(a, b):
    (a_high, a_rest), (b_high, b_rest) = split(a), split(b)
    return bf_dot(a_high, b_rest) + bf_dot(a_rest, b_high) + bf_dot(a_high, b_high)


def block(real, imag):
    return jnp.concatenate(
        [jnp.concatenate([real, -imag], axis=1), jnp.concatenate([imag, real], axis=1)], axis=0
    )


def relative(matrix, number, count):
    order = matrix.shape[1]
    dim = order // 2
    column = lax.broadcasted_iota(jnp.int32, (order, order), 1)
    row = lax.broadcasted_iota(jnp.int32, (order, order), 0)
    within = lax.rem(column, dim)
    if number == 0:
        size = dim // count
        spot, source = within // size, jnp.zeros_like(column)
        for index, partner in enumerate(partners_of(count)):
            source = jnp.where(spot == index, partner, source)
        natural = source * size + lax.rem(within, size)
    else:
        natural = jnp.bitwise_xor(within, lax.axis_index("qb") * (dim // 2))
    picked = jnp.where(row == natural + (column - within), 1.0, 0.0).astype(BF16)
    return bf_dot(matrix, picked).astype(BF16)


def prepare_kernel(low, sections, count, bits_ref, gates_ref, low_ref, *refs):
    *targets, held, wides, sems = refs
    copies = {}
    for gate in [gate for section in sections for _, _, parts in section for _, gates in parts for gate in gates] + low:
        copies[gate] = pltpu.make_async_copy(gates_ref.at[gate, bits_ref[gate]], held.at[gate], sems.at[gate])
        copies[gate].start()
    dim = held.shape[-1]

    def product(gates):
        for gate in gates:
            copies.pop(gate).wait()
        real, imag = held[gates[0], 0], held[gates[0], 1]
        for gate in gates[1:]:
            column = pair_dot(block(held[gate, 0], held[gate, 1]), jnp.concatenate([real, imag], axis=0))
            real, imag = column[:dim], column[dim:]
        return real, imag

    def joined(wide, base, parts):
        wide[...] = jnp.zeros(wide.shape, F32)
        for index, (offset, gates) in enumerate(parts):
            real, imag = product(gates)
            for t in range(2):
                at = pl.ds(t * dim, dim) if offset == base else pl.ds(t, dim, stride=2)
                if index == 0:
                    wide[0, t, at, :] = real
                    wide[1, t, at, :] = imag
                else:
                    x = jnp.concatenate(
                        [jnp.concatenate([wide[p, c, at, :] for c in range(2)], axis=1) for p in range(2)], axis=0
                    )
                    y = pair_dot(block(real, imag), x)
                    for p in range(2):
                        for c in range(2):
                            wide[p, c, at, :] = y[p * dim : (p + 1) * dim, c * dim : (c + 1) * dim]
        return [jnp.concatenate([wide[p, 0], wide[p, 1]], axis=1) for p in range(2)]

    for number, section in enumerate(sections):
        weights, targets = targets[: len(section)], targets[len(section) :]
        for target, (base, _, parts) in zip(weights, section):
            high, rest = split(block(*(joined(wides.at[number], base, parts) if len(parts) > 1 else product(parts[0][1]))))
            if number != 1 and target is weights[0]:
                high, rest = relative(high, number, count), relative(rest, number, count)
            target[...] = jnp.concatenate([high, rest, high], axis=1)
    real, imag = product(low)
    high, rest = split(block(real.T, -imag.T))
    low_ref[...] = jnp.concatenate([high, rest, high], axis=0)


def distances_of(count):
    half = count // 2
    far, near = list(range(count - 1, half - 1, -1)), list(range(half - 1, 0, -1))
    order = [0]
    while far or near:
        order += far[:2] + near[:2]
        far, near = far[2:], near[2:]
    return order


def partners_of(count):
    me = lax.axis_index("qa")
    return [jnp.bitwise_xor(me, distance) for distance in distances_of(count)]


def split_kernel(x_ref, *outs):
    for dest, out_ref in zip(partners_of(len(outs)), outs):
        out_ref[...] = x_ref[dest]


def apply_stage(weights_ref, starts, load, store):
    dim = weights_ref.shape[0] // 2
    for pair in range(0, len(starts), 2):
        group = starts[pair : pair + 2]
        x = jnp.concatenate(
            [jnp.concatenate([load(part, start) for start in group], axis=1) for part in range(2)], axis=0
        )
        high, rest = split(x)
        y = bf_dot(weights_ref[...], jnp.concatenate([rest, high, high], axis=0))
        lanes = y.shape[1] // len(group)
        for part in range(2):
            for place, start in enumerate(group):
                store(part, start, y[part * dim : (part + 1) * dim, place * lanes : (place + 1) * lanes])


def stage_starts(stage, lane_bits, rows):
    base, bits, _ = stage
    dim, stride = 2**bits, 2 ** (base - lane_bits)
    return dim, stride, [h * dim * stride + l for h in range(rows // (dim * stride)) for l in range(stride)]


def run_stage(stage, weights_ref, lane_bits, source, target=None, store=None):
    dim, stride, starts = stage_starts(stage, lane_bits, source.shape[1])

    def load(part, start):
        if not interleaved(stage):
            return source[part, pl.ds(start, dim, stride=stride), :]
        half = dim // 2
        return jnp.concatenate(
            [source[part, pl.ds(start + t * stride, half, stride=2 * stride), :] for t in range(2)], axis=0
        )

    def plain(part, start, value):
        target[part, pl.ds(start, dim, stride=stride), :] = value

    apply_stage(weights_ref, starts, load, store or plain)


def run_top_stage(stage, weights_ref, lane_bits, source, halves):
    rows = 2 * halves[0].shape[1]
    dim, stride, starts = stage_starts(stage, lane_bits, rows)

    def store(part, start, value):
        for t in range(2):
            halves[t][part, pl.ds(start, dim // 2, stride=stride), :] = value[t * dim // 2 : (t + 1) * dim // 2]

    def load(part, start):
        if not isinstance(source, tuple):
            return source[part, pl.ds(start, dim, stride=stride), :]
        return jnp.concatenate([half[part, pl.ds(start, dim // 2, stride=stride), :] for half in source], axis=0)

    apply_stage(weights_ref, starts, load, store)


def run_halves(stages, weights, lane_bits, halves, spares, last_store=None):
    for index, (stage, weights_ref) in enumerate(zip(stages, weights)):
        for t in range(2):
            store = None
            if last_store is not None and index == len(stages) - 1:
                store = functools.partial(last_store, t)
            run_stage(stage, weights_ref, lane_bits, halves[t], spares[t], store)
        halves, spares = spares, halves
    return halves


def low_gate(blocks, low_ref, whole):
    lanes = whole.shape[2]
    for spot, block_ref in blocks:
        size = block_ref.shape[0] // 2
        real = block_ref[pl.ds(0, size, stride=2), :]
        imag = block_ref[pl.ds(1, size, stride=2), :]
        high, rest = split(jnp.concatenate([real, imag], axis=1))
        y = bf_dot(jnp.concatenate([rest, high, high], axis=1), low_ref[...])
        whole[0, pl.ds(spot * size, size), :] = y[:, :lanes]
        whole[1, pl.ds(spot * size, size), :] = y[:, lanes:]


def low_kernel(spots, *refs):
    *blocks, low_ref, whole = refs
    low_gate(zip(spots, blocks), low_ref, whole)


def first_kernel(stages, lane_bits, count, spots, *refs):
    _, *blocks = refs[: 1 + len(spots)]
    refs = refs[1 + len(spots) :]
    low_ref, weights, refs = refs[0], refs[1 : 1 + len(stages)], refs[1 + len(stages) :]
    outs, (whole, *halves) = refs[:count], refs[count:]
    low_gate(zip(spots, blocks), low_ref, whole)
    run_top_stage(stages[0], weights[0], lane_bits, whole, halves[:2])
    done = run_halves(stages[1:], weights[1:], lane_bits, halves[:2], halves[2:])
    tops, mids, _, inner, _ = outs[0].shape
    dests = partners_of(count)
    for top in range(tops):
        for dest, out_ref in zip(dests, outs):
            for mid in range(mids):
                start = pl.multiple_of((mid * count + dest) * inner, inner)
                for part in range(2):
                    out_ref[top, mid, part] = done[top][part, pl.ds(start, inner), :]


def second_kernel(stages, lane_bits, count, stays, *refs):
    blocks, weights, refs = refs[:count], refs[count : count + len(stages)], refs[count + len(stages) :]
    out_ref, one, two = refs
    core = lax.axis_index("qb")
    top = core if stays else 1 - core
    for source, block_ref in zip(partners_of(count), blocks):
        _, mids, _, inner, _ = block_ref.shape
        for mid in range(mids):
            start = pl.multiple_of((mid * count + source) * inner, inner)
            for part in range(2):
                one[part, pl.ds(start, inner), :] = block_ref[top, mid, part]
    for index, (stage, weights_ref) in enumerate(zip(stages, weights)):
        run_stage(stage, weights_ref, lane_bits, one, out_ref if index == len(stages) - 1 else two)
        one, two = two, one


def third_kernel(stages, lane_bits, kept_ref, came_ref, *refs):
    weights, (out_ref, *halves, sems) = refs[: len(stages)], refs[len(stages) :]
    results = halves[4:]
    half = kept_ref.shape[1]
    run_top_stage(stages[0], weights[0], lane_bits, (kept_ref, came_ref), halves[:2])
    done = run_halves(stages[1:-1], weights[1:-1], lane_bits, halves[:2], halves[2:4])
    copies = []
    for t in range(2):
        dim, stride, _ = stage_starts(stages[-1], lane_bits, half)

        def store(part, start, value, t=t):
            results[t][pl.ds(2 * start + part, dim, stride=2 * stride), :] = value

        run_stage(stages[-1], weights[-1], lane_bits, done[t], store=store)
        size = 2 * half // PIECES
        for piece in range(PIECES):
            to = out_ref.at[pl.ds(t * 2 * half + piece * size, size)]
            copies.append(
                pltpu.make_async_copy(results[t].at[pl.ds(piece * size, size)], to, sems.at[t * PIECES + piece])
            )
            copies[-1].start()
    for copy in copies:
        copy.wait()


def call(kernel, name, out_shapes, in_specs, scratch, matmuls, *operands, limit=VMEM_LIMIT, out_spec=None, aliases=None):
    many = isinstance(out_shapes, tuple)
    vmem = out_spec or pl.BlockSpec(memory_space=pltpu.VMEM)
    return pl.pallas_call(
        kernel,
        out_shape=out_shapes,
        in_specs=in_specs,
        out_specs=(vmem,) * len(out_shapes) if many else vmem,
        scratch_shapes=scratch,
        input_output_aliases=aliases or {},
        compiler_params=pltpu.CompilerParams(vmem_limit_bytes=limit),
        cost_estimate=pl.CostEstimate(
            flops=int(matmuls * 3 * 2 * 256 * 256 * 1024), bytes_accessed=4 * 2**20, transcendentals=0
        ),
        name=name,
    )(*operands)


def per_device(state, gate_terms, path_bits):
    amps_local = state.shape[1]
    local_bits = amps_local.bit_length() - 1
    dim = gate_terms.shape[-1]
    gate_bits = dim.bit_length() - 1
    lanes, lane_bits = dim, gate_bits
    rows = amps_local // lanes
    qa = lax.axis_size("qa")
    qb = lax.axis_size("qb")
    low, sections = plan_gates(local_bits, gate_bits)
    sections = [join_windows(section, gate_bits) for section in sections]
    order = 2 * dim
    vmem = pl.BlockSpec(memory_space=pltpu.VMEM)
    hbm = pl.BlockSpec(memory_space=pltpu.HBM)
    shape = jax.ShapeDtypeStruct

    state = with_layout_constraint(state.reshape(2, rows, lanes), Layout(major_to_minor=(1, 0, 2)))
    state = state.swapaxes(0, 1).reshape(qa, 2 * rows // qa, lanes)
    blocks = call(
        split_kernel,
        "split_state",
        (shape((2 * rows // qa, lanes), F32),) * qa,
        [vmem],
        [],
        0,
        state,
    )

    blocks = list(blocks)
    blocks[1] = lax.dynamic_index_in_dim(state, partners_of(qa)[1], 0, keepdims=False)

    def exchange(blocks):
        came = [blocks[0]]
        for distance, piece in zip(distances_of(qa)[1:], blocks[1:]):
            came.append(lax.ppermute(piece, "qa", [(i, i ^ distance) for i in range(qa)]))
        return came

    blocks = exchange(blocks)
    low_w, *weights = call(
        functools.partial(prepare_kernel, low, sections, qa),
        "prepare_gates",
        (shape((3 * order, order), BF16),)
        + tuple(shape((2 * 2**bits, 6 * 2**bits), BF16) for section in sections for _, bits, _ in section),
        [pl.BlockSpec(memory_space=pltpu.SMEM), hbm],
        [
            pltpu.VMEM((gate_terms.shape[0], 2, dim, dim), F32),
            pltpu.VMEM((len(sections), 2, 2, 2 * dim, dim), F32),
            pltpu.SemaphoreType.DMA((gate_terms.shape[0],)),
        ],
        8,
        path_bits,
        gate_terms,
        limit=LARGE_VMEM,
    )
    counts = [len(section) for section in sections]
    weights = [weights[: counts[0]], weights[counts[0] : counts[0] + counts[1]], weights[counts[0] + counts[1] :]]
    inner = rows // (qa * qa)
    half = pltpu.VMEM((2, rows // 2, lanes), F32)
    early, late = list(range(qa - 3)), list(range(qa - 3, qa))
    planes = shape((2, rows, lanes), F32)
    begun = call(
        functools.partial(low_kernel, early),
        "low_gate_early",
        planes,
        [vmem] * (len(early) + 1),
        [],
        1,
        *[blocks[spot] for spot in early],
        low_w,
    )
    *blocks, _ = call(
        functools.partial(first_kernel, sections[0], lane_bits, qa, late),
        "first_section",
        (shape((qb, qa // qb, 2, inner, lanes), F32),) * qa + (planes,),
        [vmem] * (2 + len(late) + counts[0]),
        [half] * 4,
        5,
        begun,
        *[blocks[spot] for spot in late],
        low_w,
        *weights[0],
        aliases={0: qa},
    )
    blocks = exchange(blocks)
    halves = []
    for stays in (False, True):
        halves.append(
            call(
                functools.partial(second_kernel, sections[1], lane_bits, qa, stays),
                "second_section_kept" if stays else "second_section_sent",
                shape((2, rows // qb, lanes), F32),
                [vmem] * (qa + counts[1]),
                [half] * 2,
                1.5,
                *blocks,
                *weights[1],
            )
        )
        if not stays:
            came = lax.ppermute(halves[0], "qb", [(i, 1 - i) for i in range(qb)])
    final = call(
        functools.partial(third_kernel, sections[2], lane_bits),
        "third_section",
        shape((2 * rows, lanes), F32),
        [vmem] * (2 + counts[2]),
        [half] * 4 + [pltpu.VMEM((rows, lanes), F32)] * 2 + [pltpu.SemaphoreType.DMA((2 * PIECES,))],
        4,
        halves[1],
        came,
        *weights[2],
        out_spec=hbm,
    )
    return final.reshape(rows, 2, lanes).swapaxes(0, 1).reshape(2, amps_local)


def solution(mesh):
    return jax.shard_map(
        per_device,
        mesh=mesh,
        in_specs=(P(None, ("paths", "qa", "qb")), P(), P("paths")),
        out_specs=P(None, ("paths", "qa", "qb")),
        check_vma=False,
    )
```

```python
import functools

import jax
import jax.numpy as jnp
from jax import lax
from jax.experimental import pallas as pl
from jax.experimental.layout import Layout, with_layout_constraint
from jax.experimental.pallas import tpu as pltpu
from jax.sharding import PartitionSpec as P

F32 = jnp.float32
BF16 = jnp.bfloat16
VMEM_LIMIT = 14 * 1024 * 1024
LARGE_VMEM = 48 * 1024 * 1024
PIECES = 4


def window_offsets(span, gate_bits):
    return [0, span, gate_bits, span - 1, gate_bits + 1, span - 2]


def plan_gates(local_bits, gate_bits):
    outer = window_offsets(local_bits - gate_bits, gate_bits)
    inner = window_offsets(local_bits - gate_bits - 1, gate_bits)
    low, sections = [], []
    for number, offsets in enumerate((outer, inner, outer)):
        section = []
        for index, offset in enumerate(offsets):
            gate = 6 * number + index
            if offset == 0:
                low.append(gate)
            elif section and section[-1][0] == offset:
                section[-1][1].append(gate)
            else:
                section.append((offset, [gate]))
        sections.append(section)
    return low, sections


def join_windows(section, gate_bits):
    stages = []
    for offset, gates in section:
        if stages:
            offsets = [o for o, _ in stages[-1]] + [offset]
            if max(offsets) - min(offsets) <= 1:
                stages[-1].append((offset, gates))
                continue
        stages.append([(offset, gates)])
    return [
        (min(o for o, _ in parts), gate_bits + (len(parts) > 1), parts)
        for parts in stages
    ]


def interleaved(stage):
    base, _, parts = stage
    return parts[0][0] != base


def split(x):
    high = x.astype(BF16)
    return high, (x - high.astype(F32)).astype(BF16)


def bf_dot(a, b):
    return jnp.dot(a, b, preferred_element_type=F32)


def pair_dot(a, b):
    (a_high, a_rest), (b_high, b_rest) = split(a), split(b)
    return bf_dot(a_high, b_rest) + bf_dot(a_rest, b_high) + bf_dot(a_high, b_high)


def block(real, imag):
    return jnp.concatenate(
        [jnp.concatenate([real, -imag], axis=1), jnp.concatenate([imag, real], axis=1)], axis=0
    )


def relative(matrix, number, count):
    order = matrix.shape[1]
    dim = order // 2
    column = lax.broadcasted_iota(jnp.int32, (order, order), 1)
    row = lax.broadcasted_iota(jnp.int32, (order, order), 0)
    within = lax.rem(column, dim)
    if number == 0:
        size = dim // count
        spot, source = within // size, jnp.zeros_like(column)
        for index, partner in enumerate(partners_of(count)):
            source = jnp.where(spot == index, partner, source)
        natural = source * size + lax.rem(within, size)
    else:
        natural = jnp.bitwise_xor(within, lax.axis_index("qb") * (dim // 2))
    picked = jnp.where(row == natural + (column - within), 1.0, 0.0).astype(BF16)
    return bf_dot(matrix, picked).astype(BF16)


def prepare_kernel(low, sections, count, bits_ref, gates_ref, low_ref, *refs):
    *targets, held, wides, sems = refs
    copies = {}
    for gate in [gate for section in sections for _, _, parts in section for _, gates in parts for gate in gates] + low:
        copies[gate] = pltpu.make_async_copy(gates_ref.at[gate, bits_ref[gate]], held.at[gate], sems.at[gate])
        copies[gate].start()
    dim = held.shape[-1]

    def product(gates):
        for gate in gates:
            copies.pop(gate).wait()
        real, imag = held[gates[0], 0], held[gates[0], 1]
        for gate in gates[1:]:
            column = pair_dot(block(held[gate, 0], held[gate, 1]), jnp.concatenate([real, imag], axis=0))
            real, imag = column[:dim], column[dim:]
        return real, imag

    def joined(wide, base, parts):
        wide[...] = jnp.zeros(wide.shape, F32)
        for index, (offset, gates) in enumerate(parts):
            real, imag = product(gates)
            for t in range(2):
                at = pl.ds(t * dim, dim) if offset == base else pl.ds(t, dim, stride=2)
                if index == 0:
                    wide[0, t, at, :] = real
                    wide[1, t, at, :] = imag
                else:
                    x = jnp.concatenate(
                        [jnp.concatenate([wide[p, c, at, :] for c in range(2)], axis=1) for p in range(2)], axis=0
                    )
                    y = pair_dot(block(real, imag), x)
                    for p in range(2):
                        for c in range(2):
                            wide[p, c, at, :] = y[p * dim : (p + 1) * dim, c * dim : (c + 1) * dim]
        return [jnp.concatenate([wide[p, 0], wide[p, 1]], axis=1) for p in range(2)]

    for number, section in enumerate(sections):
        weights, targets = targets[: len(section)], targets[len(section) :]
        for target, (base, _, parts) in zip(weights, section):
            high, rest = split(block(*(joined(wides.at[number], base, parts) if len(parts) > 1 else product(parts[0][1]))))
            if number != 1 and target is weights[0]:
                high, rest = relative(high, number, count), relative(rest, number, count)
            target[...] = jnp.concatenate([high, rest, high], axis=1)
    real, imag = product(low)
    high, rest = split(block(real.T, -imag.T))
    low_ref[...] = jnp.concatenate([high, rest, high], axis=0)


def distances_of(count):
    half = count // 2
    middle = half + half // 2
    far = [*range(middle - 1, half - 1, -1), *range(count - 1, middle - 1, -1)]
    near = list(range(half - 1, 0, -1))
    order = [0]
    while far or near:
        order += far[:2] + near[:2]
        far, near = far[2:], near[2:]
    return order


def partners_of(count):
    me = lax.axis_index("qa")
    return [jnp.bitwise_xor(me, distance) for distance in distances_of(count)]


def split_kernel(x_ref, *outs):
    for dest, out_ref in zip(partners_of(len(outs)), outs):
        out_ref[...] = x_ref[dest]


def apply_stage(weights_ref, starts, load, store):
    dim = weights_ref.shape[0] // 2
    for pair in range(0, len(starts), 2):
        group = starts[pair : pair + 2]
        x = jnp.concatenate(
            [jnp.concatenate([load(part, start) for start in group], axis=1) for part in range(2)], axis=0
        )
        high, rest = split(x)
        y = bf_dot(weights_ref[...], jnp.concatenate([rest, high, high], axis=0))
        lanes = y.shape[1] // len(group)
        for part in range(2):
            for place, start in enumerate(group):
                store(part, start, y[part * dim : (part + 1) * dim, place * lanes : (place + 1) * lanes])


def stage_starts(stage, lane_bits, rows):
    base, bits, _ = stage
    dim, stride = 2**bits, 2 ** (base - lane_bits)
    return dim, stride, [h * dim * stride + l for h in range(rows // (dim * stride)) for l in range(stride)]


def run_stage(stage, weights_ref, lane_bits, source, target=None, store=None):
    dim, stride, starts = stage_starts(stage, lane_bits, source.shape[1])

    def load(part, start):
        if not interleaved(stage):
            return source[part, pl.ds(start, dim, stride=stride), :]
        half = dim // 2
        return jnp.concatenate(
            [source[part, pl.ds(start + t * stride, half, stride=2 * stride), :] for t in range(2)], axis=0
        )

    def plain(part, start, value):
        target[part, pl.ds(start, dim, stride=stride), :] = value

    apply_stage(weights_ref, starts, load, store or plain)


def run_top_stage(stage, weights_ref, lane_bits, source, halves):
    rows = 2 * halves[0].shape[1]
    dim, stride, starts = stage_starts(stage, lane_bits, rows)

    def store(part, start, value):
        for t in range(2):
            halves[t][part, pl.ds(start, dim // 2, stride=stride), :] = value[t * dim // 2 : (t + 1) * dim // 2]

    def load(part, start):
        if not isinstance(source, tuple):
            return source[part, pl.ds(start, dim, stride=stride), :]
        return jnp.concatenate([half[part, pl.ds(start, dim // 2, stride=stride), :] for half in source], axis=0)

    apply_stage(weights_ref, starts, load, store)


def run_halves(stages, weights, lane_bits, halves, spares, last_store=None):
    for index, (stage, weights_ref) in enumerate(zip(stages, weights)):
        for t in range(2):
            store = None
            if last_store is not None and index == len(stages) - 1:
                store = functools.partial(last_store, t)
            run_stage(stage, weights_ref, lane_bits, halves[t], spares[t], store)
        halves, spares = spares, halves
    return halves


def low_gate(blocks, low_ref, whole):
    lanes = whole.shape[2]
    for spot, block_ref in blocks:
        size = block_ref.shape[0] // 2
        real = block_ref[pl.ds(0, size, stride=2), :]
        imag = block_ref[pl.ds(1, size, stride=2), :]
        high, rest = split(jnp.concatenate([real, imag], axis=1))
        y = bf_dot(jnp.concatenate([rest, high, high], axis=1), low_ref[...])
        whole[0, pl.ds(spot * size, size), :] = y[:, :lanes]
        whole[1, pl.ds(spot * size, size), :] = y[:, lanes:]


def low_kernel(spots, *refs):
    *blocks, low_ref, whole = refs
    low_gate(zip(spots, blocks), low_ref, whole)


def first_kernel(stages, lane_bits, count, spots, *refs):
    _, *blocks = refs[: 1 + len(spots)]
    refs = refs[1 + len(spots) :]
    low_ref, weights, refs = refs[0], refs[1 : 1 + len(stages)], refs[1 + len(stages) :]
    outs, (whole, *halves) = refs[:count], refs[count:]
    low_gate(zip(spots, blocks), low_ref, whole)
    run_top_stage(stages[0], weights[0], lane_bits, whole, halves[:2])
    done = run_halves(stages[1:], weights[1:], lane_bits, halves[:2], halves[2:])
    tops, mids, _, inner, _ = outs[0].shape
    dests = partners_of(count)
    for top in range(tops):
        for dest, out_ref in zip(dests, outs):
            for mid in range(mids):
                start = pl.multiple_of((mid * count + dest) * inner, inner)
                for part in range(2):
                    out_ref[top, mid, part] = done[top][part, pl.ds(start, inner), :]


def second_kernel(stages, lane_bits, count, stays, *refs):
    blocks, weights, refs = refs[:count], refs[count : count + len(stages)], refs[count + len(stages) :]
    out_ref, one, two = refs
    core = lax.axis_index("qb")
    top = core if stays else 1 - core
    for source, block_ref in zip(partners_of(count), blocks):
        _, mids, _, inner, _ = block_ref.shape
        for mid in range(mids):
            start = pl.multiple_of((mid * count + source) * inner, inner)
            for part in range(2):
                one[part, pl.ds(start, inner), :] = block_ref[top, mid, part]
    for index, (stage, weights_ref) in enumerate(zip(stages, weights)):
        run_stage(stage, weights_ref, lane_bits, one, out_ref if index == len(stages) - 1 else two)
        one, two = two, one


def third_kernel(stages, lane_bits, kept_ref, came_ref, *refs):
    weights, (out_ref, *halves, sems) = refs[: len(stages)], refs[len(stages) :]
    results = halves[4:]
    half = kept_ref.shape[1]
    run_top_stage(stages[0], weights[0], lane_bits, (kept_ref, came_ref), halves[:2])
    done = run_halves(stages[1:-1], weights[1:-1], lane_bits, halves[:2], halves[2:4])
    copies = []
    for t in range(2):
        dim, stride, _ = stage_starts(stages[-1], lane_bits, half)

        def store(part, start, value, t=t):
            results[t][pl.ds(2 * start + part, dim, stride=2 * stride), :] = value

        run_stage(stages[-1], weights[-1], lane_bits, done[t], store=store)
        size = 2 * half // PIECES
        for piece in range(PIECES):
            to = out_ref.at[pl.ds(t * 2 * half + piece * size, size)]
            copies.append(
                pltpu.make_async_copy(results[t].at[pl.ds(piece * size, size)], to, sems.at[t * PIECES + piece])
            )
            copies[-1].start()
    for copy in copies:
        copy.wait()


def call(kernel, name, out_shapes, in_specs, scratch, matmuls, *operands, limit=VMEM_LIMIT, out_spec=None, aliases=None):
    many = isinstance(out_shapes, tuple)
    vmem = out_spec or pl.BlockSpec(memory_space=pltpu.VMEM)
    return pl.pallas_call(
        kernel,
        out_shape=out_shapes,
        in_specs=in_specs,
        out_specs=(vmem,) * len(out_shapes) if many else vmem,
        scratch_shapes=scratch,
        input_output_aliases=aliases or {},
        compiler_params=pltpu.CompilerParams(vmem_limit_bytes=limit),
        cost_estimate=pl.CostEstimate(
            flops=int(matmuls * 3 * 2 * 256 * 256 * 1024), bytes_accessed=4 * 2**20, transcendentals=0
        ),
        name=name,
    )(*operands)


def per_device(state, gate_terms, path_bits):
    amps_local = state.shape[1]
    local_bits = amps_local.bit_length() - 1
    dim = gate_terms.shape[-1]
    gate_bits = dim.bit_length() - 1
    lanes, lane_bits = dim, gate_bits
    rows = amps_local // lanes
    qa = lax.axis_size("qa")
    qb = lax.axis_size("qb")
    low, sections = plan_gates(local_bits, gate_bits)
    sections = [join_windows(section, gate_bits) for section in sections]
    order = 2 * dim
    vmem = pl.BlockSpec(memory_space=pltpu.VMEM)
    hbm = pl.BlockSpec(memory_space=pltpu.HBM)
    shape = jax.ShapeDtypeStruct

    state = with_layout_constraint(state.reshape(2, rows, lanes), Layout(major_to_minor=(1, 0, 2)))
    state = state.swapaxes(0, 1).reshape(qa, 2 * rows // qa, lanes)
    blocks = call(
        split_kernel,
        "split_state",
        (shape((2 * rows // qa, lanes), F32),) * qa,
        [vmem],
        [],
        0,
        state,
    )

    blocks = list(blocks)
    blocks[1] = lax.dynamic_index_in_dim(state, partners_of(qa)[1], 0, keepdims=False)

    def exchange(blocks):
        came = [blocks[0]]
        for distance, piece in zip(distances_of(qa)[1:], blocks[1:]):
            came.append(lax.ppermute(piece, "qa", [(i, i ^ distance) for i in range(qa)]))
        return came

    blocks = exchange(blocks)
    low_w, *weights = call(
        functools.partial(prepare_kernel, low, sections, qa),
        "prepare_gates",
        (shape((3 * order, order), BF16),)
        + tuple(shape((2 * 2**bits, 6 * 2**bits), BF16) for section in sections for _, bits, _ in section),
        [pl.BlockSpec(memory_space=pltpu.SMEM), hbm],
        [
            pltpu.VMEM((gate_terms.shape[0], 2, dim, dim), F32),
            pltpu.VMEM((len(sections), 2, 2, 2 * dim, dim), F32),
            pltpu.SemaphoreType.DMA((gate_terms.shape[0],)),
        ],
        8,
        path_bits,
        gate_terms,
        limit=LARGE_VMEM,
    )
    counts = [len(section) for section in sections]
    weights = [weights[: counts[0]], weights[counts[0] : counts[0] + counts[1]], weights[counts[0] + counts[1] :]]
    inner = rows // (qa * qa)
    half = pltpu.VMEM((2, rows // 2, lanes), F32)
    early, late = list(range(qa - 3)), list(range(qa - 3, qa))
    planes = shape((2, rows, lanes), F32)
    begun = call(
        functools.partial(low_kernel, early),
        "low_gate_early",
        planes,
        [vmem] * (len(early) + 1),
        [],
        1,
        *[blocks[spot] for spot in early],
        low_w,
    )
    *blocks, _ = call(
        functools.partial(first_kernel, sections[0], lane_bits, qa, late),
        "first_section",
        (shape((qb, qa // qb, 2, inner, lanes), F32),) * qa + (planes,),
        [vmem] * (2 + len(late) + counts[0]),
        [half] * 4,
        5,
        begun,
        *[blocks[spot] for spot in late],
        low_w,
        *weights[0],
        aliases={0: qa},
    )
    blocks = exchange(blocks)
    halves = []
    for stays in (False, True):
        halves.append(
            call(
                functools.partial(second_kernel, sections[1], lane_bits, qa, stays),
                "second_section_kept" if stays else "second_section_sent",
                shape((2, rows // qb, lanes), F32),
                [vmem] * (qa + counts[1]),
                [half] * 2,
                1.5,
                *blocks,
                *weights[1],
            )
        )
        if not stays:
            came = lax.ppermute(halves[0], "qb", [(i, 1 - i) for i in range(qb)])
    final = call(
        functools.partial(third_kernel, sections[2], lane_bits),
        "third_section",
        shape((2 * rows, lanes), F32),
        [vmem] * (2 + counts[2]),
        [half] * 4 + [pltpu.VMEM((rows, lanes), F32)] * 2 + [pltpu.SemaphoreType.DMA((2 * PIECES,))],
        4,
        halves[1],
        came,
        *weights[2],
        out_spec=hbm,
    )
    return final.reshape(rows, 2, lanes).swapaxes(0, 1).reshape(2, amps_local)


def solution(mesh):
    return jax.shard_map(
        per_device,
        mesh=mesh,
        in_specs=(P(None, ("paths", "qa", "qb")), P(), P("paths")),
        out_specs=P(None, ("paths", "qa", "qb")),
        check_vma=False,
    )
```

```python
import functools

import jax
import jax.numpy as jnp
from jax import lax
from jax.experimental import pallas as pl
from jax.experimental.layout import Layout, with_layout_constraint
from jax.experimental.pallas import tpu as pltpu
from jax.sharding import PartitionSpec as P

F32 = jnp.float32
BF16 = jnp.bfloat16
VMEM_LIMIT = 14 * 1024 * 1024
LARGE_VMEM = 48 * 1024 * 1024
PIECES = 4


def window_offsets(span, gate_bits):
    return [0, span, gate_bits, span - 1, gate_bits + 1, span - 2]


def plan_gates(local_bits, gate_bits):
    outer = window_offsets(local_bits - gate_bits, gate_bits)
    inner = window_offsets(local_bits - gate_bits - 1, gate_bits)
    low, sections = [], []
    for number, offsets in enumerate((outer, inner, outer)):
        section = []
        for index, offset in enumerate(offsets):
            gate = 6 * number + index
            if offset == 0:
                low.append(gate)
            elif section and section[-1][0] == offset:
                section[-1][1].append(gate)
            else:
                section.append((offset, [gate]))
        sections.append(section)
    return low, sections


def join_windows(section, gate_bits):
    stages = []
    for offset, gates in section:
        if stages:
            offsets = [o for o, _ in stages[-1]] + [offset]
            if max(offsets) - min(offsets) <= 1:
                stages[-1].append((offset, gates))
                continue
        stages.append([(offset, gates)])
    return [
        (min(o for o, _ in parts), gate_bits + (len(parts) > 1), parts)
        for parts in stages
    ]


def interleaved(stage):
    base, _, parts = stage
    return parts[0][0] != base


def split(x):
    high = x.astype(BF16)
    return high, (x - high.astype(F32)).astype(BF16)


def bf_dot(a, b):
    return jnp.dot(a, b, preferred_element_type=F32)


def pair_dot(a, b):
    (a_high, a_rest), (b_high, b_rest) = split(a), split(b)
    return bf_dot(a_high, b_rest) + bf_dot(a_rest, b_high) + bf_dot(a_high, b_high)


def block(real, imag):
    return jnp.concatenate(
        [jnp.concatenate([real, -imag], axis=1), jnp.concatenate([imag, real], axis=1)], axis=0
    )


def relative(matrix, number, count):
    order = matrix.shape[1]
    dim = order // 2
    column = lax.broadcasted_iota(jnp.int32, (order, order), 1)
    row = lax.broadcasted_iota(jnp.int32, (order, order), 0)
    within = lax.rem(column, dim)
    if number == 0:
        size = dim // count
        spot, source = within // size, jnp.zeros_like(column)
        for index, partner in enumerate(partners_of(count, 1)):
            source = jnp.where(spot == index, partner, source)
        natural = source * size + lax.rem(within, size)
    else:
        natural = jnp.bitwise_xor(within, lax.axis_index("qb") * (dim // 2))
    picked = jnp.where(row == natural + (column - within), 1.0, 0.0).astype(BF16)
    return bf_dot(matrix, picked).astype(BF16)


def prepare_kernel(low, sections, count, bits_ref, gates_ref, low_ref, *refs):
    *targets, held, wides, sems = refs
    copies = {}
    for gate in [gate for section in sections for _, _, parts in section for _, gates in parts for gate in gates] + low:
        copies[gate] = pltpu.make_async_copy(gates_ref.at[gate, bits_ref[gate]], held.at[gate], sems.at[gate])
        copies[gate].start()
    dim = held.shape[-1]

    def product(gates):
        for gate in gates:
            copies.pop(gate).wait()
        real, imag = held[gates[0], 0], held[gates[0], 1]
        for gate in gates[1:]:
            column = pair_dot(block(held[gate, 0], held[gate, 1]), jnp.concatenate([real, imag], axis=0))
            real, imag = column[:dim], column[dim:]
        return real, imag

    def joined(wide, base, parts):
        wide[...] = jnp.zeros(wide.shape, F32)
        for index, (offset, gates) in enumerate(parts):
            real, imag = product(gates)
            for t in range(2):
                at = pl.ds(t * dim, dim) if offset == base else pl.ds(t, dim, stride=2)
                if index == 0:
                    wide[0, t, at, :] = real
                    wide[1, t, at, :] = imag
                else:
                    x = jnp.concatenate(
                        [jnp.concatenate([wide[p, c, at, :] for c in range(2)], axis=1) for p in range(2)], axis=0
                    )
                    y = pair_dot(block(real, imag), x)
                    for p in range(2):
                        for c in range(2):
                            wide[p, c, at, :] = y[p * dim : (p + 1) * dim, c * dim : (c + 1) * dim]
        return [jnp.concatenate([wide[p, 0], wide[p, 1]], axis=1) for p in range(2)]

    for number, section in enumerate(sections):
        weights, targets = targets[: len(section)], targets[len(section) :]
        for target, (base, _, parts) in zip(weights, section):
            high, rest = split(block(*(joined(wides.at[number], base, parts) if len(parts) > 1 else product(parts[0][1]))))
            if number != 1 and target is weights[0]:
                high, rest = relative(high, number, count), relative(rest, number, count)
            target[...] = jnp.concatenate([high, rest, high], axis=1)
    real, imag = product(low)
    high, rest = split(block(real.T, -imag.T))
    low_ref[...] = jnp.concatenate([high, rest, high], axis=0)


def distances_of(count, exchange):
    half = count // 2
    middle = half + half // 2
    far = [*range(middle - 1, half - 1, -1), *range(count - 1, middle - 1, -1)]
    if exchange == 2:
        far.sort(reverse=True)
    near = list(range(half - 1, 0, -1))
    order = [0]
    while far or near:
        order += far[:2] + near[:2]
        far, near = far[2:], near[2:]
    return order


def partners_of(count, exchange):
    me = lax.axis_index("qa")
    return [jnp.bitwise_xor(me, distance) for distance in distances_of(count, exchange)]


def split_kernel(x_ref, *outs):
    for dest, out_ref in zip(partners_of(len(outs), 1), outs):
        out_ref[...] = x_ref[dest]


def apply_stage(weights_ref, starts, load, store):
    dim = weights_ref.shape[0] // 2
    for pair in range(0, len(starts), 2):
        group = starts[pair : pair + 2]
        x = jnp.concatenate(
            [jnp.concatenate([load(part, start) for start in group], axis=1) for part in range(2)], axis=0
        )
        high, rest = split(x)
        y = bf_dot(weights_ref[...], jnp.concatenate([rest, high, high], axis=0))
        lanes = y.shape[1] // len(group)
        for part in range(2):
            for place, start in enumerate(group):
                store(part, start, y[part * dim : (part + 1) * dim, place * lanes : (place + 1) * lanes])


def stage_starts(stage, lane_bits, rows):
    base, bits, _ = stage
    dim, stride = 2**bits, 2 ** (base - lane_bits)
    return dim, stride, [h * dim * stride + l for h in range(rows // (dim * stride)) for l in range(stride)]


def run_stage(stage, weights_ref, lane_bits, source, target=None, store=None):
    dim, stride, starts = stage_starts(stage, lane_bits, source.shape[1])

    def load(part, start):
        if not interleaved(stage):
            return source[part, pl.ds(start, dim, stride=stride), :]
        half = dim // 2
        return jnp.concatenate(
            [source[part, pl.ds(start + t * stride, half, stride=2 * stride), :] for t in range(2)], axis=0
        )

    def plain(part, start, value):
        target[part, pl.ds(start, dim, stride=stride), :] = value

    apply_stage(weights_ref, starts, load, store or plain)


def run_top_stage(stage, weights_ref, lane_bits, source, halves):
    rows = 2 * halves[0].shape[1]
    dim, stride, starts = stage_starts(stage, lane_bits, rows)

    def store(part, start, value):
        for t in range(2):
            halves[t][part, pl.ds(start, dim // 2, stride=stride), :] = value[t * dim // 2 : (t + 1) * dim // 2]

    def load(part, start):
        if not isinstance(source, tuple):
            return source[part, pl.ds(start, dim, stride=stride), :]
        return jnp.concatenate([half[part, pl.ds(start, dim // 2, stride=stride), :] for half in source], axis=0)

    apply_stage(weights_ref, starts, load, store)


def run_halves(stages, weights, lane_bits, halves, spares, last_store=None):
    for index, (stage, weights_ref) in enumerate(zip(stages, weights)):
        for t in range(2):
            store = None
            if last_store is not None and index == len(stages) - 1:
                store = functools.partial(last_store, t)
            run_stage(stage, weights_ref, lane_bits, halves[t], spares[t], store)
        halves, spares = spares, halves
    return halves


def low_gate(blocks, low_ref, whole):
    lanes = whole.shape[2]
    for spot, block_ref in blocks:
        size = block_ref.shape[0] // 2
        real = block_ref[pl.ds(0, size, stride=2), :]
        imag = block_ref[pl.ds(1, size, stride=2), :]
        high, rest = split(jnp.concatenate([real, imag], axis=1))
        y = bf_dot(jnp.concatenate([rest, high, high], axis=1), low_ref[...])
        whole[0, pl.ds(spot * size, size), :] = y[:, :lanes]
        whole[1, pl.ds(spot * size, size), :] = y[:, lanes:]


def low_kernel(spots, *refs):
    *blocks, low_ref, whole = refs
    low_gate(zip(spots, blocks), low_ref, whole)


def first_kernel(stages, lane_bits, count, spots, *refs):
    _, *blocks = refs[: 1 + len(spots)]
    refs = refs[1 + len(spots) :]
    low_ref, weights, refs = refs[0], refs[1 : 1 + len(stages)], refs[1 + len(stages) :]
    outs, (whole, *halves) = refs[:count], refs[count:]
    low_gate(zip(spots, blocks), low_ref, whole)
    run_top_stage(stages[0], weights[0], lane_bits, whole, halves[:2])
    done = run_halves(stages[1:], weights[1:], lane_bits, halves[:2], halves[2:])
    tops, mids, _, inner, _ = outs[0].shape
    dests = partners_of(count, 2)
    for top in range(tops):
        for dest, out_ref in zip(dests, outs):
            for mid in range(mids):
                start = pl.multiple_of((mid * count + dest) * inner, inner)
                for part in range(2):
                    out_ref[top, mid, part] = done[top][part, pl.ds(start, inner), :]


def second_kernel(stages, lane_bits, count, stays, *refs):
    blocks, weights, refs = refs[:count], refs[count : count + len(stages)], refs[count + len(stages) :]
    out_ref, one, two = refs
    core = lax.axis_index("qb")
    top = core if stays else 1 - core
    for source, block_ref in zip(partners_of(count, 2), blocks):
        _, mids, _, inner, _ = block_ref.shape
        for mid in range(mids):
            start = pl.multiple_of((mid * count + source) * inner, inner)
            for part in range(2):
                one[part, pl.ds(start, inner), :] = block_ref[top, mid, part]
    for index, (stage, weights_ref) in enumerate(zip(stages, weights)):
        run_stage(stage, weights_ref, lane_bits, one, out_ref if index == len(stages) - 1 else two)
        one, two = two, one


def third_kernel(stages, lane_bits, kept_ref, came_ref, *refs):
    weights, (out_ref, *halves, sems) = refs[: len(stages)], refs[len(stages) :]
    results = halves[4:]
    half = kept_ref.shape[1]
    run_top_stage(stages[0], weights[0], lane_bits, (kept_ref, came_ref), halves[:2])
    done = run_halves(stages[1:-1], weights[1:-1], lane_bits, halves[:2], halves[2:4])
    copies = []
    for t in range(2):
        dim, stride, _ = stage_starts(stages[-1], lane_bits, half)

        def store(part, start, value, t=t):
            results[t][pl.ds(2 * start + part, dim, stride=2 * stride), :] = value

        run_stage(stages[-1], weights[-1], lane_bits, done[t], store=store)
        size = 2 * half // PIECES
        for piece in range(PIECES):
            to = out_ref.at[pl.ds(t * 2 * half + piece * size, size)]
            copies.append(
                pltpu.make_async_copy(results[t].at[pl.ds(piece * size, size)], to, sems.at[t * PIECES + piece])
            )
            copies[-1].start()
    for copy in copies:
        copy.wait()


def call(kernel, name, out_shapes, in_specs, scratch, matmuls, *operands, limit=VMEM_LIMIT, out_spec=None, aliases=None):
    many = isinstance(out_shapes, tuple)
    vmem = out_spec or pl.BlockSpec(memory_space=pltpu.VMEM)
    return pl.pallas_call(
        kernel,
        out_shape=out_shapes,
        in_specs=in_specs,
        out_specs=(vmem,) * len(out_shapes) if many else vmem,
        scratch_shapes=scratch,
        input_output_aliases=aliases or {},
        compiler_params=pltpu.CompilerParams(vmem_limit_bytes=limit),
        cost_estimate=pl.CostEstimate(
            flops=int(matmuls * 3 * 2 * 256 * 256 * 1024), bytes_accessed=4 * 2**20, transcendentals=0
        ),
        name=name,
    )(*operands)


def per_device(state, gate_terms, path_bits):
    amps_local = state.shape[1]
    local_bits = amps_local.bit_length() - 1
    dim = gate_terms.shape[-1]
    gate_bits = dim.bit_length() - 1
    lanes, lane_bits = dim, gate_bits
    rows = amps_local // lanes
    qa = lax.axis_size("qa")
    qb = lax.axis_size("qb")
    low, sections = plan_gates(local_bits, gate_bits)
    sections = [join_windows(section, gate_bits) for section in sections]
    order = 2 * dim
    vmem = pl.BlockSpec(memory_space=pltpu.VMEM)
    hbm = pl.BlockSpec(memory_space=pltpu.HBM)
    shape = jax.ShapeDtypeStruct

    state = with_layout_constraint(state.reshape(2, rows, lanes), Layout(major_to_minor=(1, 0, 2)))
    state = state.swapaxes(0, 1).reshape(qa, 2 * rows // qa, lanes)
    blocks = call(
        split_kernel,
        "split_state",
        (shape((2 * rows // qa, lanes), F32),) * qa,
        [vmem],
        [],
        0,
        state,
    )

    blocks = list(blocks)
    blocks[1] = lax.dynamic_index_in_dim(state, partners_of(qa, 1)[1], 0, keepdims=False)

    def exchange(blocks, which):
        came = [blocks[0]]
        for distance, piece in zip(distances_of(qa, which)[1:], blocks[1:]):
            came.append(lax.ppermute(piece, "qa", [(i, i ^ distance) for i in range(qa)]))
        return came

    blocks = exchange(blocks, 1)
    low_w, *weights = call(
        functools.partial(prepare_kernel, low, sections, qa),
        "prepare_gates",
        (shape((3 * order, order), BF16),)
        + tuple(shape((2 * 2**bits, 6 * 2**bits), BF16) for section in sections for _, bits, _ in section),
        [pl.BlockSpec(memory_space=pltpu.SMEM), hbm],
        [
            pltpu.VMEM((gate_terms.shape[0], 2, dim, dim), F32),
            pltpu.VMEM((len(sections), 2, 2, 2 * dim, dim), F32),
            pltpu.SemaphoreType.DMA((gate_terms.shape[0],)),
        ],
        8,
        path_bits,
        gate_terms,
        limit=LARGE_VMEM,
    )
    counts = [len(section) for section in sections]
    weights = [weights[: counts[0]], weights[counts[0] : counts[0] + counts[1]], weights[counts[0] + counts[1] :]]
    inner = rows // (qa * qa)
    half = pltpu.VMEM((2, rows // 2, lanes), F32)
    early, late = list(range(qa - 3)), list(range(qa - 3, qa))
    planes = shape((2, rows, lanes), F32)
    begun = call(
        functools.partial(low_kernel, early),
        "low_gate_early",
        planes,
        [vmem] * (len(early) + 1),
        [],
        1,
        *[blocks[spot] for spot in early],
        low_w,
    )
    *blocks, _ = call(
        functools.partial(first_kernel, sections[0], lane_bits, qa, late),
        "first_section",
        (shape((qb, qa // qb, 2, inner, lanes), F32),) * qa + (planes,),
        [vmem] * (2 + len(late) + counts[0]),
        [half] * 4,
        5,
        begun,
        *[blocks[spot] for spot in late],
        low_w,
        *weights[0],
        aliases={0: qa},
    )
    blocks = exchange(blocks, 2)
    halves = []
    for stays in (False, True):
        halves.append(
            call(
                functools.partial(second_kernel, sections[1], lane_bits, qa, stays),
                "second_section_kept" if stays else "second_section_sent",
                shape((2, rows // qb, lanes), F32),
                [vmem] * (qa + counts[1]),
                [half] * 2,
                1.5,
                *blocks,
                *weights[1],
            )
        )
        if not stays:
            came = lax.ppermute(halves[0], "qb", [(i, 1 - i) for i in range(qb)])
    final = call(
        functools.partial(third_kernel, sections[2], lane_bits),
        "third_section",
        shape((2 * rows, lanes), F32),
        [vmem] * (2 + counts[2]),
        [half] * 4 + [pltpu.VMEM((rows, lanes), F32)] * 2 + [pltpu.SemaphoreType.DMA((2 * PIECES,))],
        4,
        halves[1],
        came,
        *weights[2],
        out_spec=hbm,
    )
    return final.reshape(rows, 2, lanes).swapaxes(0, 1).reshape(2, amps_local)


def solution(mesh):
    return jax.shard_map(
        per_device,
        mesh=mesh,
        in_specs=(P(None, ("paths", "qa", "qb")), P(), P("paths")),
        out_specs=P(None, ("paths", "qa", "qb")),
        check_vma=False,
    )
```

```python
import functools

import jax
import jax.numpy as jnp
from jax import lax
from jax.experimental import pallas as pl
from jax.experimental.layout import Layout, with_layout_constraint
from jax.experimental.pallas import tpu as pltpu
from jax.sharding import PartitionSpec as P

F32 = jnp.float32
BF16 = jnp.bfloat16
VMEM_LIMIT = 14 * 1024 * 1024
LARGE_VMEM = 48 * 1024 * 1024
PIECES = 4


def window_offsets(span, gate_bits):
    return [0, span, gate_bits, span - 1, gate_bits + 1, span - 2]


def plan_gates(local_bits, gate_bits):
    outer = window_offsets(local_bits - gate_bits, gate_bits)
    inner = window_offsets(local_bits - gate_bits - 1, gate_bits)
    low, sections = [], []
    for number, offsets in enumerate((outer, inner, outer)):
        section = []
        for index, offset in enumerate(offsets):
            gate = 6 * number + index
            if offset == 0:
                low.append(gate)
            elif section and section[-1][0] == offset:
                section[-1][1].append(gate)
            else:
                section.append((offset, [gate]))
        sections.append(section)
    return low, sections


def join_windows(section, gate_bits):
    stages = []
    for offset, gates in section:
        if stages:
            offsets = [o for o, _ in stages[-1]] + [offset]
            if max(offsets) - min(offsets) <= 1:
                stages[-1].append((offset, gates))
                continue
        stages.append([(offset, gates)])
    return [
        (min(o for o, _ in parts), gate_bits + (len(parts) > 1), parts)
        for parts in stages
    ]


def interleaved(stage):
    base, _, parts = stage
    return parts[0][0] != base


def split(x):
    high = x.astype(BF16)
    return high, (x - high.astype(F32)).astype(BF16)


def bf_dot(a, b):
    return jnp.dot(a, b, preferred_element_type=F32)


def pair_dot(a, b):
    (a_high, a_rest), (b_high, b_rest) = split(a), split(b)
    return bf_dot(a_high, b_rest) + bf_dot(a_rest, b_high) + bf_dot(a_high, b_high)


def block(real, imag):
    return jnp.concatenate(
        [jnp.concatenate([real, -imag], axis=1), jnp.concatenate([imag, real], axis=1)], axis=0
    )


def iotas(order):
    return [lax.broadcasted_iota(jnp.int32, (order, order), axis) for axis in (0, 1)]


def pick_columns(matrix, natural):
    row, column = iotas(matrix.shape[1])
    within = lax.rem(column, matrix.shape[1] // 2)
    picked = jnp.where(row == natural(within) + (column - within), 1.0, 0.0).astype(BF16)
    return bf_dot(matrix, picked).astype(BF16)


def pick_rows(matrix, natural):
    row, column = iotas(matrix.shape[0])
    within = lax.rem(row, matrix.shape[0] // 2)
    picked = jnp.where(column == natural(within) + (row - within), 1.0, 0.0).astype(BF16)
    return bf_dot(picked, matrix).astype(BF16)


def partner_at(spot, count):
    found = jnp.zeros_like(spot)
    for index, partner in enumerate(partners_of(count)):
        found = jnp.where(spot == index, partner, found)
    return found


def by_source(dim, count):
    size = dim // count
    return lambda x: partner_at(x // size, count) * size + lax.rem(x, size)


def by_core(dim):
    return lambda x: jnp.bitwise_xor(x, lax.axis_index("qb") * (dim // 2))


def straight(count):
    return count == 8


def into_blocks(x):
    high, low = (x >> 2) & 3, x & 3
    return high * 64 + partner_at(x >> 5, 8) * 8 + low * 2 + ((x >> 4) & 1)


def from_blocks(x):
    return ((x >> 2) & 3) * 32 + partner_at(x >> 4, 8) * 4 + (x & 3)


def prepare_kernel(low, sections, count, bits_ref, gates_ref, low_ref, *refs):
    *targets, held, wides, sems = refs
    copies = {}
    for gate in [gate for section in sections for _, _, parts in section for _, gates in parts for gate in gates] + low:
        copies[gate] = pltpu.make_async_copy(gates_ref.at[gate, bits_ref[gate]], held.at[gate], sems.at[gate])
        copies[gate].start()
    dim = held.shape[-1]

    def product(gates):
        for gate in gates:
            copies.pop(gate).wait()
        real, imag = held[gates[0], 0], held[gates[0], 1]
        for gate in gates[1:]:
            column = pair_dot(block(held[gate, 0], held[gate, 1]), jnp.concatenate([real, imag], axis=0))
            real, imag = column[:dim], column[dim:]
        return real, imag

    def joined(wide, base, parts):
        wide[...] = jnp.zeros(wide.shape, F32)
        for index, (offset, gates) in enumerate(parts):
            real, imag = product(gates)
            for t in range(2):
                at = pl.ds(t * dim, dim) if offset == base else pl.ds(t, dim, stride=2)
                if index == 0:
                    wide[0, t, at, :] = real
                    wide[1, t, at, :] = imag
                else:
                    x = jnp.concatenate(
                        [jnp.concatenate([wide[p, c, at, :] for c in range(2)], axis=1) for p in range(2)], axis=0
                    )
                    y = pair_dot(block(real, imag), x)
                    for p in range(2):
                        for c in range(2):
                            wide[p, c, at, :] = y[p * dim : (p + 1) * dim, c * dim : (c + 1) * dim]
        return [jnp.concatenate([wide[p, 0], wide[p, 1]], axis=1) for p in range(2)]

    for number, section in enumerate(sections):
        weights, targets = targets[: len(section)], targets[len(section) :]
        for target, (base, _, parts) in zip(weights, section):
            high, rest = split(block(*(joined(wides.at[number], base, parts) if len(parts) > 1 else product(parts[0][1]))))
            if target is weights[0]:
                order = (by_source(dim, count), from_blocks if straight(count) else None, by_core(dim))[number]
                if order is not None:
                    high, rest = pick_columns(high, order), pick_columns(rest, order)
            elif number == 0 and straight(count) and target is weights[-1]:
                high, rest = pick_rows(high, into_blocks), pick_rows(rest, into_blocks)
            target[...] = jnp.concatenate([high, rest, high], axis=1)
    real, imag = product(low)
    high, rest = split(block(real.T, -imag.T))
    low_ref[...] = jnp.concatenate([high, rest, high], axis=0)


def distances_of(count):
    half = count // 2
    far, near = list(range(count - 1, half - 1, -1)), list(range(half - 1, 0, -1))
    order = [0]
    while far or near:
        order += far[:2] + near[:2]
        far, near = far[2:], near[2:]
    return order


def partners_of(count):
    me = lax.axis_index("qa")
    return [jnp.bitwise_xor(me, distance) for distance in distances_of(count)]


def split_kernel(x_ref, *outs):
    for dest, out_ref in zip(partners_of(len(outs)), outs):
        out_ref[...] = x_ref[dest]


def apply_stage(weights_ref, starts, load, store):
    dim = weights_ref.shape[0] // 2
    for pair in range(0, len(starts), 2):
        group = starts[pair : pair + 2]
        x = jnp.concatenate(
            [jnp.concatenate([load(part, start) for start in group], axis=1) for part in range(2)], axis=0
        )
        high, rest = split(x)
        y = bf_dot(weights_ref[...], jnp.concatenate([rest, high, high], axis=0))
        lanes = y.shape[1] // len(group)
        for part in range(2):
            for place, start in enumerate(group):
                store(part, start, y[part * dim : (part + 1) * dim, place * lanes : (place + 1) * lanes])


def stage_starts(stage, lane_bits, rows):
    base, bits, _ = stage
    dim, stride = 2**bits, 2 ** (base - lane_bits)
    return dim, stride, [h * dim * stride + l for h in range(rows // (dim * stride)) for l in range(stride)]


def run_stage(stage, weights_ref, lane_bits, source, target=None, store=None):
    dim, stride, starts = stage_starts(stage, lane_bits, source.shape[1])

    def load(part, start):
        if not interleaved(stage):
            return source[part, pl.ds(start, dim, stride=stride), :]
        half = dim // 2
        return jnp.concatenate(
            [source[part, pl.ds(start + t * stride, half, stride=2 * stride), :] for t in range(2)], axis=0
        )

    def plain(part, start, value):
        target[part, pl.ds(start, dim, stride=stride), :] = value

    apply_stage(weights_ref, starts, load, store or plain)


def run_top_stage(stage, weights_ref, lane_bits, source, halves):
    rows = 2 * halves[0].shape[1]
    dim, stride, starts = stage_starts(stage, lane_bits, rows)

    def store(part, start, value):
        for t in range(2):
            halves[t][part, pl.ds(start, dim // 2, stride=stride), :] = value[t * dim // 2 : (t + 1) * dim // 2]

    def load(part, start):
        if not isinstance(source, tuple):
            return source[part, pl.ds(start, dim, stride=stride), :]
        return jnp.concatenate([half[part, pl.ds(start, dim // 2, stride=stride), :] for half in source], axis=0)

    apply_stage(weights_ref, starts, load, store)


def run_halves(stages, weights, lane_bits, halves, spares, last_store=None):
    for index, (stage, weights_ref) in enumerate(zip(stages, weights)):
        for t in range(2):
            store = None
            if last_store is not None and index == len(stages) - 1:
                store = functools.partial(last_store, t)
            run_stage(stage, weights_ref, lane_bits, halves[t], spares[t], store)
        halves, spares = spares, halves
    return halves


def low_gate(blocks, low_ref, whole):
    lanes = whole.shape[2]
    for spot, block_ref in blocks:
        size = block_ref.shape[0] // 2
        real = block_ref[pl.ds(0, size, stride=2), :]
        imag = block_ref[pl.ds(1, size, stride=2), :]
        high, rest = split(jnp.concatenate([real, imag], axis=1))
        y = bf_dot(jnp.concatenate([rest, high, high], axis=1), low_ref[...])
        whole[0, pl.ds(spot * size, size), :] = y[:, :lanes]
        whole[1, pl.ds(spot * size, size), :] = y[:, lanes:]


def low_kernel(spots, *refs):
    *blocks, low_ref, whole = refs
    low_gate(zip(spots, blocks), low_ref, whole)


def first_kernel(stages, lane_bits, count, spots, *refs):
    _, *blocks = refs[: 1 + len(spots)]
    refs = refs[1 + len(spots) :]
    low_ref, weights, refs = refs[0], refs[1 : 1 + len(stages)], refs[1 + len(stages) :]
    outs, (whole, *halves) = refs[:count], refs[count:]
    low_gate(zip(spots, blocks), low_ref, whole)
    run_top_stage(stages[0], weights[0], lane_bits, whole, halves[:2])
    if straight(count):

        def store(top, part, start, value):
            for spot, out_ref in enumerate(outs):
                for bit in range(2):
                    rows = value[(2 * spot + bit) * 16 : (2 * spot + bit + 1) * 16]
                    out_ref[top, part, 2 * bit + start] = rows

        run_halves(stages[1:], weights[1:], lane_bits, halves[:2], halves[2:], store)
        return
    done = run_halves(stages[1:], weights[1:], lane_bits, halves[:2], halves[2:])
    tops, mids, _, inner, _ = outs[0].shape
    dests = partners_of(count)
    for top in range(tops):
        for dest, out_ref in zip(dests, outs):
            for mid in range(mids):
                start = pl.multiple_of((mid * count + dest) * inner, inner)
                for part in range(2):
                    out_ref[top, mid, part] = done[top][part, pl.ds(start, inner), :]


def second_kernel(stages, lane_bits, count, stays, *refs):
    blocks, weights, refs = refs[:count], refs[count : count + len(stages)], refs[count + len(stages) :]
    out_ref, one, two = refs
    core = lax.axis_index("qb")
    top = core if stays else 1 - core
    if straight(count):
        dim, stride, starts = stage_starts(stages[0], lane_bits, one.shape[1])

        def load(part, start):
            return jnp.concatenate([block_ref[top, part, start] for block_ref in blocks], axis=0)

        def store(part, start, value):
            one[part, pl.ds(start, dim, stride=stride), :] = value

        apply_stage(weights[0], starts, load, store)
        stages, weights, blocks = stages[1:], weights[1:], []
    for source, block_ref in zip(partners_of(count), blocks):
        _, mids, _, inner, _ = block_ref.shape
        for mid in range(mids):
            start = pl.multiple_of((mid * count + source) * inner, inner)
            for part in range(2):
                one[part, pl.ds(start, inner), :] = block_ref[top, mid, part]
    for index, (stage, weights_ref) in enumerate(zip(stages, weights)):
        run_stage(stage, weights_ref, lane_bits, one, out_ref if index == len(stages) - 1 else two)
        one, two = two, one


def third_kernel(stages, lane_bits, kept_ref, came_ref, *refs):
    weights, (out_ref, *halves, sems) = refs[: len(stages)], refs[len(stages) :]
    results = halves[4:]
    half = kept_ref.shape[1]
    run_top_stage(stages[0], weights[0], lane_bits, (kept_ref, came_ref), halves[:2])
    done = run_halves(stages[1:-1], weights[1:-1], lane_bits, halves[:2], halves[2:4])
    copies = []
    for t in range(2):
        dim, stride, _ = stage_starts(stages[-1], lane_bits, half)

        def store(part, start, value, t=t):
            results[t][pl.ds(2 * start + part, dim, stride=2 * stride), :] = value

        run_stage(stages[-1], weights[-1], lane_bits, done[t], store=store)
        size = 2 * half // PIECES
        for piece in range(PIECES):
            to = out_ref.at[pl.ds(t * 2 * half + piece * size, size)]
            copies.append(
                pltpu.make_async_copy(results[t].at[pl.ds(piece * size, size)], to, sems.at[t * PIECES + piece])
            )
            copies[-1].start()
    for copy in copies:
        copy.wait()


def call(kernel, name, out_shapes, in_specs, scratch, matmuls, *operands, limit=VMEM_LIMIT, out_spec=None, aliases=None):
    many = isinstance(out_shapes, tuple)
    vmem = out_spec or pl.BlockSpec(memory_space=pltpu.VMEM)
    return pl.pallas_call(
        kernel,
        out_shape=out_shapes,
        in_specs=in_specs,
        out_specs=(vmem,) * len(out_shapes) if many else vmem,
        scratch_shapes=scratch,
        input_output_aliases=aliases or {},
        compiler_params=pltpu.CompilerParams(vmem_limit_bytes=limit),
        cost_estimate=pl.CostEstimate(
            flops=int(matmuls * 3 * 2 * 256 * 256 * 1024), bytes_accessed=4 * 2**20, transcendentals=0
        ),
        name=name,
    )(*operands)


def per_device(state, gate_terms, path_bits):
    amps_local = state.shape[1]
    local_bits = amps_local.bit_length() - 1
    dim = gate_terms.shape[-1]
    gate_bits = dim.bit_length() - 1
    lanes, lane_bits = dim, gate_bits
    rows = amps_local // lanes
    qa = lax.axis_size("qa")
    qb = lax.axis_size("qb")
    low, sections = plan_gates(local_bits, gate_bits)
    sections = [join_windows(section, gate_bits) for section in sections]
    order = 2 * dim
    vmem = pl.BlockSpec(memory_space=pltpu.VMEM)
    hbm = pl.BlockSpec(memory_space=pltpu.HBM)
    shape = jax.ShapeDtypeStruct

    state = with_layout_constraint(state.reshape(2, rows, lanes), Layout(major_to_minor=(1, 0, 2)))
    state = state.swapaxes(0, 1).reshape(qa, 2 * rows // qa, lanes)
    blocks = call(
        split_kernel,
        "split_state",
        (shape((2 * rows // qa, lanes), F32),) * qa,
        [vmem],
        [],
        0,
        state,
    )

    blocks = list(blocks)
    blocks[1] = lax.dynamic_index_in_dim(state, partners_of(qa)[1], 0, keepdims=False)

    def exchange(blocks):
        came = [blocks[0]]
        for distance, piece in zip(distances_of(qa)[1:], blocks[1:]):
            came.append(lax.ppermute(piece, "qa", [(i, i ^ distance) for i in range(qa)]))
        return came

    blocks = exchange(blocks)
    low_w, *weights = call(
        functools.partial(prepare_kernel, low, sections, qa),
        "prepare_gates",
        (shape((3 * order, order), BF16),)
        + tuple(shape((2 * 2**bits, 6 * 2**bits), BF16) for section in sections for _, bits, _ in section),
        [pl.BlockSpec(memory_space=pltpu.SMEM), hbm],
        [
            pltpu.VMEM((gate_terms.shape[0], 2, dim, dim), F32),
            pltpu.VMEM((len(sections), 2, 2, 2 * dim, dim), F32),
            pltpu.SemaphoreType.DMA((gate_terms.shape[0],)),
        ],
        8,
        path_bits,
        gate_terms,
        limit=LARGE_VMEM,
    )
    counts = [len(section) for section in sections]
    weights = [weights[: counts[0]], weights[counts[0] : counts[0] + counts[1]], weights[counts[0] + counts[1] :]]
    inner = rows // (qa * qa)
    half = pltpu.VMEM((2, rows // 2, lanes), F32)
    early, late = list(range(qa - 3)), list(range(qa - 3, qa))
    planes = shape((2, rows, lanes), F32)
    begun = call(
        functools.partial(low_kernel, early),
        "low_gate_early",
        planes,
        [vmem] * (len(early) + 1),
        [],
        1,
        *[blocks[spot] for spot in early],
        low_w,
    )
    *blocks, _ = call(
        functools.partial(first_kernel, sections[0], lane_bits, qa, late),
        "first_section",
        (shape((qb, 2, 4, 16, lanes) if straight(qa) else (qb, qa // qb, 2, inner, lanes), F32),) * qa + (planes,),
        [vmem] * (2 + len(late) + counts[0]),
        [half] * 4,
        5,
        begun,
        *[blocks[spot] for spot in late],
        low_w,
        *weights[0],
        aliases={0: qa},
    )
    blocks = exchange(blocks)
    halves = []
    for stays in (False, True):
        halves.append(
            call(
                functools.partial(second_kernel, sections[1], lane_bits, qa, stays),
                "second_section_kept" if stays else "second_section_sent",
                shape((2, rows // qb, lanes), F32),
                [vmem] * (qa + counts[1]),
                [half] * 2,
                1.5,
                *blocks,
                *weights[1],
            )
        )
        if not stays:
            came = lax.ppermute(halves[0], "qb", [(i, 1 - i) for i in range(qb)])
    final = call(
        functools.partial(third_kernel, sections[2], lane_bits),
        "third_section",
        shape((2 * rows, lanes), F32),
        [vmem] * (2 + counts[2]),
        [half] * 4 + [pltpu.VMEM((rows, lanes), F32)] * 2 + [pltpu.SemaphoreType.DMA((2 * PIECES,))],
        4,
        halves[1],
        came,
        *weights[2],
        out_spec=hbm,
    )
    return final.reshape(rows, 2, lanes).swapaxes(0, 1).reshape(2, amps_local)


def solution(mesh):
    return jax.shard_map(
        per_device,
        mesh=mesh,
        in_specs=(P(None, ("paths", "qa", "qb")), P(), P("paths")),
        out_specs=P(None, ("paths", "qa", "qb")),
        check_vma=False,
    )
```

```python
import functools

import jax
import jax.numpy as jnp
from jax import lax
from jax.experimental import pallas as pl
from jax.experimental.layout import Layout, with_layout_constraint
from jax.experimental.pallas import tpu as pltpu
from jax.sharding import PartitionSpec as P

F32 = jnp.float32
BF16 = jnp.bfloat16
VMEM_LIMIT = 14 * 1024 * 1024
LARGE_VMEM = 48 * 1024 * 1024
PIECES = 4


def window_offsets(span, gate_bits):
    return [0, span, gate_bits, span - 1, gate_bits + 1, span - 2]


def plan_gates(local_bits, gate_bits):
    outer = window_offsets(local_bits - gate_bits, gate_bits)
    inner = window_offsets(local_bits - gate_bits - 1, gate_bits)
    low, sections = [], []
    for number, offsets in enumerate((outer, inner, outer)):
        section = []
        for index, offset in enumerate(offsets):
            gate = 6 * number + index
            if offset == 0:
                low.append(gate)
            elif section and section[-1][0] == offset:
                section[-1][1].append(gate)
            else:
                section.append((offset, [gate]))
        sections.append(section)
    return low, sections


def join_windows(section, gate_bits):
    stages = []
    for offset, gates in section:
        if stages:
            offsets = [o for o, _ in stages[-1]] + [offset]
            if max(offsets) - min(offsets) <= 1:
                stages[-1].append((offset, gates))
                continue
        stages.append([(offset, gates)])
    return [
        (min(o for o, _ in parts), gate_bits + (len(parts) > 1), parts)
        for parts in stages
    ]


def interleaved(stage):
    base, _, parts = stage
    return parts[0][0] != base


def split(x):
    high = x.astype(BF16)
    return high, (x - high.astype(F32)).astype(BF16)


def bf_dot(a, b):
    return jnp.dot(a, b, preferred_element_type=F32)


def pair_dot(a, b):
    (a_high, a_rest), (b_high, b_rest) = split(a), split(b)
    return bf_dot(a_high, b_rest) + bf_dot(a_rest, b_high) + bf_dot(a_high, b_high)


def block(real, imag):
    return jnp.concatenate(
        [jnp.concatenate([real, -imag], axis=1), jnp.concatenate([imag, real], axis=1)], axis=0
    )


def iotas(order):
    return [lax.broadcasted_iota(jnp.int32, (order, order), axis) for axis in (0, 1)]


def pick_columns(matrix, natural):
    row, column = iotas(matrix.shape[1])
    within = lax.rem(column, matrix.shape[1] // 2)
    picked = jnp.where(row == natural(within) + (column - within), 1.0, 0.0).astype(BF16)
    return bf_dot(matrix, picked).astype(BF16)


def pick_rows(matrix, natural):
    row, column = iotas(matrix.shape[0])
    within = lax.rem(row, matrix.shape[0] // 2)
    picked = jnp.where(column == natural(within) + (row - within), 1.0, 0.0).astype(BF16)
    return bf_dot(picked, matrix).astype(BF16)


def partner_at(spot, count):
    found = jnp.zeros_like(spot)
    for index, partner in enumerate(partners_of(count)):
        found = jnp.where(spot == index, partner, found)
    return found


def by_source(dim, count):
    size = dim // count
    return lambda x: partner_at(x // size, count) * size + lax.rem(x, size)


def by_core(dim):
    return lambda x: jnp.bitwise_xor(x, lax.axis_index("qb") * (dim // 2))


def away_first(dim):
    return lambda x: jnp.bitwise_xor(x, (1 - lax.axis_index("qb")) * (dim // 2))


def last_far(count):
    return max(spot for spot, distance in enumerate(distances_of(count)) if distance >= count // 2)


def piece_of(blocks, other, spot, half):
    if spot != last_far(len(blocks)):
        return blocks[spot].at[half]
    return other if half else blocks[spot]


def straight(count):
    return count == 8


def into_blocks(x):
    high, low = (x >> 2) & 3, x & 3
    return high * 64 + partner_at(x >> 5, 8) * 8 + low * 2 + ((x >> 4) & 1)


def from_blocks(x):
    return ((x >> 2) & 3) * 32 + partner_at(x >> 4, 8) * 4 + (x & 3)


def prepare_kernel(low, sections, count, bits_ref, gates_ref, low_ref, *refs):
    *targets, held, wides, sems = refs
    copies = {}
    for gate in [gate for section in sections for _, _, parts in section for _, gates in parts for gate in gates] + low:
        copies[gate] = pltpu.make_async_copy(gates_ref.at[gate, bits_ref[gate]], held.at[gate], sems.at[gate])
        copies[gate].start()
    dim = held.shape[-1]

    def product(gates):
        for gate in gates:
            copies.pop(gate).wait()
        real, imag = held[gates[0], 0], held[gates[0], 1]
        for gate in gates[1:]:
            column = pair_dot(block(held[gate, 0], held[gate, 1]), jnp.concatenate([real, imag], axis=0))
            real, imag = column[:dim], column[dim:]
        return real, imag

    def joined(wide, base, parts):
        wide[...] = jnp.zeros(wide.shape, F32)
        for index, (offset, gates) in enumerate(parts):
            real, imag = product(gates)
            for t in range(2):
                at = pl.ds(t * dim, dim) if offset == base else pl.ds(t, dim, stride=2)
                if index == 0:
                    wide[0, t, at, :] = real
                    wide[1, t, at, :] = imag
                else:
                    x = jnp.concatenate(
                        [jnp.concatenate([wide[p, c, at, :] for c in range(2)], axis=1) for p in range(2)], axis=0
                    )
                    y = pair_dot(block(real, imag), x)
                    for p in range(2):
                        for c in range(2):
                            wide[p, c, at, :] = y[p * dim : (p + 1) * dim, c * dim : (c + 1) * dim]
        return [jnp.concatenate([wide[p, 0], wide[p, 1]], axis=1) for p in range(2)]

    for number, section in enumerate(sections):
        weights, targets = targets[: len(section)], targets[len(section) :]
        for target, (base, _, parts) in zip(weights, section):
            high, rest = split(block(*(joined(wides.at[number], base, parts) if len(parts) > 1 else product(parts[0][1]))))
            if target is weights[0]:
                order = (by_source(dim, count), from_blocks if straight(count) else None, by_core(dim))[number]
                if order is not None:
                    high, rest = pick_columns(high, order), pick_columns(rest, order)
                if number == 0:
                    high, rest = pick_rows(high, away_first(dim)), pick_rows(rest, away_first(dim))
            elif number == 0 and straight(count) and target is weights[-1]:
                high, rest = pick_rows(high, into_blocks), pick_rows(rest, into_blocks)
            target[...] = jnp.concatenate([high, rest, high], axis=1)
    real, imag = product(low)
    high, rest = split(block(real.T, -imag.T))
    low_ref[...] = jnp.concatenate([high, rest, high], axis=0)


def distances_of(count):
    half = count // 2
    far, near = list(range(count - 1, half - 1, -1)), list(range(half - 1, 0, -1))
    order = [0]
    while far or near:
        order += far[:2] + near[:2]
        far, near = far[2:], near[2:]
    return order


def partners_of(count):
    me = lax.axis_index("qa")
    return [jnp.bitwise_xor(me, distance) for distance in distances_of(count)]


def split_kernel(x_ref, *outs):
    for dest, out_ref in zip(partners_of(len(outs)), outs):
        out_ref[...] = x_ref[dest]


def apply_stage(weights_ref, starts, load, store):
    dim = weights_ref.shape[0] // 2
    for pair in range(0, len(starts), 2):
        group = starts[pair : pair + 2]
        x = jnp.concatenate(
            [jnp.concatenate([load(part, start) for start in group], axis=1) for part in range(2)], axis=0
        )
        high, rest = split(x)
        y = bf_dot(weights_ref[...], jnp.concatenate([rest, high, high], axis=0))
        lanes = y.shape[1] // len(group)
        for part in range(2):
            for place, start in enumerate(group):
                store(part, start, y[part * dim : (part + 1) * dim, place * lanes : (place + 1) * lanes])


def stage_starts(stage, lane_bits, rows):
    base, bits, _ = stage
    dim, stride = 2**bits, 2 ** (base - lane_bits)
    return dim, stride, [h * dim * stride + l for h in range(rows // (dim * stride)) for l in range(stride)]


def run_stage(stage, weights_ref, lane_bits, source, target=None, store=None):
    dim, stride, starts = stage_starts(stage, lane_bits, source.shape[1])

    def load(part, start):
        if not interleaved(stage):
            return source[part, pl.ds(start, dim, stride=stride), :]
        half = dim // 2
        return jnp.concatenate(
            [source[part, pl.ds(start + t * stride, half, stride=2 * stride), :] for t in range(2)], axis=0
        )

    def plain(part, start, value):
        target[part, pl.ds(start, dim, stride=stride), :] = value

    apply_stage(weights_ref, starts, load, store or plain)


def run_top_stage(stage, weights_ref, lane_bits, source, halves):
    rows = 2 * halves[0].shape[1]
    dim, stride, starts = stage_starts(stage, lane_bits, rows)

    def store(part, start, value):
        for t in range(2):
            halves[t][part, pl.ds(start, dim // 2, stride=stride), :] = value[t * dim // 2 : (t + 1) * dim // 2]

    def load(part, start):
        if not isinstance(source, tuple):
            return source[part, pl.ds(start, dim, stride=stride), :]
        return jnp.concatenate([half[part, pl.ds(start, dim // 2, stride=stride), :] for half in source], axis=0)

    apply_stage(weights_ref, starts, load, store)


def run_halves(stages, weights, lane_bits, halves, spares, last_store=None):
    for index, (stage, weights_ref) in enumerate(zip(stages, weights)):
        for t in range(2):
            store = None
            if last_store is not None and index == len(stages) - 1:
                store = functools.partial(last_store, t)
            run_stage(stage, weights_ref, lane_bits, halves[t], spares[t], store)
        halves, spares = spares, halves
    return halves


def low_gate(blocks, low_ref, whole):
    lanes = whole.shape[2]
    for spot, block_ref in blocks:
        size = block_ref.shape[0] // 2
        real = block_ref[pl.ds(0, size, stride=2), :]
        imag = block_ref[pl.ds(1, size, stride=2), :]
        high, rest = split(jnp.concatenate([real, imag], axis=1))
        y = bf_dot(jnp.concatenate([rest, high, high], axis=1), low_ref[...])
        whole[0, pl.ds(spot * size, size), :] = y[:, :lanes]
        whole[1, pl.ds(spot * size, size), :] = y[:, lanes:]


def low_kernel(spots, *refs):
    *blocks, low_ref, whole = refs
    low_gate(zip(spots, blocks), low_ref, whole)


def first_kernel(stages, lane_bits, count, spots, *refs):
    _, *blocks = refs[: 1 + len(spots)]
    refs = refs[1 + len(spots) :]
    low_ref, weights, refs = refs[0], refs[1 : 1 + len(stages)], refs[1 + len(stages) :]
    outs, (other, whole, *halves) = refs[:count], refs[count:]
    low_gate(zip(spots, blocks), low_ref, whole)
    run_top_stage(stages[0], weights[0], lane_bits, whole, halves[:2])
    if straight(count):

        def store(top, part, start, value):
            for spot in range(count):
                for bit in range(2):
                    rows = value[(2 * spot + bit) * 16 : (2 * spot + bit + 1) * 16]
                    piece_of(outs, other, spot, top)[part, 2 * bit + start] = rows

        run_halves(stages[1:], weights[1:], lane_bits, halves[:2], halves[2:], store)
        return
    done = run_halves(stages[1:], weights[1:], lane_bits, halves[:2], halves[2:])
    tops, mids, _, inner, _ = outs[0].shape
    dests = partners_of(count)
    for top in range(tops):
        for spot, dest in enumerate(dests):
            piece = piece_of(outs, other, spot, top)
            for mid in range(mids):
                start = pl.multiple_of((mid * count + dest) * inner, inner)
                for part in range(2):
                    piece[mid, part] = done[top][part, pl.ds(start, inner), :]


def second_kernel(stages, lane_bits, count, stays, *refs):
    blocks, weights, refs = refs[:count], refs[count : count + len(stages)], refs[count + len(stages) :]
    out_ref, one, two = refs
    pieces = [piece_of(blocks, blocks[last_far(count)], spot, int(stays)) for spot in range(count)]
    if straight(count):
        dim, stride, starts = stage_starts(stages[0], lane_bits, one.shape[1])

        def load(part, start):
            return jnp.concatenate([piece[part, start] for piece in pieces], axis=0)

        def store(part, start, value):
            one[part, pl.ds(start, dim, stride=stride), :] = value

        apply_stage(weights[0], starts, load, store)
        stages, weights, pieces = stages[1:], weights[1:], []
    for source, piece in zip(partners_of(count), pieces):
        mids, _, inner, _ = piece.shape
        for mid in range(mids):
            start = pl.multiple_of((mid * count + source) * inner, inner)
            for part in range(2):
                one[part, pl.ds(start, inner), :] = piece[mid, part]
    for index, (stage, weights_ref) in enumerate(zip(stages, weights)):
        run_stage(stage, weights_ref, lane_bits, one, out_ref if index == len(stages) - 1 else two)
        one, two = two, one


def third_kernel(stages, lane_bits, kept_ref, came_ref, *refs):
    weights, (out_ref, *halves, sems) = refs[: len(stages)], refs[len(stages) :]
    results = halves[4:]
    half = kept_ref.shape[1]
    run_top_stage(stages[0], weights[0], lane_bits, (kept_ref, came_ref), halves[:2])
    done = run_halves(stages[1:-1], weights[1:-1], lane_bits, halves[:2], halves[2:4])
    copies = []
    for t in range(2):
        dim, stride, _ = stage_starts(stages[-1], lane_bits, half)

        def store(part, start, value, t=t):
            results[t][pl.ds(2 * start + part, dim, stride=2 * stride), :] = value

        run_stage(stages[-1], weights[-1], lane_bits, done[t], store=store)
        size = 2 * half // PIECES
        for piece in range(PIECES):
            to = out_ref.at[pl.ds(t * 2 * half + piece * size, size)]
            copies.append(
                pltpu.make_async_copy(results[t].at[pl.ds(piece * size, size)], to, sems.at[t * PIECES + piece])
            )
            copies[-1].start()
    for copy in copies:
        copy.wait()


def call(kernel, name, out_shapes, in_specs, scratch, matmuls, *operands, limit=VMEM_LIMIT, out_spec=None, aliases=None):
    many = isinstance(out_shapes, tuple)
    vmem = out_spec or pl.BlockSpec(memory_space=pltpu.VMEM)
    return pl.pallas_call(
        kernel,
        out_shape=out_shapes,
        in_specs=in_specs,
        out_specs=(vmem,) * len(out_shapes) if many else vmem,
        scratch_shapes=scratch,
        input_output_aliases=aliases or {},
        compiler_params=pltpu.CompilerParams(vmem_limit_bytes=limit),
        cost_estimate=pl.CostEstimate(
            flops=int(matmuls * 3 * 2 * 256 * 256 * 1024), bytes_accessed=4 * 2**20, transcendentals=0
        ),
        name=name,
    )(*operands)


def per_device(state, gate_terms, path_bits):
    amps_local = state.shape[1]
    local_bits = amps_local.bit_length() - 1
    dim = gate_terms.shape[-1]
    gate_bits = dim.bit_length() - 1
    lanes, lane_bits = dim, gate_bits
    rows = amps_local // lanes
    qa = lax.axis_size("qa")
    qb = lax.axis_size("qb")
    low, sections = plan_gates(local_bits, gate_bits)
    sections = [join_windows(section, gate_bits) for section in sections]
    order = 2 * dim
    vmem = pl.BlockSpec(memory_space=pltpu.VMEM)
    hbm = pl.BlockSpec(memory_space=pltpu.HBM)
    shape = jax.ShapeDtypeStruct

    state = with_layout_constraint(state.reshape(2, rows, lanes), Layout(major_to_minor=(1, 0, 2)))
    state = state.swapaxes(0, 1).reshape(qa, 2 * rows // qa, lanes)
    blocks = call(
        split_kernel,
        "split_state",
        (shape((2 * rows // qa, lanes), F32),) * qa,
        [vmem],
        [],
        0,
        state,
    )

    blocks = list(blocks)
    blocks[1] = lax.dynamic_index_in_dim(state, partners_of(qa)[1], 0, keepdims=False)

    def exchange(blocks):
        came = [blocks[0]]
        for distance, piece in zip(distances_of(qa)[1:], blocks[1:]):
            came.append(lax.ppermute(piece, "qa", [(i, i ^ distance) for i in range(qa)]))
        return came

    blocks = exchange(blocks)
    low_w, *weights = call(
        functools.partial(prepare_kernel, low, sections, qa),
        "prepare_gates",
        (shape((3 * order, order), BF16),)
        + tuple(shape((2 * 2**bits, 6 * 2**bits), BF16) for section in sections for _, bits, _ in section),
        [pl.BlockSpec(memory_space=pltpu.SMEM), hbm],
        [
            pltpu.VMEM((gate_terms.shape[0], 2, dim, dim), F32),
            pltpu.VMEM((len(sections), 2, 2, 2 * dim, dim), F32),
            pltpu.SemaphoreType.DMA((gate_terms.shape[0],)),
        ],
        8,
        path_bits,
        gate_terms,
        limit=LARGE_VMEM,
    )
    counts = [len(section) for section in sections]
    weights = [weights[: counts[0]], weights[counts[0] : counts[0] + counts[1]], weights[counts[0] + counts[1] :]]
    inner = rows // (qa * qa)
    half = pltpu.VMEM((2, rows // 2, lanes), F32)
    early, late = list(range(qa - 3)), list(range(qa - 3, qa))
    planes = shape((2, rows, lanes), F32)
    begun = call(
        functools.partial(low_kernel, early),
        "low_gate_early",
        planes,
        [vmem] * (len(early) + 1),
        [],
        1,
        *[blocks[spot] for spot in early],
        low_w,
    )
    view = (2, 4, 16, lanes) if straight(qa) else (qa // qb, 2, inner, lanes)
    views = [shape(view if spot == last_far(qa) else (qb,) + view, F32) for spot in range(qa)]
    *blocks, other, _ = call(
        functools.partial(first_kernel, sections[0], lane_bits, qa, late),
        "first_section",
        (*views, shape(view, F32), planes),
        [vmem] * (2 + len(late) + counts[0]),
        [half] * 4,
        5,
        begun,
        *[blocks[spot] for spot in late],
        low_w,
        *weights[0],
        aliases={0: qa + 1},
    )
    blocks = exchange(blocks)
    distance = distances_of(qa)[last_far(qa)]
    other = lax.ppermute(other, "qa", [(i, i ^ distance) for i in range(qa)])
    halves = []
    for stays in (False, True):
        halves.append(
            call(
                functools.partial(second_kernel, sections[1], lane_bits, qa, stays),
                "second_section_kept" if stays else "second_section_sent",
                shape((2, rows // qb, lanes), F32),
                [vmem] * (qa + counts[1]),
                [half] * 2,
                100 if stays else 0.001,
                *[other if stays and spot == last_far(qa) else block for spot, block in enumerate(blocks)],
                *weights[1],
            )
        )
        if not stays:
            came = lax.ppermute(halves[0], "qb", [(i, 1 - i) for i in range(qb)])
    final = call(
        functools.partial(third_kernel, sections[2], lane_bits),
        "third_section",
        shape((2 * rows, lanes), F32),
        [vmem] * (2 + counts[2]),
        [half] * 4 + [pltpu.VMEM((rows, lanes), F32)] * 2 + [pltpu.SemaphoreType.DMA((2 * PIECES,))],
        4,
        halves[1],
        came,
        *weights[2],
        out_spec=hbm,
    )
    return final.reshape(rows, 2, lanes).swapaxes(0, 1).reshape(2, amps_local)


def solution(mesh):
    return jax.shard_map(
        per_device,
        mesh=mesh,
        in_specs=(P(None, ("paths", "qa", "qb")), P(), P("paths")),
        out_specs=P(None, ("paths", "qa", "qb")),
        check_vma=False,
    )
```

```python
import functools

import jax
import jax.numpy as jnp
from jax import lax
from jax.experimental import pallas as pl
from jax.experimental.layout import Layout, with_layout_constraint
from jax.experimental.pallas import tpu as pltpu
from jax.sharding import PartitionSpec as P

F32 = jnp.float32
BF16 = jnp.bfloat16
VMEM_LIMIT = 14 * 1024 * 1024
LARGE_VMEM = 48 * 1024 * 1024
PIECES = 4


def window_offsets(span, gate_bits):
    return [0, span, gate_bits, span - 1, gate_bits + 1, span - 2]


def plan_gates(local_bits, gate_bits):
    outer = window_offsets(local_bits - gate_bits, gate_bits)
    inner = window_offsets(local_bits - gate_bits - 1, gate_bits)
    low, sections = [], []
    for number, offsets in enumerate((outer, inner, outer)):
        section = []
        for index, offset in enumerate(offsets):
            gate = 6 * number + index
            if offset == 0:
                low.append(gate)
            elif section and section[-1][0] == offset:
                section[-1][1].append(gate)
            else:
                section.append((offset, [gate]))
        sections.append(section)
    return low, sections


def join_windows(section, gate_bits):
    stages = []
    for offset, gates in section:
        if stages:
            offsets = [o for o, _ in stages[-1]] + [offset]
            if max(offsets) - min(offsets) <= 1:
                stages[-1].append((offset, gates))
                continue
        stages.append([(offset, gates)])
    return [
        (min(o for o, _ in parts), gate_bits + (len(parts) > 1), parts)
        for parts in stages
    ]


def interleaved(stage):
    base, _, parts = stage
    return parts[0][0] != base


def split(x):
    high = x.astype(BF16)
    return high, (x - high.astype(F32)).astype(BF16)


def bf_dot(a, b):
    return jnp.dot(a, b, preferred_element_type=F32)


def pair_dot(a, b):
    (a_high, a_rest), (b_high, b_rest) = split(a), split(b)
    return bf_dot(a_high, b_rest) + bf_dot(a_rest, b_high) + bf_dot(a_high, b_high)


def block(real, imag):
    return jnp.concatenate(
        [jnp.concatenate([real, -imag], axis=1), jnp.concatenate([imag, real], axis=1)], axis=0
    )


def relative(matrix, number, count):
    order = matrix.shape[1]
    dim = order // 2
    column = lax.broadcasted_iota(jnp.int32, (order, order), 1)
    row = lax.broadcasted_iota(jnp.int32, (order, order), 0)
    within = lax.rem(column, dim)
    if number == 0:
        size = dim // count
        spot, source = within // size, jnp.zeros_like(column)
        for index, partner in enumerate(partners_of(count)):
            source = jnp.where(spot == index, partner, source)
        natural = source * size + lax.rem(within, size)
    else:
        natural = jnp.bitwise_xor(within, lax.axis_index("qb") * (dim // 2))
    picked = jnp.where(row == natural + (column - within), 1.0, 0.0).astype(BF16)
    return bf_dot(matrix, picked).astype(BF16)


def prepare_kernel(low, sections, count, bits_ref, gates_ref, low_ref, *refs):
    *targets, held, wides, sems = refs
    copies = {}
    for gate in [gate for section in sections for _, _, parts in section for _, gates in parts for gate in gates] + low:
        copies[gate] = pltpu.make_async_copy(gates_ref.at[gate, bits_ref[gate]], held.at[gate], sems.at[gate])
        copies[gate].start()
    dim = held.shape[-1]

    def product(gates):
        for gate in gates:
            copies.pop(gate).wait()
        real, imag = held[gates[0], 0], held[gates[0], 1]
        for gate in gates[1:]:
            column = pair_dot(block(held[gate, 0], held[gate, 1]), jnp.concatenate([real, imag], axis=0))
            real, imag = column[:dim], column[dim:]
        return real, imag

    def joined(wide, base, parts):
        wide[...] = jnp.zeros(wide.shape, F32)
        for index, (offset, gates) in enumerate(parts):
            real, imag = product(gates)
            for t in range(2):
                at = pl.ds(t * dim, dim) if offset == base else pl.ds(t, dim, stride=2)
                if index == 0:
                    wide[0, t, at, :] = real
                    wide[1, t, at, :] = imag
                else:
                    x = jnp.concatenate(
                        [jnp.concatenate([wide[p, c, at, :] for c in range(2)], axis=1) for p in range(2)], axis=0
                    )
                    y = pair_dot(block(real, imag), x)
                    for p in range(2):
                        for c in range(2):
                            wide[p, c, at, :] = y[p * dim : (p + 1) * dim, c * dim : (c + 1) * dim]
        return [jnp.concatenate([wide[p, 0], wide[p, 1]], axis=1) for p in range(2)]

    for number, section in enumerate(sections):
        weights, targets = targets[: len(section)], targets[len(section) :]
        for target, (base, _, parts) in zip(weights, section):
            high, rest = split(block(*(joined(wides.at[number], base, parts) if len(parts) > 1 else product(parts[0][1]))))
            if number != 1 and target is weights[0]:
                high, rest = relative(high, number, count), relative(rest, number, count)
            target[...] = jnp.concatenate([high, rest, high], axis=1)
    real, imag = product(low)
    high, rest = split(block(real.T, -imag.T))
    low_ref[...] = jnp.concatenate([high, rest, high], axis=0)


def distances_of(count):
    half = count // 2
    far, near = list(range(count - 1, half - 1, -1)), list(range(half - 1, 0, -1))
    order = [0]
    while far or near:
        order += far[:2] + near[:2]
        far, near = far[2:], near[2:]
    return order


def partners_of(count):
    me = lax.axis_index("qa")
    return [jnp.bitwise_xor(me, distance) for distance in distances_of(count)]


def split_kernel(x_ref, *outs):
    me, _, *dests = partners_of(len(outs) + 1)
    for dest, out_ref in zip([me, *dests], outs):
        out_ref[...] = x_ref[dest]


def apply_stage(weights_ref, starts, load, store):
    dim = weights_ref.shape[0] // 2
    for pair in range(0, len(starts), 2):
        group = starts[pair : pair + 2]
        x = jnp.concatenate(
            [jnp.concatenate([load(part, start) for start in group], axis=1) for part in range(2)], axis=0
        )
        high, rest = split(x)
        y = bf_dot(weights_ref[...], jnp.concatenate([rest, high, high], axis=0))
        lanes = y.shape[1] // len(group)
        for part in range(2):
            for place, start in enumerate(group):
                store(part, start, y[part * dim : (part + 1) * dim, place * lanes : (place + 1) * lanes])


def stage_starts(stage, lane_bits, rows):
    base, bits, _ = stage
    dim, stride = 2**bits, 2 ** (base - lane_bits)
    return dim, stride, [h * dim * stride + l for h in range(rows // (dim * stride)) for l in range(stride)]


def run_stage(stage, weights_ref, lane_bits, source, target=None, store=None):
    dim, stride, starts = stage_starts(stage, lane_bits, source.shape[1])

    def load(part, start):
        if not interleaved(stage):
            return source[part, pl.ds(start, dim, stride=stride), :]
        half = dim // 2
        return jnp.concatenate(
            [source[part, pl.ds(start + t * stride, half, stride=2 * stride), :] for t in range(2)], axis=0
        )

    def plain(part, start, value):
        target[part, pl.ds(start, dim, stride=stride), :] = value

    apply_stage(weights_ref, starts, load, store or plain)


def run_top_stage(stage, weights_ref, lane_bits, source, halves):
    rows = 2 * halves[0].shape[1]
    dim, stride, starts = stage_starts(stage, lane_bits, rows)

    def store(part, start, value):
        for t in range(2):
            halves[t][part, pl.ds(start, dim // 2, stride=stride), :] = value[t * dim // 2 : (t + 1) * dim // 2]

    def load(part, start):
        if not isinstance(source, tuple):
            return source[part, pl.ds(start, dim, stride=stride), :]
        return jnp.concatenate([half[part, pl.ds(start, dim // 2, stride=stride), :] for half in source], axis=0)

    apply_stage(weights_ref, starts, load, store)


def run_halves(stages, weights, lane_bits, halves, spares, last_store=None):
    for index, (stage, weights_ref) in enumerate(zip(stages, weights)):
        for t in range(2):
            store = None
            if last_store is not None and index == len(stages) - 1:
                store = functools.partial(last_store, t)
            run_stage(stage, weights_ref, lane_bits, halves[t], spares[t], store)
        halves, spares = spares, halves
    return halves


def low_gate(blocks, low_ref, whole):
    lanes = whole.shape[2]
    for spot, block_ref in blocks:
        size = block_ref.shape[0] // 2
        real = block_ref[pl.ds(0, size, stride=2), :]
        imag = block_ref[pl.ds(1, size, stride=2), :]
        high, rest = split(jnp.concatenate([real, imag], axis=1))
        y = bf_dot(jnp.concatenate([rest, high, high], axis=1), low_ref[...])
        whole[0, pl.ds(spot * size, size), :] = y[:, :lanes]
        whole[1, pl.ds(spot * size, size), :] = y[:, lanes:]


def low_kernel(spots, *refs):
    *blocks, low_ref, whole = refs
    low_gate(zip(spots, blocks), low_ref, whole)


def first_kernel(stages, lane_bits, count, spots, *refs):
    _, *blocks = refs[: 1 + len(spots)]
    refs = refs[1 + len(spots) :]
    low_ref, weights, refs = refs[0], refs[1 : 1 + len(stages)], refs[1 + len(stages) :]
    outs, (whole, *halves) = refs[:count], refs[count:]
    low_gate(zip(spots, blocks), low_ref, whole)
    run_top_stage(stages[0], weights[0], lane_bits, whole, halves[:2])
    done = run_halves(stages[1:], weights[1:], lane_bits, halves[:2], halves[2:])
    tops, mids, _, inner, _ = outs[0].shape
    dests = partners_of(count)
    for top in range(tops):
        for dest, out_ref in zip(dests, outs):
            for mid in range(mids):
                start = pl.multiple_of((mid * count + dest) * inner, inner)
                for part in range(2):
                    out_ref[top, mid, part] = done[top][part, pl.ds(start, inner), :]


def second_kernel(stages, lane_bits, count, stays, *refs):
    blocks, weights, refs = refs[:count], refs[count : count + len(stages)], refs[count + len(stages) :]
    out_ref, one, two = refs
    core = lax.axis_index("qb")
    top = core if stays else 1 - core
    for source, block_ref in zip(partners_of(count), blocks):
        _, mids, _, inner, _ = block_ref.shape
        for mid in range(mids):
            start = pl.multiple_of((mid * count + source) * inner, inner)
            for part in range(2):
                one[part, pl.ds(start, inner), :] = block_ref[top, mid, part]
    for index, (stage, weights_ref) in enumerate(zip(stages, weights)):
        run_stage(stage, weights_ref, lane_bits, one, out_ref if index == len(stages) - 1 else two)
        one, two = two, one


def third_kernel(stages, lane_bits, kept_ref, came_ref, *refs):
    weights, (out_ref, *halves, sems) = refs[: len(stages)], refs[len(stages) :]
    results = halves[4:]
    half = kept_ref.shape[1]
    run_top_stage(stages[0], weights[0], lane_bits, (kept_ref, came_ref), halves[:2])
    done = run_halves(stages[1:-1], weights[1:-1], lane_bits, halves[:2], halves[2:4])
    copies = []
    for t in range(2):
        dim, stride, _ = stage_starts(stages[-1], lane_bits, half)

        def store(part, start, value, t=t):
            results[t][pl.ds(2 * start + part, dim, stride=2 * stride), :] = value

        run_stage(stages[-1], weights[-1], lane_bits, done[t], store=store)
        size = 2 * half // PIECES
        for piece in range(PIECES):
            to = out_ref.at[pl.ds(t * 2 * half + piece * size, size)]
            copies.append(
                pltpu.make_async_copy(results[t].at[pl.ds(piece * size, size)], to, sems.at[t * PIECES + piece])
            )
            copies[-1].start()
    for copy in copies:
        copy.wait()


def call(kernel, name, out_shapes, in_specs, scratch, matmuls, *operands, limit=VMEM_LIMIT, out_spec=None, aliases=None):
    many = isinstance(out_shapes, tuple)
    vmem = out_spec or pl.BlockSpec(memory_space=pltpu.VMEM)
    return pl.pallas_call(
        kernel,
        out_shape=out_shapes,
        in_specs=in_specs,
        out_specs=(vmem,) * len(out_shapes) if many else vmem,
        scratch_shapes=scratch,
        input_output_aliases=aliases or {},
        compiler_params=pltpu.CompilerParams(vmem_limit_bytes=limit),
        cost_estimate=pl.CostEstimate(
            flops=int(matmuls * 3 * 2 * 256 * 256 * 1024), bytes_accessed=4 * 2**20, transcendentals=0
        ),
        name=name,
    )(*operands)


def per_device(state, gate_terms, path_bits):
    amps_local = state.shape[1]
    local_bits = amps_local.bit_length() - 1
    dim = gate_terms.shape[-1]
    gate_bits = dim.bit_length() - 1
    lanes, lane_bits = dim, gate_bits
    rows = amps_local // lanes
    qa = lax.axis_size("qa")
    qb = lax.axis_size("qb")
    low, sections = plan_gates(local_bits, gate_bits)
    sections = [join_windows(section, gate_bits) for section in sections]
    order = 2 * dim
    vmem = pl.BlockSpec(memory_space=pltpu.VMEM)
    hbm = pl.BlockSpec(memory_space=pltpu.HBM)
    shape = jax.ShapeDtypeStruct

    state = with_layout_constraint(state.reshape(2, rows, lanes), Layout(major_to_minor=(1, 0, 2)))
    state = state.swapaxes(0, 1).reshape(qa, 2 * rows // qa, lanes)
    blocks = call(
        split_kernel,
        "split_state",
        (shape((2 * rows // qa, lanes), F32),) * (qa - 1),
        [vmem],
        [],
        0,
        state,
    )

    first = lax.dynamic_index_in_dim(state, partners_of(qa)[1], 0, keepdims=False)
    blocks = [blocks[0], first, *blocks[1:]]

    def exchange(blocks):
        came = [blocks[0]]
        for distance, piece in zip(distances_of(qa)[1:], blocks[1:]):
            came.append(lax.ppermute(piece, "qa", [(i, i ^ distance) for i in range(qa)]))
        return came

    blocks = exchange(blocks)
    low_w, *weights = call(
        functools.partial(prepare_kernel, low, sections, qa),
        "prepare_gates",
        (shape((3 * order, order), BF16),)
        + tuple(shape((2 * 2**bits, 6 * 2**bits), BF16) for section in sections for _, bits, _ in section),
        [pl.BlockSpec(memory_space=pltpu.SMEM), hbm],
        [
            pltpu.VMEM((gate_terms.shape[0], 2, dim, dim), F32),
            pltpu.VMEM((len(sections), 2, 2, 2 * dim, dim), F32),
            pltpu.SemaphoreType.DMA((gate_terms.shape[0],)),
        ],
        8,
        path_bits,
        gate_terms,
        limit=LARGE_VMEM,
    )
    counts = [len(section) for section in sections]
    weights = [weights[: counts[0]], weights[counts[0] : counts[0] + counts[1]], weights[counts[0] + counts[1] :]]
    inner = rows // (qa * qa)
    half = pltpu.VMEM((2, rows // 2, lanes), F32)
    early, late = list(range(qa - 3)), list(range(qa - 3, qa))
    planes = shape((2, rows, lanes), F32)
    begun = call(
        functools.partial(low_kernel, early),
        "low_gate_early",
        planes,
        [vmem] * (len(early) + 1),
        [],
        1,
        *[blocks[spot] for spot in early],
        low_w,
    )
    *blocks, _ = call(
        functools.partial(first_kernel, sections[0], lane_bits, qa, late),
        "first_section",
        (shape((qb, qa // qb, 2, inner, lanes), F32),) * qa + (planes,),
        [vmem] * (2 + len(late) + counts[0]),
        [half] * 4,
        5,
        begun,
        *[blocks[spot] for spot in late],
        low_w,
        *weights[0],
        aliases={0: qa},
    )
    blocks = exchange(blocks)
    halves = []
    for stays in (False, True):
        halves.append(
            call(
                functools.partial(second_kernel, sections[1], lane_bits, qa, stays),
                "second_section_kept" if stays else "second_section_sent",
                shape((2, rows // qb, lanes), F32),
                [vmem] * (qa + counts[1]),
                [half] * 2,
                1.5,
                *blocks,
                *weights[1],
            )
        )
        if not stays:
            came = lax.ppermute(halves[0], "qb", [(i, 1 - i) for i in range(qb)])
    final = call(
        functools.partial(third_kernel, sections[2], lane_bits),
        "third_section",
        shape((2 * rows, lanes), F32),
        [vmem] * (2 + counts[2]),
        [half] * 4 + [pltpu.VMEM((rows, lanes), F32)] * 2 + [pltpu.SemaphoreType.DMA((2 * PIECES,))],
        4,
        halves[1],
        came,
        *weights[2],
        out_spec=hbm,
    )
    return final.reshape(rows, 2, lanes).swapaxes(0, 1).reshape(2, amps_local)


def solution(mesh):
    return jax.shard_map(
        per_device,
        mesh=mesh,
        in_specs=(P(None, ("paths", "qa", "qb")), P(), P("paths")),
        out_specs=P(None, ("paths", "qa", "qb")),
        check_vma=False,
    )
```

```python
import functools

import jax
import jax.numpy as jnp
from jax import lax
from jax.experimental import pallas as pl
from jax.experimental.layout import Layout, with_layout_constraint
from jax.experimental.pallas import tpu as pltpu
from jax.sharding import PartitionSpec as P

F32 = jnp.float32
BF16 = jnp.bfloat16
VMEM_LIMIT = 14 * 1024 * 1024
LARGE_VMEM = 48 * 1024 * 1024
PIECES = 4


def window_offsets(span, gate_bits):
    return [0, span, gate_bits, span - 1, gate_bits + 1, span - 2]


def plan_gates(local_bits, gate_bits):
    outer = window_offsets(local_bits - gate_bits, gate_bits)
    inner = window_offsets(local_bits - gate_bits - 1, gate_bits)
    low, sections = [], []
    for number, offsets in enumerate((outer, inner, outer)):
        section = []
        for index, offset in enumerate(offsets):
            gate = 6 * number + index
            if offset == 0:
                low.append(gate)
            elif section and section[-1][0] == offset:
                section[-1][1].append(gate)
            else:
                section.append((offset, [gate]))
        sections.append(section)
    return low, sections


def join_windows(section, gate_bits):
    stages = []
    for offset, gates in section:
        if stages:
            offsets = [o for o, _ in stages[-1]] + [offset]
            if max(offsets) - min(offsets) <= 1:
                stages[-1].append((offset, gates))
                continue
        stages.append([(offset, gates)])
    return [
        (min(o for o, _ in parts), gate_bits + (len(parts) > 1), parts)
        for parts in stages
    ]


def interleaved(stage):
    base, _, parts = stage
    return parts[0][0] != base


def split(x):
    high = x.astype(BF16)
    return high, (x - high.astype(F32)).astype(BF16)


def bf_dot(a, b):
    return jnp.dot(a, b, preferred_element_type=F32)


def pair_dot(a, b):
    (a_high, a_rest), (b_high, b_rest) = split(a), split(b)
    return bf_dot(a_high, b_rest) + bf_dot(a_rest, b_high) + bf_dot(a_high, b_high)


def block(real, imag):
    return jnp.concatenate(
        [jnp.concatenate([real, -imag], axis=1), jnp.concatenate([imag, real], axis=1)], axis=0
    )


def iotas(order):
    return [lax.broadcasted_iota(jnp.int32, (order, order), axis) for axis in (0, 1)]


def pick_columns(matrix, natural):
    row, column = iotas(matrix.shape[1])
    within = lax.rem(column, matrix.shape[1] // 2)
    picked = jnp.where(row == natural(within) + (column - within), 1.0, 0.0).astype(BF16)
    return bf_dot(matrix, picked).astype(BF16)


def pick_rows(matrix, natural):
    row, column = iotas(matrix.shape[0])
    within = lax.rem(row, matrix.shape[0] // 2)
    picked = jnp.where(column == natural(within) + (row - within), 1.0, 0.0).astype(BF16)
    return bf_dot(picked, matrix).astype(BF16)


def partner_at(spot, count):
    found = jnp.zeros_like(spot)
    for index, partner in enumerate(partners_of(count)):
        found = jnp.where(spot == index, partner, found)
    return found


def in_groups(matrix):
    size = matrix.shape[0] // 4
    return jnp.concatenate([matrix[at * size : (at + 1) * size] for at in (0, 2, 1, 3)], axis=0)


def by_source(dim, count):
    size = dim // count
    return lambda x: partner_at(x // size, count) * size + lax.rem(x, size)


def by_core(dim):
    return lambda x: jnp.bitwise_xor(x, lax.axis_index("qb") * (dim // 2))


def straight(count):
    return count == 8


def into_blocks(x):
    high, low = (x >> 2) & 3, x & 3
    return high * 64 + partner_at(x >> 5, 8) * 8 + low * 2 + ((x >> 4) & 1)


def from_blocks(x):
    return ((x >> 2) & 3) * 32 + partner_at(x >> 4, 8) * 4 + (x & 3)


def prepare_kernel(low, sections, count, bits_ref, gates_ref, low_ref, *refs):
    *targets, held, wides, sems = refs
    copies = {}
    for gate in [gate for section in sections for _, _, parts in section for _, gates in parts for gate in gates] + low:
        copies[gate] = pltpu.make_async_copy(gates_ref.at[gate, bits_ref[gate]], held.at[gate], sems.at[gate])
        copies[gate].start()
    dim = held.shape[-1]

    def product(gates):
        for gate in gates:
            copies.pop(gate).wait()
        real, imag = held[gates[0], 0], held[gates[0], 1]
        for gate in gates[1:]:
            column = pair_dot(block(held[gate, 0], held[gate, 1]), jnp.concatenate([real, imag], axis=0))
            real, imag = column[:dim], column[dim:]
        return real, imag

    def joined(wide, base, parts):
        wide[...] = jnp.zeros(wide.shape, F32)
        for index, (offset, gates) in enumerate(parts):
            real, imag = product(gates)
            for t in range(2):
                at = pl.ds(t * dim, dim) if offset == base else pl.ds(t, dim, stride=2)
                if index == 0:
                    wide[0, t, at, :] = real
                    wide[1, t, at, :] = imag
                else:
                    x = jnp.concatenate(
                        [jnp.concatenate([wide[p, c, at, :] for c in range(2)], axis=1) for p in range(2)], axis=0
                    )
                    y = pair_dot(block(real, imag), x)
                    for p in range(2):
                        for c in range(2):
                            wide[p, c, at, :] = y[p * dim : (p + 1) * dim, c * dim : (c + 1) * dim]
        return [jnp.concatenate([wide[p, 0], wide[p, 1]], axis=1) for p in range(2)]

    for number, section in enumerate(sections):
        weights, targets = targets[: len(section)], targets[len(section) :]
        for target, (base, _, parts) in zip(weights, section):
            high, rest = split(block(*(joined(wides.at[number], base, parts) if len(parts) > 1 else product(parts[0][1]))))
            if target is weights[0]:
                order = (by_source(dim, count), from_blocks if straight(count) else None, by_core(dim))[number]
                if order is not None:
                    high, rest = pick_columns(high, order), pick_columns(rest, order)
            elif number == 0 and straight(count) and target is weights[-1]:
                high, rest = pick_rows(high, into_blocks), pick_rows(rest, into_blocks)
            elif number == 2 and target is weights[-1]:
                high, rest = in_groups(high), in_groups(rest)
            target[...] = jnp.concatenate([high, rest, high], axis=1)
    real, imag = product(low)
    high, rest = split(block(real.T, -imag.T))
    low_ref[...] = jnp.concatenate([high, rest, high], axis=0)


def distances_of(count):
    half = count // 2
    far, near = list(range(count - 1, half - 1, -1)), list(range(half - 1, 0, -1))
    order = [0]
    while far or near:
        order += far[:2] + near[:2]
        far, near = far[2:], near[2:]
    return order


def partners_of(count):
    me = lax.axis_index("qa")
    return [jnp.bitwise_xor(me, distance) for distance in distances_of(count)]


def split_kernel(x_ref, *outs):
    me, _, *dests = partners_of(len(outs) + 1)
    for dest, out_ref in zip([me, *dests], outs):
        out_ref[...] = x_ref[dest]


def apply_stage(weights_ref, starts, load, store):
    dim = weights_ref.shape[0] // 2
    for pair in range(0, len(starts), 2):
        group = starts[pair : pair + 2]
        x = jnp.concatenate(
            [jnp.concatenate([load(part, start) for start in group], axis=1) for part in range(2)], axis=0
        )
        high, rest = split(x)
        y = bf_dot(weights_ref[...], jnp.concatenate([rest, high, high], axis=0))
        lanes = y.shape[1] // len(group)
        for part in range(2):
            for place, start in enumerate(group):
                store(part, start, y[part * dim : (part + 1) * dim, place * lanes : (place + 1) * lanes])


def stage_starts(stage, lane_bits, rows):
    base, bits, _ = stage
    dim, stride = 2**bits, 2 ** (base - lane_bits)
    return dim, stride, [h * dim * stride + l for h in range(rows // (dim * stride)) for l in range(stride)]


def stage_load(stage, lane_bits, source):
    dim, stride, _ = stage_starts(stage, lane_bits, source.shape[1])

    def load(part, start):
        if not interleaved(stage):
            return source[part, pl.ds(start, dim, stride=stride), :]
        half = dim // 2
        return jnp.concatenate(
            [source[part, pl.ds(start + t * stride, half, stride=2 * stride), :] for t in range(2)], axis=0
        )

    return load


def run_stage(stage, weights_ref, lane_bits, source, target=None, store=None):
    dim, stride, starts = stage_starts(stage, lane_bits, source.shape[1])

    def plain(part, start, value):
        target[part, pl.ds(start, dim, stride=stride), :] = value

    apply_stage(weights_ref, starts, stage_load(stage, lane_bits, source), store or plain)


def run_top_stage(stage, weights_ref, lane_bits, source, halves):
    rows = 2 * halves[0].shape[1]
    dim, stride, starts = stage_starts(stage, lane_bits, rows)

    def store(part, start, value):
        for t in range(2):
            halves[t][part, pl.ds(start, dim // 2, stride=stride), :] = value[t * dim // 2 : (t + 1) * dim // 2]

    def load(part, start):
        if not isinstance(source, tuple):
            return source[part, pl.ds(start, dim, stride=stride), :]
        return jnp.concatenate([half[part, pl.ds(start, dim // 2, stride=stride), :] for half in source], axis=0)

    apply_stage(weights_ref, starts, load, store)


def run_halves(stages, weights, lane_bits, halves, spares, last_store=None):
    for index, (stage, weights_ref) in enumerate(zip(stages, weights)):
        for t in range(2):
            store = None
            if last_store is not None and index == len(stages) - 1:
                store = functools.partial(last_store, t)
            run_stage(stage, weights_ref, lane_bits, halves[t], spares[t], store)
        halves, spares = spares, halves
    return halves


def low_gate(blocks, low_ref, whole):
    lanes = whole.shape[2]
    for spot, block_ref in blocks:
        size = block_ref.shape[0] // 2
        real = block_ref[pl.ds(0, size, stride=2), :]
        imag = block_ref[pl.ds(1, size, stride=2), :]
        high, rest = split(jnp.concatenate([real, imag], axis=1))
        y = bf_dot(jnp.concatenate([rest, high, high], axis=1), low_ref[...])
        whole[0, pl.ds(spot * size, size), :] = y[:, :lanes]
        whole[1, pl.ds(spot * size, size), :] = y[:, lanes:]


def low_kernel(spots, *refs):
    *blocks, low_ref, whole = refs
    low_gate(zip(spots, blocks), low_ref, whole)


def first_kernel(stages, lane_bits, count, spots, *refs):
    _, *blocks = refs[: 1 + len(spots)]
    refs = refs[1 + len(spots) :]
    low_ref, weights, refs = refs[0], refs[1 : 1 + len(stages)], refs[1 + len(stages) :]
    outs, (whole, *halves) = refs[:count], refs[count:]
    low_gate(zip(spots, blocks), low_ref, whole)
    run_top_stage(stages[0], weights[0], lane_bits, whole, halves[:2])
    if straight(count):

        def store(top, part, start, value):
            for spot, out_ref in enumerate(outs):
                for bit in range(2):
                    rows = value[(2 * spot + bit) * 16 : (2 * spot + bit + 1) * 16]
                    out_ref[top, part, 2 * bit + start] = rows

        run_halves(stages[1:], weights[1:], lane_bits, halves[:2], halves[2:], store)
        return
    done = run_halves(stages[1:], weights[1:], lane_bits, halves[:2], halves[2:])
    tops, mids, _, inner, _ = outs[0].shape
    dests = partners_of(count)
    for top in range(tops):
        for dest, out_ref in zip(dests, outs):
            for mid in range(mids):
                start = pl.multiple_of((mid * count + dest) * inner, inner)
                for part in range(2):
                    out_ref[top, mid, part] = done[top][part, pl.ds(start, inner), :]


def second_kernel(stages, lane_bits, count, stays, *refs):
    blocks, weights, refs = refs[:count], refs[count : count + len(stages)], refs[count + len(stages) :]
    out_ref, one, two = refs
    core = lax.axis_index("qb")
    top = core if stays else 1 - core
    if straight(count):
        dim, stride, starts = stage_starts(stages[0], lane_bits, one.shape[1])

        def load(part, start):
            return jnp.concatenate([block_ref[top, part, start] for block_ref in blocks], axis=0)

        def store(part, start, value):
            one[part, pl.ds(start, dim, stride=stride), :] = value

        apply_stage(weights[0], starts, load, store)
        stages, weights, blocks = stages[1:], weights[1:], []
    for source, block_ref in zip(partners_of(count), blocks):
        _, mids, _, inner, _ = block_ref.shape
        for mid in range(mids):
            start = pl.multiple_of((mid * count + source) * inner, inner)
            for part in range(2):
                one[part, pl.ds(start, inner), :] = block_ref[top, mid, part]
    for index, (stage, weights_ref) in enumerate(zip(stages, weights)):
        run_stage(stage, weights_ref, lane_bits, one, out_ref if index == len(stages) - 1 else two)
        one, two = two, one


def third_kernel(stages, lane_bits, kept_ref, came_ref, *refs):
    weights, (out_ref, *halves, sems) = refs[: len(stages)], refs[len(stages) :]
    results = halves[4:]
    half = kept_ref.shape[1]
    run_top_stage(stages[0], weights[0], lane_bits, (kept_ref, came_ref), halves[:2])
    done = run_halves(stages[1:-1], weights[1:-1], lane_bits, halves[:2], halves[2:4])
    copies = []
    dim, stride, starts = stage_starts(stages[-1], lane_bits, half)
    group = dim // 2

    def put(t, upper, part, start, value):
        at = 2 * (start + upper * group * stride) + part
        results[t][pl.ds(at, group, stride=2 * stride), :] = value

    def copy_out(t, first, count):
        size = 2 * half // PIECES
        for piece in range(first, first + count):
            to = out_ref.at[pl.ds(t * 2 * half + piece * size, size)]
            copies.append(
                pltpu.make_async_copy(results[t].at[pl.ds(piece * size, size)], to, sems.at[t * PIECES + piece])
            )
            copies[-1].start()

    def both_groups(upper, start, value):
        for part in range(2):
            put(0, upper, part, start, value[part * group : (part + 1) * group])

    apply_stage(weights[-1], starts, stage_load(stages[-1], lane_bits, done[0]), both_groups)
    copy_out(0, 0, PIECES)
    for upper in range(2):
        rows_ref = weights[-1].at[pl.ds(upper * dim, dim)]
        store = functools.partial(put, 1, upper)
        apply_stage(rows_ref, starts, stage_load(stages[-1], lane_bits, done[1]), store)
        copy_out(1, upper * PIECES // 2, PIECES // 2)
    for copy in copies:
        copy.wait()


def call(kernel, name, out_shapes, in_specs, scratch, matmuls, *operands, limit=VMEM_LIMIT, out_spec=None, aliases=None):
    many = isinstance(out_shapes, tuple)
    vmem = out_spec or pl.BlockSpec(memory_space=pltpu.VMEM)
    return pl.pallas_call(
        kernel,
        out_shape=out_shapes,
        in_specs=in_specs,
        out_specs=(vmem,) * len(out_shapes) if many else vmem,
        scratch_shapes=scratch,
        input_output_aliases=aliases or {},
        compiler_params=pltpu.CompilerParams(vmem_limit_bytes=limit),
        cost_estimate=pl.CostEstimate(
            flops=int(matmuls * 3 * 2 * 256 * 256 * 1024), bytes_accessed=4 * 2**20, transcendentals=0
        ),
        name=name,
    )(*operands)


def per_device(state, gate_terms, path_bits):
    amps_local = state.shape[1]
    local_bits = amps_local.bit_length() - 1
    dim = gate_terms.shape[-1]
    gate_bits = dim.bit_length() - 1
    lanes, lane_bits = dim, gate_bits
    rows = amps_local // lanes
    qa = lax.axis_size("qa")
    qb = lax.axis_size("qb")
    low, sections = plan_gates(local_bits, gate_bits)
    sections = [join_windows(section, gate_bits) for section in sections]
    order = 2 * dim
    vmem = pl.BlockSpec(memory_space=pltpu.VMEM)
    hbm = pl.BlockSpec(memory_space=pltpu.HBM)
    shape = jax.ShapeDtypeStruct

    state = with_layout_constraint(state.reshape(2, rows, lanes), Layout(major_to_minor=(1, 0, 2)))
    state = state.swapaxes(0, 1).reshape(qa, 2 * rows // qa, lanes)
    blocks = call(
        split_kernel,
        "split_state",
        (shape((2 * rows // qa, lanes), F32),) * (qa - 1),
        [vmem],
        [],
        0,
        state,
    )

    first = lax.dynamic_index_in_dim(state, partners_of(qa)[1], 0, keepdims=False)
    blocks = [blocks[0], first, *blocks[1:]]

    def exchange(blocks):
        came = [blocks[0]]
        for distance, piece in zip(distances_of(qa)[1:], blocks[1:]):
            came.append(lax.ppermute(piece, "qa", [(i, i ^ distance) for i in range(qa)]))
        return came

    blocks = exchange(blocks)
    low_w, *weights = call(
        functools.partial(prepare_kernel, low, sections, qa),
        "prepare_gates",
        (shape((3 * order, order), BF16),)
        + tuple(shape((2 * 2**bits, 6 * 2**bits), BF16) for section in sections for _, bits, _ in section),
        [pl.BlockSpec(memory_space=pltpu.SMEM), hbm],
        [
            pltpu.VMEM((gate_terms.shape[0], 2, dim, dim), F32),
            pltpu.VMEM((len(sections), 2, 2, 2 * dim, dim), F32),
            pltpu.SemaphoreType.DMA((gate_terms.shape[0],)),
        ],
        8,
        path_bits,
        gate_terms,
        limit=LARGE_VMEM,
    )
    counts = [len(section) for section in sections]
    weights = [weights[: counts[0]], weights[counts[0] : counts[0] + counts[1]], weights[counts[0] + counts[1] :]]
    inner = rows // (qa * qa)
    half = pltpu.VMEM((2, rows // 2, lanes), F32)
    early, late = list(range(qa - 3)), list(range(qa - 3, qa))
    planes = shape((2, rows, lanes), F32)
    begun = call(
        functools.partial(low_kernel, early),
        "low_gate_early",
        planes,
        [vmem] * (len(early) + 1),
        [],
        1,
        *[blocks[spot] for spot in early],
        low_w,
    )
    *blocks, _ = call(
        functools.partial(first_kernel, sections[0], lane_bits, qa, late),
        "first_section",
        (shape((qb, 2, 4, 16, lanes) if straight(qa) else (qb, qa // qb, 2, inner, lanes), F32),) * qa + (planes,),
        [vmem] * (2 + len(late) + counts[0]),
        [half] * 4,
        5,
        begun,
        *[blocks[spot] for spot in late],
        low_w,
        *weights[0],
        aliases={0: qa},
    )
    blocks = exchange(blocks)
    halves = []
    for stays in (False, True):
        halves.append(
            call(
                functools.partial(second_kernel, sections[1], lane_bits, qa, stays),
                "second_section_kept" if stays else "second_section_sent",
                shape((2, rows // qb, lanes), F32),
                [vmem] * (qa + counts[1]),
                [half] * 2,
                1.5,
                *blocks,
                *weights[1],
            )
        )
        if not stays:
            came = lax.ppermute(halves[0], "qb", [(i, 1 - i) for i in range(qb)])
    final = call(
        functools.partial(third_kernel, sections[2], lane_bits),
        "third_section",
        shape((2 * rows, lanes), F32),
        [vmem] * (2 + counts[2]),
        [half] * 4 + [pltpu.VMEM((rows, lanes), F32)] * 2 + [pltpu.SemaphoreType.DMA((2 * PIECES,))],
        4,
        halves[1],
        came,
        *weights[2],
        out_spec=hbm,
    )
    return final.reshape(rows, 2, lanes).swapaxes(0, 1).reshape(2, amps_local)


def solution(mesh):
    return jax.shard_map(
        per_device,
        mesh=mesh,
        in_specs=(P(None, ("paths", "qa", "qb")), P(), P("paths")),
        out_specs=P(None, ("paths", "qa", "qb")),
        check_vma=False,
    )
```

```python
import functools

import jax
import jax.numpy as jnp
from jax import lax
from jax.experimental import pallas as pl
from jax.experimental.layout import Layout, with_layout_constraint
from jax.experimental.pallas import tpu as pltpu
from jax.sharding import PartitionSpec as P

F32 = jnp.float32
BF16 = jnp.bfloat16
VMEM_LIMIT = 14 * 1024 * 1024
LARGE_VMEM = 48 * 1024 * 1024
PIECES = 4


def window_offsets(span, gate_bits):
    return [0, span, gate_bits, span - 1, gate_bits + 1, span - 2]


def plan_gates(local_bits, gate_bits):
    outer = window_offsets(local_bits - gate_bits, gate_bits)
    inner = window_offsets(local_bits - gate_bits - 1, gate_bits)
    low, sections = [], []
    for number, offsets in enumerate((outer, inner, outer)):
        section = []
        for index, offset in enumerate(offsets):
            gate = 6 * number + index
            if offset == 0:
                low.append(gate)
            elif section and section[-1][0] == offset:
                section[-1][1].append(gate)
            else:
                section.append((offset, [gate]))
        sections.append(section)
    return low, sections


def join_windows(section, gate_bits):
    stages = []
    for offset, gates in section:
        if stages:
            offsets = [o for o, _ in stages[-1]] + [offset]
            if max(offsets) - min(offsets) <= 1:
                stages[-1].append((offset, gates))
                continue
        stages.append([(offset, gates)])
    return [
        (min(o for o, _ in parts), gate_bits + (len(parts) > 1), parts)
        for parts in stages
    ]


def interleaved(stage):
    base, _, parts = stage
    return parts[0][0] != base


def split(x):
    high = x.astype(BF16)
    return high, (x - high.astype(F32)).astype(BF16)


def bf_dot(a, b):
    return jnp.dot(a, b, preferred_element_type=F32)


def pair_dot(a, b):
    (a_high, a_rest), (b_high, b_rest) = split(a), split(b)
    return bf_dot(a_high, b_rest) + bf_dot(a_rest, b_high) + bf_dot(a_high, b_high)


def block(real, imag):
    return jnp.concatenate(
        [jnp.concatenate([real, -imag], axis=1), jnp.concatenate([imag, real], axis=1)], axis=0
    )


def relative(matrix, number, count):
    order = matrix.shape[1]
    dim = order // 2
    column = lax.broadcasted_iota(jnp.int32, (order, order), 1)
    row = lax.broadcasted_iota(jnp.int32, (order, order), 0)
    within = lax.rem(column, dim)
    if number == 0:
        size = dim // count
        spot, source = within // size, jnp.zeros_like(column)
        for index, partner in enumerate(partners_of(count)):
            source = jnp.where(spot == index, partner, source)
        natural = source * size + lax.rem(within, size)
    else:
        natural = jnp.bitwise_xor(within, lax.axis_index("qb") * (dim // 2))
    picked = jnp.where(row == natural + (column - within), 1.0, 0.0).astype(BF16)
    return bf_dot(matrix, picked).astype(BF16)


def prepare_kernel(low, sections, count, bits_ref, gates_ref, low_ref, *refs):
    *targets, held, wides, sems = refs
    copies = {}
    for gate in [gate for section in sections for _, _, parts in section for _, gates in parts for gate in gates] + low:
        copies[gate] = pltpu.make_async_copy(gates_ref.at[gate, bits_ref[gate]], held.at[gate], sems.at[gate])
        copies[gate].start()
    dim = held.shape[-1]

    def product(gates):
        for gate in gates:
            copies.pop(gate).wait()
        real, imag = held[gates[0], 0], held[gates[0], 1]
        for gate in gates[1:]:
            column = pair_dot(block(held[gate, 0], held[gate, 1]), jnp.concatenate([real, imag], axis=0))
            real, imag = column[:dim], column[dim:]
        return real, imag

    def joined(wide, base, parts):
        wide[...] = jnp.zeros(wide.shape, F32)
        for index, (offset, gates) in enumerate(parts):
            real, imag = product(gates)
            for t in range(2):
                at = pl.ds(t * dim, dim) if offset == base else pl.ds(t, dim, stride=2)
                if index == 0:
                    wide[0, t, at, :] = real
                    wide[1, t, at, :] = imag
                else:
                    x = jnp.concatenate(
                        [jnp.concatenate([wide[p, c, at, :] for c in range(2)], axis=1) for p in range(2)], axis=0
                    )
                    y = pair_dot(block(real, imag), x)
                    for p in range(2):
                        for c in range(2):
                            wide[p, c, at, :] = y[p * dim : (p + 1) * dim, c * dim : (c + 1) * dim]
        return [jnp.concatenate([wide[p, 0], wide[p, 1]], axis=1) for p in range(2)]

    for number, section in enumerate(sections):
        weights, targets = targets[: len(section)], targets[len(section) :]
        for target, (base, _, parts) in zip(weights, section):
            high, rest = split(block(*(joined(wides.at[number], base, parts) if len(parts) > 1 else product(parts[0][1]))))
            if number != 1 and target is weights[0]:
                high, rest = relative(high, number, count), relative(rest, number, count)
            target[...] = jnp.concatenate([high, rest, high], axis=1)
    real, imag = product(low)
    high, rest = split(block(real.T, -imag.T))
    low_ref[...] = jnp.concatenate([high, rest, high], axis=0)


def distances_of(count):
    half = count // 2
    far, near = list(range(count - 1, half - 1, -1)), list(range(half - 1, 0, -1))
    order = [0]
    while far or near:
        order += sorted(far[:2]) + sorted(near[:2])
        far, near = far[2:], near[2:]
    return order


def partners_of(count):
    me = lax.axis_index("qa")
    return [jnp.bitwise_xor(me, distance) for distance in distances_of(count)]


def split_kernel(x_ref, *outs):
    me, _, *dests = partners_of(len(outs) + 1)
    for dest, out_ref in zip([me, *dests], outs):
        out_ref[...] = x_ref[dest]


def apply_stage(weights_ref, starts, load, store):
    dim = weights_ref.shape[0] // 2
    for pair in range(0, len(starts), 2):
        group = starts[pair : pair + 2]
        x = jnp.concatenate(
            [jnp.concatenate([load(part, start) for start in group], axis=1) for part in range(2)], axis=0
        )
        high, rest = split(x)
        y = bf_dot(weights_ref[...], jnp.concatenate([rest, high, high], axis=0))
        lanes = y.shape[1] // len(group)
        for part in range(2):
            for place, start in enumerate(group):
                store(part, start, y[part * dim : (part + 1) * dim, place * lanes : (place + 1) * lanes])


def stage_starts(stage, lane_bits, rows):
    base, bits, _ = stage
    dim, stride = 2**bits, 2 ** (base - lane_bits)
    return dim, stride, [h * dim * stride + l for h in range(rows // (dim * stride)) for l in range(stride)]


def run_stage(stage, weights_ref, lane_bits, source, target=None, store=None):
    dim, stride, starts = stage_starts(stage, lane_bits, source.shape[1])

    def load(part, start):
        if not interleaved(stage):
            return source[part, pl.ds(start, dim, stride=stride), :]
        half = dim // 2
        return jnp.concatenate(
            [source[part, pl.ds(start + t * stride, half, stride=2 * stride), :] for t in range(2)], axis=0
        )

    def plain(part, start, value):
        target[part, pl.ds(start, dim, stride=stride), :] = value

    apply_stage(weights_ref, starts, load, store or plain)


def run_top_stage(stage, weights_ref, lane_bits, source, halves):
    rows = 2 * halves[0].shape[1]
    dim, stride, starts = stage_starts(stage, lane_bits, rows)

    def store(part, start, value):
        for t in range(2):
            halves[t][part, pl.ds(start, dim // 2, stride=stride), :] = value[t * dim // 2 : (t + 1) * dim // 2]

    def load(part, start):
        if not isinstance(source, tuple):
            return source[part, pl.ds(start, dim, stride=stride), :]
        return jnp.concatenate([half[part, pl.ds(start, dim // 2, stride=stride), :] for half in source], axis=0)

    apply_stage(weights_ref, starts, load, store)


def run_halves(stages, weights, lane_bits, halves, spares, last_store=None):
    for index, (stage, weights_ref) in enumerate(zip(stages, weights)):
        for t in range(2):
            store = None
            if last_store is not None and index == len(stages) - 1:
                store = functools.partial(last_store, t)
            run_stage(stage, weights_ref, lane_bits, halves[t], spares[t], store)
        halves, spares = spares, halves
    return halves


def low_gate(blocks, low_ref, whole):
    lanes = whole.shape[2]
    for spot, block_ref in blocks:
        size = block_ref.shape[0] // 2
        real = block_ref[pl.ds(0, size, stride=2), :]
        imag = block_ref[pl.ds(1, size, stride=2), :]
        high, rest = split(jnp.concatenate([real, imag], axis=1))
        y = bf_dot(jnp.concatenate([rest, high, high], axis=1), low_ref[...])
        whole[0, pl.ds(spot * size, size), :] = y[:, :lanes]
        whole[1, pl.ds(spot * size, size), :] = y[:, lanes:]


def low_kernel(spots, *refs):
    *blocks, low_ref, whole = refs
    low_gate(zip(spots, blocks), low_ref, whole)


def first_kernel(stages, lane_bits, count, spots, *refs):
    _, *blocks = refs[: 1 + len(spots)]
    refs = refs[1 + len(spots) :]
    low_ref, weights, refs = refs[0], refs[1 : 1 + len(stages)], refs[1 + len(stages) :]
    outs, (whole, *halves) = refs[:count], refs[count:]
    low_gate(zip(spots, blocks), low_ref, whole)
    run_top_stage(stages[0], weights[0], lane_bits, whole, halves[:2])
    done = run_halves(stages[1:], weights[1:], lane_bits, halves[:2], halves[2:])
    tops, mids, _, inner, _ = outs[0].shape
    dests = partners_of(count)
    for top in range(tops):
        for dest, out_ref in zip(dests, outs):
            for mid in range(mids):
                start = pl.multiple_of((mid * count + dest) * inner, inner)
                for part in range(2):
                    out_ref[top, mid, part] = done[top][part, pl.ds(start, inner), :]


def second_kernel(stages, lane_bits, count, stays, *refs):
    blocks, weights, refs = refs[:count], refs[count : count + len(stages)], refs[count + len(stages) :]
    out_ref, one, two = refs
    core = lax.axis_index("qb")
    top = core if stays else 1 - core
    for source, block_ref in zip(partners_of(count), blocks):
        _, mids, _, inner, _ = block_ref.shape
        for mid in range(mids):
            start = pl.multiple_of((mid * count + source) * inner, inner)
            for part in range(2):
                one[part, pl.ds(start, inner), :] = block_ref[top, mid, part]
    for index, (stage, weights_ref) in enumerate(zip(stages, weights)):
        run_stage(stage, weights_ref, lane_bits, one, out_ref if index == len(stages) - 1 else two)
        one, two = two, one


def third_kernel(stages, lane_bits, kept_ref, came_ref, *refs):
    weights, (out_ref, *halves, sems) = refs[: len(stages)], refs[len(stages) :]
    results = halves[4:]
    half = kept_ref.shape[1]
    run_top_stage(stages[0], weights[0], lane_bits, (kept_ref, came_ref), halves[:2])
    done = run_halves(stages[1:-1], weights[1:-1], lane_bits, halves[:2], halves[2:4])
    copies = []
    for t in range(2):
        dim, stride, _ = stage_starts(stages[-1], lane_bits, half)

        def store(part, start, value, t=t):
            results[t][pl.ds(2 * start + part, dim, stride=2 * stride), :] = value

        run_stage(stages[-1], weights[-1], lane_bits, done[t], store=store)
        size = 2 * half // PIECES
        for piece in range(PIECES):
            to = out_ref.at[pl.ds(t * 2 * half + piece * size, size)]
            copies.append(
                pltpu.make_async_copy(results[t].at[pl.ds(piece * size, size)], to, sems.at[t * PIECES + piece])
            )
            copies[-1].start()
    for copy in copies:
        copy.wait()


def call(kernel, name, out_shapes, in_specs, scratch, matmuls, *operands, limit=VMEM_LIMIT, out_spec=None, aliases=None):
    many = isinstance(out_shapes, tuple)
    vmem = out_spec or pl.BlockSpec(memory_space=pltpu.VMEM)
    return pl.pallas_call(
        kernel,
        out_shape=out_shapes,
        in_specs=in_specs,
        out_specs=(vmem,) * len(out_shapes) if many else vmem,
        scratch_shapes=scratch,
        input_output_aliases=aliases or {},
        compiler_params=pltpu.CompilerParams(vmem_limit_bytes=limit),
        cost_estimate=pl.CostEstimate(
            flops=int(matmuls * 3 * 2 * 256 * 256 * 1024), bytes_accessed=4 * 2**20, transcendentals=0
        ),
        name=name,
    )(*operands)


def per_device(state, gate_terms, path_bits):
    amps_local = state.shape[1]
    local_bits = amps_local.bit_length() - 1
    dim = gate_terms.shape[-1]
    gate_bits = dim.bit_length() - 1
    lanes, lane_bits = dim, gate_bits
    rows = amps_local // lanes
    qa = lax.axis_size("qa")
    qb = lax.axis_size("qb")
    low, sections = plan_gates(local_bits, gate_bits)
    sections = [join_windows(section, gate_bits) for section in sections]
    order = 2 * dim
    vmem = pl.BlockSpec(memory_space=pltpu.VMEM)
    hbm = pl.BlockSpec(memory_space=pltpu.HBM)
    shape = jax.ShapeDtypeStruct

    state = with_layout_constraint(state.reshape(2, rows, lanes), Layout(major_to_minor=(1, 0, 2)))
    state = state.swapaxes(0, 1).reshape(qa, 2 * rows // qa, lanes)
    blocks = call(
        split_kernel,
        "split_state",
        (shape((2 * rows // qa, lanes), F32),) * (qa - 1),
        [vmem],
        [],
        0,
        state,
    )

    first = lax.dynamic_index_in_dim(state, partners_of(qa)[1], 0, keepdims=False)
    blocks = [blocks[0], first, *blocks[1:]]

    def exchange(blocks):
        came = [blocks[0]]
        for distance, piece in zip(distances_of(qa)[1:], blocks[1:]):
            came.append(lax.ppermute(piece, "qa", [(i, i ^ distance) for i in range(qa)]))
        return came

    blocks = exchange(blocks)
    low_w, *weights = call(
        functools.partial(prepare_kernel, low, sections, qa),
        "prepare_gates",
        (shape((3 * order, order), BF16),)
        + tuple(shape((2 * 2**bits, 6 * 2**bits), BF16) for section in sections for _, bits, _ in section),
        [pl.BlockSpec(memory_space=pltpu.SMEM), hbm],
        [
            pltpu.VMEM((gate_terms.shape[0], 2, dim, dim), F32),
            pltpu.VMEM((len(sections), 2, 2, 2 * dim, dim), F32),
            pltpu.SemaphoreType.DMA((gate_terms.shape[0],)),
        ],
        8,
        path_bits,
        gate_terms,
        limit=LARGE_VMEM,
    )
    counts = [len(section) for section in sections]
    weights = [weights[: counts[0]], weights[counts[0] : counts[0] + counts[1]], weights[counts[0] + counts[1] :]]
    inner = rows // (qa * qa)
    half = pltpu.VMEM((2, rows // 2, lanes), F32)
    early, late = list(range(qa - 3)), list(range(qa - 3, qa))
    planes = shape((2, rows, lanes), F32)
    begun = call(
        functools.partial(low_kernel, early),
        "low_gate_early",
        planes,
        [vmem] * (len(early) + 1),
        [],
        1,
        *[blocks[spot] for spot in early],
        low_w,
    )
    *blocks, _ = call(
        functools.partial(first_kernel, sections[0], lane_bits, qa, late),
        "first_section",
        (shape((qb, qa // qb, 2, inner, lanes), F32),) * qa + (planes,),
        [vmem] * (2 + len(late) + counts[0]),
        [half] * 4,
        5,
        begun,
        *[blocks[spot] for spot in late],
        low_w,
        *weights[0],
        aliases={0: qa},
    )
    blocks = exchange(blocks)
    halves = []
    for stays in (False, True):
        halves.append(
            call(
                functools.partial(second_kernel, sections[1], lane_bits, qa, stays),
                "second_section_kept" if stays else "second_section_sent",
                shape((2, rows // qb, lanes), F32),
                [vmem] * (qa + counts[1]),
                [half] * 2,
                1.5,
                *blocks,
                *weights[1],
            )
        )
        if not stays:
            came = lax.ppermute(halves[0], "qb", [(i, 1 - i) for i in range(qb)])
    final = call(
        functools.partial(third_kernel, sections[2], lane_bits),
        "third_section",
        shape((2 * rows, lanes), F32),
        [vmem] * (2 + counts[2]),
        [half] * 4 + [pltpu.VMEM((rows, lanes), F32)] * 2 + [pltpu.SemaphoreType.DMA((2 * PIECES,))],
        4,
        halves[1],
        came,
        *weights[2],
        out_spec=hbm,
    )
    return final.reshape(rows, 2, lanes).swapaxes(0, 1).reshape(2, amps_local)


def solution(mesh):
    return jax.shard_map(
        per_device,
        mesh=mesh,
        in_specs=(P(None, ("paths", "qa", "qb")), P(), P("paths")),
        out_specs=P(None, ("paths", "qa", "qb")),
        check_vma=False,
    )
```

```python
import functools

import jax
import jax.numpy as jnp
from jax import lax
from jax.experimental import pallas as pl
from jax.experimental.layout import Layout, with_layout_constraint
from jax.experimental.pallas import tpu as pltpu
from jax.sharding import PartitionSpec as P

F32 = jnp.float32
BF16 = jnp.bfloat16
VMEM_LIMIT = 14 * 1024 * 1024
LARGE_VMEM = 48 * 1024 * 1024
PIECES = 4


def window_offsets(span, gate_bits):
    return [0, span, gate_bits, span - 1, gate_bits + 1, span - 2]


def plan_gates(local_bits, gate_bits):
    outer = window_offsets(local_bits - gate_bits, gate_bits)
    inner = window_offsets(local_bits - gate_bits - 1, gate_bits)
    low, sections = [], []
    for number, offsets in enumerate((outer, inner, outer)):
        section = []
        for index, offset in enumerate(offsets):
            gate = 6 * number + index
            if offset == 0:
                low.append(gate)
            elif section and section[-1][0] == offset:
                section[-1][1].append(gate)
            else:
                section.append((offset, [gate]))
        sections.append(section)
    return low, sections


def join_windows(section, gate_bits):
    stages = []
    for offset, gates in section:
        if stages:
            offsets = [o for o, _ in stages[-1]] + [offset]
            if max(offsets) - min(offsets) <= 1:
                stages[-1].append((offset, gates))
                continue
        stages.append([(offset, gates)])
    return [
        (min(o for o, _ in parts), gate_bits + (len(parts) > 1), parts)
        for parts in stages
    ]


def interleaved(stage):
    base, _, parts = stage
    return parts[0][0] != base


def split(x):
    high = x.astype(BF16)
    return high, (x - high.astype(F32)).astype(BF16)


def bf_dot(a, b):
    return jnp.dot(a, b, preferred_element_type=F32)


def pair_dot(a, b):
    (a_high, a_rest), (b_high, b_rest) = split(a), split(b)
    return bf_dot(a_high, b_rest) + bf_dot(a_rest, b_high) + bf_dot(a_high, b_high)


def block(real, imag):
    return jnp.concatenate(
        [jnp.concatenate([real, -imag], axis=1), jnp.concatenate([imag, real], axis=1)], axis=0
    )


def relative(matrix, number, count):
    order = matrix.shape[1]
    dim = order // 2
    column = lax.broadcasted_iota(jnp.int32, (order, order), 1)
    row = lax.broadcasted_iota(jnp.int32, (order, order), 0)
    within = lax.rem(column, dim)
    if number == 0:
        size = dim // count
        spot, source = within // size, jnp.zeros_like(column)
        for index, partner in enumerate(partners_of(count)):
            source = jnp.where(spot == index, partner, source)
        natural = source * size + lax.rem(within, size)
    else:
        natural = jnp.bitwise_xor(within, lax.axis_index("qb") * (dim // 2))
    picked = jnp.where(row == natural + (column - within), 1.0, 0.0).astype(BF16)
    return bf_dot(matrix, picked).astype(BF16)


def prepare_kernel(low, sections, count, bits_ref, gates_ref, low_ref, *refs):
    *targets, held, wides, sems = refs
    copies = {}
    for gate in [gate for section in sections for _, _, parts in section for _, gates in parts for gate in gates] + low:
        copies[gate] = pltpu.make_async_copy(gates_ref.at[gate, bits_ref[gate]], held.at[gate], sems.at[gate])
        copies[gate].start()
    dim = held.shape[-1]

    def product(gates):
        for gate in gates:
            copies.pop(gate).wait()
        real, imag = held[gates[0], 0], held[gates[0], 1]
        for gate in gates[1:]:
            column = pair_dot(block(held[gate, 0], held[gate, 1]), jnp.concatenate([real, imag], axis=0))
            real, imag = column[:dim], column[dim:]
        return real, imag

    def joined(wide, base, parts):
        wide[...] = jnp.zeros(wide.shape, F32)
        for index, (offset, gates) in enumerate(parts):
            real, imag = product(gates)
            for t in range(2):
                at = pl.ds(t * dim, dim) if offset == base else pl.ds(t, dim, stride=2)
                if index == 0:
                    wide[0, t, at, :] = real
                    wide[1, t, at, :] = imag
                else:
                    x = jnp.concatenate(
                        [jnp.concatenate([wide[p, c, at, :] for c in range(2)], axis=1) for p in range(2)], axis=0
                    )
                    y = pair_dot(block(real, imag), x)
                    for p in range(2):
                        for c in range(2):
                            wide[p, c, at, :] = y[p * dim : (p + 1) * dim, c * dim : (c + 1) * dim]
        return [jnp.concatenate([wide[p, 0], wide[p, 1]], axis=1) for p in range(2)]

    for number, section in enumerate(sections):
        weights, targets = targets[: len(section)], targets[len(section) :]
        for target, (base, _, parts) in zip(weights, section):
            high, rest = split(block(*(joined(wides.at[number], base, parts) if len(parts) > 1 else product(parts[0][1]))))
            if number != 1 and target is weights[0]:
                high, rest = relative(high, number, count), relative(rest, number, count)
            target[...] = jnp.concatenate([high, rest, high], axis=1)
    real, imag = product(low)
    high, rest = split(block(real.T, -imag.T))
    low_ref[...] = jnp.concatenate([high, rest, high], axis=0)


def distances_of(count):
    half = count // 2
    far, near = list(range(count - 1, half - 1, -1)), list(range(half - 1, 0, -1))
    order = [0]
    while far or near:
        order += far[:2] + near[:2]
        far, near = far[2:], near[2:]
    return order


def partners_of(count):
    me, core = lax.axis_index("qa"), lax.axis_index("qb")
    return [
        jnp.bitwise_xor(me, jnp.bitwise_xor(distance, core) if distance > 1 else distance)
        for distance in distances_of(count)
    ]


def split_kernel(x_ref, *outs):
    me, _, *dests = partners_of(len(outs) + 1)
    for dest, out_ref in zip([me, *dests], outs):
        out_ref[...] = x_ref[dest]


def apply_stage(weights_ref, starts, load, store):
    dim = weights_ref.shape[0] // 2
    for pair in range(0, len(starts), 2):
        group = starts[pair : pair + 2]
        x = jnp.concatenate(
            [jnp.concatenate([load(part, start) for start in group], axis=1) for part in range(2)], axis=0
        )
        high, rest = split(x)
        y = bf_dot(weights_ref[...], jnp.concatenate([rest, high, high], axis=0))
        lanes = y.shape[1] // len(group)
        for part in range(2):
            for place, start in enumerate(group):
                store(part, start, y[part * dim : (part + 1) * dim, place * lanes : (place + 1) * lanes])


def stage_starts(stage, lane_bits, rows):
    base, bits, _ = stage
    dim, stride = 2**bits, 2 ** (base - lane_bits)
    return dim, stride, [h * dim * stride + l for h in range(rows // (dim * stride)) for l in range(stride)]


def run_stage(stage, weights_ref, lane_bits, source, target=None, store=None):
    dim, stride, starts = stage_starts(stage, lane_bits, source.shape[1])

    def load(part, start):
        if not interleaved(stage):
            return source[part, pl.ds(start, dim, stride=stride), :]
        half = dim // 2
        return jnp.concatenate(
            [source[part, pl.ds(start + t * stride, half, stride=2 * stride), :] for t in range(2)], axis=0
        )

    def plain(part, start, value):
        target[part, pl.ds(start, dim, stride=stride), :] = value

    apply_stage(weights_ref, starts, load, store or plain)


def run_top_stage(stage, weights_ref, lane_bits, source, halves):
    rows = 2 * halves[0].shape[1]
    dim, stride, starts = stage_starts(stage, lane_bits, rows)

    def store(part, start, value):
        for t in range(2):
            halves[t][part, pl.ds(start, dim // 2, stride=stride), :] = value[t * dim // 2 : (t + 1) * dim // 2]

    def load(part, start):
        if not isinstance(source, tuple):
            return source[part, pl.ds(start, dim, stride=stride), :]
        return jnp.concatenate([half[part, pl.ds(start, dim // 2, stride=stride), :] for half in source], axis=0)

    apply_stage(weights_ref, starts, load, store)


def run_halves(stages, weights, lane_bits, halves, spares, last_store=None):
    for index, (stage, weights_ref) in enumerate(zip(stages, weights)):
        for t in range(2):
            store = None
            if last_store is not None and index == len(stages) - 1:
                store = functools.partial(last_store, t)
            run_stage(stage, weights_ref, lane_bits, halves[t], spares[t], store)
        halves, spares = spares, halves
    return halves


def low_gate(blocks, low_ref, whole):
    lanes = whole.shape[2]
    for spot, block_ref in blocks:
        size = block_ref.shape[0] // 2
        real = block_ref[pl.ds(0, size, stride=2), :]
        imag = block_ref[pl.ds(1, size, stride=2), :]
        high, rest = split(jnp.concatenate([real, imag], axis=1))
        y = bf_dot(jnp.concatenate([rest, high, high], axis=1), low_ref[...])
        whole[0, pl.ds(spot * size, size), :] = y[:, :lanes]
        whole[1, pl.ds(spot * size, size), :] = y[:, lanes:]


def low_kernel(spots, *refs):
    *blocks, low_ref, whole = refs
    low_gate(zip(spots, blocks), low_ref, whole)


def first_kernel(stages, lane_bits, count, spots, *refs):
    _, *blocks = refs[: 1 + len(spots)]
    refs = refs[1 + len(spots) :]
    low_ref, weights, refs = refs[0], refs[1 : 1 + len(stages)], refs[1 + len(stages) :]
    outs, (whole, *halves) = refs[:count], refs[count:]
    low_gate(zip(spots, blocks), low_ref, whole)
    run_top_stage(stages[0], weights[0], lane_bits, whole, halves[:2])
    done = run_halves(stages[1:], weights[1:], lane_bits, halves[:2], halves[2:])
    tops, mids, _, inner, _ = outs[0].shape
    dests = partners_of(count)
    for top in range(tops):
        for dest, out_ref in zip(dests, outs):
            for mid in range(mids):
                start = pl.multiple_of((mid * count + dest) * inner, inner)
                for part in range(2):
                    out_ref[top, mid, part] = done[top][part, pl.ds(start, inner), :]


def second_kernel(stages, lane_bits, count, stays, *refs):
    blocks, weights, refs = refs[:count], refs[count : count + len(stages)], refs[count + len(stages) :]
    out_ref, one, two = refs
    core = lax.axis_index("qb")
    top = core if stays else 1 - core
    for source, block_ref in zip(partners_of(count), blocks):
        _, mids, _, inner, _ = block_ref.shape
        for mid in range(mids):
            start = pl.multiple_of((mid * count + source) * inner, inner)
            for part in range(2):
                one[part, pl.ds(start, inner), :] = block_ref[top, mid, part]
    for index, (stage, weights_ref) in enumerate(zip(stages, weights)):
        run_stage(stage, weights_ref, lane_bits, one, out_ref if index == len(stages) - 1 else two)
        one, two = two, one


def third_kernel(stages, lane_bits, kept_ref, came_ref, *refs):
    weights, (out_ref, *halves, sems) = refs[: len(stages)], refs[len(stages) :]
    results = halves[4:]
    half = kept_ref.shape[1]
    run_top_stage(stages[0], weights[0], lane_bits, (kept_ref, came_ref), halves[:2])
    done = run_halves(stages[1:-1], weights[1:-1], lane_bits, halves[:2], halves[2:4])
    copies = []
    for t in range(2):
        dim, stride, _ = stage_starts(stages[-1], lane_bits, half)

        def store(part, start, value, t=t):
            results[t][pl.ds(2 * start + part, dim, stride=2 * stride), :] = value

        run_stage(stages[-1], weights[-1], lane_bits, done[t], store=store)
        size = 2 * half // PIECES
        for piece in range(PIECES):
            to = out_ref.at[pl.ds(t * 2 * half + piece * size, size)]
            copies.append(
                pltpu.make_async_copy(results[t].at[pl.ds(piece * size, size)], to, sems.at[t * PIECES + piece])
            )
            copies[-1].start()
    for copy in copies:
        copy.wait()


def call(kernel, name, out_shapes, in_specs, scratch, matmuls, *operands, limit=VMEM_LIMIT, out_spec=None, aliases=None):
    many = isinstance(out_shapes, tuple)
    vmem = out_spec or pl.BlockSpec(memory_space=pltpu.VMEM)
    return pl.pallas_call(
        kernel,
        out_shape=out_shapes,
        in_specs=in_specs,
        out_specs=(vmem,) * len(out_shapes) if many else vmem,
        scratch_shapes=scratch,
        input_output_aliases=aliases or {},
        compiler_params=pltpu.CompilerParams(vmem_limit_bytes=limit),
        cost_estimate=pl.CostEstimate(
            flops=int(matmuls * 3 * 2 * 256 * 256 * 1024), bytes_accessed=4 * 2**20, transcendentals=0
        ),
        name=name,
    )(*operands)


def per_device(state, gate_terms, path_bits):
    amps_local = state.shape[1]
    local_bits = amps_local.bit_length() - 1
    dim = gate_terms.shape[-1]
    gate_bits = dim.bit_length() - 1
    lanes, lane_bits = dim, gate_bits
    rows = amps_local // lanes
    qa = lax.axis_size("qa")
    qb = lax.axis_size("qb")
    low, sections = plan_gates(local_bits, gate_bits)
    sections = [join_windows(section, gate_bits) for section in sections]
    order = 2 * dim
    vmem = pl.BlockSpec(memory_space=pltpu.VMEM)
    hbm = pl.BlockSpec(memory_space=pltpu.HBM)
    shape = jax.ShapeDtypeStruct

    state = with_layout_constraint(state.reshape(2, rows, lanes), Layout(major_to_minor=(1, 0, 2)))
    state = state.swapaxes(0, 1).reshape(qa, 2 * rows // qa, lanes)
    blocks = call(
        split_kernel,
        "split_state",
        (shape((2 * rows // qa, lanes), F32),) * (qa - 1),
        [vmem],
        [],
        0,
        state,
    )

    first = lax.dynamic_index_in_dim(state, partners_of(qa)[1], 0, keepdims=False)
    blocks = [blocks[0], first, *blocks[1:]]

    def exchange(blocks):
        came = [blocks[0]]
        for distance, piece in zip(distances_of(qa)[1:], blocks[1:]):
            pairs = []
            for i in range(qa):
                for core in range(qb):
                    to = i ^ distance ^ (core if distance > 1 else 0)
                    pairs.append((i * qb + core, to * qb + core))
            came.append(lax.ppermute(piece, ("qa", "qb"), pairs))
        return came

    blocks = exchange(blocks)
    low_w, *weights = call(
        functools.partial(prepare_kernel, low, sections, qa),
        "prepare_gates",
        (shape((3 * order, order), BF16),)
        + tuple(shape((2 * 2**bits, 6 * 2**bits), BF16) for section in sections for _, bits, _ in section),
        [pl.BlockSpec(memory_space=pltpu.SMEM), hbm],
        [
            pltpu.VMEM((gate_terms.shape[0], 2, dim, dim), F32),
            pltpu.VMEM((len(sections), 2, 2, 2 * dim, dim), F32),
            pltpu.SemaphoreType.DMA((gate_terms.shape[0],)),
        ],
        8,
        path_bits,
        gate_terms,
        limit=LARGE_VMEM,
    )
    counts = [len(section) for section in sections]
    weights = [weights[: counts[0]], weights[counts[0] : counts[0] + counts[1]], weights[counts[0] + counts[1] :]]
    inner = rows // (qa * qa)
    half = pltpu.VMEM((2, rows // 2, lanes), F32)
    early, late = list(range(qa - 3)), list(range(qa - 3, qa))
    planes = shape((2, rows, lanes), F32)
    begun = call(
        functools.partial(low_kernel, early),
        "low_gate_early",
        planes,
        [vmem] * (len(early) + 1),
        [],
        1,
        *[blocks[spot] for spot in early],
        low_w,
    )
    *blocks, _ = call(
        functools.partial(first_kernel, sections[0], lane_bits, qa, late),
        "first_section",
        (shape((qb, qa // qb, 2, inner, lanes), F32),) * qa + (planes,),
        [vmem] * (2 + len(late) + counts[0]),
        [half] * 4,
        5,
        begun,
        *[blocks[spot] for spot in late],
        low_w,
        *weights[0],
        aliases={0: qa},
    )
    blocks = exchange(blocks)
    halves = []
    for stays in (False, True):
        halves.append(
            call(
                functools.partial(second_kernel, sections[1], lane_bits, qa, stays),
                "second_section_kept" if stays else "second_section_sent",
                shape((2, rows // qb, lanes), F32),
                [vmem] * (qa + counts[1]),
                [half] * 2,
                1.5,
                *blocks,
                *weights[1],
            )
        )
        if not stays:
            came = lax.ppermute(halves[0], "qb", [(i, 1 - i) for i in range(qb)])
    final = call(
        functools.partial(third_kernel, sections[2], lane_bits),
        "third_section",
        shape((2 * rows, lanes), F32),
        [vmem] * (2 + counts[2]),
        [half] * 4 + [pltpu.VMEM((rows, lanes), F32)] * 2 + [pltpu.SemaphoreType.DMA((2 * PIECES,))],
        4,
        halves[1],
        came,
        *weights[2],
        out_spec=hbm,
    )
    return final.reshape(rows, 2, lanes).swapaxes(0, 1).reshape(2, amps_local)


def solution(mesh):
    return jax.shard_map(
        per_device,
        mesh=mesh,
        in_specs=(P(None, ("paths", "qa", "qb")), P(), P("paths")),
        out_specs=P(None, ("paths", "qa", "qb")),
        check_vma=False,
    )
```

```python
import functools

import jax
import jax.numpy as jnp
from jax import lax
from jax.experimental import pallas as pl
from jax.experimental.layout import Layout, with_layout_constraint
from jax.experimental.pallas import tpu as pltpu
from jax.sharding import PartitionSpec as P

F32 = jnp.float32
BF16 = jnp.bfloat16
VMEM_LIMIT = 14 * 1024 * 1024
LARGE_VMEM = 48 * 1024 * 1024
PIECES = 4


def window_offsets(span, gate_bits):
    return [0, span, gate_bits, span - 1, gate_bits + 1, span - 2]


def plan_gates(local_bits, gate_bits):
    outer = window_offsets(local_bits - gate_bits, gate_bits)
    inner = window_offsets(local_bits - gate_bits - 1, gate_bits)
    low, sections = [], []
    for number, offsets in enumerate((outer, inner, outer)):
        section = []
        for index, offset in enumerate(offsets):
            gate = 6 * number + index
            if offset == 0:
                low.append(gate)
            elif section and section[-1][0] == offset:
                section[-1][1].append(gate)
            else:
                section.append((offset, [gate]))
        sections.append(section)
    return low, sections


def join_windows(section, gate_bits):
    stages = []
    for offset, gates in section:
        if stages:
            offsets = [o for o, _ in stages[-1]] + [offset]
            if max(offsets) - min(offsets) <= 1:
                stages[-1].append((offset, gates))
                continue
        stages.append([(offset, gates)])
    return [
        (min(o for o, _ in parts), gate_bits + (len(parts) > 1), parts)
        for parts in stages
    ]


def interleaved(stage):
    base, _, parts = stage
    return parts[0][0] != base


def split(x):
    high = x.astype(BF16)
    return high, (x - high.astype(F32)).astype(BF16)


def bf_dot(a, b):
    return jnp.dot(a, b, preferred_element_type=F32)


def pair_dot(a, b):
    (a_high, a_rest), (b_high, b_rest) = split(a), split(b)
    return bf_dot(a_high, b_rest) + bf_dot(a_rest, b_high) + bf_dot(a_high, b_high)


def block(real, imag):
    return jnp.concatenate(
        [jnp.concatenate([real, -imag], axis=1), jnp.concatenate([imag, real], axis=1)], axis=0
    )


def relative(matrix, number, count):
    order = matrix.shape[1]
    dim = order // 2
    column = lax.broadcasted_iota(jnp.int32, (order, order), 1)
    row = lax.broadcasted_iota(jnp.int32, (order, order), 0)
    within = lax.rem(column, dim)
    if number == 0:
        size = dim // count
        spot, source = within // size, jnp.zeros_like(column)
        for index, partner in enumerate(partners_of(count)):
            source = jnp.where(spot == index, partner, source)
        natural = source * size + lax.rem(within, size)
    else:
        natural = jnp.bitwise_xor(within, lax.axis_index("qb") * (dim // 2))
    picked = jnp.where(row == natural + (column - within), 1.0, 0.0).astype(BF16)
    return bf_dot(matrix, picked).astype(BF16)


def prepare_kernel(low, sections, count, bits_ref, gates_ref, low_ref, *refs):
    *targets, held, wides, sems = refs
    copies = {}
    for gate in [gate for section in sections for _, _, parts in section for _, gates in parts for gate in gates] + low:
        copies[gate] = pltpu.make_async_copy(gates_ref.at[gate, bits_ref[gate]], held.at[gate], sems.at[gate])
        copies[gate].start()
    dim = held.shape[-1]

    def product(gates):
        for gate in gates:
            copies.pop(gate).wait()
        real, imag = held[gates[0], 0], held[gates[0], 1]
        for gate in gates[1:]:
            column = pair_dot(block(held[gate, 0], held[gate, 1]), jnp.concatenate([real, imag], axis=0))
            real, imag = column[:dim], column[dim:]
        return real, imag

    def joined(wide, base, parts):
        wide[...] = jnp.zeros(wide.shape, F32)
        for index, (offset, gates) in enumerate(parts):
            real, imag = product(gates)
            for t in range(2):
                at = pl.ds(t * dim, dim) if offset == base else pl.ds(t, dim, stride=2)
                if index == 0:
                    wide[0, t, at, :] = real
                    wide[1, t, at, :] = imag
                else:
                    x = jnp.concatenate(
                        [jnp.concatenate([wide[p, c, at, :] for c in range(2)], axis=1) for p in range(2)], axis=0
                    )
                    y = pair_dot(block(real, imag), x)
                    for p in range(2):
                        for c in range(2):
                            wide[p, c, at, :] = y[p * dim : (p + 1) * dim, c * dim : (c + 1) * dim]
        return [jnp.concatenate([wide[p, 0], wide[p, 1]], axis=1) for p in range(2)]

    for number, section in enumerate(sections):
        weights, targets = targets[: len(section)], targets[len(section) :]
        for target, (base, _, parts) in zip(weights, section):
            high, rest = split(block(*(joined(wides.at[number], base, parts) if len(parts) > 1 else product(parts[0][1]))))
            if number != 1 and target is weights[0]:
                high, rest = relative(high, number, count), relative(rest, number, count)
            target[...] = jnp.concatenate([high, rest, high], axis=1)
    real, imag = product(low)
    high, rest = split(block(real.T, -imag.T))
    low_ref[...] = jnp.concatenate([high, rest, high], axis=0)


def distances_of(count):
    half = count // 2
    far, near = list(range(count - 1, half - 1, -1)), list(range(half - 1, 0, -1))
    order = [0]
    while far or near:
        order += sorted(far[:2]) + sorted(near[:2])
        far, near = far[2:], near[2:]
    return order


def partners_of(count):
    me, core = lax.axis_index("qa"), lax.axis_index("qb")
    return [
        jnp.bitwise_xor(me, jnp.bitwise_xor(distance, core) if distance > 1 else distance)
        for distance in distances_of(count)
    ]


def split_kernel(x_ref, *outs):
    me, _, *dests = partners_of(len(outs) + 1)
    for dest, out_ref in zip([me, *dests], outs):
        out_ref[...] = x_ref[dest]


def apply_stage(weights_ref, starts, load, store):
    dim = weights_ref.shape[0] // 2
    for pair in range(0, len(starts), 2):
        group = starts[pair : pair + 2]
        x = jnp.concatenate(
            [jnp.concatenate([load(part, start) for start in group], axis=1) for part in range(2)], axis=0
        )
        high, rest = split(x)
        y = bf_dot(weights_ref[...], jnp.concatenate([rest, high, high], axis=0))
        lanes = y.shape[1] // len(group)
        for part in range(2):
            for place, start in enumerate(group):
                store(part, start, y[part * dim : (part + 1) * dim, place * lanes : (place + 1) * lanes])


def stage_starts(stage, lane_bits, rows):
    base, bits, _ = stage
    dim, stride = 2**bits, 2 ** (base - lane_bits)
    return dim, stride, [h * dim * stride + l for h in range(rows // (dim * stride)) for l in range(stride)]


def run_stage(stage, weights_ref, lane_bits, source, target=None, store=None):
    dim, stride, starts = stage_starts(stage, lane_bits, source.shape[1])

    def load(part, start):
        if not interleaved(stage):
            return source[part, pl.ds(start, dim, stride=stride), :]
        half = dim // 2
        return jnp.concatenate(
            [source[part, pl.ds(start + t * stride, half, stride=2 * stride), :] for t in range(2)], axis=0
        )

    def plain(part, start, value):
        target[part, pl.ds(start, dim, stride=stride), :] = value

    apply_stage(weights_ref, starts, load, store or plain)


def run_top_stage(stage, weights_ref, lane_bits, source, halves):
    rows = 2 * halves[0].shape[1]
    dim, stride, starts = stage_starts(stage, lane_bits, rows)

    def store(part, start, value):
        for t in range(2):
            halves[t][part, pl.ds(start, dim // 2, stride=stride), :] = value[t * dim // 2 : (t + 1) * dim // 2]

    def load(part, start):
        if not isinstance(source, tuple):
            return source[part, pl.ds(start, dim, stride=stride), :]
        return jnp.concatenate([half[part, pl.ds(start, dim // 2, stride=stride), :] for half in source], axis=0)

    apply_stage(weights_ref, starts, load, store)


def run_halves(stages, weights, lane_bits, halves, spares, last_store=None):
    for index, (stage, weights_ref) in enumerate(zip(stages, weights)):
        for t in range(2):
            store = None
            if last_store is not None and index == len(stages) - 1:
                store = functools.partial(last_store, t)
            run_stage(stage, weights_ref, lane_bits, halves[t], spares[t], store)
        halves, spares = spares, halves
    return halves


def low_gate(blocks, low_ref, whole):
    lanes = whole.shape[2]
    for spot, block_ref in blocks:
        size = block_ref.shape[0] // 2
        real = block_ref[pl.ds(0, size, stride=2), :]
        imag = block_ref[pl.ds(1, size, stride=2), :]
        high, rest = split(jnp.concatenate([real, imag], axis=1))
        y = bf_dot(jnp.concatenate([rest, high, high], axis=1), low_ref[...])
        whole[0, pl.ds(spot * size, size), :] = y[:, :lanes]
        whole[1, pl.ds(spot * size, size), :] = y[:, lanes:]


def low_kernel(spots, *refs):
    *blocks, low_ref, whole = refs
    low_gate(zip(spots, blocks), low_ref, whole)


def first_kernel(stages, lane_bits, count, spots, *refs):
    _, *blocks = refs[: 1 + len(spots)]
    refs = refs[1 + len(spots) :]
    low_ref, weights, refs = refs[0], refs[1 : 1 + len(stages)], refs[1 + len(stages) :]
    outs, (whole, *halves) = refs[:count], refs[count:]
    low_gate(zip(spots, blocks), low_ref, whole)
    run_top_stage(stages[0], weights[0], lane_bits, whole, halves[:2])
    done = run_halves(stages[1:], weights[1:], lane_bits, halves[:2], halves[2:])
    tops, mids, _, inner, _ = outs[0].shape
    dests = partners_of(count)
    for top in range(tops):
        for dest, out_ref in zip(dests, outs):
            for mid in range(mids):
                start = pl.multiple_of((mid * count + dest) * inner, inner)
                for part in range(2):
                    out_ref[top, mid, part] = done[top][part, pl.ds(start, inner), :]


def second_kernel(stages, lane_bits, count, stays, *refs):
    blocks, weights, refs = refs[:count], refs[count : count + len(stages)], refs[count + len(stages) :]
    out_ref, one, two = refs
    core = lax.axis_index("qb")
    top = core if stays else 1 - core
    for source, block_ref in zip(partners_of(count), blocks):
        _, mids, _, inner, _ = block_ref.shape
        for mid in range(mids):
            start = pl.multiple_of((mid * count + source) * inner, inner)
            for part in range(2):
                one[part, pl.ds(start, inner), :] = block_ref[top, mid, part]
    for index, (stage, weights_ref) in enumerate(zip(stages, weights)):
        run_stage(stage, weights_ref, lane_bits, one, out_ref if index == len(stages) - 1 else two)
        one, two = two, one


def third_kernel(stages, lane_bits, kept_ref, came_ref, *refs):
    weights, (out_ref, *halves, sems) = refs[: len(stages)], refs[len(stages) :]
    results = halves[4:]
    half = kept_ref.shape[1]
    run_top_stage(stages[0], weights[0], lane_bits, (kept_ref, came_ref), halves[:2])
    done = run_halves(stages[1:-1], weights[1:-1], lane_bits, halves[:2], halves[2:4])
    copies = []
    for t in range(2):
        dim, stride, _ = stage_starts(stages[-1], lane_bits, half)

        def store(part, start, value, t=t):
            results[t][pl.ds(2 * start + part, dim, stride=2 * stride), :] = value

        run_stage(stages[-1], weights[-1], lane_bits, done[t], store=store)
        size = 2 * half // PIECES
        for piece in range(PIECES):
            to = out_ref.at[pl.ds(t * 2 * half + piece * size, size)]
            copies.append(
                pltpu.make_async_copy(results[t].at[pl.ds(piece * size, size)], to, sems.at[t * PIECES + piece])
            )
            copies[-1].start()
    for copy in copies:
        copy.wait()


def call(kernel, name, out_shapes, in_specs, scratch, matmuls, *operands, limit=VMEM_LIMIT, out_spec=None, aliases=None):
    many = isinstance(out_shapes, tuple)
    vmem = out_spec or pl.BlockSpec(memory_space=pltpu.VMEM)
    return pl.pallas_call(
        kernel,
        out_shape=out_shapes,
        in_specs=in_specs,
        out_specs=(vmem,) * len(out_shapes) if many else vmem,
        scratch_shapes=scratch,
        input_output_aliases=aliases or {},
        compiler_params=pltpu.CompilerParams(vmem_limit_bytes=limit),
        cost_estimate=pl.CostEstimate(
            flops=int(matmuls * 3 * 2 * 256 * 256 * 1024), bytes_accessed=4 * 2**20, transcendentals=0
        ),
        name=name,
    )(*operands)


def per_device(state, gate_terms, path_bits):
    amps_local = state.shape[1]
    local_bits = amps_local.bit_length() - 1
    dim = gate_terms.shape[-1]
    gate_bits = dim.bit_length() - 1
    lanes, lane_bits = dim, gate_bits
    rows = amps_local // lanes
    qa = lax.axis_size("qa")
    qb = lax.axis_size("qb")
    low, sections = plan_gates(local_bits, gate_bits)
    sections = [join_windows(section, gate_bits) for section in sections]
    order = 2 * dim
    vmem = pl.BlockSpec(memory_space=pltpu.VMEM)
    hbm = pl.BlockSpec(memory_space=pltpu.HBM)
    shape = jax.ShapeDtypeStruct

    state = with_layout_constraint(state.reshape(2, rows, lanes), Layout(major_to_minor=(1, 0, 2)))
    state = state.swapaxes(0, 1).reshape(qa, 2 * rows // qa, lanes)
    blocks = call(
        split_kernel,
        "split_state",
        (shape((2 * rows // qa, lanes), F32),) * (qa - 1),
        [vmem],
        [],
        0,
        state,
    )

    first = lax.dynamic_index_in_dim(state, partners_of(qa)[1], 0, keepdims=False)
    blocks = [blocks[0], first, *blocks[1:]]

    def exchange(blocks):
        came = [blocks[0]]
        for distance, piece in zip(distances_of(qa)[1:], blocks[1:]):
            pairs = []
            for i in range(qa):
                for core in range(qb):
                    to = i ^ distance ^ (core if distance > 1 else 0)
                    pairs.append((i * qb + core, to * qb + core))
            came.append(lax.ppermute(piece, ("qa", "qb"), pairs))
        return came

    blocks = exchange(blocks)
    low_w, *weights = call(
        functools.partial(prepare_kernel, low, sections, qa),
        "prepare_gates",
        (shape((3 * order, order), BF16),)
        + tuple(shape((2 * 2**bits, 6 * 2**bits), BF16) for section in sections for _, bits, _ in section),
        [pl.BlockSpec(memory_space=pltpu.SMEM), hbm],
        [
            pltpu.VMEM((gate_terms.shape[0], 2, dim, dim), F32),
            pltpu.VMEM((len(sections), 2, 2, 2 * dim, dim), F32),
            pltpu.SemaphoreType.DMA((gate_terms.shape[0],)),
        ],
        8,
        path_bits,
        gate_terms,
        limit=LARGE_VMEM,
    )
    counts = [len(section) for section in sections]
    weights = [weights[: counts[0]], weights[counts[0] : counts[0] + counts[1]], weights[counts[0] + counts[1] :]]
    inner = rows // (qa * qa)
    half = pltpu.VMEM((2, rows // 2, lanes), F32)
    early, late = list(range(qa - 3)), list(range(qa - 3, qa))
    planes = shape((2, rows, lanes), F32)
    begun = call(
        functools.partial(low_kernel, early),
        "low_gate_early",
        planes,
        [vmem] * (len(early) + 1),
        [],
        1,
        *[blocks[spot] for spot in early],
        low_w,
    )
    *blocks, _ = call(
        functools.partial(first_kernel, sections[0], lane_bits, qa, late),
        "first_section",
        (shape((qb, qa // qb, 2, inner, lanes), F32),) * qa + (planes,),
        [vmem] * (2 + len(late) + counts[0]),
        [half] * 4,
        5,
        begun,
        *[blocks[spot] for spot in late],
        low_w,
        *weights[0],
        aliases={0: qa},
    )
    blocks = exchange(blocks)
    halves = []
    for stays in (False, True):
        halves.append(
            call(
                functools.partial(second_kernel, sections[1], lane_bits, qa, stays),
                "second_section_kept" if stays else "second_section_sent",
                shape((2, rows // qb, lanes), F32),
                [vmem] * (qa + counts[1]),
                [half] * 2,
                1.5,
                *blocks,
                *weights[1],
            )
        )
        if not stays:
            came = lax.ppermute(halves[0], "qb", [(i, 1 - i) for i in range(qb)])
    final = call(
        functools.partial(third_kernel, sections[2], lane_bits),
        "third_section",
        shape((2 * rows, lanes), F32),
        [vmem] * (2 + counts[2]),
        [half] * 4 + [pltpu.VMEM((rows, lanes), F32)] * 2 + [pltpu.SemaphoreType.DMA((2 * PIECES,))],
        4,
        halves[1],
        came,
        *weights[2],
        out_spec=hbm,
    )
    return final.reshape(rows, 2, lanes).swapaxes(0, 1).reshape(2, amps_local)


def solution(mesh):
    return jax.shard_map(
        per_device,
        mesh=mesh,
        in_specs=(P(None, ("paths", "qa", "qb")), P(), P("paths")),
        out_specs=P(None, ("paths", "qa", "qb")),
        check_vma=False,
    )
```
